32 devices in a mesh: seq: 16 (over z, x, core), head: 2 (over y).
Axes of the slice: x: 2, y: 2, z: 4, core: 2. Of those that a mesh axis runs over, the one named last changes fastest.
Arguments:
- tokens: bfloat16 [2048, 768], P(('seq', 'head')), may hold values from -6 to 6
- out_grad: bfloat16 [2048, 768], P(('seq', 'head')), may hold values from -6 to 6
- short_lengths: int32 [3], replicated, may hold values from 1 to 512, 1024 in all
- attn_gain: bfloat16 [768], P(('seq', 'head')), may hold values from 0.099609375 to 1.8984375
- qkv_weight: bfloat16 [768, 3, 768], P('seq', None, 'head'), may hold values from -0.21875 to 0.21875
- out_weight: bfloat16 [768, 768], P('head', 'seq'), may hold values from -2.5 to 2.5
- mlp_gain: bfloat16 [768], P(('seq', 'head')), may hold values from 0.099609375 to 1.8984375
- in_weight: bfloat16 [768, 2, 1152], P('seq', None, 'head'), may hold values from -0.21875 to 0.21875
- down_weight: bfloat16 [1152, 768], P('head', 'seq'), may hold values from -0.1875 to 0.1875
Outputs:
- mixed: bfloat16 [2048, 768], P(('seq', 'head'))
- tokens_grad: float32 [2048, 768], P(('seq', 'head'))
- attn_gain_grad: float32 [768], P(('seq', 'head'))
- qkv_weight_grad: float32 [768, 3, 768], P('seq', None, 'head')
- out_weight_grad: float32 [768, 768], P('head', 'seq')
- mlp_gain_grad: float32 [768], P(('seq', 'head'))
- in_weight_grad: float32 [768, 2, 1152], P('seq', None, 'head')
- down_weight_grad: float32 [1152, 768], P('head', 'seq')
The draws below stay inside these ranges and needn't reach their ends.
Inputs may be any that keep to these rules, and one draw needn't show every extreme that they name: `short_lengths`: the long document 0 fills the first 1024 rows; the short documents follow in this order, their lengths sum to 1024, and one of them has exactly 512 tokens.
All inputs are finite; a program needn't handle non-finite values.
Results may differ from the reference program's by a relative error of at most 0.02.
Values may be sent and summed in bfloat16 or wider, within the bound.
A program may use at most 192 MiB of HBM per device.

```python
import math
import jax
import jax.numpy as jnp
import numpy as np
from jax import lax

D = 768
HEADS = 12
HEAD_DIM = 64
FF = 1152
TOKENS = 2048
NSHORT = 3
SHORT_TOTAL = 1024
SHORT_MOST = 512


def block_levels(rng, extent, cuts, smallest, largest):
    def one(axis_at, blocks):
        heights = jax.random.uniform(jax.random.fold_in(jax.random.fold_in(rng, 6), axis_at), (blocks,), jnp.float32, smallest / len(cuts), largest / len(cuts))
        return jnp.repeat(jnp.exp(heights), extent[axis_at] // blocks).reshape((-1,) + (1,) * (len(extent) - axis_at - 1))

    loudness = one(*cuts[0])
    for cut in cuts[1:]:
        loudness = loudness * one(*cut)
    return loudness


def profile(amount, total, reach, slope):
    loads = [(1 << 20) // math.isqrt(grade ** slope) + 1 for grade in range(2, amount + 1)]
    spare, holding = total - reach - (amount - 1), [1] * (amount - 1)
    while spare > 0:
        free = [i for i in range(amount - 1) if holding[i] < reach]
        pool, remaining = sum([loads[i] for i in free]), spare
        for i in free:
            extra = min(reach - holding[i], max(1, remaining * loads[i] // pool), spare)
            holding[i] = holding[i] + extra
            spare = spare - extra
    return np.array([reach] + holding)


def uneven(own_key, number_of, total, bound, lean):
    if number_of == 2:
        one = jax.random.randint(own_key, (), max(1, total - bound), min(bound, total - 1) + 1)
        return jnp.stack([one, total - one])
    sizes = jnp.asarray(profile(number_of, total, bound, lean), jnp.int32)
    couples = (number_of - 1) // 2
    source_of, sink = sizes[1:1 + 2 * couples:2], sizes[2:2 + 2 * couples:2]
    margin = jnp.minimum(source_of - 1, bound - sink)
    moved = jax.random.randint(jax.random.fold_in(own_key, 1), (couples,), 0, 1 << 20) % (margin + 1)
    sizes = sizes.at[1:1 + 2 * couples:2].set(source_of - moved).at[2:2 + 2 * couples:2].set(sink + moved)
    return sizes[jax.random.permutation(jax.random.fold_in(own_key, 2), number_of)]


def scatter_about(stream_key, extent, width, bound, pieces=(), kind=jnp.bfloat16):
    drawn = width * jax.random.normal(stream_key, extent, jnp.float32)
    if pieces:
        drawn = drawn * block_levels(stream_key, extent, pieces, -0.22, 0.18)
    return jnp.clip(drawn, -bound, bound).astype(kind)


def setup_inputs(seed: int = 0) -> dict:
    keys = jax.random.split(jax.random.key(seed), 10)
    tokens = scatter_about(keys[0], (TOKENS, D), 1.0, 6.0, ((0, 32),))
    out_grad = scatter_about(keys[1], (TOKENS, D), 1.0, 6.0, ((0, 32),))
    short_lengths = uneven(keys[2], NSHORT, SHORT_TOTAL, SHORT_MOST, 0).astype(jnp.int32)
    attn_gain = jnp.clip(1.0 + 0.18 * jax.random.normal(keys[3], (D,), jnp.float32), 0.099609375, 1.8984375).astype(jnp.bfloat16)
    qkv_weight = scatter_about(keys[4], (D, 3, D), D ** -0.5, 0.21875, ((0, 16), (2, 2)))
    out_weight = scatter_about(keys[5], (D, D), (max(1, 16 * D // TOKENS)) ** -0.5, 2.5, ((0, 2), (1, 16)))
    mlp_gain = jnp.clip(1.0 + 0.18 * jax.random.normal(keys[6], (D,), jnp.float32), 0.099609375, 1.8984375).astype(jnp.bfloat16)
    in_weight = scatter_about(keys[7], (D, 2, FF), D ** -0.5, 0.21875, ((0, 16), (2, 2)))
    down_weight = scatter_about(keys[8], (FF, D), FF ** -0.5, 0.1875, ((0, 2), (1, 16)))
    return {"tokens": tokens, "out_grad": out_grad, "short_lengths": short_lengths, "attn_gain": attn_gain, "qkv_weight": qkv_weight, "out_weight": out_weight, "mlp_gain": mlp_gain, "in_weight": in_weight, "down_weight": down_weight}


@jax.custom_vjp
def low(v):
    return lax.optimization_barrier(v.astype(jnp.bfloat16)).astype(jnp.float32)

@jax.custom_vjp
def low_back(v):
    return v

def low_keep(v):
    return (low(v), None)

def low_pass(kept, grad):
    return (grad,)

def back_keep(v):
    return (v, None)

def back_low(kept, grad):
    return (low(grad),)
low.defvjp(low_keep, low_pass)
low_back.defvjp(back_keep, back_low)
norm_eps = 1e-05
rope_base = 160000.0
score_scale = 0.125
masked_low = -1e+30

def layer_norm(inputs, gain_vector):
    row_mean = lax.optimization_barrier(jnp.mean(inputs, axis=-1, keepdims=True))
    centred = inputs - row_mean
    spread = lax.optimization_barrier(jnp.mean(centred * centred, axis=-1, keepdims=True))
    return centred * lax.rsqrt(spread + norm_eps) * gain_vector

def doc_layout(short_lengths, row_ids, total_rows):
    lengths_int = short_lengths.astype(jnp.int32)
    long_end = (total_rows - jnp.sum(lengths_int)).astype(jnp.int32)
    before = (jnp.cumsum(lengths_int).astype(jnp.int32) - lengths_int).astype(jnp.int32)
    bounds = (long_end + before).astype(jnp.int32)
    passed = row_ids[:, None] >= bounds[None, :]
    doc_ids = lax.optimization_barrier(jnp.sum(passed.astype(jnp.int32), axis=1)).astype(jnp.int32)
    starts = lax.optimization_barrier(jnp.max(jnp.where(passed, bounds[None, :], jnp.zeros_like(bounds)[None, :]), axis=1)).astype(jnp.int32)
    return (doc_ids, (row_ids - starts).astype(jnp.int32))

def rope_tables(positions):
    steps_half = jnp.arange(HEAD_DIM // 2, dtype=jnp.float32)
    inverse = jnp.exp(steps_half * (-2.0 * math.log(rope_base) / HEAD_DIM))
    angles = positions.astype(jnp.float32)[:, None] * inverse[None, :]
    cosines = jnp.cos(angles)
    sines = jnp.sin(angles)
    return (jnp.concatenate([cosines, cosines], axis=1), jnp.concatenate([sines, sines], axis=1))

def rotate(heads_in, cosines, sines):
    half_dim = heads_in.shape[-1] // 2
    turned = jnp.concatenate([-heads_in[..., half_dim:], heads_in[..., :half_dim]], axis=-1)
    return heads_in * cosines[:, None, :] + turned * sines[:, None, :]

def attend(queries, key_rows, value_rows, doc_ids):
    block_size = math.gcd(TOKENS, 128)
    block_total = TOKENS // block_size
    query_parts = queries.reshape(block_total, block_size, HEADS, HEAD_DIM)
    doc_parts = doc_ids.reshape(block_total, block_size)

    def query_block(operands):
        query_part, doc_part = operands
        scores = low_back(jnp.einsum('qhd,khd->hqk', query_part, key_rows, precision=lax.Precision.HIGHEST) * score_scale)
        same_doc = doc_part[None, :, None] == doc_ids[None, None, :]
        scores = jnp.where(same_doc, scores, masked_low)
        row_max = lax.optimization_barrier(jnp.max(scores, axis=2, keepdims=True))
        expo = jnp.exp(scores - row_max)
        weights = expo / lax.optimization_barrier(jnp.sum(expo, axis=2, keepdims=True))
        return jnp.einsum('hqk,khd->qhd', low(weights), value_rows, precision=lax.Precision.HIGHEST)
    result = lax.map(jax.checkpoint(query_block), (query_parts, doc_parts))
    return result.reshape(TOKENS, HEADS, HEAD_DIM)

def forward(tokens, attn_gain, qkv_weight, out_weight, mlp_gain, in_weight, down_weight, doc_ids, cosines, sines):
    normed = low(layer_norm(tokens, attn_gain))
    projected = low_back(jnp.einsum('td,dgc->tgc', normed, qkv_weight, precision=lax.Precision.HIGHEST))
    queries = low(rotate(projected[:, 0].reshape(TOKENS, HEADS, HEAD_DIM), cosines, sines))
    key_rows = low(rotate(projected[:, 1].reshape(TOKENS, HEADS, HEAD_DIM), cosines, sines))
    value_rows = low(projected[:, 2].reshape(TOKENS, HEADS, HEAD_DIM))
    attended = low_back(low(attend(queries, key_rows, value_rows, doc_ids).reshape(TOKENS, D)))
    resid = tokens + low_back(jnp.dot(attended, out_weight, precision=lax.Precision.HIGHEST))
    normed_two = low(layer_norm(resid, mlp_gain))
    gate_up = low_back(jnp.einsum('td,dgf->tgf', normed_two, in_weight, precision=lax.Precision.HIGHEST))
    hidden = low(jax.nn.gelu(gate_up[:, 0], approximate=False) * gate_up[:, 1])
    return resid + low_back(jnp.dot(hidden, down_weight, precision=lax.Precision.HIGHEST))

def reference(tokens, out_grad, short_lengths, attn_gain, qkv_weight, out_weight, mlp_gain, in_weight, down_weight):
    row_ids = jnp.arange(TOKENS, dtype=jnp.int32)
    doc_ids, positions = doc_layout(short_lengths, row_ids, TOKENS)
    cosines, sines = rope_tables(positions)

    def forward_of(tokens_in, gain_one, qkv_in, out_in, gain_two, in_in, down_in):
        return forward(tokens_in, gain_one, qkv_in, out_in, gain_two, in_in, down_in, doc_ids, cosines, sines)
    mixed, pullback = jax.vjp(forward_of, tokens.astype(jnp.float32), attn_gain.astype(jnp.float32), qkv_weight.astype(jnp.float32), out_weight.astype(jnp.float32), mlp_gain.astype(jnp.float32), in_weight.astype(jnp.float32), down_weight.astype(jnp.float32))
    grads = pullback(out_grad.astype(jnp.float32))
    return (mixed.astype(jnp.bfloat16), grads[0], grads[1], grads[2], grads[3], grads[4], grads[5], grads[6])
```

```python
import math

import jax
import jax.numpy as jnp
from jax import lax
from jax.experimental import pallas as pl
from jax.experimental.pallas import tpu as pltpu
from jax.sharding import PartitionSpec as P

HEAD_DIM = 64


norm_eps = 1e-05
rope_base = 160000.0
score_scale = 0.125
masked_low = -1e30


def layer_norm(inputs, gain_vector):
    row_mean = jnp.mean(inputs, axis=-1, keepdims=True)
    centred = inputs - row_mean
    spread = jnp.mean(centred * centred, axis=-1, keepdims=True)
    return centred * lax.rsqrt(spread + norm_eps) * gain_vector


def doc_layout(short_lengths, row_ids, total_rows):
    long_end = total_rows - jnp.sum(short_lengths)
    before = jnp.cumsum(short_lengths) - short_lengths
    bounds = long_end + before
    passed = row_ids[:, None] >= bounds[None, :]
    doc_ids = jnp.sum(passed.astype(jnp.int32), axis=1)
    starts = jnp.max(jnp.where(passed, bounds[None, :], jnp.zeros_like(bounds)[None, :]), axis=1)
    return (doc_ids, row_ids - starts)


def rope_tables(positions):
    steps_half = jnp.arange(HEAD_DIM // 2, dtype=jnp.float32)
    inverse = jnp.exp(steps_half * (-2.0 * math.log(rope_base) / HEAD_DIM))
    angles = positions.astype(jnp.float32)[:, None] * inverse[None, :]
    cosines = jnp.cos(angles)
    sines = jnp.sin(angles)
    return (jnp.concatenate([cosines, cosines], axis=1), jnp.concatenate([sines, sines], axis=1))


def rotate(heads_in, cosines, sines):
    half_dim = heads_in.shape[-1] // 2
    turned = jnp.concatenate([-heads_in[..., half_dim:], heads_in[..., :half_dim]], axis=-1)
    return heads_in * cosines[:, None, :] + turned * sines[:, None, :]


def block_length(row_count, shard_rows):
    shards = row_count // shard_rows
    return shard_rows * math.gcd(shards, max(1, 1024 // shard_rows))


def over_blocks(carry_state, row_count, shard_rows, block_fn):
    block_size = block_length(row_count, shard_rows)

    def block_step(inner_state, block_index):
        return (block_fn(inner_state, block_index * block_size, block_size), None)

    carry_state, _ = lax.scan(
        block_step, carry_state, jnp.arange(row_count // block_size, dtype=jnp.int32)
    )
    return carry_state


def group_peers(axes, seq_count, head_count):
    seq, head = lax.axis_index("seq"), lax.axis_index("head")
    if axes == "seq":
        return seq, [((seq + k) % seq_count, head) for k in range(1, seq_count)]
    if axes == "head":
        return head, [(seq, (head + k) % head_count) for k in range(1, head_count)]
    mine = seq * head_count + head
    total = seq_count * head_count
    others = [(mine + k) % total for k in range(1, total)]
    return mine, [(other // head_count, other % head_count) for other in others]


def peer_index(axes, peer, head_count):
    if axes == "seq":
        return peer[0]
    if axes == "head":
        return peer[1]
    return peer[0] * head_count + peer[1]


def exchange(operands, groups, spread, collective_id):
    seq_count, head_count = lax.axis_size("seq"), lax.axis_size("head")
    size_of = {"seq": seq_count, "head": head_count, "all": seq_count * head_count}
    count = len(operands)
    widest = "all" if "all" in groups else groups[0]
    most = max(size_of[g] for g in groups)

    def kernel(*refs):
        sources, results = refs[:count], refs[count : 2 * count]
        send_sem, recv_sem, own_sem = refs[2 * count :]
        barrier = pltpu.get_barrier_semaphore()
        _, everyone = group_peers(widest, seq_count, head_count)
        for peer in everyone:
            pl.semaphore_signal(barrier, inc=1, device_id=peer, device_id_type=pl.DeviceIdType.MESH)
        pl.semaphore_wait(barrier, len(everyone))
        copies = []
        for i in range(count):
            mine, peers = group_peers(groups[i], seq_count, head_count)
            own = pltpu.make_async_copy(
                sources[i].at[mine] if spread[i] else sources[i], results[i].at[mine], own_sem.at[i]
            )
            own.start()
            for k, peer in enumerate(peers):
                there = peer_index(groups[i], peer, head_count)
                copy = pltpu.make_async_remote_copy(
                    src_ref=sources[i].at[there] if spread[i] else sources[i],
                    dst_ref=results[i].at[mine],
                    send_sem=send_sem.at[i, k],
                    recv_sem=recv_sem.at[i, k],
                    device_id=peer,
                    device_id_type=pl.DeviceIdType.MESH,
                )
                copy.start()
                copies.append(copy)
            copies.append(own)
        for copy in copies:
            copy.wait()

    shapes = [
        jax.ShapeDtypeStruct(o.shape if s else (size_of[g],) + o.shape, o.dtype)
        for o, g, s in zip(operands, groups, spread)
    ]
    return pl.pallas_call(
        kernel,
        out_shape=shapes,
        in_specs=[pl.BlockSpec(memory_space=pltpu.VMEM)] * count,
        out_specs=[pl.BlockSpec(memory_space=pltpu.VMEM)] * count,
        scratch_shapes=[
            pltpu.SemaphoreType.DMA((count, most)),
            pltpu.SemaphoreType.DMA((count, most)),
            pltpu.SemaphoreType.DMA((count,)),
        ],
        compiler_params=pltpu.CompilerParams(
            collective_id=collective_id, has_side_effects=True, vmem_limit_bytes=56 << 20
        ),
    )(*operands)


def scores_of(queries, key_part):
    return (
        jnp.einsum("qhd,khd->hqk", queries, key_part, preferred_element_type=jnp.float32)
        * score_scale
    )


def block_grads(queries, grad_rows, log_sums, row_dots, key_part, value_part, same_doc):
    scores = scores_of(queries, key_part)
    softmax_part = jnp.where(same_doc, jnp.exp(scores - log_sums[:, :, None]), 0.0)
    grad_probs = jnp.einsum(
        "qhd,khd->hqk", grad_rows, value_part, preferred_element_type=jnp.float32
    )
    dscore = (softmax_part * (grad_probs - row_dots[:, :, None])).astype(jnp.bfloat16)
    return (softmax_part, dscore)


def on_device(
    tokens,
    out_grad,
    short_lengths,
    attn_gain,
    qkv_weight,
    out_weight,
    mlp_gain,
    in_weight,
    down_weight,
):
    half_rows = tokens.shape[0]
    head_count = lax.axis_size("head")
    seq_count = lax.axis_size("seq")
    block_rows = half_rows * head_count
    total_rows = block_rows * seq_count
    local_ids = lax.axis_index("seq") * block_rows + jnp.arange(block_rows, dtype=jnp.int32)
    local_docs, local_pos = doc_layout(short_lengths, local_ids, total_rows)
    cosines, sines = rope_tables(local_pos)
    small = seq_count * head_count <= 32
    if small:
        gain_tile = jnp.zeros((16, 128), jnp.bfloat16)
        gain_tile = gain_tile.at[0, : attn_gain.shape[0]].set(attn_gain)
        gain_tile = gain_tile.at[1, : mlp_gain.shape[0]].set(mlp_gain)
        gain_tiles, qkv_full, out_full, in_parts, down_parts = exchange(
            (gain_tile, qkv_weight.transpose(1, 0, 2), out_weight, in_weight.transpose(1, 0, 2), down_weight),
            ("all", "seq", "seq", "all", "all"),
            (False,) * 5,
            0,
        )
        gain_first = gain_tiles[:, 0, : attn_gain.shape[0]].reshape(-1)
        gain_second = gain_tiles[:, 1, : mlp_gain.shape[0]].reshape(-1)
        qkv_full = qkv_full.transpose(0, 2, 1, 3).reshape(-1, 3, qkv_weight.shape[2])
        out_full = out_full.transpose(1, 0, 2).reshape(out_weight.shape[0], -1)
        in_parts = in_parts.transpose(0, 2, 1, 3)
    else:
        qkv_full, out_full = (
            lax.all_gather(qkv_weight, "seq", axis=0, tiled=True),
            lax.all_gather(out_weight, "seq", axis=1, tiled=True),
        )
        gain_first, gain_second, in_parts, down_parts = (
            lax.all_gather(attn_gain, ("seq", "head"), axis=0, tiled=True),
            lax.all_gather(mlp_gain, ("seq", "head"), axis=0, tiled=True),
            lax.all_gather(in_weight[None], ("seq", "head"), axis=0, tiled=True),
            lax.all_gather(down_weight[None], ("seq", "head"), axis=0, tiled=True),
        )
    in_parts = in_parts.reshape(seq_count, head_count, in_weight.shape[0], 2, in_weight.shape[2])
    down_parts = down_parts.reshape(
        seq_count, head_count, down_weight.shape[0], down_weight.shape[1]
    )
    heads_here = qkv_full.shape[2] // HEAD_DIM
    inputs = tokens.astype(jnp.float32)
    gain_one = gain_first.astype(jnp.float32)
    normed = layer_norm(inputs, gain_one).astype(jnp.bfloat16)
    normed_block = lax.all_gather(normed, "head", axis=0, tiled=True)
    projected = jnp.einsum(
        "rd,dgc->rgc", normed_block, qkv_full, preferred_element_type=jnp.float32
    )
    queries = rotate(
        projected[:, 0].reshape(block_rows, heads_here, HEAD_DIM), cosines, sines
    ).astype(jnp.bfloat16)
    key_rows = rotate(
        projected[:, 1].reshape(block_rows, heads_here, HEAD_DIM), cosines, sines
    ).astype(jnp.bfloat16)
    value_flat = projected[:, 2].astype(jnp.bfloat16)
    value_rows = value_flat.reshape(block_rows, heads_here, HEAD_DIM)
    key_flat = key_rows.reshape(block_rows, -1)
    query_flat = queries.reshape(block_rows, -1)

    def forward_fold(carry_state, portion):
        piece_keys, piece_values = portion

        def forward_block(inner_state, block_begin, block_size):
            running_max, running_sum, weighted = inner_state
            key_part = lax.dynamic_slice_in_dim(piece_keys, block_begin, block_size, 0).reshape(
                block_size, heads_here, HEAD_DIM
            )
            value_part = lax.dynamic_slice_in_dim(piece_values, block_begin, block_size, 0).reshape(
                block_size, heads_here, HEAD_DIM
            )
            other_docs, _ = doc_layout(
                short_lengths, block_begin + jnp.arange(block_size, dtype=jnp.int32), total_rows
            )
            same_doc = (local_docs[:, None] == other_docs[None, :])[None]
            scores = scores_of(queries, key_part)
            new_max = jnp.maximum(
                running_max, jnp.max(jnp.where(same_doc, scores, masked_low), axis=2)
            )
            factor = jnp.exp(running_max - new_max)
            softmax_part = jnp.where(same_doc, jnp.exp(scores - new_max[:, :, None]), 0.0)
            running_sum = running_sum * factor + jnp.sum(softmax_part, axis=2)
            weighted = weighted * factor.T[:, :, None] + jnp.einsum(
                "hqk,khd->qhd",
                softmax_part.astype(jnp.bfloat16),
                value_part,
                preferred_element_type=jnp.float32,
            )
            return (new_max, running_sum, weighted)

        return over_blocks(carry_state, piece_keys.shape[0], block_rows, forward_block)

    zeros_three = jnp.zeros((block_rows, heads_here, HEAD_DIM), jnp.float32)
    start_state = (
        jnp.full((heads_here, block_rows), masked_low, jnp.float32),
        jnp.zeros((heads_here, block_rows), jnp.float32),
        zeros_three,
    )
    if small:
        all_keys, all_values, all_queries = (
            a.reshape(-1, a.shape[2])
            for a in exchange((key_flat, value_flat, query_flat), ("seq",) * 3, (False,) * 3, 1)
        )
    else:
        all_keys, all_values, all_queries = (
            lax.all_gather(a, "seq", axis=0, tiled=True) for a in (key_flat, value_flat, query_flat)
        )
    running_max, running_sum, weighted = forward_fold(start_state, (all_keys, all_values))
    attended = weighted / running_sum.T[:, :, None]
    log_sums = running_max + jnp.log(running_sum)
    attended_low = attended.reshape(block_rows, -1).astype(jnp.bfloat16)
    branch = jnp.dot(attended_low, out_full, preferred_element_type=jnp.float32)
    branch_rows = lax.psum_scatter(
        branch.astype(jnp.bfloat16), "head", scatter_dimension=0, tiled=True
    ).astype(jnp.float32)
    resid = inputs + branch_rows
    gain_two = gain_second.astype(jnp.float32)
    normed_two = layer_norm(resid, gain_two).astype(jnp.bfloat16)
    normed_split = normed_two.reshape(half_rows, seq_count, -1)
    gate_up = jnp.einsum(
        "rse,shegf->rghf", normed_split, in_parts, preferred_element_type=jnp.float32
    ).reshape(half_rows, 2, -1)

    def activate(gate_part, up_part):
        return jax.nn.gelu(gate_part, approximate=False) * up_part

    hidden, activate_pull = jax.vjp(activate, gate_up[:, 0], gate_up[:, 1])
    hidden_low = hidden.astype(jnp.bfloat16)
    hidden_split = hidden_low.reshape(half_rows, head_count, -1)
    mlp_out = jnp.einsum(
        "rhf,shfe->rse", hidden_split, down_parts, preferred_element_type=jnp.float32
    ).reshape(half_rows, -1)
    mixed = (resid + mlp_out).astype(jnp.bfloat16)
    grad_out = out_grad.astype(jnp.float32)
    grad_split = out_grad.reshape(half_rows, seq_count, -1)
    grad_hidden = jnp.einsum(
        "rse,shfe->rhf", grad_split, down_parts, preferred_element_type=jnp.float32
    ).reshape(half_rows, -1)
    grad_gate, grad_up = activate_pull(grad_hidden)
    grad_gate_up = (
        jnp.stack([grad_gate, grad_up], axis=1)
        .astype(jnp.bfloat16)
        .reshape(half_rows, 2, head_count, -1)
    )
    down_grad = jnp.einsum(
        "rhf,rse->shfe", hidden_split, grad_split, preferred_element_type=jnp.float32
    ).reshape(seq_count * head_count, down_weight.shape[0], down_weight.shape[1])
    in_grad = jnp.einsum(
        "rse,rghf->shegf", normed_split, grad_gate_up, preferred_element_type=jnp.float32
    ).reshape(seq_count * head_count, in_weight.shape[0], 2, in_weight.shape[2])
    grad_normed_two = jnp.einsum(
        "rghf,shegf->rse", grad_gate_up, in_parts, preferred_element_type=jnp.float32
    ).reshape(half_rows, -1)
    _, norm_two_pull = jax.vjp(layer_norm, resid, gain_two)
    grad_resid_norm, gain_two_grad = norm_two_pull(grad_normed_two)
    grad_resid = grad_out + grad_resid_norm
    grad_branch = lax.all_gather(grad_resid.astype(jnp.bfloat16), "head", axis=0, tiled=True)
    out_grad_weight = jnp.einsum(
        "rc,rd->cd", attended_low, grad_branch, preferred_element_type=jnp.float32
    )
    grad_attended = jnp.einsum(
        "rd,cd->rc", grad_branch, out_full, preferred_element_type=jnp.float32
    ).astype(jnp.bfloat16)
    grad_three = grad_attended.reshape(block_rows, heads_here, HEAD_DIM)
    row_dots = jnp.sum(grad_three.astype(jnp.float32) * attended, axis=2).T
    if small:
        stats = jnp.zeros((16, block_rows), jnp.float32)
        stats = stats.at[:heads_here].set(log_sums).at[8 : 8 + heads_here].set(row_dots)
        all_grads, all_stats = exchange((grad_attended, stats), ("seq",) * 2, (False,) * 2, 2)
        all_grads = all_grads.reshape(-1, all_grads.shape[2])
        all_sums = all_stats[:, :heads_here].transpose(0, 2, 1).reshape(-1, heads_here)
        all_dots = all_stats[:, 8 : 8 + heads_here].transpose(0, 2, 1).reshape(-1, heads_here)
    else:
        all_grads, all_sums, all_dots = (
            lax.all_gather(a, "seq", axis=0, tiled=True) for a in (grad_attended, log_sums.T, row_dots.T)
        )

    def query_terms(query_grad, key_part, value_part, other_docs):
        same_doc = (local_docs[:, None] == other_docs[None, :])[None]
        _, dscore = block_grads(
            queries, grad_three, log_sums, row_dots, key_part, value_part, same_doc
        )
        return (
            query_grad
            + jnp.einsum("hqk,khd->qhd", dscore, key_part, preferred_element_type=jnp.float32)
            * score_scale
        )

    def key_terms(key_grad, value_grad, query_part, grad_part, sums_part, dots_part, other_docs):
        same_doc = (other_docs[:, None] == local_docs[None, :])[None]
        softmax_part, dscore = block_grads(
            query_part, grad_part, sums_part, dots_part, key_rows, value_rows, same_doc
        )
        value_grad = value_grad + jnp.einsum(
            "hqk,qhd->khd",
            softmax_part.astype(jnp.bfloat16),
            grad_part,
            preferred_element_type=jnp.float32,
        )
        key_grad = (
            key_grad
            + jnp.einsum("hqk,qhd->khd", dscore, query_part, preferred_element_type=jnp.float32)
            * score_scale
        )
        return (key_grad, value_grad)

    def piece_rows(source, block_begin, block_size):
        return lax.dynamic_slice_in_dim(source, block_begin, block_size, 0).reshape(
            block_size, heads_here, HEAD_DIM
        )

    def piece_stats(block_begin, block_size):
        sums_part = lax.dynamic_slice_in_dim(all_sums, block_begin, block_size, 0).T
        dots_part = lax.dynamic_slice_in_dim(all_dots, block_begin, block_size, 0).T
        other_docs, _ = doc_layout(
            short_lengths, block_begin + jnp.arange(block_size, dtype=jnp.int32), total_rows
        )
        return (sums_part, dots_part, other_docs)

    def fold_keys(carry_state, portion):
        piece_keys, piece_values = portion

        def key_block(inner_state, block_begin, block_size):
            _, _, other_docs = piece_stats(block_begin, block_size)
            return query_terms(
                inner_state,
                piece_rows(piece_keys, block_begin, block_size),
                piece_rows(piece_values, block_begin, block_size),
                other_docs,
            )

        return over_blocks(carry_state, piece_keys.shape[0], block_rows, key_block)

    query_grad = fold_keys(
        zeros_three,
        (all_keys, all_values),
    )

    def fold_queries(carry_state, portion):
        piece_queries, piece_grads = portion

        def query_block(inner_state, block_begin, block_size):
            sums_part, dots_part, other_docs = piece_stats(block_begin, block_size)
            return key_terms(
                inner_state[0],
                inner_state[1],
                piece_rows(piece_queries, block_begin, block_size),
                piece_rows(piece_grads, block_begin, block_size),
                sums_part,
                dots_part,
                other_docs,
            )

        return over_blocks(carry_state, piece_queries.shape[0], block_rows, query_block)

    key_grad, value_grad = fold_queries(
        (zeros_three, zeros_three),
        (all_queries, all_grads),
    )

    def rotate_local(heads_in):
        return rotate(heads_in, cosines, sines)

    _, rotate_pull = jax.vjp(rotate_local, zeros_three)
    query_back = rotate_pull(query_grad)[0]
    key_back = rotate_pull(key_grad)[0]
    grad_qkv = jnp.stack(
        [
            query_back.reshape(block_rows, -1),
            key_back.reshape(block_rows, -1),
            value_grad.reshape(block_rows, -1),
        ],
        axis=1,
    ).astype(jnp.bfloat16)
    qkv_grad = jnp.einsum("rd,rgc->dgc", normed_block, grad_qkv, preferred_element_type=jnp.float32)
    grad_normed_one = jnp.einsum(
        "rgc,dgc->rd", grad_qkv, qkv_full, preferred_element_type=jnp.float32
    )
    grad_normed_rows = lax.psum_scatter(
        grad_normed_one.astype(jnp.bfloat16), "head", scatter_dimension=0, tiled=True
    ).astype(jnp.float32)
    _, norm_one_pull = jax.vjp(layer_norm, inputs, gain_one)
    grad_inputs_norm, gain_one_grad = norm_one_pull(grad_normed_rows)
    tokens_grad = grad_resid + grad_inputs_norm
    if small:
        rows_in = qkv_weight.shape[0]
        low_qkv = qkv_grad.astype(jnp.bfloat16).reshape(seq_count, rows_in, 3, -1).transpose(0, 2, 1, 3)
        low_out = out_grad_weight.astype(jnp.bfloat16).reshape(-1, seq_count, out_weight.shape[1]).transpose(1, 0, 2)
        low_in = in_grad.astype(jnp.bfloat16).transpose(0, 2, 1, 3)
        low_down = down_grad.astype(jnp.bfloat16)
        width = attn_gain.shape[0]
        gains = jnp.zeros((seq_count * head_count, 16, 128), jnp.float32)
        gains = gains.at[:, 0, :width].set(gain_one_grad.reshape(-1, width))
        gains = gains.at[:, 1, :width].set(gain_two_grad.reshape(-1, width))
        qkv_terms, out_terms, in_terms, down_terms, gain_terms = exchange(
            (low_qkv, low_out, low_in, low_down, gains),
            ("seq", "seq", "all", "all", "all"),
            (True,) * 5,
            3,
        )
        qkv_weight_grad = jnp.sum(qkv_terms.astype(jnp.float32), axis=0).transpose(1, 0, 2)
        out_weight_grad = jnp.sum(out_terms.astype(jnp.float32), axis=0)
        in_weight_grad = jnp.sum(in_terms.astype(jnp.float32), axis=0).transpose(1, 0, 2)
        down_weight_grad = jnp.sum(down_terms.astype(jnp.float32), axis=0)
        gain_sums = jnp.sum(gain_terms, axis=0)
        attn_gain_grad, mlp_gain_grad = gain_sums[0, :width], gain_sums[1, :width]
    else:
        qkv_weight_grad, out_weight_grad = (
            lax.psum_scatter(qkv_grad, "seq", scatter_dimension=0, tiled=True),
            lax.psum_scatter(out_grad_weight, "seq", scatter_dimension=1, tiled=True),
        )
        attn_gain_grad, mlp_gain_grad, in_weight_grad, down_weight_grad = (
            lax.psum_scatter(gain_one_grad, ("seq", "head"), scatter_dimension=0, tiled=True),
            lax.psum_scatter(gain_two_grad, ("seq", "head"), scatter_dimension=0, tiled=True),
            lax.psum_scatter(in_grad, ("seq", "head"), scatter_dimension=0, tiled=True),
            lax.psum_scatter(down_grad, ("seq", "head"), scatter_dimension=0, tiled=True),
        )
    return (
        mixed,
        tokens_grad,
        attn_gain_grad,
        qkv_weight_grad,
        out_weight_grad,
        mlp_gain_grad,
        in_weight_grad.reshape(in_weight.shape),
        down_weight_grad.reshape(down_weight.shape),
    )


def solution(mesh):
    placed = (
        P(("seq", "head"), None),
        P(("seq", "head"), None),
        P(),
        P(("seq", "head")),
        P("seq", None, "head"),
        P("head", "seq"),
        P(("seq", "head")),
        P("seq", None, "head"),
        P("head", "seq"),
    )
    return jax.shard_map(
        on_device,
        mesh=mesh,
        in_specs=placed,
        out_specs=(
            P(("seq", "head"), None),
            P(("seq", "head"), None),
            P(("seq", "head")),
            P("seq", None, "head"),
            P("head", "seq"),
            P(("seq", "head")),
            P("seq", None, "head"),
            P("head", "seq"),
        ),
        check_vma=False,
    )
```

```python
import math

import jax
import jax.numpy as jnp
from jax import lax
from jax.experimental import pallas as pl
from jax.experimental.pallas import tpu as pltpu
from jax.sharding import PartitionSpec as P

HEAD_DIM = 64


norm_eps = 1e-05
rope_base = 160000.0
score_scale = 0.125
masked_low = -1e30


def layer_norm(inputs, gain_vector):
    row_mean = jnp.mean(inputs, axis=-1, keepdims=True)
    centred = inputs - row_mean
    spread = jnp.mean(centred * centred, axis=-1, keepdims=True)
    return centred * lax.rsqrt(spread + norm_eps) * gain_vector


def doc_layout(short_lengths, row_ids, total_rows):
    long_end = total_rows - jnp.sum(short_lengths)
    before = jnp.cumsum(short_lengths) - short_lengths
    bounds = long_end + before
    passed = row_ids[:, None] >= bounds[None, :]
    doc_ids = jnp.sum(passed.astype(jnp.int32), axis=1)
    starts = jnp.max(jnp.where(passed, bounds[None, :], jnp.zeros_like(bounds)[None, :]), axis=1)
    return (doc_ids, row_ids - starts)


def rope_tables(positions):
    steps_half = jnp.arange(HEAD_DIM // 2, dtype=jnp.float32)
    inverse = jnp.exp(steps_half * (-2.0 * math.log(rope_base) / HEAD_DIM))
    angles = positions.astype(jnp.float32)[:, None] * inverse[None, :]
    cosines = jnp.cos(angles)
    sines = jnp.sin(angles)
    return (jnp.concatenate([cosines, cosines], axis=1), jnp.concatenate([sines, sines], axis=1))


def rotate(heads_in, cosines, sines):
    half_dim = heads_in.shape[-1] // 2
    turned = jnp.concatenate([-heads_in[..., half_dim:], heads_in[..., :half_dim]], axis=-1)
    return heads_in * cosines[:, None, :] + turned * sines[:, None, :]


def block_length(row_count, shard_rows):
    shards = row_count // shard_rows
    return shard_rows * math.gcd(shards, max(1, 1024 // shard_rows))


def over_blocks(carry_state, row_count, shard_rows, block_fn):
    block_size = block_length(row_count, shard_rows)

    def block_step(inner_state, block_index):
        return (block_fn(inner_state, block_index * block_size, block_size), None)

    carry_state, _ = lax.scan(
        block_step, carry_state, jnp.arange(row_count // block_size, dtype=jnp.int32)
    )
    return carry_state


def scores_of(queries, key_part):
    return (
        jnp.einsum("qhd,khd->hqk", queries, key_part, preferred_element_type=jnp.float32)
        * score_scale
    )


def block_grads(queries, grad_rows, log_sums, row_dots, key_part, value_part, same_doc):
    scores = scores_of(queries, key_part)
    softmax_part = jnp.where(same_doc, jnp.exp(scores - log_sums[:, :, None]), 0.0)
    grad_probs = jnp.einsum(
        "qhd,khd->hqk", grad_rows, value_part, preferred_element_type=jnp.float32
    )
    dscore = (softmax_part * (grad_probs - row_dots[:, :, None])).astype(jnp.bfloat16)
    return (softmax_part, dscore)


def on_device(
    tokens,
    out_grad,
    short_lengths,
    attn_gain,
    qkv_weight,
    out_weight,
    mlp_gain,
    in_weight,
    down_weight,
):
    half_rows = tokens.shape[0]
    head_count = lax.axis_size("head")
    seq_count = lax.axis_size("seq")
    block_rows = half_rows * head_count
    total_rows = block_rows * seq_count
    local_ids = lax.axis_index("seq") * block_rows + jnp.arange(block_rows, dtype=jnp.int32)
    local_docs, local_pos = doc_layout(short_lengths, local_ids, total_rows)
    cosines, sines = rope_tables(local_pos)
    qkv_full, out_full = (
        lax.all_gather(qkv_weight, "seq", axis=0, tiled=True),
        lax.all_gather(out_weight, "seq", axis=1, tiled=True),
    )
    gain_first, gain_second, in_parts, down_parts = (
        lax.all_gather(attn_gain, ("seq", "head"), axis=0, tiled=True),
        lax.all_gather(mlp_gain, ("seq", "head"), axis=0, tiled=True),
        lax.all_gather(in_weight[None], ("seq", "head"), axis=0, tiled=True),
        lax.all_gather(down_weight[None], ("seq", "head"), axis=0, tiled=True),
    )
    in_parts = in_parts.reshape(seq_count, head_count, in_weight.shape[0], 2, in_weight.shape[2])
    down_parts = down_parts.reshape(
        seq_count, head_count, down_weight.shape[0], down_weight.shape[1]
    )
    heads_here = qkv_full.shape[2] // HEAD_DIM
    inputs = tokens.astype(jnp.float32)
    gain_one = gain_first.astype(jnp.float32)
    normed = layer_norm(inputs, gain_one).astype(jnp.bfloat16)
    normed_block = lax.all_gather(normed, "head", axis=0, tiled=True)
    projected = jnp.einsum(
        "rd,dgc->rgc", normed_block, qkv_full, preferred_element_type=jnp.float32
    )
    queries = rotate(
        projected[:, 0].reshape(block_rows, heads_here, HEAD_DIM), cosines, sines
    ).astype(jnp.bfloat16)
    key_rows = rotate(
        projected[:, 1].reshape(block_rows, heads_here, HEAD_DIM), cosines, sines
    ).astype(jnp.bfloat16)
    value_flat = projected[:, 2].astype(jnp.bfloat16)
    value_rows = value_flat.reshape(block_rows, heads_here, HEAD_DIM)
    key_flat = key_rows.reshape(block_rows, -1)
    query_flat = queries.reshape(block_rows, -1)

    def forward_fold(carry_state, portion):
        piece_keys, piece_values = portion

        def forward_block(inner_state, block_begin, block_size):
            running_max, running_sum, weighted = inner_state
            key_part = lax.dynamic_slice_in_dim(piece_keys, block_begin, block_size, 0).reshape(
                block_size, heads_here, HEAD_DIM
            )
            value_part = lax.dynamic_slice_in_dim(piece_values, block_begin, block_size, 0).reshape(
                block_size, heads_here, HEAD_DIM
            )
            other_docs, _ = doc_layout(
                short_lengths, block_begin + jnp.arange(block_size, dtype=jnp.int32), total_rows
            )
            same_doc = (local_docs[:, None] == other_docs[None, :])[None]
            scores = scores_of(queries, key_part)
            new_max = jnp.maximum(
                running_max, jnp.max(jnp.where(same_doc, scores, masked_low), axis=2)
            )
            factor = jnp.exp(running_max - new_max)
            softmax_part = jnp.where(same_doc, jnp.exp(scores - new_max[:, :, None]), 0.0)
            running_sum = running_sum * factor + jnp.sum(softmax_part, axis=2)
            weighted = weighted * factor.T[:, :, None] + jnp.einsum(
                "hqk,khd->qhd",
                softmax_part.astype(jnp.bfloat16),
                value_part,
                preferred_element_type=jnp.float32,
            )
            return (new_max, running_sum, weighted)

        return over_blocks(carry_state, piece_keys.shape[0], block_rows, forward_block)

    zeros_three = jnp.zeros((block_rows, heads_here, HEAD_DIM), jnp.float32)
    start_state = (
        jnp.full((heads_here, block_rows), masked_low, jnp.float32),
        jnp.zeros((heads_here, block_rows), jnp.float32),
        zeros_three,
    )
    running_max, running_sum, weighted = forward_fold(
        start_state,
        (
            lax.all_gather(key_flat, "seq", axis=0, tiled=True),
            lax.all_gather(value_flat, "seq", axis=0, tiled=True),
        ),
    )
    attended = weighted / running_sum.T[:, :, None]
    log_sums = running_max + jnp.log(running_sum)
    attended_low = attended.reshape(block_rows, -1).astype(jnp.bfloat16)
    branch = jnp.dot(attended_low, out_full, preferred_element_type=jnp.float32)
    branch_rows = lax.psum_scatter(
        branch.astype(jnp.bfloat16), "head", scatter_dimension=0, tiled=True
    ).astype(jnp.float32)
    resid = inputs + branch_rows
    gain_two = gain_second.astype(jnp.float32)
    normed_two = layer_norm(resid, gain_two).astype(jnp.bfloat16)
    normed_split = normed_two.reshape(half_rows, seq_count, -1)
    gate_up = jnp.einsum(
        "rse,shegf->rghf", normed_split, in_parts, preferred_element_type=jnp.float32
    ).reshape(half_rows, 2, -1)

    def activate(gate_part, up_part):
        return jax.nn.gelu(gate_part, approximate=False) * up_part

    hidden, activate_pull = jax.vjp(activate, gate_up[:, 0], gate_up[:, 1])
    hidden_low = hidden.astype(jnp.bfloat16)
    hidden_split = hidden_low.reshape(half_rows, head_count, -1)
    mlp_out = jnp.einsum(
        "rhf,shfe->rse", hidden_split, down_parts, preferred_element_type=jnp.float32
    ).reshape(half_rows, -1)
    mixed = (resid + mlp_out).astype(jnp.bfloat16)
    grad_out = out_grad.astype(jnp.float32)
    grad_split = out_grad.reshape(half_rows, seq_count, -1)
    grad_hidden = jnp.einsum(
        "rse,shfe->rhf", grad_split, down_parts, preferred_element_type=jnp.float32
    ).reshape(half_rows, -1)
    grad_gate, grad_up = activate_pull(grad_hidden)
    grad_gate_up = (
        jnp.stack([grad_gate, grad_up], axis=1)
        .astype(jnp.bfloat16)
        .reshape(half_rows, 2, head_count, -1)
    )
    down_grad = jnp.einsum(
        "rhf,rse->shfe", hidden_split, grad_split, preferred_element_type=jnp.float32
    ).reshape(seq_count * head_count, down_weight.shape[0], down_weight.shape[1])
    in_grad = jnp.einsum(
        "rse,rghf->shegf", normed_split, grad_gate_up, preferred_element_type=jnp.float32
    ).reshape(seq_count * head_count, in_weight.shape[0], 2, in_weight.shape[2])
    grad_normed_two = jnp.einsum(
        "rghf,shegf->rse", grad_gate_up, in_parts, preferred_element_type=jnp.float32
    ).reshape(half_rows, -1)
    _, norm_two_pull = jax.vjp(layer_norm, resid, gain_two)
    grad_resid_norm, gain_two_grad = norm_two_pull(grad_normed_two)
    grad_resid = grad_out + grad_resid_norm
    grad_branch = lax.all_gather(grad_resid.astype(jnp.bfloat16), "head", axis=0, tiled=True)
    out_grad_weight = jnp.einsum(
        "rc,rd->cd", attended_low, grad_branch, preferred_element_type=jnp.float32
    )
    grad_attended = jnp.einsum(
        "rd,cd->rc", grad_branch, out_full, preferred_element_type=jnp.float32
    ).astype(jnp.bfloat16)
    grad_three = grad_attended.reshape(block_rows, heads_here, HEAD_DIM)
    row_dots = jnp.sum(grad_three.astype(jnp.float32) * attended, axis=2).T
    all_sums, all_dots = (
        lax.all_gather(log_sums.T, "seq", axis=0, tiled=True),
        lax.all_gather(row_dots.T, "seq", axis=0, tiled=True),
    )

    def query_terms(query_grad, key_part, value_part, other_docs):
        same_doc = (local_docs[:, None] == other_docs[None, :])[None]
        _, dscore = block_grads(
            queries, grad_three, log_sums, row_dots, key_part, value_part, same_doc
        )
        return (
            query_grad
            + jnp.einsum("hqk,khd->qhd", dscore, key_part, preferred_element_type=jnp.float32)
            * score_scale
        )

    def key_terms(key_grad, value_grad, query_part, grad_part, sums_part, dots_part, other_docs):
        same_doc = (other_docs[:, None] == local_docs[None, :])[None]
        softmax_part, dscore = block_grads(
            query_part, grad_part, sums_part, dots_part, key_rows, value_rows, same_doc
        )
        value_grad = value_grad + jnp.einsum(
            "hqk,qhd->khd",
            softmax_part.astype(jnp.bfloat16),
            grad_part,
            preferred_element_type=jnp.float32,
        )
        key_grad = (
            key_grad
            + jnp.einsum("hqk,qhd->khd", dscore, query_part, preferred_element_type=jnp.float32)
            * score_scale
        )
        return (key_grad, value_grad)

    def piece_rows(source, block_begin, block_size):
        return lax.dynamic_slice_in_dim(source, block_begin, block_size, 0).reshape(
            block_size, heads_here, HEAD_DIM
        )

    def piece_stats(block_begin, block_size):
        sums_part = lax.dynamic_slice_in_dim(all_sums, block_begin, block_size, 0).T
        dots_part = lax.dynamic_slice_in_dim(all_dots, block_begin, block_size, 0).T
        other_docs, _ = doc_layout(
            short_lengths, block_begin + jnp.arange(block_size, dtype=jnp.int32), total_rows
        )
        return (sums_part, dots_part, other_docs)

    def fold_keys(carry_state, portion):
        piece_keys, piece_values = portion

        def key_block(inner_state, block_begin, block_size):
            _, _, other_docs = piece_stats(block_begin, block_size)
            return query_terms(
                inner_state,
                piece_rows(piece_keys, block_begin, block_size),
                piece_rows(piece_values, block_begin, block_size),
                other_docs,
            )

        return over_blocks(carry_state, piece_keys.shape[0], block_rows, key_block)

    query_grad = fold_keys(
        zeros_three,
        (
            lax.all_gather(key_flat, "seq", axis=0, tiled=True),
            lax.all_gather(value_flat, "seq", axis=0, tiled=True),
        ),
    )

    def fold_queries(carry_state, portion):
        piece_queries, piece_grads = portion

        def query_block(inner_state, block_begin, block_size):
            sums_part, dots_part, other_docs = piece_stats(block_begin, block_size)
            return key_terms(
                inner_state[0],
                inner_state[1],
                piece_rows(piece_queries, block_begin, block_size),
                piece_rows(piece_grads, block_begin, block_size),
                sums_part,
                dots_part,
                other_docs,
            )

        return over_blocks(carry_state, piece_queries.shape[0], block_rows, query_block)

    key_grad, value_grad = fold_queries(
        (zeros_three, zeros_three),
        (
            lax.all_gather(query_flat, "seq", axis=0, tiled=True),
            lax.all_gather(grad_attended, "seq", axis=0, tiled=True),
        ),
    )

    def rotate_local(heads_in):
        return rotate(heads_in, cosines, sines)

    _, rotate_pull = jax.vjp(rotate_local, zeros_three)
    query_back = rotate_pull(query_grad)[0]
    key_back = rotate_pull(key_grad)[0]
    grad_qkv = jnp.stack(
        [
            query_back.reshape(block_rows, -1),
            key_back.reshape(block_rows, -1),
            value_grad.reshape(block_rows, -1),
        ],
        axis=1,
    ).astype(jnp.bfloat16)
    qkv_grad = jnp.einsum("rd,rgc->dgc", normed_block, grad_qkv, preferred_element_type=jnp.float32)
    grad_normed_one = jnp.einsum(
        "rgc,dgc->rd", grad_qkv, qkv_full, preferred_element_type=jnp.float32
    )
    grad_normed_rows = lax.psum_scatter(
        grad_normed_one.astype(jnp.bfloat16), "head", scatter_dimension=0, tiled=True
    ).astype(jnp.float32)
    _, norm_one_pull = jax.vjp(layer_norm, inputs, gain_one)
    grad_inputs_norm, gain_one_grad = norm_one_pull(grad_normed_rows)
    tokens_grad = grad_resid + grad_inputs_norm
    qkv_weight_grad, out_weight_grad = (
        lax.psum_scatter(qkv_grad, "seq", scatter_dimension=0, tiled=True),
        lax.psum_scatter(out_grad_weight, "seq", scatter_dimension=1, tiled=True),
    )
    attn_gain_grad, mlp_gain_grad, in_weight_grad, down_weight_grad = (
        lax.psum_scatter(gain_one_grad, ("seq", "head"), scatter_dimension=0, tiled=True),
        lax.psum_scatter(gain_two_grad, ("seq", "head"), scatter_dimension=0, tiled=True),
        lax.psum_scatter(in_grad, ("seq", "head"), scatter_dimension=0, tiled=True),
        lax.psum_scatter(down_grad, ("seq", "head"), scatter_dimension=0, tiled=True),
    )
    return (
        mixed,
        tokens_grad,
        attn_gain_grad,
        qkv_weight_grad,
        out_weight_grad,
        mlp_gain_grad,
        in_weight_grad.reshape(in_weight.shape),
        down_weight_grad.reshape(down_weight.shape),
    )


LOW = jnp.bfloat16
FULL = jnp.float32


def dot(a, b):
    return jnp.dot(a, b, preferred_element_type=FULL)


def dot_nt(a, b):
    return lax.dot_general(a, b, (((1,), (1,)), ((), ())), preferred_element_type=FULL)


def turned(a):
    return a.astype(FULL).T


def centred_norm(rows):
    centred = rows - jnp.mean(rows, axis=-1, keepdims=True)
    scale = lax.rsqrt(jnp.mean(centred * centred, axis=-1, keepdims=True) + norm_eps)
    return centred * scale, scale


def norm_back(unit, scale, weighted):
    mean_w = jnp.mean(weighted, axis=-1, keepdims=True)
    mean_wn = jnp.mean(weighted * unit, axis=-1, keepdims=True)
    return (weighted - mean_w - unit * mean_wn) * scale


def whole_layer(*refs):
    (
        short_ref, tok_ref, gout_ref, gain_ref, wq_ref, ffp_ref, wot_ref,
        mixed_ref, tgrad_ref, gains_ref, qkvg_ref, ffg_ref, outg_ref,
        xh, gt, gn, gb, wh, wht, ffw, wo, h1, cs, qa, ka, kt, vt, vr, pt, ot, ol, og, res,
        ms, ms_c, ms_a, ms_y, db, dos, dop, dot_t, ds, dqt, dq, d1, d1_c, d1_a, d1_r1, d1_s1, d1_r2, d1_s2, d1_r3,
        dw, dw_in, gf, gf_x, gf_s, gf_z, gf_f, gf_b, gf_c, go, go_x, go_s, go_z, go_f, go_b, go_c, gy, gy_in,
        s_tok, r_tok, s_gain, r_gain, s_wq, r_wq, s_g, r_g, s_ff, r_ff, s_wo, r_wo,
        s_o, r_o, s_ms, r_ms, s_db, r_db, s_do, r_do, s_d1, r_d1, s_dw, r_dw, s_gf, r_gf, s_go, r_go, s_gy, r_gy,
    ) = refs
    seq, head = lax.axis_index("seq"), lax.axis_index("head")
    z, x, c, y = seq // 4, (seq // 2) % 2, seq % 2, head
    zh, zb = z // 2, z % 2
    slot = zb * 2 + x
    active = slot < 3
    slot3 = jnp.minimum(slot, 2)
    pending = []

    def flip(value, bit):
        return value if bit == 0 else 1 - value

    def at(z_, x_, c_, y_):
        return (z_ * 4 + x_ * 2 + c_, y_)

    def far_z(k):
        return flip(zh, k // 2) * 2 + flip(zb, k % 2)

    def partner(dim):
        return {
            "x": at(z, 1 - x, c, y),
            "y": at(z, x, c, 1 - y),
            "z": at(far_z(1), x, c, y),
            "c": at(z, x, 1 - c, y),
            "h": at(far_z(2), x, c, y),
        }[dim]

    def push(src, dst, send, recv, device, when=None):
        copy = pltpu.make_async_remote_copy(
            src_ref=src, dst_ref=dst, send_sem=send, recv_sem=recv,
            device_id=device, device_id_type=pl.DeviceIdType.MESH,
        )
        if when is None:
            copy.start()
        else:
            pl.when(when)(copy.start)
        pending.append((when, copy))

    def arrive(dst, recv, when=None):
        copy = pltpu.make_async_remote_copy(
            src_ref=dst, dst_ref=dst, send_sem=recv, recv_sem=recv,
            device_id=partner("c"), device_id_type=pl.DeviceIdType.MESH,
        )
        if when is None:
            copy.wait_recv()
        else:
            pl.when(when)(copy.wait_recv)

    barrier = pltpu.get_barrier_semaphore()
    peers = []
    for k in range(1, 32):
        kz, kx, kc, ky = k // 8, (k // 4) % 2, (k // 2) % 2, k % 2
        if kz < 2 or ky == 0:
            peers.append(at(far_z(kz), flip(x, kx), flip(c, kc), flip(y, ky)))
    for peer in peers:
        pl.semaphore_signal(barrier, inc=1, device_id=peer, device_id_type=pl.DeviceIdType.MESH)
    pl.semaphore_wait(barrier, len(peers))

    xh[zb, x, c, y] = tok_ref[...]
    orders = (("x", "y", "z"), ("y", "z", "x"), ("z", "x", "y"))

    def third(t):
        return pl.ds(t * 256, 256)

    def blocks(ref, opened, lanes, flipped=None, core=None):
        there = {"z": zb, "x": x, "y": y, "c": c if core is None else core}
        if flipped is not None:
            there[flipped] = 1 - there[flipped]
        index = tuple(slice(None) if d in opened else there[d] for d in ("z", "x", "c", "y"))
        return ref.at[index + (slice(None), lanes)]

    for t in range(3):
        view = blocks(xh, (), third(t))
        push(view, view, s_tok.at[0, t], r_tok.at[0, t], partner(orders[t][0]))

    gt[zh, zb, x, c, y] = gain_ref[...]
    gain_order = ("x", "y", "z", "h", "c")

    def gain_view(opened, flipped=None):
        there = {"h": zh, "z": zb, "x": x, "c": c, "y": y}
        if flipped is not None:
            there[flipped] = 1 - there[flipped]
        return gt.at[tuple(slice(None) if d in opened else there[d] for d in ("h", "z", "x", "c", "y"))]

    def gain_send(k):
        view = gain_view(gain_order[:k])
        push(view, view, s_gain.at[k], r_gain.at[k], partner(gain_order[k]))

    def gain_wait(k):
        arrive(gain_view(gain_order[:k], gain_order[k]), r_gain.at[k])

    gain_send(0)

    own_rows = pl.ds(pl.multiple_of(seq * 48, 16), 48)
    for k in range(16):
        z_, x_, c_ = far_z(k // 4), flip(x, (k // 2) % 2), flip(c, k % 2)
        slot_ = (z_ % 2) * 2 + x_
        piece = wq_ref.at[jnp.minimum(slot_ * 2 + c_, 5)]
        if k == 0:
            wh[own_rows, :] = piece[...]
        else:
            push(piece, wh.at[own_rows, :], s_wq.at[k], r_wq.at[k], at(z_, x_, c_, y), slot_ < 3)

    gb[c, y] = gout_ref[...]
    group = ((0, 1), (1, 0), (1, 1))
    for k, (kc, ky) in enumerate(group):
        push(gb.at[c, y], gb.at[c, y], s_g.at[k], r_g.at[k], at(z, x, flip(c, kc), flip(y, ky)))

    core_rows = pl.ds(pl.multiple_of(c * 48, 16), 48)
    wo_lanes = pl.ds(pl.multiple_of(y * 384, 128), 384)
    wo_others = pl.ds(pl.multiple_of((1 - y) * 384, 128), 384)
    ffw[z, x, core_rows, :] = ffp_ref[c]
    wo[z, x, c, :, wo_lanes] = wot_ref[...]
    for k in range(1, 4):
        push(wot_ref, wo.at[z, x, c, :, wo_lanes], s_wo.at[k], r_wo.at[k], at(far_z(k), x, c, y))
    for k in range(1, 8):
        c_ = flip(c, k % 2)
        push(ffp_ref.at[c_], ffw.at[z, x, core_rows, :], s_ff.at[k], r_ff.at[k], at(far_z(k // 2), x, c_, y))

    for step in (1, 2):
        for t in range(3):
            arrive(blocks(xh, orders[t][: step - 1], third(t), orders[t][step - 1]), r_tok.at[step - 1, t])
            view = blocks(xh, orders[t][:step], third(t))
            push(view, view, s_tok.at[step, t], r_tok.at[step, t], partner(orders[t][step]))
        gain_wait(step - 1)
        gain_send(step)
    gain_wait(2)
    gain_send(3)
    for t in range(3):
        arrive(blocks(xh, orders[t][:2], third(t), orders[t][2]), r_tok.at[2, t])
        view = blocks(xh, ("x", "y", "z"), third(t))
        push(view, view, s_tok.at[3, t], r_tok.at[3, t], partner("c"))

    half_rows = 1024
    row = lax.broadcasted_iota(jnp.int32, (32, half_rows), 1) + zh * half_rows
    feature = lax.broadcasted_iota(jnp.int32, (32, half_rows), 0)
    bound = jnp.int32(2 * half_rows)
    for b in range(short_ref.shape[0]):
        bound = bound - short_ref[b]
    doc = jnp.zeros_like(row)
    start = jnp.zeros_like(row)
    for b in range(short_ref.shape[0]):
        passed = row >= bound
        doc = doc + jnp.where(passed, 1, 0)
        start = jnp.where(passed, bound, start)
        bound = bound + short_ref[b]
    inverse = jnp.exp(feature.astype(FULL) * (-2.0 * math.log(rope_base) / HEAD_DIM))
    angles = (row - start).astype(FULL) * inverse
    cs[0] = jnp.cos(angles)
    cs[1] = jnp.sin(angles)
    same = jnp.where(feature == doc, 1.0, 0.0)
    cs[2] = same
    qa[64:96, :] = ((same - 1.0) * 1e30).astype(LOW)
    qa[96:128, :] = jnp.zeros((32, half_rows), LOW)

    gain_wait(3)
    gain_send(4)
    gain_wait(4)
    tiles = gt[...].reshape(512, 128)
    width = 24
    pick = lax.broadcasted_iota(jnp.int32, (128, 768), 1) % width == lax.broadcasted_iota(jnp.int32, (128, 768), 0)
    spread = dot(tiles, jnp.where(pick, 1.0, 0.0).astype(LOW))
    source = lax.broadcasted_iota(jnp.int32, (512, 768), 0)
    wanted = (lax.broadcasted_iota(jnp.int32, (512, 768), 1) // width) * 16
    gn[0:1, :] = jnp.sum(jnp.where(source == wanted, spread, 0.0), axis=0, keepdims=True)
    gn[1:2, :] = jnp.sum(jnp.where(source == wanted + 1, spread, 0.0), axis=0, keepdims=True)

    for t in range(3):
        arrive(blocks(xh, ("x", "y", "z"), third(t), "c"), r_tok.at[3, t])
    for k in range(1, 16):
        source_seq = far_z(k // 4) * 4 + flip(x, (k // 2) % 2) * 2 + flip(c, k % 2)
        arrive(wh.at[pl.ds(pl.multiple_of(source_seq * 48, 16), 48), :], r_wq.at[k], active)

    @pl.when(active)
    def _():
        gain = gn[0:1, :]

        def normed_block(b, carry):
            rows = xh[b // 8, (b // 4) % 2, (b // 2) % 2, b % 2].astype(FULL)
            unit, _ = centred_norm(rows)
            h1[pl.ds(pl.multiple_of(b * 64, 64), 64), :] = (unit * gain).astype(LOW)
            return carry

        lax.fori_loop(0, 16, normed_block, 0)
        wht[...] = turned(wh[...]).astype(LOW)
        for part in range(4):
            cols = pl.ds(part * 256, 256)
            proj = dot_nt(wht[...], h1[cols, :])
            cosine, sine = cs[0, :, cols], cs[1, :, cols]
            q1, q2, k1, k2 = proj[0:32], proj[32:64], proj[64:96], proj[96:128]
            qr = jnp.concatenate([q1 * cosine - q2 * sine, q2 * cosine + q1 * sine], axis=0)
            kr = jnp.concatenate([k1 * cosine - k2 * sine, k2 * cosine + k1 * sine], axis=0)
            qa[0:64, cols] = (qr * score_scale).astype(LOW)
            kt[:, cols] = kr.astype(LOW)
            vt[:, cols] = proj[128:192].astype(LOW)
            pad = jnp.zeros((32, 256), FULL)
            ka[cols, :] = jnp.concatenate([kr, cs[2, :, cols], pad], axis=0).T.astype(LOW)
            vr[cols, :] = proj[128:192].T.astype(LOW)

    def ff_forward(kz):
        z_ = far_z(kz)
        for kc in range(2):
            if (kz, kc) != (0, 0):
                rows = pl.ds(pl.multiple_of(flip(c, kc) * 48, 16), 48)
                arrive(ffw.at[z_, x, rows, :], r_ff.at[kz * 2 + kc])
        push(ffw.at[z_, x], ffw.at[z_, x], s_ff.at[8 + kz], r_ff.at[8 + kz], partner("x"))

    for part in range(4):
        cols = pl.ds(part * 256, 256)

        @pl.when(active)
        def _(part=part, cols=cols):
            scores = dot(ka[...], qa[:, cols])
            expo = jnp.exp(scores - jnp.max(scores, axis=0, keepdims=True))
            prob = (expo * (1.0 / jnp.sum(expo, axis=0, keepdims=True))).astype(LOW)
            pt[:, cols] = prob
            result = dot(vt[...], prob)
            ot[part] = result
            ol[part] = result.astype(LOW)

        for y_ in range(2):
            mine = jnp.logical_and(slot == part, y == y_)

            @pl.when(jnp.logical_and(active, mine))
            def _(part=part):
                og[y, slot3, c] = ol[part]

            push(
                ol.at[part], og.at[y, slot3, c], s_o.at[part, y_], r_o.at[slot3, y],
                at(zh * 2 + part // 2, part % 2, c, y_), jnp.logical_and(active, jnp.logical_not(mine)),
            )
        ff_forward(part)
        if part == 1:
            for k in range(1, 4):
                arrive(wo.at[far_z(k), x, c, :, wo_lanes], r_wo.at[k])
            view = wo.at[:, x, c, :, wo_lanes]
            push(view, view, s_wo.at[4], r_wo.at[4], partner("x"))
        if part == 3:
            arrive(wo.at[:, 1 - x, c, :, wo_lanes], r_wo.at[4])
            view = wo.at[:, :, c, :, wo_lanes]
            push(view, view, s_wo.at[5], r_wo.at[5], partner("y"))

    for slot_ in range(3):
        for y_ in range(2):
            mine = jnp.logical_and(slot == slot_, y == y_)
            arrive(og.at[y_, slot_, c], r_o.at[slot_, y_], jnp.logical_not(mine))
    push(og.at[:, :, c], og.at[:, :, c], s_o.at[4, 0], r_o.at[3, 0], partner("c"))
    arrive(wo.at[:, :, c, :, wo_others], r_wo.at[5])
    push(wo.at[:, :, c], wo.at[:, :, c], s_wo.at[6], r_wo.at[6], partner("c"))
    arrive(og.at[:, :, 1 - c], r_o.at[3, 0])
    arrive(wo.at[:, :, 1 - c], r_wo.at[6])

    gain_two = gn[1:2, :]
    branch = dot(wo[...].reshape(768, 768), og[...].reshape(768, 256)).T
    resid = xh[zb, x].reshape(256, 768).astype(FULL) + branch
    res[...] = resid.reshape(2, 2, 64, 768)
    unit_two, _ = centred_norm(resid)
    h2 = (unit_two * gain_two).astype(LOW)

    for kz in range(4):
        arrive(ffw.at[far_z(kz), 1 - x], r_ff.at[8 + kz])
    for k, (kc, ky) in enumerate(group):
        arrive(gb.at[flip(c, kc), flip(y, ky)], r_g.at[k])
    w_in = ffw[:, :, :, 0:576].reshape(768, 576)
    w_down = ffw[:, :, :, 576:864].reshape(768, 288)
    gate_up = dot(h2, w_in)
    gate, up = gate_up[:, :288], gate_up[:, 288:]
    grad_out = gb[...].reshape(256, 768)
    grad_hidden = dot(grad_out, w_down)
    chance = 0.5 * (1.0 + lax.erf(gate * (1.0 / math.sqrt(2.0))))
    density = jnp.exp(gate * gate * -0.5) * (1.0 / math.sqrt(2.0 * math.pi))
    curve = gate * chance
    hidden = (curve * up).astype(LOW)
    grad_gate = grad_hidden * up * (chance + gate * density)
    grad_gate_up = jnp.concatenate([grad_gate, grad_hidden * curve], axis=1).astype(LOW)

    def halve(kind, part):
        ms[kind] = part.astype(LOW).reshape(2, 2, 64, 768)
        push(ms.at[kind, 1 - c], ms_c.at[kind], s_ms.at[kind, 0], r_ms.at[kind, 0], partner("c"))

    def quarter(kind):
        arrive(ms_c.at[kind], r_ms.at[kind, 0])
        ms_a[kind] = (ms[kind, c, 1 - y].astype(FULL) + ms_c[kind, 1 - y].astype(FULL)).astype(LOW)
        push(ms_a.at[kind], ms_y.at[kind], s_ms.at[kind, 1], r_ms.at[kind, 1], partner("y"))

    def quarter_sum(kind):
        arrive(ms_y.at[kind], r_ms.at[kind, 1])
        return ms[kind, c, y].astype(FULL) + ms_c[kind, y].astype(FULL) + ms_y[kind].astype(FULL)

    halve(0, dot_nt(grad_gate_up, w_in))
    halve(1, dot_nt(hidden, w_down))
    quarter(0)
    h2_t = turned(h2).astype(LOW)
    gf[:, :, :, 0:576] = dot(h2_t, grad_gate_up).astype(LOW).reshape(4, 2, 96, 576)
    g_t = turned(grad_out).astype(LOW)
    gf[:, :, :, 576:864] = dot(g_t, hidden).astype(LOW).reshape(4, 2, 96, 288)
    for kz in range(4):
        z_ = far_z(kz)
        push(gf.at[z_, 1 - x], gf_x.at[z_], s_gf.at[0, kz], r_gf.at[0, kz], partner("x"))
    quarter(1)

    own_res = res[c, y]
    unit_two, scale_two = centred_norm(own_res)
    grad_h2 = quarter_sum(0)
    grad_resid = gout_ref[...].astype(FULL) + norm_back(unit_two, scale_two, grad_h2 * gain_two)
    tgrad_ref[...] = grad_resid
    grad_branch = grad_resid.astype(LOW)
    db[c, y] = grad_branch
    grad_o = dot(grad_branch, wo[...].reshape(768, 768)).astype(LOW)
    own_block = zb * 8 + x * 4 + c * 2 + y
    for slot_ in range(3):
        for y_ in range(2):
            lanes = y_ * 384 + slot_ * 128
            dos[y_, slot_] = grad_o[:, lanes : lanes + 128]
            for c_ in range(2):
                mine = jnp.logical_and(jnp.logical_and(slot == slot_, y == y_), c == c_)

                @pl.when(mine)
                def _(slot_=slot_, y_=y_):
                    dop[zb, x, c, y] = dos[y_, slot_]

                push(
                    dos.at[y_, slot_], dop.at[zb, x, c, y], s_do.at[slot_ * 4 + y_ * 2 + c_], r_do.at[own_block],
                    at(zh * 2 + slot_ // 2, slot_ % 2, c_, y_), jnp.logical_not(mine),
                )
    for k, (kc, ky) in enumerate(group):
        push(db.at[c, y], db.at[c, y], s_db.at[k], r_db.at[k], at(z, x, flip(c, kc), flip(y, ky)))
    mixed_ref[...] = (own_res + quarter_sum(1)).astype(LOW)
    for k, (kc, ky) in enumerate(group):
        arrive(db.at[flip(c, kc), flip(y, ky)], r_db.at[k])
    db_t = turned(db[...].reshape(256, 768)).astype(LOW)
    o_part = og[...].reshape(2, 6, 64, 256)
    o_pick = jnp.where(y == 0, o_part[0], o_part[1])
    o_pick = jnp.where(c == 0, o_pick[0:3], o_pick[3:6]).reshape(192, 256)
    go[...] = dot_nt(db_t, o_pick).astype(LOW).reshape(4, 2, 96, 192)
    for kz in range(4):
        z_ = far_z(kz)
        push(go.at[z_, 1 - x], go_x.at[z_], s_go.at[0, kz], r_go.at[0, kz], partner("x"))

    for b in range(16):
        z_, x_, c_, y_ = b // 8, (b // 4) % 2, (b // 2) % 2, b % 2
        arrive(dop.at[z_, x_, c_, y_], r_do.at[b], jnp.logical_and(active, own_block != b))

    @pl.when(active)
    def _():
        pair = turned(dop[...].reshape(1024, 128))
        dot_t[...] = jnp.where(c == 0, pair[0:64], pair[64:128]).astype(LOW)

    def sum_x(kz, mine, other, total, send, recv, landing):
        z_ = far_z(kz)
        arrive(other.at[z_], recv.at[0, kz])
        total[z_] = (mine[z_, x].astype(FULL) + other[z_].astype(FULL)).astype(LOW)
        if kz:
            push(total.at[z_], landing.at[kz - 1], send.at[1, kz], recv.at[1, kz], at(z_, x, c, y))

    for part in range(4):
        cols = pl.ds(part * 256, 256)

        @pl.when(active)
        def _(part=part, cols=cols):
            grad_t = dot_t[:, cols]
            delta = jnp.sum(grad_t.astype(FULL) * ot[part], axis=0, keepdims=True)
            grad_p = dot(vr[...], grad_t)
            score_grad = (pt[:, cols].astype(FULL) * (grad_p - delta)).astype(LOW)
            ds[:, cols] = score_grad
            back = dot(kt[...], score_grad) * score_scale
            cosine, sine = cs[0, :, cols], cs[1, :, cols]
            b1, b2 = back[0:32], back[32:64]
            dqt[0:64, cols] = jnp.concatenate([b1 * cosine + b2 * sine, b2 * cosine - b1 * sine], axis=0).astype(LOW)

        sum_x(part, gf, gf_x, gf_s, s_gf, r_gf, gf_z)

    @pl.when(active)
    def _():
        for part in range(4):
            cols = pl.ds(part * 256, 256)
            back = dot_nt(qa[0:64, :], ds[cols, :])
            cosine, sine = cs[0, :, cols], cs[1, :, cols]
            b1, b2 = back[0:32], back[32:64]
            dqt[64:128, cols] = jnp.concatenate([b1 * cosine + b2 * sine, b2 * cosine - b1 * sine], axis=0).astype(LOW)
            dqt[128:192, cols] = dot_nt(dot_t[...], pt[cols, :]).astype(LOW)
            dq[cols, :] = turned(dqt[:, cols]).astype(LOW)

    for part in range(4):
        cols = pl.ds(part * 256, 256)

        @pl.when(active)
        def _(part=part, cols=cols):
            d1[part // 2, part % 2] = dot_nt(dq[cols, :], wh[...]).astype(LOW).reshape(2, 2, 64, 768)

        push(
            d1.at[part // 2, part % 2, 1 - c], d1_c.at[part // 2, part % 2],
            s_d1.at[0, part], r_d1.at[0, part], partner("c"), active,
        )
    for part in range(4):
        sum_x(part, go, go_x, go_s, s_go, r_go, go_z)

    @pl.when(jnp.logical_not(active))
    def _():
        d1_a[...] = jnp.zeros_like(d1_a)

    for part in range(4):
        arrive(d1_c.at[part // 2, part % 2], r_d1.at[0, part], active)

        @pl.when(active)
        def _(part=part):
            both = d1[part // 2, part % 2, c].astype(FULL) + d1_c[part // 2, part % 2].astype(FULL)
            d1_a[part // 2, part % 2] = both.astype(LOW)

    def remaining(t, step):
        return tuple(d for d in ("z", "x", "y") if d not in orders[t][:step])

    landing = (d1_r1, d1_r2, d1_r3)

    def step_view(t, step, flipped):
        dim = orders[t][step]
        place = {"z": zb, "x": x, "y": y}[dim]
        place = 1 - place if flipped else place
        index = tuple(place if d == dim else slice(None) for d in remaining(t, step))
        if step == 0:
            return d1_a.at[index + (slice(None), third(t))]
        return (d1_s1, d1_s2)[step - 1].at[(t,) + index]

    def step_push(t, step):
        push(
            step_view(t, step, True), landing[step].at[t], s_d1.at[1 + step, t], r_d1.at[1 + step, t],
            partner(orders[t][step]),
        )

    def step_sum(t, step):
        arrive(landing[step].at[t], r_d1.at[1 + step, t])
        return step_view(t, step, False)[...].astype(FULL) + landing[step][t].astype(FULL)

    for t in range(3):
        step_push(t, 0)

    @pl.when(active)
    def _():
        grad = dot(dqt[...], h1[...])
        dw[...] = grad.T.astype(LOW).reshape(16, 48, 192)

    own_head = zh * 6 + slot3 * 2 + c

    @pl.when(active)
    def _():
        dw_in[own_head] = dw[seq]

    for k in range(1, 16):
        z_, x_, c_ = far_z(k // 4), flip(x, (k // 2) % 2), flip(c, k % 2)
        push(dw.at[z_ * 4 + x_ * 2 + c_], dw_in.at[own_head], s_dw.at[k], r_dw.at[own_head], at(z_, x_, c_, y), active)

    for t in range(3):
        d1_s1[t] = step_sum(t, 0).astype(LOW)
        step_push(t, 1)

    def sum_z(total, landed, wide, low, send, recv, coming):
        value = total[z].astype(FULL)
        for k in range(1, 4):
            arrive(landed.at[k - 1], recv.at[1, k])
            value = value + landed[k - 1].astype(FULL)
        wide[...] = value.reshape(wide.shape)
        low[...] = wide[1 - c].astype(LOW)
        push(low, coming, send.at[2, 0], recv.at[2, 0], partner("c"))

    sum_z(gf_s, gf_z, gf_f, gf_b, s_gf, r_gf, gf_c)
    for t in range(3):
        d1_s2[t] = step_sum(t, 1).astype(LOW)
        step_push(t, 2)
    sum_z(go_s, go_z, go_f, go_b, s_go, r_go, go_c)
    arrive(gf_c, r_gf.at[2, 0])
    ffg_ref[c] = gf_f[c]
    ffg_ref[1 - c] = gf_c[...].astype(FULL)
    mlp_terms = jnp.zeros((48, 1), FULL)
    for c_ in range(2):
        terms = ffg_ref[c_, :, 0:576] * ffp_ref[c_, :, 0:576].astype(FULL)
        mlp_terms = mlp_terms + jnp.sum(terms, axis=1, keepdims=True)
    for h_ in range(2):
        for j in range(6):
            arrive(dw_in.at[h_ * 6 + j], r_dw.at[h_ * 6 + j], jnp.logical_not(jnp.logical_and(active, own_head == h_ * 6 + j)))
    attn_terms = jnp.zeros((48, 1), FULL)
    for j in range(6):
        both = dw_in[j].astype(FULL) + dw_in[6 + j].astype(FULL)
        qkvg_ref[j] = both
        attn_terms = attn_terms + jnp.sum(both * wq_ref[j].astype(FULL), axis=1, keepdims=True)
    lane = lax.broadcasted_iota(jnp.int32, (48, 128), 1)
    gy[...] = jnp.where(lane == 0, attn_terms, jnp.where(lane == 1, mlp_terms, 0.0))
    push(gy, gy_in, s_gy.at[0], r_gy.at[0], partner("y"))
    arrive(go_c, r_go.at[2, 0])
    outg_ref[c] = go_f[c]
    outg_ref[1 - c] = go_c[...].astype(FULL)

    unit_one, scale_one = centred_norm(tok_ref[...].astype(FULL))
    for t in range(3):
        res[0, 0, :, third(t)] = step_sum(t, 2)
    tgrad_ref[...] = tgrad_ref[...] + norm_back(unit_one, scale_one, res[0, 0] * gn[0:1, :])
    arrive(gy_in, r_gy.at[0])
    gains_ref[...] = gy[...] + gy_in[...]
    for when, copy in pending:
        if when is None:
            copy.wait_send()
        else:
            pl.when(when)(copy.wait_send)


def on_device_fast(tokens, out_grad, short_lengths, attn_gain, qkv_weight, out_weight, mlp_gain, in_weight, down_weight):
    rows, width = tokens.shape
    depth = qkv_weight.shape[0]
    heads_here = qkv_weight.shape[2] // HEAD_DIM
    count = attn_gain.shape[0]
    gain_tile = jnp.pad(jnp.stack([attn_gain, mlp_gain]), ((0, 14), (0, 128 - count)))
    projections = qkv_weight.reshape(depth, 3, heads_here, HEAD_DIM).transpose(2, 0, 1, 3)
    projections = projections.reshape(heads_here, depth, 3 * HEAD_DIM)
    inner = jnp.concatenate([in_weight, down_weight.T[:, None]], axis=1)
    inner = inner.reshape(depth, 3, 2, -1).transpose(2, 0, 1, 3).reshape(2, depth, -1)
    ff = inner.shape[2]
    feats = out_weight.shape[0]

    def vm(shape, kind=LOW):
        return pltpu.VMEM(shape, kind)

    def sem(*shape):
        return pltpu.SemaphoreType.DMA(shape)

    scratch = [
        vm((2, 2, 2, 2, 64, 768)), vm((2, 2, 2, 2, 2, 16, 128)), vm((8, 768), FULL), vm((2, 2, 64, 768)),
        vm((768, 192)), vm((192, 768)), vm((4, 2, 96, 864)), vm((4, 2, 2, 48, 768)), vm((1024, 768)),
        vm((3, 32, 1024), FULL), vm((128, 1024)), vm((1024, 128)), vm((64, 1024)), vm((64, 1024)), vm((1024, 64)),
        vm((1024, 1024)), vm((4, 64, 256), FULL), vm((4, 64, 256)), vm((2, 3, 2, 64, 256)), vm((2, 2, 64, 768), FULL),
        vm((2, 2, 2, 64, 768)), vm((2, 2, 64, 768)), vm((2, 64, 768)), vm((2, 64, 768)), vm((2, 2, 64, 768)),
        vm((2, 3, 64, 128)), vm((2, 2, 2, 2, 64, 128)), vm((64, 1024)), vm((1024, 1024)), vm((192, 1024)),
        vm((1024, 192)), vm((2, 2, 2, 2, 64, 768)), vm((2, 2, 2, 64, 768)), vm((2, 2, 2, 64, 768)),
        vm((3, 2, 2, 64, 256)), vm((3, 2, 2, 64, 256)), vm((3, 2, 64, 256)), vm((3, 2, 64, 256)), vm((3, 64, 256)),
        vm((16, 48, 192)), vm((12, 48, 192)),
        vm((4, 2, 96, 864)), vm((4, 96, 864)), vm((4, 96, 864)), vm((3, 96, 864)), vm((2, 48, 864), FULL),
        vm((48, 864)), vm((48, 864)),
        vm((4, 2, 96, 192)), vm((4, 96, 192)), vm((4, 96, 192)), vm((3, 96, 192)), vm((2, 48, 192), FULL),
        vm((48, 192)), vm((48, 192)),
        vm((48, 128), FULL), vm((48, 128), FULL),
        sem(4, 3), sem(4, 3), sem(5), sem(5), sem(16), sem(16), sem(3), sem(3), sem(12), sem(12), sem(7), sem(7),
        sem(5, 2), sem(4, 2), sem(2, 2), sem(2, 2), sem(3), sem(3), sem(12), sem(16), sem(4, 4), sem(4, 4),
        sem(16), sem(12), sem(3, 4), sem(3, 4), sem(3, 4), sem(3, 4), sem(1), sem(1),
    ]
    vmem = pl.BlockSpec(memory_space=pltpu.VMEM)
    mixed, tokens_grad, gains, qkv_grad, ff_grad, out_grads = pl.pallas_call(
        whole_layer,
        out_shape=[
            jax.ShapeDtypeStruct((rows, width), LOW),
            jax.ShapeDtypeStruct((rows, width), FULL),
            jax.ShapeDtypeStruct((depth, 128), FULL),
            jax.ShapeDtypeStruct((heads_here, depth, 3 * HEAD_DIM), FULL),
            jax.ShapeDtypeStruct((2, depth, ff), FULL),
            jax.ShapeDtypeStruct((2, depth, feats // 2), FULL),
        ],
        in_specs=[pl.BlockSpec(memory_space=pltpu.SMEM)] + [vmem] * 6,
        out_specs=[vmem] * 6,
        scratch_shapes=scratch,
        compiler_params=pltpu.CompilerParams(collective_id=0, has_side_effects=True, vmem_limit_bytes=60 << 20),
    )(short_lengths, tokens, out_grad, gain_tile, projections, inner, out_weight.T)
    mine = lax.dynamic_slice_in_dim(gains, lax.axis_index("head") * count, count, 0)
    attn_gain_grad = mine[:, 0] / attn_gain.astype(FULL)
    mlp_gain_grad = mine[:, 1] / mlp_gain.astype(FULL)
    qkv_weight_grad = qkv_grad.reshape(heads_here, depth, 3, HEAD_DIM).transpose(1, 2, 0, 3).reshape(qkv_weight.shape)
    ff_grad = ff_grad.reshape(2, depth, 3, -1)
    in_weight_grad = ff_grad[:, :, :2].transpose(1, 2, 0, 3).reshape(in_weight.shape)
    down_weight_grad = ff_grad[:, :, 2].transpose(0, 2, 1).reshape(down_weight.shape)
    out_weight_grad = out_grads.transpose(0, 2, 1).reshape(out_weight.shape)
    return (
        mixed, tokens_grad, attn_gain_grad, qkv_weight_grad, out_weight_grad, mlp_gain_grad,
        in_weight_grad, down_weight_grad,
    )


def solution(mesh):
    placed = (
        P(("seq", "head"), None),
        P(("seq", "head"), None),
        P(),
        P(("seq", "head")),
        P("seq", None, "head"),
        P("head", "seq"),
        P(("seq", "head")),
        P("seq", None, "head"),
        P("head", "seq"),
    )
    fits = mesh.shape["seq"] == 16 and mesh.shape["head"] == 2
    return jax.shard_map(
        on_device_fast if fits else on_device,
        mesh=mesh,
        in_specs=placed,
        out_specs=(
            P(("seq", "head"), None),
            P(("seq", "head"), None),
            P(("seq", "head")),
            P("seq", None, "head"),
            P("head", "seq"),
            P(("seq", "head")),
            P("seq", None, "head"),
            P("head", "seq"),
        ),
        check_vma=False,
    )
```

```python
import math

import jax
import jax.numpy as jnp
from jax import lax
from jax.experimental import pallas as pl
from jax.experimental.pallas import tpu as pltpu
from jax.sharding import PartitionSpec as P

HEAD_DIM = 64


norm_eps = 1e-05
rope_base = 160000.0
score_scale = 0.125
masked_low = -1e30


def layer_norm(inputs, gain_vector):
    row_mean = jnp.mean(inputs, axis=-1, keepdims=True)
    centred = inputs - row_mean
    spread = jnp.mean(centred * centred, axis=-1, keepdims=True)
    return centred * lax.rsqrt(spread + norm_eps) * gain_vector


def doc_layout(short_lengths, row_ids, total_rows):
    long_end = total_rows - jnp.sum(short_lengths)
    before = jnp.cumsum(short_lengths) - short_lengths
    bounds = long_end + before
    passed = row_ids[:, None] >= bounds[None, :]
    doc_ids = jnp.sum(passed.astype(jnp.int32), axis=1)
    starts = jnp.max(jnp.where(passed, bounds[None, :], jnp.zeros_like(bounds)[None, :]), axis=1)
    return (doc_ids, row_ids - starts)


def rope_tables(positions):
    steps_half = jnp.arange(HEAD_DIM // 2, dtype=jnp.float32)
    inverse = jnp.exp(steps_half * (-2.0 * math.log(rope_base) / HEAD_DIM))
    angles = positions.astype(jnp.float32)[:, None] * inverse[None, :]
    cosines = jnp.cos(angles)
    sines = jnp.sin(angles)
    return (jnp.concatenate([cosines, cosines], axis=1), jnp.concatenate([sines, sines], axis=1))


def rotate(heads_in, cosines, sines):
    half_dim = heads_in.shape[-1] // 2
    turned = jnp.concatenate([-heads_in[..., half_dim:], heads_in[..., :half_dim]], axis=-1)
    return heads_in * cosines[:, None, :] + turned * sines[:, None, :]


def block_length(row_count, shard_rows):
    shards = row_count // shard_rows
    return shard_rows * math.gcd(shards, max(1, 1024 // shard_rows))


def over_blocks(carry_state, row_count, shard_rows, block_fn):
    block_size = block_length(row_count, shard_rows)

    def block_step(inner_state, block_index):
        return (block_fn(inner_state, block_index * block_size, block_size), None)

    carry_state, _ = lax.scan(
        block_step, carry_state, jnp.arange(row_count // block_size, dtype=jnp.int32)
    )
    return carry_state


def scores_of(queries, key_part):
    return (
        jnp.einsum("qhd,khd->hqk", queries, key_part, preferred_element_type=jnp.float32)
        * score_scale
    )


def block_grads(queries, grad_rows, log_sums, row_dots, key_part, value_part, same_doc):
    scores = scores_of(queries, key_part)
    softmax_part = jnp.where(same_doc, jnp.exp(scores - log_sums[:, :, None]), 0.0)
    grad_probs = jnp.einsum(
        "qhd,khd->hqk", grad_rows, value_part, preferred_element_type=jnp.float32
    )
    dscore = (softmax_part * (grad_probs - row_dots[:, :, None])).astype(jnp.bfloat16)
    return (softmax_part, dscore)


def on_device(
    tokens,
    out_grad,
    short_lengths,
    attn_gain,
    qkv_weight,
    out_weight,
    mlp_gain,
    in_weight,
    down_weight,
):
    half_rows = tokens.shape[0]
    head_count = lax.axis_size("head")
    seq_count = lax.axis_size("seq")
    block_rows = half_rows * head_count
    total_rows = block_rows * seq_count
    local_ids = lax.axis_index("seq") * block_rows + jnp.arange(block_rows, dtype=jnp.int32)
    local_docs, local_pos = doc_layout(short_lengths, local_ids, total_rows)
    cosines, sines = rope_tables(local_pos)
    qkv_full, out_full = (
        lax.all_gather(qkv_weight, "seq", axis=0, tiled=True),
        lax.all_gather(out_weight, "seq", axis=1, tiled=True),
    )
    gain_first, gain_second, in_parts, down_parts = (
        lax.all_gather(attn_gain, ("seq", "head"), axis=0, tiled=True),
        lax.all_gather(mlp_gain, ("seq", "head"), axis=0, tiled=True),
        lax.all_gather(in_weight[None], ("seq", "head"), axis=0, tiled=True),
        lax.all_gather(down_weight[None], ("seq", "head"), axis=0, tiled=True),
    )
    in_parts = in_parts.reshape(seq_count, head_count, in_weight.shape[0], 2, in_weight.shape[2])
    down_parts = down_parts.reshape(
        seq_count, head_count, down_weight.shape[0], down_weight.shape[1]
    )
    heads_here = qkv_full.shape[2] // HEAD_DIM
    inputs = tokens.astype(jnp.float32)
    gain_one = gain_first.astype(jnp.float32)
    normed = layer_norm(inputs, gain_one).astype(jnp.bfloat16)
    normed_block = lax.all_gather(normed, "head", axis=0, tiled=True)
    projected = jnp.einsum(
        "rd,dgc->rgc", normed_block, qkv_full, preferred_element_type=jnp.float32
    )
    queries = rotate(
        projected[:, 0].reshape(block_rows, heads_here, HEAD_DIM), cosines, sines
    ).astype(jnp.bfloat16)
    key_rows = rotate(
        projected[:, 1].reshape(block_rows, heads_here, HEAD_DIM), cosines, sines
    ).astype(jnp.bfloat16)
    value_flat = projected[:, 2].astype(jnp.bfloat16)
    value_rows = value_flat.reshape(block_rows, heads_here, HEAD_DIM)
    key_flat = key_rows.reshape(block_rows, -1)
    query_flat = queries.reshape(block_rows, -1)

    def forward_fold(carry_state, portion):
        piece_keys, piece_values = portion

        def forward_block(inner_state, block_begin, block_size):
            running_max, running_sum, weighted = inner_state
            key_part = lax.dynamic_slice_in_dim(piece_keys, block_begin, block_size, 0).reshape(
                block_size, heads_here, HEAD_DIM
            )
            value_part = lax.dynamic_slice_in_dim(piece_values, block_begin, block_size, 0).reshape(
                block_size, heads_here, HEAD_DIM
            )
            other_docs, _ = doc_layout(
                short_lengths, block_begin + jnp.arange(block_size, dtype=jnp.int32), total_rows
            )
            same_doc = (local_docs[:, None] == other_docs[None, :])[None]
            scores = scores_of(queries, key_part)
            new_max = jnp.maximum(
                running_max, jnp.max(jnp.where(same_doc, scores, masked_low), axis=2)
            )
            factor = jnp.exp(running_max - new_max)
            softmax_part = jnp.where(same_doc, jnp.exp(scores - new_max[:, :, None]), 0.0)
            running_sum = running_sum * factor + jnp.sum(softmax_part, axis=2)
            weighted = weighted * factor.T[:, :, None] + jnp.einsum(
                "hqk,khd->qhd",
                softmax_part.astype(jnp.bfloat16),
                value_part,
                preferred_element_type=jnp.float32,
            )
            return (new_max, running_sum, weighted)

        return over_blocks(carry_state, piece_keys.shape[0], block_rows, forward_block)

    zeros_three = jnp.zeros((block_rows, heads_here, HEAD_DIM), jnp.float32)
    start_state = (
        jnp.full((heads_here, block_rows), masked_low, jnp.float32),
        jnp.zeros((heads_here, block_rows), jnp.float32),
        zeros_three,
    )
    running_max, running_sum, weighted = forward_fold(
        start_state,
        (
            lax.all_gather(key_flat, "seq", axis=0, tiled=True),
            lax.all_gather(value_flat, "seq", axis=0, tiled=True),
        ),
    )
    attended = weighted / running_sum.T[:, :, None]
    log_sums = running_max + jnp.log(running_sum)
    attended_low = attended.reshape(block_rows, -1).astype(jnp.bfloat16)
    branch = jnp.dot(attended_low, out_full, preferred_element_type=jnp.float32)
    branch_rows = lax.psum_scatter(
        branch.astype(jnp.bfloat16), "head", scatter_dimension=0, tiled=True
    ).astype(jnp.float32)
    resid = inputs + branch_rows
    gain_two = gain_second.astype(jnp.float32)
    normed_two = layer_norm(resid, gain_two).astype(jnp.bfloat16)
    normed_split = normed_two.reshape(half_rows, seq_count, -1)
    gate_up = jnp.einsum(
        "rse,shegf->rghf", normed_split, in_parts, preferred_element_type=jnp.float32
    ).reshape(half_rows, 2, -1)

    def activate(gate_part, up_part):
        return jax.nn.gelu(gate_part, approximate=False) * up_part

    hidden, activate_pull = jax.vjp(activate, gate_up[:, 0], gate_up[:, 1])
    hidden_low = hidden.astype(jnp.bfloat16)
    hidden_split = hidden_low.reshape(half_rows, head_count, -1)
    mlp_out = jnp.einsum(
        "rhf,shfe->rse", hidden_split, down_parts, preferred_element_type=jnp.float32
    ).reshape(half_rows, -1)
    mixed = (resid + mlp_out).astype(jnp.bfloat16)
    grad_out = out_grad.astype(jnp.float32)
    grad_split = out_grad.reshape(half_rows, seq_count, -1)
    grad_hidden = jnp.einsum(
        "rse,shfe->rhf", grad_split, down_parts, preferred_element_type=jnp.float32
    ).reshape(half_rows, -1)
    grad_gate, grad_up = activate_pull(grad_hidden)
    grad_gate_up = (
        jnp.stack([grad_gate, grad_up], axis=1)
        .astype(jnp.bfloat16)
        .reshape(half_rows, 2, head_count, -1)
    )
    down_grad = jnp.einsum(
        "rhf,rse->shfe", hidden_split, grad_split, preferred_element_type=jnp.float32
    ).reshape(seq_count * head_count, down_weight.shape[0], down_weight.shape[1])
    in_grad = jnp.einsum(
        "rse,rghf->shegf", normed_split, grad_gate_up, preferred_element_type=jnp.float32
    ).reshape(seq_count * head_count, in_weight.shape[0], 2, in_weight.shape[2])
    grad_normed_two = jnp.einsum(
        "rghf,shegf->rse", grad_gate_up, in_parts, preferred_element_type=jnp.float32
    ).reshape(half_rows, -1)
    _, norm_two_pull = jax.vjp(layer_norm, resid, gain_two)
    grad_resid_norm, gain_two_grad = norm_two_pull(grad_normed_two)
    grad_resid = grad_out + grad_resid_norm
    grad_branch = lax.all_gather(grad_resid.astype(jnp.bfloat16), "head", axis=0, tiled=True)
    out_grad_weight = jnp.einsum(
        "rc,rd->cd", attended_low, grad_branch, preferred_element_type=jnp.float32
    )
    grad_attended = jnp.einsum(
        "rd,cd->rc", grad_branch, out_full, preferred_element_type=jnp.float32
    ).astype(jnp.bfloat16)
    grad_three = grad_attended.reshape(block_rows, heads_here, HEAD_DIM)
    row_dots = jnp.sum(grad_three.astype(jnp.float32) * attended, axis=2).T
    all_sums, all_dots = (
        lax.all_gather(log_sums.T, "seq", axis=0, tiled=True),
        lax.all_gather(row_dots.T, "seq", axis=0, tiled=True),
    )

    def query_terms(query_grad, key_part, value_part, other_docs):
        same_doc = (local_docs[:, None] == other_docs[None, :])[None]
        _, dscore = block_grads(
            queries, grad_three, log_sums, row_dots, key_part, value_part, same_doc
        )
        return (
            query_grad
            + jnp.einsum("hqk,khd->qhd", dscore, key_part, preferred_element_type=jnp.float32)
            * score_scale
        )

    def key_terms(key_grad, value_grad, query_part, grad_part, sums_part, dots_part, other_docs):
        same_doc = (other_docs[:, None] == local_docs[None, :])[None]
        softmax_part, dscore = block_grads(
            query_part, grad_part, sums_part, dots_part, key_rows, value_rows, same_doc
        )
        value_grad = value_grad + jnp.einsum(
            "hqk,qhd->khd",
            softmax_part.astype(jnp.bfloat16),
            grad_part,
            preferred_element_type=jnp.float32,
        )
        key_grad = (
            key_grad
            + jnp.einsum("hqk,qhd->khd", dscore, query_part, preferred_element_type=jnp.float32)
            * score_scale
        )
        return (key_grad, value_grad)

    def piece_rows(source, block_begin, block_size):
        return lax.dynamic_slice_in_dim(source, block_begin, block_size, 0).reshape(
            block_size, heads_here, HEAD_DIM
        )

    def piece_stats(block_begin, block_size):
        sums_part = lax.dynamic_slice_in_dim(all_sums, block_begin, block_size, 0).T
        dots_part = lax.dynamic_slice_in_dim(all_dots, block_begin, block_size, 0).T
        other_docs, _ = doc_layout(
            short_lengths, block_begin + jnp.arange(block_size, dtype=jnp.int32), total_rows
        )
        return (sums_part, dots_part, other_docs)

    def fold_keys(carry_state, portion):
        piece_keys, piece_values = portion

        def key_block(inner_state, block_begin, block_size):
            _, _, other_docs = piece_stats(block_begin, block_size)
            return query_terms(
                inner_state,
                piece_rows(piece_keys, block_begin, block_size),
                piece_rows(piece_values, block_begin, block_size),
                other_docs,
            )

        return over_blocks(carry_state, piece_keys.shape[0], block_rows, key_block)

    query_grad = fold_keys(
        zeros_three,
        (
            lax.all_gather(key_flat, "seq", axis=0, tiled=True),
            lax.all_gather(value_flat, "seq", axis=0, tiled=True),
        ),
    )

    def fold_queries(carry_state, portion):
        piece_queries, piece_grads = portion

        def query_block(inner_state, block_begin, block_size):
            sums_part, dots_part, other_docs = piece_stats(block_begin, block_size)
            return key_terms(
                inner_state[0],
                inner_state[1],
                piece_rows(piece_queries, block_begin, block_size),
                piece_rows(piece_grads, block_begin, block_size),
                sums_part,
                dots_part,
                other_docs,
            )

        return over_blocks(carry_state, piece_queries.shape[0], block_rows, query_block)

    key_grad, value_grad = fold_queries(
        (zeros_three, zeros_three),
        (
            lax.all_gather(query_flat, "seq", axis=0, tiled=True),
            lax.all_gather(grad_attended, "seq", axis=0, tiled=True),
        ),
    )

    def rotate_local(heads_in):
        return rotate(heads_in, cosines, sines)

    _, rotate_pull = jax.vjp(rotate_local, zeros_three)
    query_back = rotate_pull(query_grad)[0]
    key_back = rotate_pull(key_grad)[0]
    grad_qkv = jnp.stack(
        [
            query_back.reshape(block_rows, -1),
            key_back.reshape(block_rows, -1),
            value_grad.reshape(block_rows, -1),
        ],
        axis=1,
    ).astype(jnp.bfloat16)
    qkv_grad = jnp.einsum("rd,rgc->dgc", normed_block, grad_qkv, preferred_element_type=jnp.float32)
    grad_normed_one = jnp.einsum(
        "rgc,dgc->rd", grad_qkv, qkv_full, preferred_element_type=jnp.float32
    )
    grad_normed_rows = lax.psum_scatter(
        grad_normed_one.astype(jnp.bfloat16), "head", scatter_dimension=0, tiled=True
    ).astype(jnp.float32)
    _, norm_one_pull = jax.vjp(layer_norm, inputs, gain_one)
    grad_inputs_norm, gain_one_grad = norm_one_pull(grad_normed_rows)
    tokens_grad = grad_resid + grad_inputs_norm
    qkv_weight_grad, out_weight_grad = (
        lax.psum_scatter(qkv_grad, "seq", scatter_dimension=0, tiled=True),
        lax.psum_scatter(out_grad_weight, "seq", scatter_dimension=1, tiled=True),
    )
    attn_gain_grad, mlp_gain_grad, in_weight_grad, down_weight_grad = (
        lax.psum_scatter(gain_one_grad, ("seq", "head"), scatter_dimension=0, tiled=True),
        lax.psum_scatter(gain_two_grad, ("seq", "head"), scatter_dimension=0, tiled=True),
        lax.psum_scatter(in_grad, ("seq", "head"), scatter_dimension=0, tiled=True),
        lax.psum_scatter(down_grad, ("seq", "head"), scatter_dimension=0, tiled=True),
    )
    return (
        mixed,
        tokens_grad,
        attn_gain_grad,
        qkv_weight_grad,
        out_weight_grad,
        mlp_gain_grad,
        in_weight_grad.reshape(in_weight.shape),
        down_weight_grad.reshape(down_weight.shape),
    )


LOW = jnp.bfloat16
FULL = jnp.float32


def dot(a, b):
    return jnp.dot(a, b, preferred_element_type=FULL)


def dot_nt(a, b):
    return lax.dot_general(a, b, (((1,), (1,)), ((), ())), preferred_element_type=FULL)


def turned(a):
    return a.astype(FULL).T


def centred_norm(rows):
    centred = rows - jnp.mean(rows, axis=-1, keepdims=True)
    scale = lax.rsqrt(jnp.mean(centred * centred, axis=-1, keepdims=True) + norm_eps)
    return centred * scale, scale


def norm_back(unit, scale, weighted):
    mean_w = jnp.mean(weighted, axis=-1, keepdims=True)
    mean_wn = jnp.mean(weighted * unit, axis=-1, keepdims=True)
    return (weighted - mean_w - unit * mean_wn) * scale


def whole_layer(*refs):
    (
        short_ref, tok_ref, gout_ref, gain_a, gain_m, qkv_ref, out_ref, in_ref, down_ref,
        mixed_out, tgrad_out, gains_out, qkvg_out, outg_out, ing_out, downg_out,
        mixed_ref, tgrad_ref, gains_ref, qkvg_ref, outg_ref, ing_ref, downg_ref,
        gain_ref, wq_ref, ffp_ref, wot_ref, xh, gt, gn, gb, wh, wht, ffw, wo, h1, cs, qa, ka, kt, vt, vr, pt, ot, ol, og, res,
        ms, ms_c, ms_a, ms_y, db, dos, dop, dot_t, ds, dqt, dq, d1, d1_c, d1_a, d1_r1, d1_s1, d1_r2, d1_s2, d1_r3,
        dw, dw_in, gf, gf_x, gf_s, gf_z, gf_f, gf_b, gf_c, go, go_x, go_s, go_z, go_f, go_b, go_c, gy, gy_in,
        s_tok, r_tok, s_gain, r_gain, s_wq, r_wq, s_g, r_g, s_ff, r_ff, s_wo, r_wo,
        s_o, r_o, s_ms, r_ms, s_db, r_db, s_do, r_do, s_d1, r_d1, s_dw, r_dw, s_gf, r_gf, s_go, r_go, s_gy, r_gy, s_out,
    ) = refs
    seq, head = lax.axis_index("seq"), lax.axis_index("head")
    z, x, c, y = seq // 4, (seq // 2) % 2, seq % 2, head
    zh, zb = z // 2, z % 2
    slot = zb * 2 + x
    active = slot < 3
    slot3 = jnp.minimum(slot, 2)
    pending, delivered = [], []

    def flip(value, bit):
        return value if bit == 0 else 1 - value

    def at(z_, x_, c_, y_):
        return (z_ * 4 + x_ * 2 + c_, y_)

    def far_z(k):
        return flip(zh, k // 2) * 2 + flip(zb, k % 2)

    def partner(dim):
        return {
            "x": at(z, 1 - x, c, y),
            "y": at(z, x, c, 1 - y),
            "z": at(far_z(1), x, c, y),
            "c": at(z, x, 1 - c, y),
            "h": at(far_z(2), x, c, y),
        }[dim]

    def push(src, dst, send, recv, device, when=None):
        copy = pltpu.make_async_remote_copy(
            src_ref=src, dst_ref=dst, send_sem=send, recv_sem=recv,
            device_id=device, device_id_type=pl.DeviceIdType.MESH,
        )
        if when is None:
            copy.start()
        else:
            pl.when(when)(copy.start)
        pending.append((when, copy))

    def deliver(k, src, dst):
        copy = pltpu.make_async_copy(src, dst, s_out.at[k])
        copy.start()
        delivered.append(copy)

    def arrive(dst, recv, when=None):
        copy = pltpu.make_async_remote_copy(
            src_ref=dst, dst_ref=dst, send_sem=recv, recv_sem=recv,
            device_id=partner("c"), device_id_type=pl.DeviceIdType.MESH,
        )
        if when is None:
            copy.wait_recv()
        else:
            pl.when(when)(copy.wait_recv)

    barrier = pltpu.get_barrier_semaphore()
    peers = []
    for k in range(1, 32):
        kz, kx, kc, ky = k // 8, (k // 4) % 2, (k // 2) % 2, k % 2
        if kz < 2 or ky == 0:
            peers.append(at(far_z(kz), flip(x, kx), flip(c, kc), flip(y, ky)))
    for peer in peers:
        pl.semaphore_signal(barrier, inc=1, device_id=peer, device_id_type=pl.DeviceIdType.MESH)

    gain_ref[...] = jnp.zeros_like(gain_ref)
    gain_ref[0:1, 0 : gain_a.shape[1]] = gain_a[...].astype(FULL)
    gain_ref[1:2, 0 : gain_m.shape[1]] = gain_m[...].astype(FULL)
    wot_ref[...] = out_ref[...]
    for g in range(3):
        for j in range(6):
            wq_ref[j, :, g * 64 : g * 64 + 64] = qkv_ref[g, :, j * 64 : j * 64 + 64]
    for c_ in range(2):
        lanes = slice(c_ * 288, c_ * 288 + 288)
        for g in range(2):
            ffp_ref[c_, :, g * 288 : g * 288 + 288] = in_ref[:, g, lanes]
        ffp_ref[c_, :, 576:864] = down_ref[:, lanes]
    pl.semaphore_wait(barrier, len(peers))

    xh[zb, x, c, y] = tok_ref[...]
    orders = (("x", "y", "z"), ("y", "z", "x"), ("z", "x", "y"))

    def third(t):
        return pl.ds(t * 256, 256)

    def blocks(ref, opened, lanes, flipped=None, core=None):
        there = {"z": zb, "x": x, "y": y, "c": c if core is None else core}
        if flipped is not None:
            there[flipped] = 1 - there[flipped]
        index = tuple(slice(None) if d in opened else there[d] for d in ("z", "x", "c", "y"))
        return ref.at[index + (slice(None), lanes)]

    for t in range(3):
        view = blocks(xh, (), third(t))
        push(view, view, s_tok.at[0, t], r_tok.at[0, t], partner(orders[t][0]))

    gt[zh, zb, x, c, y] = gain_ref[...]
    gain_order = ("x", "y", "z", "h", "c")

    def gain_view(opened, flipped=None):
        there = {"h": zh, "z": zb, "x": x, "c": c, "y": y}
        if flipped is not None:
            there[flipped] = 1 - there[flipped]
        return gt.at[tuple(slice(None) if d in opened else there[d] for d in ("h", "z", "x", "c", "y"))]

    def gain_send(k):
        view = gain_view(gain_order[:k])
        push(view, view, s_gain.at[k], r_gain.at[k], partner(gain_order[k]))

    def gain_wait(k):
        arrive(gain_view(gain_order[:k], gain_order[k]), r_gain.at[k])

    gain_send(0)

    core_rows = pl.ds(pl.multiple_of(c * 48, 16), 48)
    wo_lanes = pl.ds(pl.multiple_of(y * 384, 128), 384)
    wo_others = pl.ds(pl.multiple_of((1 - y) * 384, 128), 384)

    def ff_push(k):
        c_ = flip(c, k % 2)
        push(ffp_ref.at[c_], ffw.at[z, x, core_rows, :], s_ff.at[k], r_ff.at[k], at(far_z(k // 2), x, c_, y))

    def ff_forward(kz):
        z_ = far_z(kz)
        for kc in range(2):
            if (kz, kc) != (0, 0):
                rows = pl.ds(pl.multiple_of(flip(c, kc) * 48, 16), 48)
                arrive(ffw.at[z_, x, rows, :], r_ff.at[kz * 2 + kc])
        push(ffw.at[z_, x], ffw.at[z_, x], s_ff.at[8 + kz], r_ff.at[8 + kz], partner("x"))

    def wo_forward_x():
        for k in range(1, 4):
            arrive(wo.at[far_z(k), x, c, :, wo_lanes], r_wo.at[k])
        view = wo.at[:, x, c, :, wo_lanes]
        push(view, view, s_wo.at[4], r_wo.at[4], partner("x"))

    def wo_forward_y():
        arrive(wo.at[:, 1 - x, c, :, wo_lanes], r_wo.at[4])
        view = wo.at[:, :, c, :, wo_lanes]
        push(view, view, s_wo.at[5], r_wo.at[5], partner("y"))

    def wo_forward_core():
        arrive(wo.at[:, :, c, :, wo_others], r_wo.at[5])
        push(wo.at[:, :, c], wo.at[:, :, c], s_wo.at[6], r_wo.at[6], partner("c"))

    ffw[z, x, core_rows, :] = ffp_ref[c]
    wo[z, x, c, :, wo_lanes] = wot_ref[...]
    ff_push(1)
    for k in range(1, 4):
        push(wot_ref, wo.at[z, x, c, :, wo_lanes], s_wo.at[k], r_wo.at[k], at(far_z(k), x, c, y))

    own_rows = pl.ds(pl.multiple_of(seq * 48, 16), 48)
    for k in range(16):
        z_, x_, c_ = far_z(k // 4), flip(x, (k // 2) % 2), flip(c, k % 2)
        slot_ = (z_ % 2) * 2 + x_
        piece = wq_ref.at[jnp.minimum(slot_ * 2 + c_, 5)]
        if k == 0:
            wh[own_rows, :] = piece[...]
        else:
            push(piece, wh.at[own_rows, :], s_wq.at[k], r_wq.at[k], at(z_, x_, c_, y), slot_ < 3)

    for k in range(2, 8):
        ff_push(k)

    gb[c, y] = gout_ref[...]
    group = ((0, 1), (1, 0), (1, 1))
    for k, (kc, ky) in enumerate(group):
        push(gb.at[c, y], gb.at[c, y], s_g.at[k], r_g.at[k], at(z, x, flip(c, kc), flip(y, ky)))

    def token_step(step):
        for t in range(3):
            arrive(blocks(xh, orders[t][: step - 1], third(t), orders[t][step - 1]), r_tok.at[step - 1, t])
            view = blocks(xh, orders[t][:step], third(t))
            push(view, view, s_tok.at[step, t], r_tok.at[step, t], partner(orders[t][step]))
        gain_wait(step - 1)
        gain_send(step)

    ff_forward(0)
    token_step(1)
    wo_forward_x()
    token_step(2)
    ff_forward(1)
    wo_forward_y()
    gain_wait(2)
    gain_send(3)
    for t in range(3):
        arrive(blocks(xh, orders[t][:2], third(t), orders[t][2]), r_tok.at[2, t])
        view = blocks(xh, ("x", "y", "z"), third(t))
        push(view, view, s_tok.at[3, t], r_tok.at[3, t], partner("c"))

    half_rows = 1024
    row = lax.broadcasted_iota(jnp.int32, (32, half_rows), 1) + zh * half_rows
    feature = lax.broadcasted_iota(jnp.int32, (32, half_rows), 0)
    bound = jnp.int32(2 * half_rows)
    for b in range(short_ref.shape[0]):
        bound = bound - short_ref[b]
    doc = jnp.zeros_like(row)
    start = jnp.zeros_like(row)
    for b in range(short_ref.shape[0]):
        passed = row >= bound
        doc = doc + jnp.where(passed, 1, 0)
        start = jnp.where(passed, bound, start)
        bound = bound + short_ref[b]
    inverse = jnp.exp(feature.astype(FULL) * (-2.0 * math.log(rope_base) / HEAD_DIM))
    angles = (row - start).astype(FULL) * inverse
    cs[0] = jnp.cos(angles)
    cs[1] = jnp.sin(angles)
    same = jnp.where(feature == doc, 1.0, 0.0)
    cs[2] = same
    qa[64:96, :] = ((same - 1.0) * 1e30).astype(LOW)
    qa[96:128, :] = jnp.zeros((32, half_rows), LOW)

    gain_wait(3)
    gain_send(4)
    gain_wait(4)
    tiles = gt[...].reshape(256, 128).astype(LOW)
    width = 24
    pick = lax.broadcasted_iota(jnp.int32, (128, 768), 1) % width == lax.broadcasted_iota(jnp.int32, (128, 768), 0)
    spread = dot(tiles, jnp.where(pick, 1.0, 0.0).astype(LOW))
    source = lax.broadcasted_iota(jnp.int32, (256, 768), 0)
    wanted = (lax.broadcasted_iota(jnp.int32, (256, 768), 1) // width) * 8
    gn[0:1, :] = jnp.sum(jnp.where(source == wanted, spread, 0.0), axis=0, keepdims=True)
    gn[1:2, :] = jnp.sum(jnp.where(source == wanted + 1, spread, 0.0), axis=0, keepdims=True)

    ff_forward(2)
    for t in range(3):
        arrive(blocks(xh, ("x", "y", "z"), third(t), "c"), r_tok.at[3, t])
    for k in range(1, 16):
        source_seq = far_z(k // 4) * 4 + flip(x, (k // 2) % 2) * 2 + flip(c, k % 2)
        arrive(wh.at[pl.ds(pl.multiple_of(source_seq * 48, 16), 48), :], r_wq.at[k], active)

    @pl.when(active)
    def _():
        gain = gn[0:1, :]

        def normed_block(b, carry):
            rows = xh[b // 8, (b // 4) % 2, (b // 2) % 2, b % 2].astype(FULL)
            unit, _ = centred_norm(rows)
            h1[pl.ds(pl.multiple_of(b * 64, 64), 64), :] = (unit * gain).astype(LOW)
            return carry

        lax.fori_loop(0, 16, normed_block, 0)
        wht[...] = turned(wh[...]).astype(LOW)
        for part in range(4):
            cols = pl.ds(part * 256, 256)
            proj = dot_nt(wht[...], h1[cols, :])
            cosine, sine = cs[0, :, cols], cs[1, :, cols]
            q1, q2, k1, k2 = proj[0:32], proj[32:64], proj[64:96], proj[96:128]
            qr = jnp.concatenate([q1 * cosine - q2 * sine, q2 * cosine + q1 * sine], axis=0)
            kr = jnp.concatenate([k1 * cosine - k2 * sine, k2 * cosine + k1 * sine], axis=0)
            qa[0:64, cols] = (qr * score_scale).astype(LOW)
            kt[:, cols] = kr.astype(LOW)
            vt[:, cols] = proj[128:192].astype(LOW)
            pad = jnp.zeros((32, 256), FULL)
            ka[cols, :] = jnp.concatenate([kr, cs[2, :, cols], pad], axis=0).T.astype(LOW)
            vr[cols, :] = proj[128:192].T.astype(LOW)

    ff_forward(3)
    wo_forward_core()

    for part in range(4):
        cols = pl.ds(part * 256, 256)

        @pl.when(active)
        def _(part=part, cols=cols):
            scores = dot(ka[...], qa[:, cols])
            expo = jnp.exp(scores - jnp.max(scores, axis=0, keepdims=True))
            prob = (expo * (1.0 / jnp.sum(expo, axis=0, keepdims=True))).astype(LOW)
            pt[:, cols] = prob
            result = dot(vt[...], prob)
            ot[part] = result
            ol[part] = result.astype(LOW)

        for y_ in range(2):
            mine = jnp.logical_and(slot == part, y == y_)

            @pl.when(jnp.logical_and(active, mine))
            def _(part=part):
                og[y, slot3, c] = ol[part]

            push(
                ol.at[part], og.at[y, slot3, c], s_o.at[part, y_], r_o.at[slot3, y],
                at(zh * 2 + part // 2, part % 2, c, y_), jnp.logical_and(active, jnp.logical_not(mine)),
            )

    for slot_ in range(3):
        for y_ in range(2):
            mine = jnp.logical_and(slot == slot_, y == y_)
            arrive(og.at[y_, slot_, c], r_o.at[slot_, y_], jnp.logical_not(mine))
    push(og.at[:, :, c], og.at[:, :, c], s_o.at[4, 0], r_o.at[3, 0], partner("c"))
    arrive(og.at[:, :, 1 - c], r_o.at[3, 0])
    arrive(wo.at[:, :, 1 - c], r_wo.at[6])

    gain_two = gn[1:2, :]
    branch = dot(wo[...].reshape(768, 768), og[...].reshape(768, 256)).T
    resid = xh[zb, x].reshape(256, 768).astype(FULL) + branch
    res[...] = resid.reshape(2, 2, 64, 768)
    unit_two, _ = centred_norm(resid)
    h2 = (unit_two * gain_two).astype(LOW)

    for kz in range(4):
        arrive(ffw.at[far_z(kz), 1 - x], r_ff.at[8 + kz])
    for k, (kc, ky) in enumerate(group):
        arrive(gb.at[flip(c, kc), flip(y, ky)], r_g.at[k])
    w_in = ffw[:, :, :, 0:576].reshape(768, 576)
    w_down = ffw[:, :, :, 576:864].reshape(768, 288)
    gate_up = dot(h2, w_in)
    gate, up = gate_up[:, :288], gate_up[:, 288:]
    grad_out = gb[...].reshape(256, 768)
    grad_hidden = dot(grad_out, w_down)
    chance = 0.5 * (1.0 + lax.erf(gate * (1.0 / math.sqrt(2.0))))
    density = jnp.exp(gate * gate * -0.5) * (1.0 / math.sqrt(2.0 * math.pi))
    curve = gate * chance
    hidden = (curve * up).astype(LOW)
    grad_gate = grad_hidden * up * (chance + gate * density)
    grad_gate_up = jnp.concatenate([grad_gate, grad_hidden * curve], axis=1).astype(LOW)

    def halve(kind, part):
        ms[kind] = part.astype(LOW).reshape(2, 2, 64, 768)
        push(ms.at[kind, 1 - c], ms_c.at[kind], s_ms.at[kind, 0], r_ms.at[kind, 0], partner("c"))

    def quarter(kind):
        arrive(ms_c.at[kind], r_ms.at[kind, 0])
        ms_a[kind] = (ms[kind, c, 1 - y].astype(FULL) + ms_c[kind, 1 - y].astype(FULL)).astype(LOW)
        push(ms_a.at[kind], ms_y.at[kind], s_ms.at[kind, 1], r_ms.at[kind, 1], partner("y"))

    def quarter_sum(kind):
        arrive(ms_y.at[kind], r_ms.at[kind, 1])
        return ms[kind, c, y].astype(FULL) + ms_c[kind, y].astype(FULL) + ms_y[kind].astype(FULL)

    halve(0, dot_nt(grad_gate_up, w_in))
    halve(1, dot_nt(hidden, w_down))
    quarter(0)
    h2_t = turned(h2).astype(LOW)
    gf[:, :, :, 0:576] = dot(h2_t, grad_gate_up).astype(LOW).reshape(4, 2, 96, 576)
    g_t = turned(grad_out).astype(LOW)
    gf[:, :, :, 576:864] = dot(g_t, hidden).astype(LOW).reshape(4, 2, 96, 288)
    for kz in (3, 2, 1, 0):
        z_ = far_z(kz)
        push(gf.at[z_, 1 - x], gf_x.at[z_], s_gf.at[0, kz], r_gf.at[0, kz], partner("x"))
    quarter(1)

    own_res = res[c, y]
    unit_two, scale_two = centred_norm(own_res)
    grad_h2 = quarter_sum(0)
    grad_resid = gout_ref[...].astype(FULL) + norm_back(unit_two, scale_two, grad_h2 * gain_two)
    tgrad_ref[...] = grad_resid
    grad_branch = grad_resid.astype(LOW)
    db[c, y] = grad_branch
    grad_o = dot(grad_branch, wo[...].reshape(768, 768)).astype(LOW)
    own_block = zb * 8 + x * 4 + c * 2 + y
    for slot_ in range(3):
        for y_ in range(2):
            lanes = y_ * 384 + slot_ * 128
            dos[y_, slot_] = grad_o[:, lanes : lanes + 128]
            for c_ in range(2):
                mine = jnp.logical_and(jnp.logical_and(slot == slot_, y == y_), c == c_)

                @pl.when(mine)
                def _(slot_=slot_, y_=y_):
                    dop[zb, x, c, y] = dos[y_, slot_]

                push(
                    dos.at[y_, slot_], dop.at[zb, x, c, y], s_do.at[slot_ * 4 + y_ * 2 + c_], r_do.at[own_block],
                    at(zh * 2 + slot_ // 2, slot_ % 2, c_, y_), jnp.logical_not(mine),
                )
    for k, (kc, ky) in enumerate(group):
        push(db.at[c, y], db.at[c, y], s_db.at[k], r_db.at[k], at(z, x, flip(c, kc), flip(y, ky)))
    mixed_ref[...] = (own_res + quarter_sum(1)).astype(LOW)
    deliver(0, mixed_ref, mixed_out)
    def sum_x(kz, mine, other, total, send, recv, landing):
        z_ = far_z(kz)
        arrive(other.at[z_], recv.at[0, kz])
        total[z_] = (mine[z_, x].astype(FULL) + other[z_].astype(FULL)).astype(LOW)
        if kz:
            push(total.at[z_], landing.at[kz - 1], send.at[1, kz], recv.at[1, kz], at(z_, x, c, y))

    def out_share():
        for k, (kc, ky) in enumerate(group):
            arrive(db.at[flip(c, kc), flip(y, ky)], r_db.at[k])
        db_t = turned(db[...].reshape(256, 768)).astype(LOW)
        o_part = og[...].reshape(2, 6, 64, 256)
        o_pick = jnp.where(y == 0, o_part[0], o_part[1])
        o_pick = jnp.where(c == 0, o_pick[0:3], o_pick[3:6]).reshape(192, 256)
        go[...] = dot_nt(db_t, o_pick).astype(LOW).reshape(4, 2, 96, 192)
        for kz in (3, 2, 1, 0):
            z_ = far_z(kz)
            push(go.at[z_, 1 - x], go_x.at[z_], s_go.at[0, kz], r_go.at[0, kz], partner("x"))

    sum_x(3, gf, gf_x, gf_s, s_gf, r_gf, gf_z)

    for b in range(16):
        z_, x_, c_, y_ = b // 8, (b // 4) % 2, (b // 2) % 2, b % 2
        arrive(dop.at[z_, x_, c_, y_], r_do.at[b], jnp.logical_and(active, own_block != b))

    @pl.when(active)
    def _():
        pair = turned(dop[...].reshape(1024, 128))
        dot_t[...] = jnp.where(c == 0, pair[0:64], pair[64:128]).astype(LOW)

    for part in range(4):
        cols = pl.ds(part * 256, 256)

        @pl.when(active)
        def _(part=part, cols=cols):
            grad_t = dot_t[:, cols]
            delta = jnp.sum(grad_t.astype(FULL) * ot[part], axis=0, keepdims=True)
            grad_p = dot(vr[...], grad_t)
            score_grad = (pt[:, cols].astype(FULL) * (grad_p - delta)).astype(LOW)
            ds[:, cols] = score_grad
            back = dot(kt[...], score_grad) * score_scale
            cosine, sine = cs[0, :, cols], cs[1, :, cols]
            b1, b2 = back[0:32], back[32:64]
            dqt[0:64, cols] = jnp.concatenate([b1 * cosine + b2 * sine, b2 * cosine - b1 * sine], axis=0).astype(LOW)

        if part == 0:
            out_share()
        if part < 3:
            sum_x(2 - part, gf, gf_x, gf_s, s_gf, r_gf, gf_z)

    @pl.when(active)
    def _():
        for part in range(4):
            cols = pl.ds(part * 256, 256)
            back = dot_nt(qa[0:64, :], ds[cols, :])
            cosine, sine = cs[0, :, cols], cs[1, :, cols]
            b1, b2 = back[0:32], back[32:64]
            dqt[64:128, cols] = jnp.concatenate([b1 * cosine + b2 * sine, b2 * cosine - b1 * sine], axis=0).astype(LOW)
            dqt[128:192, cols] = dot_nt(dot_t[...], pt[cols, :]).astype(LOW)
            dq[cols, :] = turned(dqt[:, cols]).astype(LOW)

    for part in range(4):
        cols = pl.ds(part * 256, 256)

        @pl.when(active)
        def _(part=part, cols=cols):
            d1[part // 2, part % 2] = dot_nt(dq[cols, :], wh[...]).astype(LOW).reshape(2, 2, 64, 768)

        push(
            d1.at[part // 2, part % 2, 1 - c], d1_c.at[part // 2, part % 2],
            s_d1.at[0, part], r_d1.at[0, part], partner("c"), active,
        )
    for part in (3, 2, 1, 0):
        sum_x(part, go, go_x, go_s, s_go, r_go, go_z)

    @pl.when(jnp.logical_not(active))
    def _():
        d1_a[...] = jnp.zeros_like(d1_a)

    for part in range(4):
        arrive(d1_c.at[part // 2, part % 2], r_d1.at[0, part], active)

        @pl.when(active)
        def _(part=part):
            both = d1[part // 2, part % 2, c].astype(FULL) + d1_c[part // 2, part % 2].astype(FULL)
            d1_a[part // 2, part % 2] = both.astype(LOW)

    def remaining(t, step):
        return tuple(d for d in ("z", "x", "y") if d not in orders[t][:step])

    landing = (d1_r1, d1_r2, d1_r3)

    def step_view(t, step, flipped):
        dim = orders[t][step]
        place = {"z": zb, "x": x, "y": y}[dim]
        place = 1 - place if flipped else place
        index = tuple(place if d == dim else slice(None) for d in remaining(t, step))
        if step == 0:
            return d1_a.at[index + (slice(None), third(t))]
        return (d1_s1, d1_s2)[step - 1].at[(t,) + index]

    def step_push(t, step):
        push(
            step_view(t, step, True), landing[step].at[t], s_d1.at[1 + step, t], r_d1.at[1 + step, t],
            partner(orders[t][step]),
        )

    def step_sum(t, step):
        arrive(landing[step].at[t], r_d1.at[1 + step, t])
        return step_view(t, step, False)[...].astype(FULL) + landing[step][t].astype(FULL)

    for t in range(3):
        step_push(t, 0)

    @pl.when(active)
    def _():
        grad = dot(dqt[...], h1[...])
        dw[...] = grad.T.astype(LOW).reshape(16, 48, 192)

    own_head = zh * 6 + slot3 * 2 + c

    @pl.when(active)
    def _():
        dw_in[own_head] = dw[seq]

    for k in range(1, 16):
        z_, x_, c_ = far_z(k // 4), flip(x, (k // 2) % 2), flip(c, k % 2)
        push(dw.at[z_ * 4 + x_ * 2 + c_], dw_in.at[own_head], s_dw.at[k], r_dw.at[own_head], at(z_, x_, c_, y), active)

    for t in range(3):
        d1_s1[t] = step_sum(t, 0).astype(LOW)
        step_push(t, 1)

    def sum_z(total, landed, wide, low, send, recv, coming):
        value = total[z].astype(FULL)
        for k in range(1, 4):
            arrive(landed.at[k - 1], recv.at[1, k])
            value = value + landed[k - 1].astype(FULL)
        wide[...] = value.reshape(wide.shape)
        low[...] = wide[1 - c].astype(LOW)
        push(low, coming, send.at[2, 0], recv.at[2, 0], partner("c"))

    sum_z(gf_s, gf_z, gf_f, gf_b, s_gf, r_gf, gf_c)
    for t in range(3):
        d1_s2[t] = step_sum(t, 1).astype(LOW)
        step_push(t, 2)
    sum_z(go_s, go_z, go_f, go_b, s_go, r_go, go_c)
    arrive(gf_c, r_gf.at[2, 0])
    def by_core(own, other):
        return jnp.where(c == 0, own, other), jnp.where(c == 0, other, own)

    mlp_terms = jnp.zeros((48, 1), FULL)
    for c_, grads in enumerate(by_core(gf_f[c], gf_c[...].astype(FULL))):
        lanes = slice(c_ * 288, c_ * 288 + 288)
        for g in range(2):
            ing_ref[:, g, lanes] = grads[:, g * 288 : g * 288 + 288]
        downg_ref[:, lanes] = grads[:, 576:864]
        terms = grads[:, 0:576] * ffp_ref[c_, :, 0:576].astype(FULL)
        mlp_terms = mlp_terms + jnp.sum(terms, axis=1, keepdims=True)
    deliver(1, ing_ref, ing_out)
    deliver(2, downg_ref, downg_out)
    for h_ in range(2):
        for j in range(6):
            arrive(dw_in.at[h_ * 6 + j], r_dw.at[h_ * 6 + j], jnp.logical_not(jnp.logical_and(active, own_head == h_ * 6 + j)))
    attn_terms = jnp.zeros((48, 1), FULL)
    for j in range(6):
        both = dw_in[j].astype(FULL) + dw_in[6 + j].astype(FULL)
        for g in range(3):
            qkvg_ref[g, :, j * 64 : j * 64 + 64] = both[:, g * 64 : g * 64 + 64]
        attn_terms = attn_terms + jnp.sum(both * wq_ref[j].astype(FULL), axis=1, keepdims=True)
    deliver(3, qkvg_ref, qkvg_out)
    lane = lax.broadcasted_iota(jnp.int32, (48, 128), 1)
    gy[...] = jnp.where(lane == 0, attn_terms, jnp.where(lane == 1, mlp_terms, 0.0))
    push(gy, gy_in, s_gy.at[0], r_gy.at[0], partner("y"))
    arrive(go_c, r_go.at[2, 0])
    for c_, grads in enumerate(by_core(go_f[c], go_c[...].astype(FULL))):
        outg_ref[:, c_ * 192 : c_ * 192 + 192] = grads
    deliver(4, outg_ref, outg_out)

    unit_one, scale_one = centred_norm(tok_ref[...].astype(FULL))
    for t in range(3):
        res[0, 0, :, third(t)] = step_sum(t, 2)
    tgrad_ref[...] = tgrad_ref[...] + norm_back(unit_one, scale_one, res[0, 0] * gn[0:1, :])
    deliver(5, tgrad_ref, tgrad_out)
    arrive(gy_in, r_gy.at[0])
    sums = (gy[...] + gy_in[...]).T
    count = gain_a.shape[1]
    sums = jnp.where(y == 0, sums[0:2, :count], sums[0:2, count : 2 * count])
    gains_ref[...] = jnp.zeros_like(gains_ref)
    gains_ref[0:2, 0:count] = sums / gain_ref[0:2, 0:count]
    deliver(6, gains_ref, gains_out)
    for copy in delivered:
        copy.wait()
    for when, copy in pending:
        if when is None:
            copy.wait_send()
        else:
            pl.when(when)(copy.wait_send)


def hand_on(*refs):
    sources, results, held, sems = refs[:7], refs[7:15], refs[15:21], refs[21]
    count = results[6].shape[1]
    results[6][...] = sources[6][0:1, :count]
    results[7][...] = sources[6][1:2, :count]
    inward = [pltpu.make_async_copy(a, b, sems.at[0, k]) for k, (a, b) in enumerate(zip(sources[:6], held))]
    outward = [pltpu.make_async_copy(a, b, sems.at[1, k]) for k, (a, b) in enumerate(zip(held, results[:6]))]
    for copy in inward:
        copy.start()
    for first, second in zip(inward, outward):
        first.wait()
        second.start()
    for copy in outward:
        copy.wait()


def on_device_fast(tokens, out_grad, short_lengths, attn_gain, qkv_weight, out_weight, mlp_gain, in_weight, down_weight):
    rows, width = tokens.shape
    depth = qkv_weight.shape[0]
    heads_here = qkv_weight.shape[2] // HEAD_DIM
    count = attn_gain.shape[0]
    ff = in_weight.shape[2] // 2 * 3
    feats = out_weight.shape[0]

    def vm(shape, kind=LOW):
        return pltpu.VMEM(shape, kind)

    def sem(*shape):
        return pltpu.SemaphoreType.DMA(shape)

    finals = [
        ((rows, width), LOW), ((rows, width), FULL), ((8, 128), FULL), ((3, depth, 384), FULL),
        ((depth, feats), FULL), ((depth, 2, 576), FULL), ((depth, 576), FULL),
    ]
    scratch = [vm(*shape) for shape in finals] + [
        vm((8, 128), FULL), vm((heads_here, depth, 192)), vm((2, depth, ff)), vm((depth, feats)),
        vm((2, 2, 2, 2, 64, 768)), vm((2, 2, 2, 2, 2, 8, 128), FULL), vm((8, 768), FULL), vm((2, 2, 64, 768)),
        vm((768, 192)), vm((192, 768)), vm((4, 2, 96, 864)), vm((4, 2, 2, 48, 768)), vm((1024, 768)),
        vm((3, 32, 1024), FULL), vm((128, 1024)), vm((1024, 128)), vm((64, 1024)), vm((64, 1024)), vm((1024, 64)),
        vm((1024, 1024)), vm((4, 64, 256), FULL), vm((4, 64, 256)), vm((2, 3, 2, 64, 256)), vm((2, 2, 64, 768), FULL),
        vm((2, 2, 2, 64, 768)), vm((2, 2, 64, 768)), vm((2, 64, 768)), vm((2, 64, 768)), vm((2, 2, 64, 768)),
        vm((2, 3, 64, 128)), vm((2, 2, 2, 2, 64, 128)), vm((64, 1024)), vm((1024, 1024)), vm((192, 1024)),
        vm((1024, 192)), vm((2, 2, 2, 2, 64, 768)), vm((2, 2, 2, 64, 768)), vm((2, 2, 2, 64, 768)),
        vm((3, 2, 2, 64, 256)), vm((3, 2, 2, 64, 256)), vm((3, 2, 64, 256)), vm((3, 2, 64, 256)), vm((3, 64, 256)),
        vm((16, 48, 192)), vm((12, 48, 192)),
        vm((4, 2, 96, 864)), vm((4, 96, 864)), vm((4, 96, 864)), vm((3, 96, 864)), vm((2, 48, 864), FULL),
        vm((48, 864)), vm((48, 864)),
        vm((4, 2, 96, 192)), vm((4, 96, 192)), vm((4, 96, 192)), vm((3, 96, 192)), vm((2, 48, 192), FULL),
        vm((48, 192)), vm((48, 192)),
        vm((48, 128), FULL), vm((48, 128), FULL),
        sem(4, 3), sem(4, 3), sem(5), sem(5), sem(16), sem(16), sem(3), sem(3), sem(12), sem(12), sem(7), sem(7),
        sem(5, 2), sem(4, 2), sem(2, 2), sem(2, 2), sem(3), sem(3), sem(12), sem(16), sem(4, 4), sem(4, 4),
        sem(16), sem(12), sem(3, 4), sem(3, 4), sem(3, 4), sem(3, 4), sem(1), sem(1), sem(7),
    ]
    vmem = pl.BlockSpec(memory_space=pltpu.VMEM)
    anywhere = pl.BlockSpec(memory_space=pl.ANY)
    shapes = [jax.ShapeDtypeStruct(*shape) for shape in finals]
    mixed, tokens_grad, gains, qkv_grad, out_grads, in_grad, down_grad = pl.pallas_call(
        whole_layer,
        out_shape=shapes,
        in_specs=[pl.BlockSpec(memory_space=pltpu.SMEM)] + [vmem] * 8,
        out_specs=[anywhere] * 7,
        scratch_shapes=scratch,
        compiler_params=pltpu.CompilerParams(collective_id=0, has_side_effects=True, vmem_limit_bytes=60 << 20),
    )(
        short_lengths, tokens, out_grad, attn_gain[None], mlp_gain[None],
        qkv_weight.transpose(1, 0, 2), out_weight.T, in_weight, down_weight.T,
    )
    grads = (mixed, tokens_grad, qkv_grad, out_grads, in_grad, down_grad)
    count = attn_gain.shape[0]
    mixed, tokens_grad, qkv_grad, out_grads, in_grad, down_grad, attn_gain_grad, mlp_gain_grad = pl.pallas_call(
        hand_on,
        out_shape=[jax.ShapeDtypeStruct(a.shape, a.dtype) for a in grads] + [jax.ShapeDtypeStruct((1, count), FULL)] * 2,
        in_specs=[anywhere] * 6 + [vmem],
        out_specs=[anywhere] * 6 + [vmem] * 2,
        scratch_shapes=[vm(a.shape, a.dtype) for a in grads] + [sem(2, 6)],
    )(*grads, gains)
    return (
        mixed, tokens_grad, attn_gain_grad[0], qkv_grad.transpose(1, 0, 2), out_grads.T, mlp_gain_grad[0],
        in_grad, down_grad.T,
    )


def solution(mesh):
    placed = (
        P(("seq", "head"), None),
        P(("seq", "head"), None),
        P(),
        P(("seq", "head")),
        P("seq", None, "head"),
        P("head", "seq"),
        P(("seq", "head")),
        P("seq", None, "head"),
        P("head", "seq"),
    )
    fits = mesh.shape["seq"] == 16 and mesh.shape["head"] == 2
    return jax.shard_map(
        on_device_fast if fits else on_device,
        mesh=mesh,
        in_specs=placed,
        out_specs=(
            P(("seq", "head"), None),
            P(("seq", "head"), None),
            P(("seq", "head")),
            P("seq", None, "head"),
            P("head", "seq"),
            P(("seq", "head")),
            P("seq", None, "head"),
            P("head", "seq"),
        ),
        check_vma=False,
    )
```

```python
import math

import jax
import jax.numpy as jnp
from jax import lax
from jax.experimental import pallas as pl
from jax.experimental.pallas import tpu as pltpu
from jax.sharding import PartitionSpec as P

HEAD_DIM = 64


norm_eps = 1e-05
rope_base = 160000.0
score_scale = 0.125
masked_low = -1e30


def layer_norm(inputs, gain_vector):
    row_mean = jnp.mean(inputs, axis=-1, keepdims=True)
    centred = inputs - row_mean
    spread = jnp.mean(centred * centred, axis=-1, keepdims=True)
    return centred * lax.rsqrt(spread + norm_eps) * gain_vector


def doc_layout(short_lengths, row_ids, total_rows):
    long_end = total_rows - jnp.sum(short_lengths)
    before = jnp.cumsum(short_lengths) - short_lengths
    bounds = long_end + before
    passed = row_ids[:, None] >= bounds[None, :]
    doc_ids = jnp.sum(passed.astype(jnp.int32), axis=1)
    starts = jnp.max(jnp.where(passed, bounds[None, :], jnp.zeros_like(bounds)[None, :]), axis=1)
    return (doc_ids, row_ids - starts)


def rope_tables(positions):
    steps_half = jnp.arange(HEAD_DIM // 2, dtype=jnp.float32)
    inverse = jnp.exp(steps_half * (-2.0 * math.log(rope_base) / HEAD_DIM))
    angles = positions.astype(jnp.float32)[:, None] * inverse[None, :]
    cosines = jnp.cos(angles)
    sines = jnp.sin(angles)
    return (jnp.concatenate([cosines, cosines], axis=1), jnp.concatenate([sines, sines], axis=1))


def rotate(heads_in, cosines, sines):
    half_dim = heads_in.shape[-1] // 2
    turned = jnp.concatenate([-heads_in[..., half_dim:], heads_in[..., :half_dim]], axis=-1)
    return heads_in * cosines[:, None, :] + turned * sines[:, None, :]


def block_length(row_count, shard_rows):
    shards = row_count // shard_rows
    return shard_rows * math.gcd(shards, max(1, 1024 // shard_rows))


def over_blocks(carry_state, row_count, shard_rows, block_fn):
    block_size = block_length(row_count, shard_rows)

    def block_step(inner_state, block_index):
        return (block_fn(inner_state, block_index * block_size, block_size), None)

    carry_state, _ = lax.scan(
        block_step, carry_state, jnp.arange(row_count // block_size, dtype=jnp.int32)
    )
    return carry_state


def scores_of(queries, key_part):
    return (
        jnp.einsum("qhd,khd->hqk", queries, key_part, preferred_element_type=jnp.float32)
        * score_scale
    )


def block_grads(queries, grad_rows, log_sums, row_dots, key_part, value_part, same_doc):
    scores = scores_of(queries, key_part)
    softmax_part = jnp.where(same_doc, jnp.exp(scores - log_sums[:, :, None]), 0.0)
    grad_probs = jnp.einsum(
        "qhd,khd->hqk", grad_rows, value_part, preferred_element_type=jnp.float32
    )
    dscore = (softmax_part * (grad_probs - row_dots[:, :, None])).astype(jnp.bfloat16)
    return (softmax_part, dscore)


def on_device(
    tokens,
    out_grad,
    short_lengths,
    attn_gain,
    qkv_weight,
    out_weight,
    mlp_gain,
    in_weight,
    down_weight,
):
    half_rows = tokens.shape[0]
    head_count = lax.axis_size("head")
    seq_count = lax.axis_size("seq")
    block_rows = half_rows * head_count
    total_rows = block_rows * seq_count
    local_ids = lax.axis_index("seq") * block_rows + jnp.arange(block_rows, dtype=jnp.int32)
    local_docs, local_pos = doc_layout(short_lengths, local_ids, total_rows)
    cosines, sines = rope_tables(local_pos)
    qkv_full, out_full = (
        lax.all_gather(qkv_weight, "seq", axis=0, tiled=True),
        lax.all_gather(out_weight, "seq", axis=1, tiled=True),
    )
    gain_first, gain_second, in_parts, down_parts = (
        lax.all_gather(attn_gain, ("seq", "head"), axis=0, tiled=True),
        lax.all_gather(mlp_gain, ("seq", "head"), axis=0, tiled=True),
        lax.all_gather(in_weight[None], ("seq", "head"), axis=0, tiled=True),
        lax.all_gather(down_weight[None], ("seq", "head"), axis=0, tiled=True),
    )
    in_parts = in_parts.reshape(seq_count, head_count, in_weight.shape[0], 2, in_weight.shape[2])
    down_parts = down_parts.reshape(
        seq_count, head_count, down_weight.shape[0], down_weight.shape[1]
    )
    heads_here = qkv_full.shape[2] // HEAD_DIM
    inputs = tokens.astype(jnp.float32)
    gain_one = gain_first.astype(jnp.float32)
    normed = layer_norm(inputs, gain_one).astype(jnp.bfloat16)
    normed_block = lax.all_gather(normed, "head", axis=0, tiled=True)
    projected = jnp.einsum(
        "rd,dgc->rgc", normed_block, qkv_full, preferred_element_type=jnp.float32
    )
    queries = rotate(
        projected[:, 0].reshape(block_rows, heads_here, HEAD_DIM), cosines, sines
    ).astype(jnp.bfloat16)
    key_rows = rotate(
        projected[:, 1].reshape(block_rows, heads_here, HEAD_DIM), cosines, sines
    ).astype(jnp.bfloat16)
    value_flat = projected[:, 2].astype(jnp.bfloat16)
    value_rows = value_flat.reshape(block_rows, heads_here, HEAD_DIM)
    key_flat = key_rows.reshape(block_rows, -1)
    query_flat = queries.reshape(block_rows, -1)

    def forward_fold(carry_state, portion):
        piece_keys, piece_values = portion

        def forward_block(inner_state, block_begin, block_size):
            running_max, running_sum, weighted = inner_state
            key_part = lax.dynamic_slice_in_dim(piece_keys, block_begin, block_size, 0).reshape(
                block_size, heads_here, HEAD_DIM
            )
            value_part = lax.dynamic_slice_in_dim(piece_values, block_begin, block_size, 0).reshape(
                block_size, heads_here, HEAD_DIM
            )
            other_docs, _ = doc_layout(
                short_lengths, block_begin + jnp.arange(block_size, dtype=jnp.int32), total_rows
            )
            same_doc = (local_docs[:, None] == other_docs[None, :])[None]
            scores = scores_of(queries, key_part)
            new_max = jnp.maximum(
                running_max, jnp.max(jnp.where(same_doc, scores, masked_low), axis=2)
            )
            factor = jnp.exp(running_max - new_max)
            softmax_part = jnp.where(same_doc, jnp.exp(scores - new_max[:, :, None]), 0.0)
            running_sum = running_sum * factor + jnp.sum(softmax_part, axis=2)
            weighted = weighted * factor.T[:, :, None] + jnp.einsum(
                "hqk,khd->qhd",
                softmax_part.astype(jnp.bfloat16),
                value_part,
                preferred_element_type=jnp.float32,
            )
            return (new_max, running_sum, weighted)

        return over_blocks(carry_state, piece_keys.shape[0], block_rows, forward_block)

    zeros_three = jnp.zeros((block_rows, heads_here, HEAD_DIM), jnp.float32)
    start_state = (
        jnp.full((heads_here, block_rows), masked_low, jnp.float32),
        jnp.zeros((heads_here, block_rows), jnp.float32),
        zeros_three,
    )
    running_max, running_sum, weighted = forward_fold(
        start_state,
        (
            lax.all_gather(key_flat, "seq", axis=0, tiled=True),
            lax.all_gather(value_flat, "seq", axis=0, tiled=True),
        ),
    )
    attended = weighted / running_sum.T[:, :, None]
    log_sums = running_max + jnp.log(running_sum)
    attended_low = attended.reshape(block_rows, -1).astype(jnp.bfloat16)
    branch = jnp.dot(attended_low, out_full, preferred_element_type=jnp.float32)
    branch_rows = lax.psum_scatter(
        branch.astype(jnp.bfloat16), "head", scatter_dimension=0, tiled=True
    ).astype(jnp.float32)
    resid = inputs + branch_rows
    gain_two = gain_second.astype(jnp.float32)
    normed_two = layer_norm(resid, gain_two).astype(jnp.bfloat16)
    normed_split = normed_two.reshape(half_rows, seq_count, -1)
    gate_up = jnp.einsum(
        "rse,shegf->rghf", normed_split, in_parts, preferred_element_type=jnp.float32
    ).reshape(half_rows, 2, -1)

    def activate(gate_part, up_part):
        return jax.nn.gelu(gate_part, approximate=False) * up_part

    hidden, activate_pull = jax.vjp(activate, gate_up[:, 0], gate_up[:, 1])
    hidden_low = hidden.astype(jnp.bfloat16)
    hidden_split = hidden_low.reshape(half_rows, head_count, -1)
    mlp_out = jnp.einsum(
        "rhf,shfe->rse", hidden_split, down_parts, preferred_element_type=jnp.float32
    ).reshape(half_rows, -1)
    mixed = (resid + mlp_out).astype(jnp.bfloat16)
    grad_out = out_grad.astype(jnp.float32)
    grad_split = out_grad.reshape(half_rows, seq_count, -1)
    grad_hidden = jnp.einsum(
        "rse,shfe->rhf", grad_split, down_parts, preferred_element_type=jnp.float32
    ).reshape(half_rows, -1)
    grad_gate, grad_up = activate_pull(grad_hidden)
    grad_gate_up = (
        jnp.stack([grad_gate, grad_up], axis=1)
        .astype(jnp.bfloat16)
        .reshape(half_rows, 2, head_count, -1)
    )
    down_grad = jnp.einsum(
        "rhf,rse->shfe", hidden_split, grad_split, preferred_element_type=jnp.float32
    ).reshape(seq_count * head_count, down_weight.shape[0], down_weight.shape[1])
    in_grad = jnp.einsum(
        "rse,rghf->shegf", normed_split, grad_gate_up, preferred_element_type=jnp.float32
    ).reshape(seq_count * head_count, in_weight.shape[0], 2, in_weight.shape[2])
    grad_normed_two = jnp.einsum(
        "rghf,shegf->rse", grad_gate_up, in_parts, preferred_element_type=jnp.float32
    ).reshape(half_rows, -1)
    _, norm_two_pull = jax.vjp(layer_norm, resid, gain_two)
    grad_resid_norm, gain_two_grad = norm_two_pull(grad_normed_two)
    grad_resid = grad_out + grad_resid_norm
    grad_branch = lax.all_gather(grad_resid.astype(jnp.bfloat16), "head", axis=0, tiled=True)
    out_grad_weight = jnp.einsum(
        "rc,rd->cd", attended_low, grad_branch, preferred_element_type=jnp.float32
    )
    grad_attended = jnp.einsum(
        "rd,cd->rc", grad_branch, out_full, preferred_element_type=jnp.float32
    ).astype(jnp.bfloat16)
    grad_three = grad_attended.reshape(block_rows, heads_here, HEAD_DIM)
    row_dots = jnp.sum(grad_three.astype(jnp.float32) * attended, axis=2).T
    all_sums, all_dots = (
        lax.all_gather(log_sums.T, "seq", axis=0, tiled=True),
        lax.all_gather(row_dots.T, "seq", axis=0, tiled=True),
    )

    def query_terms(query_grad, key_part, value_part, other_docs):
        same_doc = (local_docs[:, None] == other_docs[None, :])[None]
        _, dscore = block_grads(
            queries, grad_three, log_sums, row_dots, key_part, value_part, same_doc
        )
        return (
            query_grad
            + jnp.einsum("hqk,khd->qhd", dscore, key_part, preferred_element_type=jnp.float32)
            * score_scale
        )

    def key_terms(key_grad, value_grad, query_part, grad_part, sums_part, dots_part, other_docs):
        same_doc = (other_docs[:, None] == local_docs[None, :])[None]
        softmax_part, dscore = block_grads(
            query_part, grad_part, sums_part, dots_part, key_rows, value_rows, same_doc
        )
        value_grad = value_grad + jnp.einsum(
            "hqk,qhd->khd",
            softmax_part.astype(jnp.bfloat16),
            grad_part,
            preferred_element_type=jnp.float32,
        )
        key_grad = (
            key_grad
            + jnp.einsum("hqk,qhd->khd", dscore, query_part, preferred_element_type=jnp.float32)
            * score_scale
        )
        return (key_grad, value_grad)

    def piece_rows(source, block_begin, block_size):
        return lax.dynamic_slice_in_dim(source, block_begin, block_size, 0).reshape(
            block_size, heads_here, HEAD_DIM
        )

    def piece_stats(block_begin, block_size):
        sums_part = lax.dynamic_slice_in_dim(all_sums, block_begin, block_size, 0).T
        dots_part = lax.dynamic_slice_in_dim(all_dots, block_begin, block_size, 0).T
        other_docs, _ = doc_layout(
            short_lengths, block_begin + jnp.arange(block_size, dtype=jnp.int32), total_rows
        )
        return (sums_part, dots_part, other_docs)

    def fold_keys(carry_state, portion):
        piece_keys, piece_values = portion

        def key_block(inner_state, block_begin, block_size):
            _, _, other_docs = piece_stats(block_begin, block_size)
            return query_terms(
                inner_state,
                piece_rows(piece_keys, block_begin, block_size),
                piece_rows(piece_values, block_begin, block_size),
                other_docs,
            )

        return over_blocks(carry_state, piece_keys.shape[0], block_rows, key_block)

    query_grad = fold_keys(
        zeros_three,
        (
            lax.all_gather(key_flat, "seq", axis=0, tiled=True),
            lax.all_gather(value_flat, "seq", axis=0, tiled=True),
        ),
    )

    def fold_queries(carry_state, portion):
        piece_queries, piece_grads = portion

        def query_block(inner_state, block_begin, block_size):
            sums_part, dots_part, other_docs = piece_stats(block_begin, block_size)
            return key_terms(
                inner_state[0],
                inner_state[1],
                piece_rows(piece_queries, block_begin, block_size),
                piece_rows(piece_grads, block_begin, block_size),
                sums_part,
                dots_part,
                other_docs,
            )

        return over_blocks(carry_state, piece_queries.shape[0], block_rows, query_block)

    key_grad, value_grad = fold_queries(
        (zeros_three, zeros_three),
        (
            lax.all_gather(query_flat, "seq", axis=0, tiled=True),
            lax.all_gather(grad_attended, "seq", axis=0, tiled=True),
        ),
    )

    def rotate_local(heads_in):
        return rotate(heads_in, cosines, sines)

    _, rotate_pull = jax.vjp(rotate_local, zeros_three)
    query_back = rotate_pull(query_grad)[0]
    key_back = rotate_pull(key_grad)[0]
    grad_qkv = jnp.stack(
        [
            query_back.reshape(block_rows, -1),
            key_back.reshape(block_rows, -1),
            value_grad.reshape(block_rows, -1),
        ],
        axis=1,
    ).astype(jnp.bfloat16)
    qkv_grad = jnp.einsum("rd,rgc->dgc", normed_block, grad_qkv, preferred_element_type=jnp.float32)
    grad_normed_one = jnp.einsum(
        "rgc,dgc->rd", grad_qkv, qkv_full, preferred_element_type=jnp.float32
    )
    grad_normed_rows = lax.psum_scatter(
        grad_normed_one.astype(jnp.bfloat16), "head", scatter_dimension=0, tiled=True
    ).astype(jnp.float32)
    _, norm_one_pull = jax.vjp(layer_norm, inputs, gain_one)
    grad_inputs_norm, gain_one_grad = norm_one_pull(grad_normed_rows)
    tokens_grad = grad_resid + grad_inputs_norm
    qkv_weight_grad, out_weight_grad = (
        lax.psum_scatter(qkv_grad, "seq", scatter_dimension=0, tiled=True),
        lax.psum_scatter(out_grad_weight, "seq", scatter_dimension=1, tiled=True),
    )
    attn_gain_grad, mlp_gain_grad, in_weight_grad, down_weight_grad = (
        lax.psum_scatter(gain_one_grad, ("seq", "head"), scatter_dimension=0, tiled=True),
        lax.psum_scatter(gain_two_grad, ("seq", "head"), scatter_dimension=0, tiled=True),
        lax.psum_scatter(in_grad, ("seq", "head"), scatter_dimension=0, tiled=True),
        lax.psum_scatter(down_grad, ("seq", "head"), scatter_dimension=0, tiled=True),
    )
    return (
        mixed,
        tokens_grad,
        attn_gain_grad,
        qkv_weight_grad,
        out_weight_grad,
        mlp_gain_grad,
        in_weight_grad.reshape(in_weight.shape),
        down_weight_grad.reshape(down_weight.shape),
    )


LOW = jnp.bfloat16
FULL = jnp.float32


def dot(a, b):
    return jnp.dot(a, b, preferred_element_type=FULL)


def dot_nt(a, b):
    return lax.dot_general(a, b, (((1,), (1,)), ((), ())), preferred_element_type=FULL)


def turned(a):
    return a.astype(FULL).T


def centred_norm(rows):
    centred = rows - jnp.mean(rows, axis=-1, keepdims=True)
    scale = lax.rsqrt(jnp.mean(centred * centred, axis=-1, keepdims=True) + norm_eps)
    return centred * scale, scale


def norm_back(unit, scale, weighted):
    mean_w = jnp.mean(weighted, axis=-1, keepdims=True)
    mean_wn = jnp.mean(weighted * unit, axis=-1, keepdims=True)
    return (weighted - mean_w - unit * mean_wn) * scale


def whole_layer(*refs):
    (
        short_ref, tok_ref, gout_ref, gain_a, gain_m, qkv_ref, out_ref, in_ref, down_ref,
        mixed_out, tgrad_out, gains_out, qkvg_out, outg_out, ing_out, downg_out,
        mixed_ref, tgrad_ref, gains_ref, qkvg_ref, outg_ref, ing_ref, downg_ref,
        gain_ref, wq_ref, ffp_ref, wot_ref, xh, gt, gn, gb, wh, wht, ffw, wo, h1, cs, qa, ka, kt, vt, vr, pt, ot, ol, og, res,
        ms, ms_c, ms_a, ms_y, db, dos, dop, dot_t, ds, dqt, dq, d1, d1_c, d1_a, d1_r1, d1_s1, d1_r2, d1_s2, d1_r3,
        dw, dw_in, gf, gf_k, gf_s, gf_z, gf_y, gf_f, gf_b, gf_c, go, go_k, go_s, go_z, go_y, go_f, go_b, go_c, gy, gy_in,
        s_tok, r_tok, s_gain, r_gain, s_wq, r_wq, s_g, r_g, s_ff, r_ff, s_wo, r_wo,
        s_o, r_o, s_ms, r_ms, s_db, r_db, s_do, r_do, s_d1, r_d1, s_dw, r_dw, s_gf, r_gf, s_go, r_go, s_gy, r_gy, s_out,
    ) = refs
    seq, head = lax.axis_index("seq"), lax.axis_index("head")
    z, x, c, y = seq // 4, (seq // 2) % 2, seq % 2, head
    zh, zb = z // 2, z % 2
    slot = zb * 2 + x
    active = slot < 3
    slot3 = jnp.minimum(slot, 2)
    pending, delivered = [], []

    def flip(value, bit):
        return value if bit == 0 else 1 - value

    def at(z_, x_, c_, y_):
        return (z_ * 4 + x_ * 2 + c_, y_)

    def far_z(k):
        return flip(zh, k // 2) * 2 + flip(zb, k % 2)

    def partner(dim):
        return {
            "x": at(z, 1 - x, c, y),
            "y": at(z, x, c, 1 - y),
            "z": at(far_z(1), x, c, y),
            "c": at(z, x, 1 - c, y),
            "h": at(far_z(2), x, c, y),
        }[dim]

    def push(src, dst, send, recv, device, when=None):
        copy = pltpu.make_async_remote_copy(
            src_ref=src, dst_ref=dst, send_sem=send, recv_sem=recv,
            device_id=device, device_id_type=pl.DeviceIdType.MESH,
        )
        if when is None:
            copy.start()
        else:
            pl.when(when)(copy.start)
        pending.append((when, copy))

    def deliver(k, src, dst):
        copy = pltpu.make_async_copy(src, dst, s_out.at[k])
        copy.start()
        delivered.append(copy)

    def arrive(dst, recv, when=None):
        copy = pltpu.make_async_remote_copy(
            src_ref=dst, dst_ref=dst, send_sem=recv, recv_sem=recv,
            device_id=partner("c"), device_id_type=pl.DeviceIdType.MESH,
        )
        if when is None:
            copy.wait_recv()
        else:
            pl.when(when)(copy.wait_recv)

    barrier = pltpu.get_barrier_semaphore()
    peers = []
    for k in range(1, 32):
        kz, kx, kc, ky = k // 8, (k // 4) % 2, (k // 2) % 2, k % 2
        if kz < 2 or ky == 0:
            peers.append(at(far_z(kz), flip(x, kx), flip(c, kc), flip(y, ky)))
    for peer in peers:
        pl.semaphore_signal(barrier, inc=1, device_id=peer, device_id_type=pl.DeviceIdType.MESH)

    gain_ref[...] = jnp.zeros_like(gain_ref)
    gain_ref[0:1, 0 : gain_a.shape[1]] = gain_a[...].astype(FULL)
    gain_ref[1:2, 0 : gain_m.shape[1]] = gain_m[...].astype(FULL)
    wot_ref[...] = out_ref[...]
    for g in range(3):
        for j in range(6):
            wq_ref[j, :, g * 64 : g * 64 + 64] = qkv_ref[g, :, j * 64 : j * 64 + 64]
    for c_ in range(2):
        lanes = slice(c_ * 288, c_ * 288 + 288)
        for g in range(2):
            ffp_ref[c_, :, g * 288 : g * 288 + 288] = in_ref[:, g, lanes]
        ffp_ref[c_, :, 576:864] = down_ref[:, lanes]
    pl.semaphore_wait(barrier, len(peers))

    xh[zb, c, x, y] = tok_ref[...]
    orders = (("z", "x", "y"), ("z", "y", "x"), ("z", "x", "y"))

    def third(t):
        return pl.ds(t * 256, 256)

    def blocks(ref, opened, lanes, flipped=None, core=None):
        there = {"z": zb, "x": x, "y": y, "c": c if core is None else core}
        if flipped is not None:
            there[flipped] = 1 - there[flipped]
        index = tuple(slice(None) if d in opened else there[d] for d in ("z", "c", "x", "y"))
        return ref.at[index + (slice(None), lanes)]

    for t in range(3):
        view = blocks(xh, (), third(t))
        push(view, view, s_tok.at[0, t], r_tok.at[0, t], partner(orders[t][0]))

    gt[zh, zb, x, c, y] = gain_ref[...]
    gain_order = ("c", "h", "x", "y", "z")

    def gain_view(opened, flipped=None):
        there = {"h": zh, "z": zb, "x": x, "c": c, "y": y}
        if flipped is not None:
            there[flipped] = 1 - there[flipped]
        return gt.at[tuple(slice(None) if d in opened else there[d] for d in ("h", "z", "x", "c", "y"))]

    def gain_send(k):
        view = gain_view(gain_order[:k])
        push(view, view, s_gain.at[k], r_gain.at[k], partner(gain_order[k]))

    def gain_wait(k):
        arrive(gain_view(gain_order[:k], gain_order[k]), r_gain.at[k])

    gain_send(0)

    wo_lanes = pl.ds(pl.multiple_of(y * 384, 128), 384)
    wo_others = pl.ds(pl.multiple_of((1 - y) * 384, 128), 384)

    def ff_share(src, z_, x_, k, dim):
        push(src, ffw.at[z_, x_, c], s_ff.at[k], r_ff.at[k], partner(dim))

    def ff_arrive(kz, kx, k):
        arrive(ffw.at[far_z(kz), flip(x, kx), c], r_ff.at[k])

    def ff_cross():
        ff_arrive(0, 1, 0)
        ff_share(ffw.at[z, 1 - x, c], z, 1 - x, 2, "h")
        ff_share(ffw.at[z, 1 - x, c], z, 1 - x, 4, "z")

    def ff_relay():
        for kx in range(2):
            ff_arrive(2, kx, 1 + kx)
            z_, x_ = far_z(2), flip(x, kx)
            ff_share(ffw.at[z_, x_, c], z_, x_, 5 + kx, "z")

    def ff_core(kz):
        z_ = far_z(kz)
        push(ffw.at[z_, :, c], ffw.at[z_, :, c], s_ff.at[8 + kz], r_ff.at[8 + kz], partner("c"))

    def ff_near():
        for kx in range(2):
            ff_arrive(1, kx, 3 + kx)
        ff_core(1)

    def ff_last():
        for kx in range(2):
            ff_arrive(3, kx, 5 + kx)
        ff_core(3)

    def wo_forward_x():
        for k in range(1, 4):
            arrive(wo.at[far_z(k), x, c, :, wo_lanes], r_wo.at[k])
        view = wo.at[:, x, c, :, wo_lanes]
        push(view, view, s_wo.at[4], r_wo.at[4], partner("x"))

    def wo_forward_y():
        arrive(wo.at[:, 1 - x, c, :, wo_lanes], r_wo.at[4])
        view = wo.at[:, :, c, :, wo_lanes]
        push(view, view, s_wo.at[5], r_wo.at[5], partner("y"))

    def wo_forward_core():
        arrive(wo.at[:, :, c, :, wo_others], r_wo.at[5])
        push(wo.at[:, :, c], wo.at[:, :, c], s_wo.at[6], r_wo.at[6], partner("c"))

    ffw[z, x, c] = ffp_ref[x]
    wo[z, x, c, :, wo_lanes] = wot_ref[...]
    def wo_push():
        for k in (2, 3, 1):
            push(wot_ref, wo.at[z, x, c, :, wo_lanes], s_wo.at[k], r_wo.at[k], at(far_z(k), x, c, y))

    own_rows = pl.ds(pl.multiple_of(seq * 48, 16), 48)
    wh[own_rows, :] = wq_ref[jnp.minimum(slot * 2 + c, 5)]

    def head_push():
        for k in range(1, 16):
            z_, x_, c_ = far_z(k // 4), flip(x, (k // 2) % 2), flip(c, k % 2)
            slot_ = (z_ % 2) * 2 + x_
            piece = wq_ref.at[jnp.minimum(slot_ * 2 + c_, 5)]
            push(piece, wh.at[own_rows, :], s_wq.at[k], r_wq.at[k], at(z_, x_, c_, y), slot_ < 3)

    gb[x, y] = gout_ref[...]
    group = ((0, 1), (1, 0), (1, 1))

    def member(kx, ky):
        return at(z, flip(x, kx), c, flip(y, ky))

    def grad_push():
        for k, (kx, ky) in enumerate(group):
            push(gb.at[x, y], gb.at[x, y], s_g.at[k], r_g.at[k], member(kx, ky))

    def token_step(step):
        for t in range(3):
            arrive(blocks(xh, orders[t][: step - 1], third(t), orders[t][step - 1]), r_tok.at[step - 1, t])
            view = blocks(xh, orders[t][:step], third(t))
            push(view, view, s_tok.at[step, t], r_tok.at[step, t], partner(orders[t][step]))
        gain_wait(step)
        gain_send(step + 1)

    events = {
        "fx": lambda: ff_share(ffp_ref.at[1 - x], z, x, 0, "x"),
        "f2": lambda: ff_share(ffp_ref.at[x], z, x, 1, "h"),
        "f1": lambda: ff_share(ffp_ref.at[x], z, x, 3, "z"),
        "fc": ff_cross,
        "fr": ff_relay,
        "c0": lambda: ff_core(0),
        "c1": ff_near,
        "c2": lambda: ff_core(2),
        "c3": ff_last,
        "w": head_push,
        "g": grad_push,
        "oz": wo_push,
        "ox": wo_forward_x,
        "oy": wo_forward_y,
        "oc": wo_forward_core,
    }

    def run(point):
        for name in plan[point]:
            events[name]()

    plan = (
        ("w",),
        ("f2", "fx", "f1", "oz"),
        ("fc", "ox", "g"),
        ("fr", "c0", "c1", "oy"),
        ("c2",),
        (),
        (),
        (),
        ("c3", "oc"),
    )
    run(0)
    gain_wait(0)
    gain_send(1)
    token_step(1)
    run(1)
    token_step(2)
    run(2)
    gain_wait(3)
    gain_send(4)
    run(3)

    half_rows = 1024
    lane = lax.broadcasted_iota(jnp.int32, (32, half_rows), 1)
    row = lane % 64 + (lane // 64 % 2) * 64 + (lane // 256 % 2) * 128 + (lane // 128 % 2) * 256 + (lane // 512) * 512
    row = row + zh * half_rows
    feature = lax.broadcasted_iota(jnp.int32, (32, half_rows), 0)
    bound = jnp.int32(2 * half_rows)
    for b in range(short_ref.shape[0]):
        bound = bound - short_ref[b]
    doc = jnp.zeros_like(row)
    start = jnp.zeros_like(row)
    for b in range(short_ref.shape[0]):
        passed = row >= bound
        doc = doc + jnp.where(passed, 1, 0)
        start = jnp.where(passed, bound, start)
        bound = bound + short_ref[b]
    inverse = jnp.exp(feature.astype(FULL) * (-2.0 * math.log(rope_base) / HEAD_DIM))
    angles = (row - start).astype(FULL) * inverse
    cs[0] = jnp.cos(angles)
    cs[1] = jnp.sin(angles)
    same = jnp.where(feature == doc, 1.0, 0.0)
    cs[2] = same
    qa[64:96, :] = ((same - 1.0) * 1e30).astype(LOW)
    qa[96:128, :] = jnp.zeros((32, half_rows), LOW)

    gain_wait(4)
    tiles = gt[...].reshape(256, 128).astype(LOW)
    width = 24
    pick = lax.broadcasted_iota(jnp.int32, (128, 768), 1) % width == lax.broadcasted_iota(jnp.int32, (128, 768), 0)
    spread = dot(tiles, jnp.where(pick, 1.0, 0.0).astype(LOW))
    source = lax.broadcasted_iota(jnp.int32, (256, 768), 0)
    wanted = (lax.broadcasted_iota(jnp.int32, (256, 768), 1) // width) * 8
    gn[0:1, :] = jnp.sum(jnp.where(source == wanted, spread, 0.0), axis=0, keepdims=True)
    gn[1:2, :] = jnp.sum(jnp.where(source == wanted + 1, spread, 0.0), axis=0, keepdims=True)

    for t in range(3):
        arrive(blocks(xh, orders[t][:2], third(t), orders[t][2]), r_tok.at[2, t])

    def rows_of(z_, c_):
        return pl.ds(pl.multiple_of(z_ * 512 + c_ * 256, 256), 256)

    for z_ in range(2):
        rows = rows_of(z_, c)

        @pl.when(active)
        def _(z_=z_, rows=rows):
            unit, _ = centred_norm(xh[z_, c].reshape(256, 768).astype(FULL))
            h1[rows, :] = (unit * gn[0:1, :]).astype(LOW)

        push(h1.at[rows, :], h1.at[rows, :], s_tok.at[3, z_], r_tok.at[3, z_], partner("c"), active)
    for k in range(1, 16):
        source_seq = far_z(k // 4) * 4 + flip(x, (k // 2) % 2) * 2 + flip(c, k % 2)
        arrive(wh.at[pl.ds(pl.multiple_of(source_seq * 48, 16), 48), :], r_wq.at[k], active)

    @pl.when(active)
    def _():
        wht[...] = turned(wh[...]).astype(LOW)

    for part in range(4):
        z_, c_ = part % 2, flip(c, part // 2)
        cols = rows_of(z_, c_)
        if part >= 2:
            arrive(h1.at[cols, :], r_tok.at[3, z_], active)

        @pl.when(active)
        def _(cols=cols):
            proj = dot_nt(wht[...], h1[cols, :])
            cosine, sine = cs[0, :, cols], cs[1, :, cols]
            q1, q2, k1, k2 = proj[0:32], proj[32:64], proj[64:96], proj[96:128]
            qr = jnp.concatenate([q1 * cosine - q2 * sine, q2 * cosine + q1 * sine], axis=0)
            kr = jnp.concatenate([k1 * cosine - k2 * sine, k2 * cosine + k1 * sine], axis=0)
            qa[0:64, cols] = (qr * score_scale).astype(LOW)
            kt[:, cols] = kr.astype(LOW)
            vt[:, cols] = proj[128:192].astype(LOW)
            pad = jnp.zeros((32, 256), FULL)
            ka[cols, :] = jnp.concatenate([kr, cs[2, :, cols], pad], axis=0).T.astype(LOW)
            vr[cols, :] = proj[128:192].T.astype(LOW)

    run(4)

    for part in range(4):
        cols = pl.ds(part * 256, 256)

        @pl.when(active)
        def _(part=part, cols=cols):
            scores = dot(ka[...], qa[:, cols])
            expo = jnp.exp(scores - jnp.max(scores, axis=0, keepdims=True))
            prob = (expo * (1.0 / jnp.sum(expo, axis=0, keepdims=True))).astype(LOW)
            pt[:, cols] = prob
            result = dot(vt[...], prob)
            ot[part] = result
            ol[part] = result.astype(LOW)

        own_group = jnp.logical_and(zb == part // 2, c == part % 2)
        for k in range(4):
            x_, y_ = k // 2, k % 2
            mine = jnp.logical_and(own_group, jnp.logical_and(x == x_, y == y_))

            @pl.when(jnp.logical_and(active, mine))
            def _(part=part):
                og[y, slot3, c] = ol[part]

            push(
                ol.at[part], og.at[y, slot3, c], s_o.at[part, k], r_o.at[slot3, c, y],
                at(zh * 2 + part // 2, x_, part % 2, y_), jnp.logical_and(active, jnp.logical_not(mine)),
            )
        run(5 + part)

    for slot_ in range(3):
        for c_ in range(2):
            for y_ in range(2):
                mine = jnp.logical_and(slot == slot_, jnp.logical_and(c == c_, y == y_))
                arrive(og.at[y_, slot_, c_], r_o.at[slot_, c_, y_], jnp.logical_not(mine))
    arrive(wo.at[:, :, 1 - c], r_wo.at[6])

    gain_two = gn[1:2, :]
    branch = dot(wo[...].reshape(768, 768), og[...].reshape(768, 256)).T
    resid = xh[zb, c].reshape(256, 768).astype(FULL) + branch
    res[...] = resid.reshape(2, 2, 64, 768)
    unit_two, _ = centred_norm(resid)
    h2 = (unit_two * gain_two).astype(LOW)

    for kz in range(4):
        arrive(ffw.at[far_z(kz), :, 1 - c], r_ff.at[8 + kz])
    for k, (kx, ky) in enumerate(group):
        arrive(gb.at[flip(x, kx), flip(y, ky)], r_g.at[k])
    w_in = ffw[:, :, :, :, 0:576].reshape(768, 576)
    w_down = ffw[:, :, :, :, 576:864].reshape(768, 288)
    gate_up = dot(h2, w_in)
    gate, up = gate_up[:, :288], gate_up[:, 288:]
    grad_out = gb[...].reshape(256, 768)
    grad_hidden = dot(grad_out, w_down)
    chance = 0.5 * (1.0 + lax.erf(gate * (1.0 / math.sqrt(2.0))))
    density = jnp.exp(gate * gate * -0.5) * (1.0 / math.sqrt(2.0 * math.pi))
    curve = gate * chance
    hidden = (curve * up).astype(LOW)
    grad_gate = grad_hidden * up * (chance + gate * density)
    grad_gate_up = jnp.concatenate([grad_gate, grad_hidden * curve], axis=1).astype(LOW)

    columns = (slice(0, 384), slice(384, 768))

    def halve(kind, part):
        ms[kind] = part.astype(LOW).reshape(2, 2, 64, 768)
        push(ms.at[kind, 1 - x, :, :, columns[0]], ms_c.at[kind, 0], s_ms.at[kind, 0, 0], r_ms.at[kind, 0, 0], partner("x"))
        push(ms.at[kind, :, 1 - y, :, columns[1]], ms_c.at[kind, 1], s_ms.at[kind, 1, 0], r_ms.at[kind, 1, 0], partner("y"))

    def quarter(kind):
        for t in range(2):
            arrive(ms_c.at[kind, t], r_ms.at[kind, t, 0])
            mine = ms[kind, x, 1 - y, :, columns[0]] if t == 0 else ms[kind, 1 - x, y, :, columns[1]]
            other = ms_c[kind, t, 1 - y] if t == 0 else ms_c[kind, t, 1 - x]
            ms_a[kind, t] = (mine.astype(FULL) + other.astype(FULL)).astype(LOW)
            push(ms_a.at[kind, t], ms_y.at[kind, t], s_ms.at[kind, t, 1], r_ms.at[kind, t, 1], partner("yx"[t]))

    def quarter_sum(kind):
        sums = []
        for t in range(2):
            arrive(ms_y.at[kind, t], r_ms.at[kind, t, 1])
            other = ms_c[kind, t, y] if t == 0 else ms_c[kind, t, x]
            mine = ms[kind, x, y, :, columns[t]].astype(FULL) + other.astype(FULL)
            sums.append(mine + ms_y[kind, t].astype(FULL))
        return jnp.concatenate(sums, axis=1)

    halve(0, dot_nt(grad_gate_up, w_in))
    h2_t = turned(h2).astype(LOW)
    gf[:, :, :, :, 0:576] = dot(h2_t, grad_gate_up).astype(LOW).reshape(4, 2, 2, 48, 576)
    g_t = turned(grad_out).astype(LOW)
    gf[:, :, :, :, 576:864] = dot(g_t, hidden).astype(LOW).reshape(4, 2, 2, 48, 288)

    def sums_of(whole, crossed, low, near, far, wide, last, coming, send, recv):
        def cross():
            for kz in (3, 1, 2, 0):
                z_ = far_z(kz)
                push(whole.at[z_, :, 1 - c], crossed.at[z_], send.at[0, kz], recv.at[0, kz], partner("c"))

        def pair(kz):
            z_ = far_z(kz)
            arrive(crossed.at[z_], recv.at[0, kz])
            return whole[z_, :, c].astype(FULL) + crossed[z_].astype(FULL)

        def to_near(kz):
            z_ = far_z(kz)
            low[z_] = pair(kz).astype(LOW)
            push(low.at[z_], near.at[kz // 2], send.at[1, kz // 2], recv.at[1, kz // 2], partner("z"))

        def to_far():
            value = pair(2)
            arrive(near.at[1], recv.at[1, 1])
            low[far_z(2)] = (value + near[1].astype(FULL)).astype(LOW)
            push(low.at[far_z(2)], far, send.at[2, 0], recv.at[2, 0], partner("h"))

        def finish():
            value = pair(0)
            arrive(near.at[0], recv.at[1, 0])
            arrive(far, recv.at[2, 0])
            wide[...] = value + near[0].astype(FULL) + far[...].astype(FULL)
            last[...] = wide[1 - x].astype(LOW)
            push(last, coming, send.at[3, 0], recv.at[3, 0], partner("x"))

        def result():
            arrive(coming, recv.at[3, 0])
            own, other = wide[x], coming[...].astype(FULL)
            return jnp.where(x == 0, own, other), jnp.where(x == 0, other, own)

        return cross, to_near, to_far, finish, result

    ff_sums = sums_of(gf, gf_k, gf_s, gf_z, gf_y, gf_f, gf_b, gf_c, s_gf, r_gf)
    out_sums = sums_of(go, go_k, go_s, go_z, go_y, go_f, go_b, go_c, s_go, r_go)

    def out_share():
        for k, (kx, ky) in enumerate(group):
            arrive(db.at[flip(x, kx), flip(y, ky)], r_db.at[k])
        db_t = turned(db[...].reshape(256, 768)).astype(LOW)
        o_part = og[...].reshape(2, 6, 64, 256)
        o_pick = jnp.where(y == 0, o_part[0], o_part[1])
        o_pick = jnp.where(x == 0, o_pick[0:3], o_pick[3:6]).reshape(192, 256)
        go[...] = dot_nt(db_t, o_pick).astype(LOW).reshape(4, 2, 2, 48, 192)
        out_sums[0]()

    def mixed_done():
        mixed_ref[...] = (res[x, y] + quarter_sum(1)).astype(LOW)
        deliver(0, mixed_ref, mixed_out)

    later = {
        "md": mixed_done,
        "mx": lambda: quarter(1),
        "n3": lambda: ff_sums[1](3),
        "n1": lambda: ff_sums[1](1),
        "f": ff_sums[2],
        "e": ff_sums[3],
        "O": out_share,
        "O3": lambda: out_sums[1](3),
        "O1": lambda: out_sums[1](1),
        "Of": out_sums[2],
        "Oe": out_sums[3],
    }
    then = (
        ("n3",),
        ("mx", "n1"),
        (),
        ("O", "f"),
        ("O3", "O1", "md"),
        (),
        (),
        ("Of",),
        ("Oe", "e"),
        (),
    )

    def run_later(point):
        for name in then[point]:
            later[name]()

    ff_sums[0]()
    quarter(0)
    halve(1, dot_nt(hidden, w_down))
    run_later(0)
    own_res = res[x, y]
    unit_two, scale_two = centred_norm(own_res)
    grad_h2 = quarter_sum(0)
    grad_resid = gout_ref[...].astype(FULL) + norm_back(unit_two, scale_two, grad_h2 * gain_two)
    tgrad_ref[...] = grad_resid
    grad_branch = grad_resid.astype(LOW)
    db[x, y] = grad_branch
    grad_o = dot(grad_branch, wo[...].reshape(768, 768)).astype(LOW)
    own_block = zb * 8 + c * 4 + x * 2 + y
    for slot_ in range(3):
        for y_ in range(2):
            lanes = y_ * 384 + slot_ * 128
            dos[y_, slot_] = grad_o[:, lanes : lanes + 128]
            for c_ in range(2):
                mine = jnp.logical_and(jnp.logical_and(slot == slot_, y == y_), c == c_)

                @pl.when(mine)
                def _(slot_=slot_, y_=y_):
                    dop[zb, c, x, y] = dos[y_, slot_]

                push(
                    dos.at[y_, slot_], dop.at[zb, c, x, y], s_do.at[slot_ * 4 + y_ * 2 + c_], r_do.at[own_block],
                    at(zh * 2 + slot_ // 2, slot_ % 2, c_, y_), jnp.logical_not(mine),
                )
    run_later(1)
    for k, (kx, ky) in enumerate(group):
        push(db.at[x, y], db.at[x, y], s_db.at[k], r_db.at[k], member(kx, ky))
    run_later(2)

    for b in range(16):
        z_, c_, x_, y_ = b // 8, (b // 4) % 2, (b // 2) % 2, b % 2
        arrive(dop.at[z_, c_, x_, y_], r_do.at[b], jnp.logical_and(active, own_block != b))

    @pl.when(active)
    def _():
        pair = turned(dop[...].reshape(1024, 128))
        dot_t[...] = jnp.where(c == 0, pair[0:64], pair[64:128]).astype(LOW)

    for part in range(4):
        cols = pl.ds(part * 256, 256)

        @pl.when(active)
        def _(part=part, cols=cols):
            grad_t = dot_t[:, cols]
            delta = jnp.sum(grad_t.astype(FULL) * ot[part], axis=0, keepdims=True)
            grad_p = dot(vr[...], grad_t)
            score_grad = (pt[:, cols].astype(FULL) * (grad_p - delta)).astype(LOW)
            ds[:, cols] = score_grad
            back = dot(kt[...], score_grad) * score_scale
            cosine, sine = cs[0, :, cols], cs[1, :, cols]
            b1, b2 = back[0:32], back[32:64]
            dqt[0:64, cols] = jnp.concatenate([b1 * cosine + b2 * sine, b2 * cosine - b1 * sine], axis=0).astype(LOW)

        run_later(3 + part)

    @pl.when(active)
    def _():
        for part in range(4):
            cols = pl.ds(part * 256, 256)
            back = dot_nt(qa[0:64, :], ds[cols, :])
            cosine, sine = cs[0, :, cols], cs[1, :, cols]
            b1, b2 = back[0:32], back[32:64]
            dqt[64:128, cols] = jnp.concatenate([b1 * cosine + b2 * sine, b2 * cosine - b1 * sine], axis=0).astype(LOW)
            dqt[128:192, cols] = dot_nt(dot_t[...], pt[cols, :]).astype(LOW)
            dq[cols, :] = turned(dqt[:, cols]).astype(LOW)

    for part in range(4):
        z_, c_ = part % 2, flip(c, 1 - part // 2)

        @pl.when(active)
        def _(z_=z_, c_=c_):
            rows = pl.ds(pl.multiple_of(z_ * 512 + c_ * 256, 256), 256)
            d1[z_, c_] = dot_nt(dq[rows, :], wh[...]).astype(LOW).reshape(2, 2, 64, 768)

        if part < 2:
            push(d1.at[z_, c_], d1_c.at[z_], s_d1.at[0, z_], r_d1.at[0, z_], partner("c"), active)
    run_later(7)

    @pl.when(active)
    def _():
        grad = dot(dqt[...], h1[...])
        dw[...] = grad.T.astype(LOW).reshape(16, 48, 192)

    @pl.when(jnp.logical_not(active))
    def _():
        d1_a[...] = jnp.zeros_like(d1_a)

    for z_ in range(2):
        arrive(d1_c.at[z_], r_d1.at[0, z_], active)

        @pl.when(active)
        def _(z_=z_):
            d1_a[z_] = (d1[z_, c].astype(FULL) + d1_c[z_].astype(FULL)).astype(LOW)

    back_orders = (("x", "y", "z"), ("y", "z", "x"), ("z", "x", "y"))

    def remaining(t, step):
        return tuple(d for d in ("z", "x", "y") if d not in back_orders[t][:step])

    landing = (d1_r1, d1_r2, d1_r3)

    def step_view(t, step, flipped):
        dim = back_orders[t][step]
        place = {"z": zb, "x": x, "y": y}[dim]
        place = 1 - place if flipped else place
        index = tuple(place if d == dim else slice(None) for d in remaining(t, step))
        if step == 0:
            return d1_a.at[index + (slice(None), third(t))]
        return (d1_s1, d1_s2)[step - 1].at[(t,) + index]

    def step_push(t, step):
        push(
            step_view(t, step, True), landing[step].at[t], s_d1.at[1 + step, t], r_d1.at[1 + step, t],
            partner(back_orders[t][step]),
        )

    def step_sum(t, step):
        arrive(landing[step].at[t], r_d1.at[1 + step, t])
        return step_view(t, step, False)[...].astype(FULL) + landing[step][t].astype(FULL)

    for t in range(3):
        step_push(t, 0)

    own_head = zh * 6 + slot3 * 2 + c

    @pl.when(active)
    def _():
        dw_in[own_head] = dw[seq]

    for k in range(1, 16):
        z_, x_, c_ = far_z(k // 4), flip(x, (k // 2) % 2), flip(c, k % 2)
        push(dw.at[z_ * 4 + x_ * 2 + c_], dw_in.at[own_head], s_dw.at[k], r_dw.at[own_head], at(z_, x_, c_, y), active)

    for t in range(3):
        d1_s1[t] = step_sum(t, 0).astype(LOW)
        step_push(t, 1)

    run_later(8)
    for t in range(3):
        d1_s2[t] = step_sum(t, 1).astype(LOW)
        step_push(t, 2)
    run_later(9)
    mlp_terms = jnp.zeros((48, 1), FULL)
    for x_, grads in enumerate(ff_sums[4]()):
        lanes = slice(x_ * 288, x_ * 288 + 288)
        for g in range(2):
            ing_ref[:, g, lanes] = grads[:, g * 288 : g * 288 + 288]
        downg_ref[:, lanes] = grads[:, 576:864]
        terms = grads[:, 0:576] * ffp_ref[x_, :, 0:576].astype(FULL)
        mlp_terms = mlp_terms + jnp.sum(terms, axis=1, keepdims=True)
    deliver(1, ing_ref, ing_out)
    deliver(2, downg_ref, downg_out)
    for h_ in range(2):
        for j in range(6):
            arrive(dw_in.at[h_ * 6 + j], r_dw.at[h_ * 6 + j], jnp.logical_not(jnp.logical_and(active, own_head == h_ * 6 + j)))
    attn_terms = jnp.zeros((48, 1), FULL)
    for j in range(6):
        both = dw_in[j].astype(FULL) + dw_in[6 + j].astype(FULL)
        for g in range(3):
            qkvg_ref[g, :, j * 64 : j * 64 + 64] = both[:, g * 64 : g * 64 + 64]
        attn_terms = attn_terms + jnp.sum(both * wq_ref[j].astype(FULL), axis=1, keepdims=True)
    deliver(3, qkvg_ref, qkvg_out)
    lane = lax.broadcasted_iota(jnp.int32, (48, 128), 1)
    gy[...] = jnp.where(lane == 0, attn_terms, jnp.where(lane == 1, mlp_terms, 0.0))
    push(gy, gy_in, s_gy.at[0], r_gy.at[0], partner("y"))
    for x_, grads in enumerate(out_sums[4]()):
        outg_ref[:, x_ * 192 : x_ * 192 + 192] = grads
    deliver(4, outg_ref, outg_out)

    unit_one, scale_one = centred_norm(tok_ref[...].astype(FULL))
    for t in range(3):
        res[0, 0, :, third(t)] = step_sum(t, 2)
    tgrad_ref[...] = tgrad_ref[...] + norm_back(unit_one, scale_one, res[0, 0] * gn[0:1, :])
    deliver(5, tgrad_ref, tgrad_out)
    arrive(gy_in, r_gy.at[0])
    sums = (gy[...] + gy_in[...]).T
    count = gain_a.shape[1]
    sums = jnp.where(y == 0, sums[0:2, :count], sums[0:2, count : 2 * count])
    gains_ref[...] = jnp.zeros_like(gains_ref)
    gains_ref[0:2, 0:count] = sums / gain_ref[0:2, 0:count]
    deliver(6, gains_ref, gains_out)
    for copy in delivered:
        copy.wait()
    for when, copy in pending:
        if when is None:
            copy.wait_send()
        else:
            pl.when(when)(copy.wait_send)


def hand_on(*refs):
    sources, results, held, sems = refs[:7], refs[7:15], refs[15:21], refs[21]
    count = results[6].shape[1]
    results[6][...] = sources[6][0:1, :count]
    results[7][...] = sources[6][1:2, :count]
    inward = [pltpu.make_async_copy(a, b, sems.at[0, k]) for k, (a, b) in enumerate(zip(sources[:6], held))]
    outward = [pltpu.make_async_copy(a, b, sems.at[1, k]) for k, (a, b) in enumerate(zip(held, results[:6]))]
    for copy in inward:
        copy.start()
    for first, second in zip(inward, outward):
        first.wait()
        second.start()
    for copy in outward:
        copy.wait()


def on_device_fast(tokens, out_grad, short_lengths, attn_gain, qkv_weight, out_weight, mlp_gain, in_weight, down_weight):
    rows, width = tokens.shape
    depth = qkv_weight.shape[0]
    heads_here = qkv_weight.shape[2] // HEAD_DIM
    count = attn_gain.shape[0]
    ff = in_weight.shape[2] // 2 * 3
    feats = out_weight.shape[0]

    def vm(shape, kind=LOW):
        return pltpu.VMEM(shape, kind)

    def sem(*shape):
        return pltpu.SemaphoreType.DMA(shape)

    finals = [
        ((rows, width), LOW), ((rows, width), FULL), ((8, 128), FULL), ((3, depth, 384), FULL),
        ((depth, feats), FULL), ((depth, 2, 576), FULL), ((depth, 576), FULL),
    ]
    scratch = [vm(*shape) for shape in finals] + [
        vm((8, 128), FULL), vm((heads_here, depth, 192)), vm((2, depth, ff)), vm((depth, feats)),
        vm((2, 2, 2, 2, 64, 768)), vm((2, 2, 2, 2, 2, 8, 128), FULL), vm((8, 768), FULL), vm((2, 2, 64, 768)),
        vm((768, 192)), vm((192, 768)), vm((4, 2, 2, 48, 864)), vm((4, 2, 2, 48, 768)), vm((1024, 768)),
        vm((3, 32, 1024), FULL), vm((128, 1024)), vm((1024, 128)), vm((64, 1024)), vm((64, 1024)), vm((1024, 64)),
        vm((1024, 1024)), vm((4, 64, 256), FULL), vm((4, 64, 256)), vm((2, 3, 2, 64, 256)), vm((2, 2, 64, 768), FULL),
        vm((2, 2, 2, 64, 768)), vm((2, 2, 2, 64, 384)), vm((2, 2, 64, 384)), vm((2, 2, 64, 384)), vm((2, 2, 64, 768)),
        vm((2, 3, 64, 128)), vm((2, 2, 2, 2, 64, 128)), vm((64, 1024)), vm((1024, 1024)), vm((192, 1024)),
        vm((1024, 192)), vm((2, 2, 2, 2, 64, 768)), vm((2, 2, 2, 64, 768)), vm((2, 2, 2, 64, 768)),
        vm((3, 2, 2, 64, 256)), vm((3, 2, 2, 64, 256)), vm((3, 2, 64, 256)), vm((3, 2, 64, 256)), vm((3, 64, 256)),
        vm((16, 48, 192)), vm((12, 48, 192)),
        vm((4, 2, 2, 48, 864)), vm((4, 2, 48, 864)), vm((4, 2, 48, 864)), vm((2, 2, 48, 864)), vm((2, 48, 864)),
        vm((2, 48, 864), FULL), vm((48, 864)), vm((48, 864)),
        vm((4, 2, 2, 48, 192)), vm((4, 2, 48, 192)), vm((4, 2, 48, 192)), vm((2, 2, 48, 192)), vm((2, 48, 192)),
        vm((2, 48, 192), FULL), vm((48, 192)), vm((48, 192)),
        vm((48, 128), FULL), vm((48, 128), FULL),
        sem(4, 3), sem(4, 3), sem(5), sem(5), sem(16), sem(16), sem(3), sem(3), sem(12), sem(12), sem(7), sem(7),
        sem(4, 4), sem(3, 2, 2), sem(2, 2, 2), sem(2, 2, 2), sem(3), sem(3), sem(12), sem(16), sem(4, 4), sem(4, 4),
        sem(16), sem(12), sem(4, 4), sem(4, 4), sem(4, 4), sem(4, 4), sem(1), sem(1), sem(7),
    ]
    vmem = pl.BlockSpec(memory_space=pltpu.VMEM)
    anywhere = pl.BlockSpec(memory_space=pl.ANY)
    shapes = [jax.ShapeDtypeStruct(*shape) for shape in finals]
    mixed, tokens_grad, gains, qkv_grad, out_grads, in_grad, down_grad = pl.pallas_call(
        whole_layer,
        out_shape=shapes,
        in_specs=[pl.BlockSpec(memory_space=pltpu.SMEM)] + [vmem] * 8,
        out_specs=[anywhere] * 7,
        scratch_shapes=scratch,
        compiler_params=pltpu.CompilerParams(collective_id=0, has_side_effects=True, vmem_limit_bytes=60 << 20),
    )(
        short_lengths, tokens, out_grad, attn_gain[None], mlp_gain[None],
        qkv_weight.transpose(1, 0, 2), out_weight.T, in_weight, down_weight.T,
    )
    grads = (mixed, tokens_grad, qkv_grad, out_grads, in_grad, down_grad)
    count = attn_gain.shape[0]
    mixed, tokens_grad, qkv_grad, out_grads, in_grad, down_grad, attn_gain_grad, mlp_gain_grad = pl.pallas_call(
        hand_on,
        out_shape=[jax.ShapeDtypeStruct(a.shape, a.dtype) for a in grads] + [jax.ShapeDtypeStruct((1, count), FULL)] * 2,
        in_specs=[anywhere] * 6 + [vmem],
        out_specs=[anywhere] * 6 + [vmem] * 2,
        scratch_shapes=[vm(a.shape, a.dtype) for a in grads] + [sem(2, 6)],
    )(*grads, gains)
    return (
        mixed, tokens_grad, attn_gain_grad[0], qkv_grad.transpose(1, 0, 2), out_grads.T, mlp_gain_grad[0],
        in_grad, down_grad.T,
    )


def solution(mesh):
    placed = (
        P(("seq", "head"), None),
        P(("seq", "head"), None),
        P(),
        P(("seq", "head")),
        P("seq", None, "head"),
        P("head", "seq"),
        P(("seq", "head")),
        P("seq", None, "head"),
        P("head", "seq"),
    )
    fits = mesh.shape["seq"] == 16 and mesh.shape["head"] == 2
    return jax.shard_map(
        on_device_fast if fits else on_device,
        mesh=mesh,
        in_specs=placed,
        out_specs=(
            P(("seq", "head"), None),
            P(("seq", "head"), None),
            P(("seq", "head")),
            P("seq", None, "head"),
            P("head", "seq"),
            P(("seq", "head")),
            P("seq", None, "head"),
            P("head", "seq"),
        ),
        check_vma=False,
    )
```

```python
import math

import jax
import jax.numpy as jnp
from jax import lax
from jax.experimental import pallas as pl
from jax.experimental.pallas import tpu as pltpu
from jax.sharding import PartitionSpec as P

HEAD_DIM = 64


norm_eps = 1e-05
rope_base = 160000.0
score_scale = 0.125
masked_low = -1e30


def layer_norm(inputs, gain_vector):
    row_mean = jnp.mean(inputs, axis=-1, keepdims=True)
    centred = inputs - row_mean
    spread = jnp.mean(centred * centred, axis=-1, keepdims=True)
    return centred * lax.rsqrt(spread + norm_eps) * gain_vector


def doc_layout(short_lengths, row_ids, total_rows):
    long_end = total_rows - jnp.sum(short_lengths)
    before = jnp.cumsum(short_lengths) - short_lengths
    bounds = long_end + before
    passed = row_ids[:, None] >= bounds[None, :]
    doc_ids = jnp.sum(passed.astype(jnp.int32), axis=1)
    starts = jnp.max(jnp.where(passed, bounds[None, :], jnp.zeros_like(bounds)[None, :]), axis=1)
    return (doc_ids, row_ids - starts)


def rope_tables(positions):
    steps_half = jnp.arange(HEAD_DIM // 2, dtype=jnp.float32)
    inverse = jnp.exp(steps_half * (-2.0 * math.log(rope_base) / HEAD_DIM))
    angles = positions.astype(jnp.float32)[:, None] * inverse[None, :]
    cosines = jnp.cos(angles)
    sines = jnp.sin(angles)
    return (jnp.concatenate([cosines, cosines], axis=1), jnp.concatenate([sines, sines], axis=1))


def rotate(heads_in, cosines, sines):
    half_dim = heads_in.shape[-1] // 2
    turned = jnp.concatenate([-heads_in[..., half_dim:], heads_in[..., :half_dim]], axis=-1)
    return heads_in * cosines[:, None, :] + turned * sines[:, None, :]


def block_length(row_count, shard_rows):
    shards = row_count // shard_rows
    return shard_rows * math.gcd(shards, max(1, 1024 // shard_rows))


def over_blocks(carry_state, row_count, shard_rows, block_fn):
    block_size = block_length(row_count, shard_rows)

    def block_step(inner_state, block_index):
        return (block_fn(inner_state, block_index * block_size, block_size), None)

    carry_state, _ = lax.scan(
        block_step, carry_state, jnp.arange(row_count // block_size, dtype=jnp.int32)
    )
    return carry_state


def scores_of(queries, key_part):
    return (
        jnp.einsum("qhd,khd->hqk", queries, key_part, preferred_element_type=jnp.float32)
        * score_scale
    )


def block_grads(queries, grad_rows, log_sums, row_dots, key_part, value_part, same_doc):
    scores = scores_of(queries, key_part)
    softmax_part = jnp.where(same_doc, jnp.exp(scores - log_sums[:, :, None]), 0.0)
    grad_probs = jnp.einsum(
        "qhd,khd->hqk", grad_rows, value_part, preferred_element_type=jnp.float32
    )
    dscore = (softmax_part * (grad_probs - row_dots[:, :, None])).astype(jnp.bfloat16)
    return (softmax_part, dscore)


def on_device(
    tokens,
    out_grad,
    short_lengths,
    attn_gain,
    qkv_weight,
    out_weight,
    mlp_gain,
    in_weight,
    down_weight,
):
    half_rows = tokens.shape[0]
    head_count = lax.axis_size("head")
    seq_count = lax.axis_size("seq")
    block_rows = half_rows * head_count
    total_rows = block_rows * seq_count
    local_ids = lax.axis_index("seq") * block_rows + jnp.arange(block_rows, dtype=jnp.int32)
    local_docs, local_pos = doc_layout(short_lengths, local_ids, total_rows)
    cosines, sines = rope_tables(local_pos)
    qkv_full, out_full = (
        lax.all_gather(qkv_weight, "seq", axis=0, tiled=True),
        lax.all_gather(out_weight, "seq", axis=1, tiled=True),
    )
    gain_first, gain_second, in_parts, down_parts = (
        lax.all_gather(attn_gain, ("seq", "head"), axis=0, tiled=True),
        lax.all_gather(mlp_gain, ("seq", "head"), axis=0, tiled=True),
        lax.all_gather(in_weight[None], ("seq", "head"), axis=0, tiled=True),
        lax.all_gather(down_weight[None], ("seq", "head"), axis=0, tiled=True),
    )
    in_parts = in_parts.reshape(seq_count, head_count, in_weight.shape[0], 2, in_weight.shape[2])
    down_parts = down_parts.reshape(
        seq_count, head_count, down_weight.shape[0], down_weight.shape[1]
    )
    heads_here = qkv_full.shape[2] // HEAD_DIM
    inputs = tokens.astype(jnp.float32)
    gain_one = gain_first.astype(jnp.float32)
    normed = layer_norm(inputs, gain_one).astype(jnp.bfloat16)
    normed_block = lax.all_gather(normed, "head", axis=0, tiled=True)
    projected = jnp.einsum(
        "rd,dgc->rgc", normed_block, qkv_full, preferred_element_type=jnp.float32
    )
    queries = rotate(
        projected[:, 0].reshape(block_rows, heads_here, HEAD_DIM), cosines, sines
    ).astype(jnp.bfloat16)
    key_rows = rotate(
        projected[:, 1].reshape(block_rows, heads_here, HEAD_DIM), cosines, sines
    ).astype(jnp.bfloat16)
    value_flat = projected[:, 2].astype(jnp.bfloat16)
    value_rows = value_flat.reshape(block_rows, heads_here, HEAD_DIM)
    key_flat = key_rows.reshape(block_rows, -1)
    query_flat = queries.reshape(block_rows, -1)

    def forward_fold(carry_state, portion):
        piece_keys, piece_values = portion

        def forward_block(inner_state, block_begin, block_size):
            running_max, running_sum, weighted = inner_state
            key_part = lax.dynamic_slice_in_dim(piece_keys, block_begin, block_size, 0).reshape(
                block_size, heads_here, HEAD_DIM
            )
            value_part = lax.dynamic_slice_in_dim(piece_values, block_begin, block_size, 0).reshape(
                block_size, heads_here, HEAD_DIM
            )
            other_docs, _ = doc_layout(
                short_lengths, block_begin + jnp.arange(block_size, dtype=jnp.int32), total_rows
            )
            same_doc = (local_docs[:, None] == other_docs[None, :])[None]
            scores = scores_of(queries, key_part)
            new_max = jnp.maximum(
                running_max, jnp.max(jnp.where(same_doc, scores, masked_low), axis=2)
            )
            factor = jnp.exp(running_max - new_max)
            softmax_part = jnp.where(same_doc, jnp.exp(scores - new_max[:, :, None]), 0.0)
            running_sum = running_sum * factor + jnp.sum(softmax_part, axis=2)
            weighted = weighted * factor.T[:, :, None] + jnp.einsum(
                "hqk,khd->qhd",
                softmax_part.astype(jnp.bfloat16),
                value_part,
                preferred_element_type=jnp.float32,
            )
            return (new_max, running_sum, weighted)

        return over_blocks(carry_state, piece_keys.shape[0], block_rows, forward_block)

    zeros_three = jnp.zeros((block_rows, heads_here, HEAD_DIM), jnp.float32)
    start_state = (
        jnp.full((heads_here, block_rows), masked_low, jnp.float32),
        jnp.zeros((heads_here, block_rows), jnp.float32),
        zeros_three,
    )
    running_max, running_sum, weighted = forward_fold(
        start_state,
        (
            lax.all_gather(key_flat, "seq", axis=0, tiled=True),
            lax.all_gather(value_flat, "seq", axis=0, tiled=True),
        ),
    )
    attended = weighted / running_sum.T[:, :, None]
    log_sums = running_max + jnp.log(running_sum)
    attended_low = attended.reshape(block_rows, -1).astype(jnp.bfloat16)
    branch = jnp.dot(attended_low, out_full, preferred_element_type=jnp.float32)
    branch_rows = lax.psum_scatter(
        branch.astype(jnp.bfloat16), "head", scatter_dimension=0, tiled=True
    ).astype(jnp.float32)
    resid = inputs + branch_rows
    gain_two = gain_second.astype(jnp.float32)
    normed_two = layer_norm(resid, gain_two).astype(jnp.bfloat16)
    normed_split = normed_two.reshape(half_rows, seq_count, -1)
    gate_up = jnp.einsum(
        "rse,shegf->rghf", normed_split, in_parts, preferred_element_type=jnp.float32
    ).reshape(half_rows, 2, -1)

    def activate(gate_part, up_part):
        return jax.nn.gelu(gate_part, approximate=False) * up_part

    hidden, activate_pull = jax.vjp(activate, gate_up[:, 0], gate_up[:, 1])
    hidden_low = hidden.astype(jnp.bfloat16)
    hidden_split = hidden_low.reshape(half_rows, head_count, -1)
    mlp_out = jnp.einsum(
        "rhf,shfe->rse", hidden_split, down_parts, preferred_element_type=jnp.float32
    ).reshape(half_rows, -1)
    mixed = (resid + mlp_out).astype(jnp.bfloat16)
    grad_out = out_grad.astype(jnp.float32)
    grad_split = out_grad.reshape(half_rows, seq_count, -1)
    grad_hidden = jnp.einsum(
        "rse,shfe->rhf", grad_split, down_parts, preferred_element_type=jnp.float32
    ).reshape(half_rows, -1)
    grad_gate, grad_up = activate_pull(grad_hidden)
    grad_gate_up = (
        jnp.stack([grad_gate, grad_up], axis=1)
        .astype(jnp.bfloat16)
        .reshape(half_rows, 2, head_count, -1)
    )
    down_grad = jnp.einsum(
        "rhf,rse->shfe", hidden_split, grad_split, preferred_element_type=jnp.float32
    ).reshape(seq_count * head_count, down_weight.shape[0], down_weight.shape[1])
    in_grad = jnp.einsum(
        "rse,rghf->shegf", normed_split, grad_gate_up, preferred_element_type=jnp.float32
    ).reshape(seq_count * head_count, in_weight.shape[0], 2, in_weight.shape[2])
    grad_normed_two = jnp.einsum(
        "rghf,shegf->rse", grad_gate_up, in_parts, preferred_element_type=jnp.float32
    ).reshape(half_rows, -1)
    _, norm_two_pull = jax.vjp(layer_norm, resid, gain_two)
    grad_resid_norm, gain_two_grad = norm_two_pull(grad_normed_two)
    grad_resid = grad_out + grad_resid_norm
    grad_branch = lax.all_gather(grad_resid.astype(jnp.bfloat16), "head", axis=0, tiled=True)
    out_grad_weight = jnp.einsum(
        "rc,rd->cd", attended_low, grad_branch, preferred_element_type=jnp.float32
    )
    grad_attended = jnp.einsum(
        "rd,cd->rc", grad_branch, out_full, preferred_element_type=jnp.float32
    ).astype(jnp.bfloat16)
    grad_three = grad_attended.reshape(block_rows, heads_here, HEAD_DIM)
    row_dots = jnp.sum(grad_three.astype(jnp.float32) * attended, axis=2).T
    all_sums, all_dots = (
        lax.all_gather(log_sums.T, "seq", axis=0, tiled=True),
        lax.all_gather(row_dots.T, "seq", axis=0, tiled=True),
    )

    def query_terms(query_grad, key_part, value_part, other_docs):
        same_doc = (local_docs[:, None] == other_docs[None, :])[None]
        _, dscore = block_grads(
            queries, grad_three, log_sums, row_dots, key_part, value_part, same_doc
        )
        return (
            query_grad
            + jnp.einsum("hqk,khd->qhd", dscore, key_part, preferred_element_type=jnp.float32)
            * score_scale
        )

    def key_terms(key_grad, value_grad, query_part, grad_part, sums_part, dots_part, other_docs):
        same_doc = (other_docs[:, None] == local_docs[None, :])[None]
        softmax_part, dscore = block_grads(
            query_part, grad_part, sums_part, dots_part, key_rows, value_rows, same_doc
        )
        value_grad = value_grad + jnp.einsum(
            "hqk,qhd->khd",
            softmax_part.astype(jnp.bfloat16),
            grad_part,
            preferred_element_type=jnp.float32,
        )
        key_grad = (
            key_grad
            + jnp.einsum("hqk,qhd->khd", dscore, query_part, preferred_element_type=jnp.float32)
            * score_scale
        )
        return (key_grad, value_grad)

    def piece_rows(source, block_begin, block_size):
        return lax.dynamic_slice_in_dim(source, block_begin, block_size, 0).reshape(
            block_size, heads_here, HEAD_DIM
        )

    def piece_stats(block_begin, block_size):
        sums_part = lax.dynamic_slice_in_dim(all_sums, block_begin, block_size, 0).T
        dots_part = lax.dynamic_slice_in_dim(all_dots, block_begin, block_size, 0).T
        other_docs, _ = doc_layout(
            short_lengths, block_begin + jnp.arange(block_size, dtype=jnp.int32), total_rows
        )
        return (sums_part, dots_part, other_docs)

    def fold_keys(carry_state, portion):
        piece_keys, piece_values = portion

        def key_block(inner_state, block_begin, block_size):
            _, _, other_docs = piece_stats(block_begin, block_size)
            return query_terms(
                inner_state,
                piece_rows(piece_keys, block_begin, block_size),
                piece_rows(piece_values, block_begin, block_size),
                other_docs,
            )

        return over_blocks(carry_state, piece_keys.shape[0], block_rows, key_block)

    query_grad = fold_keys(
        zeros_three,
        (
            lax.all_gather(key_flat, "seq", axis=0, tiled=True),
            lax.all_gather(value_flat, "seq", axis=0, tiled=True),
        ),
    )

    def fold_queries(carry_state, portion):
        piece_queries, piece_grads = portion

        def query_block(inner_state, block_begin, block_size):
            sums_part, dots_part, other_docs = piece_stats(block_begin, block_size)
            return key_terms(
                inner_state[0],
                inner_state[1],
                piece_rows(piece_queries, block_begin, block_size),
                piece_rows(piece_grads, block_begin, block_size),
                sums_part,
                dots_part,
                other_docs,
            )

        return over_blocks(carry_state, piece_queries.shape[0], block_rows, query_block)

    key_grad, value_grad = fold_queries(
        (zeros_three, zeros_three),
        (
            lax.all_gather(query_flat, "seq", axis=0, tiled=True),
            lax.all_gather(grad_attended, "seq", axis=0, tiled=True),
        ),
    )

    def rotate_local(heads_in):
        return rotate(heads_in, cosines, sines)

    _, rotate_pull = jax.vjp(rotate_local, zeros_three)
    query_back = rotate_pull(query_grad)[0]
    key_back = rotate_pull(key_grad)[0]
    grad_qkv = jnp.stack(
        [
            query_back.reshape(block_rows, -1),
            key_back.reshape(block_rows, -1),
            value_grad.reshape(block_rows, -1),
        ],
        axis=1,
    ).astype(jnp.bfloat16)
    qkv_grad = jnp.einsum("rd,rgc->dgc", normed_block, grad_qkv, preferred_element_type=jnp.float32)
    grad_normed_one = jnp.einsum(
        "rgc,dgc->rd", grad_qkv, qkv_full, preferred_element_type=jnp.float32
    )
    grad_normed_rows = lax.psum_scatter(
        grad_normed_one.astype(jnp.bfloat16), "head", scatter_dimension=0, tiled=True
    ).astype(jnp.float32)
    _, norm_one_pull = jax.vjp(layer_norm, inputs, gain_one)
    grad_inputs_norm, gain_one_grad = norm_one_pull(grad_normed_rows)
    tokens_grad = grad_resid + grad_inputs_norm
    qkv_weight_grad, out_weight_grad = (
        lax.psum_scatter(qkv_grad, "seq", scatter_dimension=0, tiled=True),
        lax.psum_scatter(out_grad_weight, "seq", scatter_dimension=1, tiled=True),
    )
    attn_gain_grad, mlp_gain_grad, in_weight_grad, down_weight_grad = (
        lax.psum_scatter(gain_one_grad, ("seq", "head"), scatter_dimension=0, tiled=True),
        lax.psum_scatter(gain_two_grad, ("seq", "head"), scatter_dimension=0, tiled=True),
        lax.psum_scatter(in_grad, ("seq", "head"), scatter_dimension=0, tiled=True),
        lax.psum_scatter(down_grad, ("seq", "head"), scatter_dimension=0, tiled=True),
    )
    return (
        mixed,
        tokens_grad,
        attn_gain_grad,
        qkv_weight_grad,
        out_weight_grad,
        mlp_gain_grad,
        in_weight_grad.reshape(in_weight.shape),
        down_weight_grad.reshape(down_weight.shape),
    )


LOW = jnp.bfloat16
FULL = jnp.float32


def dot(a, b):
    return jnp.dot(a, b, preferred_element_type=FULL)


def dot_nt(a, b):
    return lax.dot_general(a, b, (((1,), (1,)), ((), ())), preferred_element_type=FULL)


def turned(a):
    return a.astype(FULL).T


def centred_norm(rows):
    centred = rows - jnp.mean(rows, axis=-1, keepdims=True)
    scale = lax.rsqrt(jnp.mean(centred * centred, axis=-1, keepdims=True) + norm_eps)
    return centred * scale, scale


def norm_back(unit, scale, weighted):
    mean_w = jnp.mean(weighted, axis=-1, keepdims=True)
    mean_wn = jnp.mean(weighted * unit, axis=-1, keepdims=True)
    return (weighted - mean_w - unit * mean_wn) * scale


def whole_layer(*refs):
    (
        short_ref, gain_a, gain_m, tok_in, gout_in, qkv_in, out_in, in_in, down_in,
        mixed_out, tgrad_out, gains_out, qkvg_out, outg_out, ing_out, downg_out,
        mixed_ref, tgrad_ref, gains_ref, qkvg_ref, outg_ref, ing_ref, downg_ref,
        tok_ref, gout_ref, qkv_ref, wot_ref, in_ref, down_ref, gain_ref, wq_ref, ffp_ref, xh, gt, gn, gb, wh_p, wh, wht, ffw, wo, h1, cs, qa, ka, kt, vt, vr, pt, ot, ol, og, res,
        ms, ms_c, ms_a, ms_y, ms_d, db, dos, dop, dot_t, ds, dqt, dq, d1, d1_c, d1_a, d1_r1, d1_s1, d1_r2, d1_s2, d1_r3,
        dw, dw_c, dw_p, dw_in, gf, gf_k, gf_s, gf_z, gf_y, gf_f, gf_b, gf_c, go, go_k, go_s, go_z, go_y, go_f, go_b, go_c, gy, gy_in,
        s_tok, r_tok, s_gain, r_gain, s_wq, r_wq, s_g, r_g, s_ff, r_ff, s_wo, r_wo,
        s_o, r_o, s_ms, r_ms, s_db, r_db, s_do, r_do, s_d1, r_d1, s_dw, r_dw, s_gf, r_gf, s_go, r_go, s_gy, r_gy, s_out, s_in,
    ) = refs
    seq, head = lax.axis_index("seq"), lax.axis_index("head")
    z, x, c, y = seq // 4, (seq // 2) % 2, seq % 2, head
    zh, zb = z // 2, z % 2
    slot = zb * 2 + x
    active = slot < 3
    slot3 = jnp.minimum(slot, 2)
    pending, delivered = [], []

    def flip(value, bit):
        return value if bit == 0 else 1 - value

    def at(z_, x_, c_, y_):
        return (z_ * 4 + x_ * 2 + c_, y_)

    def far_z(k):
        return flip(zh, k // 2) * 2 + flip(zb, k % 2)

    def partner(dim):
        return {
            "x": at(z, 1 - x, c, y),
            "y": at(z, x, c, 1 - y),
            "z": at(far_z(1), x, c, y),
            "c": at(z, x, 1 - c, y),
            "h": at(far_z(2), x, c, y),
        }[dim]

    def push(src, dst, send, recv, device, when=None):
        copy = pltpu.make_async_remote_copy(
            src_ref=src, dst_ref=dst, send_sem=send, recv_sem=recv,
            device_id=device, device_id_type=pl.DeviceIdType.MESH,
        )
        if when is None:
            copy.start()
        else:
            pl.when(when)(copy.start)
        pending.append((when, copy))

    def deliver(k, src, dst):
        copy = pltpu.make_async_copy(src, dst, s_out.at[k])
        copy.start()
        delivered.append(copy)

    def arrive(dst, recv, when=None):
        copy = pltpu.make_async_remote_copy(
            src_ref=dst, dst_ref=dst, send_sem=recv, recv_sem=recv,
            device_id=partner("c"), device_id_type=pl.DeviceIdType.MESH,
        )
        if when is None:
            copy.wait_recv()
        else:
            pl.when(when)(copy.wait_recv)

    loads = (
        (tok_in, tok_ref), (qkv_in, qkv_ref), (in_in, in_ref), (down_in, down_ref), (out_in, wot_ref), (gout_in, gout_ref),
    )
    loads = [pltpu.make_async_copy(a, b, s_in.at[k]) for k, (a, b) in enumerate(loads)]
    barrier = pltpu.get_barrier_semaphore()
    peers = []
    for k in range(1, 32):
        kz, kx, kc, ky = k // 8, (k // 4) % 2, (k // 2) % 2, k % 2
        if kz < 2 or ky == 0:
            peers.append(at(far_z(kz), flip(x, kx), flip(c, kc), flip(y, ky)))
    for peer in peers:
        pl.semaphore_signal(barrier, inc=1, device_id=peer, device_id_type=pl.DeviceIdType.MESH)

    for load in loads:
        load.start()
    gain_ref[...] = jnp.zeros_like(gain_ref)
    gain_ref[0:1, 0 : gain_a.shape[1]] = gain_a[...].astype(FULL)
    gain_ref[1:2, 0 : gain_m.shape[1]] = gain_m[...].astype(FULL)
    for load in loads:
        load.wait()
    for g in range(3):
        for j in range(6):
            lanes = j % 2 * 192 + g * 64
            wq_ref[j // 2, :, lanes : lanes + 64] = qkv_ref[g, :, j * 64 : j * 64 + 64]
    for c_ in range(2):
        lanes = slice(c_ * 288, c_ * 288 + 288)
        for g in range(2):
            ffp_ref[c_, :, g * 288 : g * 288 + 288] = in_ref[:, g, lanes]
        ffp_ref[c_, :, 576:864] = down_ref[:, lanes]
    pl.semaphore_wait(barrier, len(peers))

    xh[zb, c, x, y] = tok_ref[...]
    orders = (("z", "x", "y"), ("z", "y", "x"), ("z", "x", "y"))

    def third(t):
        return pl.ds(t * 256, 256)

    def blocks(ref, opened, lanes, flipped=None, core=None):
        there = {"z": zb, "x": x, "y": y, "c": c if core is None else core}
        if flipped is not None:
            there[flipped] = 1 - there[flipped]
        index = tuple(slice(None) if d in opened else there[d] for d in ("z", "c", "x", "y"))
        return ref.at[index + (slice(None), lanes)]

    for t in range(3):
        view = blocks(xh, (), third(t))
        push(view, view, s_tok.at[0, t], r_tok.at[0, t], partner(orders[t][0]))

    gt[zh, zb, x, c, y] = gain_ref[...]

    def gain_place(k):
        return gt.at[flip(zh, k // 2), flip(zb, k % 2), x, c, y]

    for k in range(1, 4):
        push(gain_place(0), gain_place(0), s_gain.at[k], r_gain.at[k], at(far_z(k), x, c, y))

    def plane(k):
        return flip(x, k // 4), flip(c, k // 2 % 2), flip(y, k % 2)

    def gain_share():
        for k in range(1, 4):
            arrive(gain_place(k), r_gain.at[k])
        for k in range(1, 8):
            x_, c_, y_ = plane(k)
            view = gt.at[:, :, x, c, y]
            push(view, view, s_gain.at[3 + k], r_gain.at[3 + k], at(z, x_, c_, y_))

    def gain_all():
        for k in range(1, 8):
            x_, c_, y_ = plane(k)
            arrive(gt.at[:, :, x_, c_, y_], r_gain.at[3 + k])

    wo_lanes = pl.ds(pl.multiple_of(y * 384, 128), 384)
    wo_others = pl.ds(pl.multiple_of((1 - y) * 384, 128), 384)

    def ff_share(src, z_, x_, k, dim):
        push(src, ffw.at[z_, x_, c], s_ff.at[k], r_ff.at[k], partner(dim))

    def ff_arrive(kz, kx, k):
        arrive(ffw.at[far_z(kz), flip(x, kx), c], r_ff.at[k])

    def ff_cross():
        ff_arrive(0, 1, 0)
        ff_share(ffw.at[z, 1 - x, c], z, 1 - x, 2, "h")
        ff_share(ffw.at[z, 1 - x, c], z, 1 - x, 4, "z")

    def ff_relay():
        for kx in range(2):
            ff_arrive(2, kx, 1 + kx)
            z_, x_ = far_z(2), flip(x, kx)
            ff_share(ffw.at[z_, x_, c], z_, x_, 5 + kx, "z")

    def ff_core(kz):
        z_ = far_z(kz)
        push(ffw.at[z_, :, c], ffw.at[z_, :, c], s_ff.at[8 + kz], r_ff.at[8 + kz], partner("c"))

    def ff_near():
        for kx in range(2):
            ff_arrive(1, kx, 3 + kx)
        ff_core(1)

    def ff_last():
        for kx in range(2):
            ff_arrive(3, kx, 5 + kx)
        ff_core(3)

    def wo_forward_x():
        for k in range(1, 4):
            arrive(wo.at[far_z(k), x, c, :, wo_lanes], r_wo.at[k])
        view = wo.at[:, x, c, :, wo_lanes]
        push(view, view, s_wo.at[4], r_wo.at[4], partner("x"))

    def wo_forward_y():
        arrive(wo.at[:, 1 - x, c, :, wo_lanes], r_wo.at[4])
        view = wo.at[:, :, c, :, wo_lanes]
        push(view, view, s_wo.at[5], r_wo.at[5], partner("y"))

    def wo_forward_core():
        arrive(wo.at[:, :, c, :, wo_others], r_wo.at[5])
        push(wo.at[:, :, c], wo.at[:, :, c], s_wo.at[6], r_wo.at[6], partner("c"))

    ffw[z, x, c] = ffp_ref[x]
    wo[z, x, c, :, wo_lanes] = wot_ref[...]
    def wo_push():
        for k in (2, 3, 1):
            push(wot_ref, wo.at[z, x, c, :, wo_lanes], s_wo.at[k], r_wo.at[k], at(far_z(k), x, c, y))

    own_pair_at = z * 2 + x
    wh_p[c, own_pair_at] = wq_ref[slot3]

    def head_push():
        for k in (7, 5, 6, 4, 3, 2, 1):
            z_, x_ = far_z(k // 2), flip(x, k % 2)
            slot_ = z_ % 2 * 2 + x_
            piece = wq_ref.at[jnp.minimum(slot_, 2)]
            push(piece, wh_p.at[c, own_pair_at], s_wq.at[k], r_wq.at[k], at(z_, x_, c, y), slot_ < 3)

    gb[x, y] = gout_ref[...]
    group = ((0, 1), (1, 0), (1, 1))

    def member(kx, ky):
        return at(z, flip(x, kx), c, flip(y, ky))

    def grad_push():
        for k, (kx, ky) in enumerate(group):
            push(gb.at[x, y], gb.at[x, y], s_g.at[k], r_g.at[k], member(kx, ky))

    def token_step(step):
        for t in range(3):
            arrive(blocks(xh, orders[t][: step - 1], third(t), orders[t][step - 1]), r_tok.at[step - 1, t])
            view = blocks(xh, orders[t][:step], third(t))
            push(view, view, s_tok.at[step, t], r_tok.at[step, t], partner(orders[t][step]))

    events = {
        "fx": lambda: ff_share(ffp_ref.at[1 - x], z, x, 0, "x"),
        "f2": lambda: ff_share(ffp_ref.at[x], z, x, 1, "h"),
        "f1": lambda: ff_share(ffp_ref.at[x], z, x, 3, "z"),
        "fc": ff_cross,
        "fr": ff_relay,
        "c0": lambda: ff_core(0),
        "c1": ff_near,
        "c2": lambda: ff_core(2),
        "c3": ff_last,
        "w": head_push,
        "g": grad_push,
        "oz": wo_push,
        "ox": wo_forward_x,
        "oy": wo_forward_y,
        "oc": wo_forward_core,
    }

    def run(point):
        for name in plan[point]:
            events[name]()

    plan = (
        ("w",),
        ("f2", "fx", "f1", "oz"),
        ("fc", "ox", "g"),
        ("fr", "c0", "c1", "oy"),
        ("c2",),
        (),
        (),
        (),
        ("c3", "oc"),
    )
    run(0)
    token_step(1)
    gain_share()
    run(1)
    token_step(2)
    run(2)
    run(3)

    half_rows = 1024
    lane = lax.broadcasted_iota(jnp.int32, (32, half_rows), 1)
    row = lane % 64 + (lane // 64 % 2) * 64 + (lane // 256 % 2) * 128 + (lane // 128 % 2) * 256 + (lane // 512) * 512
    row = row + zh * half_rows
    feature = lax.broadcasted_iota(jnp.int32, (32, half_rows), 0)
    bound = jnp.int32(2 * half_rows)
    for b in range(short_ref.shape[0]):
        bound = bound - short_ref[b]
    doc = jnp.zeros_like(row)
    start = jnp.zeros_like(row)
    for b in range(short_ref.shape[0]):
        passed = row >= bound
        doc = doc + jnp.where(passed, 1, 0)
        start = jnp.where(passed, bound, start)
        bound = bound + short_ref[b]
    inverse = jnp.exp(feature.astype(FULL) * (-2.0 * math.log(rope_base) / HEAD_DIM))
    angles = (row - start).astype(FULL) * inverse
    cs[0] = jnp.cos(angles)
    cs[1] = jnp.sin(angles)
    same = jnp.where(feature == doc, 1.0, 0.0)
    cs[2] = same
    qa[64:96, :] = ((same - 1.0) * 1e30).astype(LOW)
    qa[96:128, :] = jnp.zeros((32, half_rows), LOW)

    gain_all()
    tiles = gt[...].reshape(256, 128).astype(LOW)
    width = 24
    pick = lax.broadcasted_iota(jnp.int32, (128, 768), 1) % width == lax.broadcasted_iota(jnp.int32, (128, 768), 0)
    spread = dot(tiles, jnp.where(pick, 1.0, 0.0).astype(LOW))
    source = lax.broadcasted_iota(jnp.int32, (256, 768), 0)
    wanted = (lax.broadcasted_iota(jnp.int32, (256, 768), 1) // width) * 8
    gn[0:1, :] = jnp.sum(jnp.where(source == wanted, spread, 0.0), axis=0, keepdims=True)
    gn[1:2, :] = jnp.sum(jnp.where(source == wanted + 1, spread, 0.0), axis=0, keepdims=True)

    for t in range(3):
        arrive(blocks(xh, orders[t][:2], third(t), orders[t][2]), r_tok.at[2, t])

    def rows_of(z_, c_):
        return pl.ds(pl.multiple_of(z_ * 512 + c_ * 256, 256), 256)

    for k in range(1, 8):
        arrive(wh_p.at[c, far_z(k // 2) * 2 + flip(x, k % 2)], r_wq.at[k], active)
    push(wh_p.at[c], wh_p.at[c], s_wq.at[0], r_wq.at[0], partner("c"), active)

    for z_ in range(2):
        rows = rows_of(z_, c)

        @pl.when(active)
        def _(z_=z_, rows=rows):
            unit, _ = centred_norm(xh[z_, c].reshape(256, 768).astype(FULL))
            h1[rows, :] = (unit * gn[0:1, :]).astype(LOW)

        push(h1.at[rows, :], h1.at[rows, :], s_tok.at[3, z_], r_tok.at[3, z_], partner("c"), active)
    arrive(wh_p.at[1 - c], r_wq.at[0], active)

    @pl.when(active)
    def _():
        for c_ in range(2):
            wh[:, c_] = jnp.where(c == 0, wh_p[c_, :, :, 0:192], wh_p[c_, :, :, 192:384])
        wht[...] = turned(wh[...].reshape(768, 192)).astype(LOW)

    for part in range(4):
        z_, c_ = part % 2, flip(c, part // 2)
        cols = rows_of(z_, c_)
        if part >= 2:
            arrive(h1.at[cols, :], r_tok.at[3, z_], active)

        @pl.when(active)
        def _(cols=cols):
            proj = dot_nt(wht[...], h1[cols, :])
            cosine, sine = cs[0, :, cols], cs[1, :, cols]
            q1, q2, k1, k2 = proj[0:32], proj[32:64], proj[64:96], proj[96:128]
            qr = jnp.concatenate([q1 * cosine - q2 * sine, q2 * cosine + q1 * sine], axis=0)
            kr = jnp.concatenate([k1 * cosine - k2 * sine, k2 * cosine + k1 * sine], axis=0)
            qa[0:64, cols] = (qr * score_scale).astype(LOW)
            kt[:, cols] = kr.astype(LOW)
            vt[:, cols] = proj[128:192].astype(LOW)
            pad = jnp.zeros((32, 256), FULL)
            ka[cols, :] = jnp.concatenate([kr, cs[2, :, cols], pad], axis=0).T.astype(LOW)
            vr[cols, :] = proj[128:192].T.astype(LOW)

    run(4)

    for part in range(4):
        cols = pl.ds(part * 256, 256)

        @pl.when(active)
        def _(part=part, cols=cols):
            scores = dot(ka[...], qa[:, cols])
            expo = jnp.exp(scores - jnp.max(scores, axis=0, keepdims=True))
            prob = (expo * (1.0 / jnp.sum(expo, axis=0, keepdims=True))).astype(LOW)
            pt[:, cols] = prob
            result = dot(vt[...], prob)
            ot[part] = result
            ol[part] = result.astype(LOW)

        own_group = jnp.logical_and(zb == part // 2, c == part % 2)
        for k in range(4):
            x_, y_ = k // 2, k % 2
            mine = jnp.logical_and(own_group, jnp.logical_and(x == x_, y == y_))

            @pl.when(jnp.logical_and(active, mine))
            def _(part=part):
                og[y, slot3, c] = ol[part]

            push(
                ol.at[part], og.at[y, slot3, c], s_o.at[part, k], r_o.at[slot3, c, y],
                at(zh * 2 + part // 2, x_, part % 2, y_), jnp.logical_and(active, jnp.logical_not(mine)),
            )
        run(5 + part)

    for slot_ in range(3):
        for c_ in range(2):
            for y_ in range(2):
                mine = jnp.logical_and(slot == slot_, jnp.logical_and(c == c_, y == y_))
                arrive(og.at[y_, slot_, c_], r_o.at[slot_, c_, y_], jnp.logical_not(mine))
    arrive(wo.at[:, :, 1 - c], r_wo.at[6])

    gain_two = gn[1:2, :]
    branch = dot(wo[...].reshape(768, 768), og[...].reshape(768, 256)).T
    resid = xh[zb, c].reshape(256, 768).astype(FULL) + branch
    res[...] = resid.reshape(2, 2, 64, 768)
    unit_two, _ = centred_norm(resid)
    h2 = (unit_two * gain_two).astype(LOW)

    for kz in range(4):
        arrive(ffw.at[far_z(kz), :, 1 - c], r_ff.at[8 + kz])
    for k, (kx, ky) in enumerate(group):
        arrive(gb.at[flip(x, kx), flip(y, ky)], r_g.at[k])
    w_in = ffw[:, :, :, :, 0:576].reshape(768, 576)
    w_down = ffw[:, :, :, :, 576:864].reshape(768, 288)
    gate_up = dot(h2, w_in)
    gate, up = gate_up[:, :288], gate_up[:, 288:]
    grad_out = gb[...].reshape(256, 768)
    grad_hidden = dot(grad_out, w_down)
    chance = 0.5 * (1.0 + lax.erf(gate * (1.0 / math.sqrt(2.0))))
    density = jnp.exp(gate * gate * -0.5) * (1.0 / math.sqrt(2.0 * math.pi))
    curve = gate * chance
    hidden = (curve * up).astype(LOW)
    grad_gate = grad_hidden * up * (chance + gate * density)
    grad_gate_up = jnp.concatenate([grad_gate, grad_hidden * curve], axis=1).astype(LOW)

    columns = (slice(0, 384), slice(384, 768))

    def halve(kind, part):
        ms[kind] = part.astype(LOW).reshape(2, 2, 64, 768)
        push(ms.at[kind, 1 - x, :, :, columns[0]], ms_c.at[kind, 0], s_ms.at[kind, 0, 0], r_ms.at[kind, 0, 0], partner("x"))
        push(ms.at[kind, :, 1 - y, :, columns[1]], ms_c.at[kind, 1], s_ms.at[kind, 1, 0], r_ms.at[kind, 1, 0], partner("y"))

    def quarter(kind):
        for t in range(2):
            arrive(ms_c.at[kind, t], r_ms.at[kind, t, 0])
            mine = ms[kind, x, 1 - y, :, columns[0]] if t == 0 else ms[kind, 1 - x, y, :, columns[1]]
            other = ms_c[kind, t, 1 - y] if t == 0 else ms_c[kind, t, 1 - x]
            ms_a[kind, t] = (mine.astype(FULL) + other.astype(FULL)).astype(LOW)
            push(ms_a.at[kind, t], ms_y.at[kind, t], s_ms.at[kind, t, 1], r_ms.at[kind, t, 1], partner("yx"[t]))

    def quarter_sum(kind):
        sums = []
        for t in range(2):
            arrive(ms_y.at[kind, t], r_ms.at[kind, t, 1])
            other = ms_c[kind, t, y] if t == 0 else ms_c[kind, t, x]
            mine = ms[kind, x, y, :, columns[t]].astype(FULL) + other.astype(FULL)
            sums.append(mine + ms_y[kind, t].astype(FULL))
        return jnp.concatenate(sums, axis=1)

    ms[0] = dot_nt(grad_gate_up, w_in).astype(LOW).reshape(2, 2, 64, 768)
    for k, (kx, ky) in enumerate(group):
        push(ms.at[0, flip(x, kx), flip(y, ky)], ms_d.at[k], s_g.at[3 + k], r_g.at[3 + k], member(kx, ky))
    h2_t = turned(h2).astype(LOW)
    gf[:, :, :, :, 0:576] = dot(h2_t, grad_gate_up).astype(LOW).reshape(4, 2, 2, 48, 576)
    g_t = turned(grad_out).astype(LOW)
    gf[:, :, :, :, 576:864] = dot(g_t, hidden).astype(LOW).reshape(4, 2, 2, 48, 288)

    def sums_of(whole, crossed, low, near, far, wide, last, coming, send, recv):
        def cross():
            for kz in (3, 1, 2, 0):
                z_ = far_z(kz)
                push(whole.at[z_, :, 1 - c], crossed.at[z_], send.at[0, kz], recv.at[0, kz], partner("c"))

        def pair(kz):
            z_ = far_z(kz)
            arrive(crossed.at[z_], recv.at[0, kz])
            return whole[z_, :, c].astype(FULL) + crossed[z_].astype(FULL)

        def to_near(kz):
            z_ = far_z(kz)
            low[z_] = pair(kz).astype(LOW)
            push(low.at[z_], near.at[kz // 2], send.at[1, kz // 2], recv.at[1, kz // 2], partner("z"))

        def to_far():
            value = pair(2)
            arrive(near.at[1], recv.at[1, 1])
            low[far_z(2)] = (value + near[1].astype(FULL)).astype(LOW)
            push(low.at[far_z(2)], far, send.at[2, 0], recv.at[2, 0], partner("h"))

        def finish():
            value = pair(0)
            arrive(near.at[0], recv.at[1, 0])
            arrive(far, recv.at[2, 0])
            wide[...] = value + near[0].astype(FULL) + far[...].astype(FULL)
            last[...] = wide[1 - x].astype(LOW)
            push(last, coming, send.at[3, 0], recv.at[3, 0], partner("x"))

        def result():
            arrive(coming, recv.at[3, 0])
            own, other = wide[x], coming[...].astype(FULL)
            return jnp.where(x == 0, own, other), jnp.where(x == 0, other, own)

        return cross, to_near, to_far, finish, result

    ff_sums = sums_of(gf, gf_k, gf_s, gf_z, gf_y, gf_f, gf_b, gf_c, s_gf, r_gf)
    out_sums = sums_of(go, go_k, go_s, go_z, go_y, go_f, go_b, go_c, s_go, r_go)

    def out_share():
        for k, (kx, ky) in enumerate(group):
            arrive(db.at[flip(x, kx), flip(y, ky)], r_db.at[k])
        db_t = turned(db[...].reshape(256, 768)).astype(LOW)
        o_part = og[...].reshape(2, 6, 64, 256)
        o_pick = jnp.where(y == 0, o_part[0], o_part[1])
        o_pick = jnp.where(x == 0, o_pick[0:3], o_pick[3:6]).reshape(192, 256)
        go[...] = dot_nt(db_t, o_pick).astype(LOW).reshape(4, 2, 2, 48, 192)
        out_sums[0]()

    def mixed_done():
        mixed_ref[...] = (res[x, y] + quarter_sum(1)).astype(LOW)
        deliver(0, mixed_ref, mixed_out)

    later = {
        "md": mixed_done,
        "mx": lambda: quarter(1),
        "n3": lambda: ff_sums[1](3),
        "n1": lambda: ff_sums[1](1),
        "f": ff_sums[2],
        "e": ff_sums[3],
        "O": out_share,
        "O3": lambda: out_sums[1](3),
        "O1": lambda: out_sums[1](1),
        "Of": out_sums[2],
        "Oe": out_sums[3],
    }
    then = (
        ("n3",),
        ("n1", "mx"),
        (),
        (),
        ("f", "md"),
        (),
        (),
        ("O",),
        ("e", "O3", "O1", "Of"),
        ("Oe",),
    )

    def run_later(point):
        for name in then[point]:
            later[name]()

    ff_sums[0]()
    halve(1, dot_nt(hidden, w_down))
    run_later(0)
    own_res = res[x, y]
    unit_two, scale_two = centred_norm(own_res)
    grad_h2 = ms[0, x, y].astype(FULL)
    for k in range(3):
        arrive(ms_d.at[k], r_g.at[3 + k])
        grad_h2 = grad_h2 + ms_d[k].astype(FULL)
    grad_resid = gout_ref[...].astype(FULL) + norm_back(unit_two, scale_two, grad_h2 * gain_two)
    tgrad_ref[...] = grad_resid
    grad_branch = grad_resid.astype(LOW)
    db[x, y] = grad_branch
    grad_o = dot(grad_branch, wo[...].reshape(768, 768)).astype(LOW)
    own_block = zb * 8 + c * 4 + x * 2 + y
    for slot_ in range(3):
        for y_ in range(2):
            lanes = y_ * 384 + slot_ * 128
            dos[y_, slot_] = grad_o[:, lanes : lanes + 128]
            for c_ in range(2):
                mine = jnp.logical_and(jnp.logical_and(slot == slot_, y == y_), c == c_)

                @pl.when(mine)
                def _(slot_=slot_, y_=y_):
                    dop[zb, c, x, y] = dos[y_, slot_]

                push(
                    dos.at[y_, slot_], dop.at[zb, c, x, y], s_do.at[slot_ * 4 + y_ * 2 + c_], r_do.at[own_block],
                    at(zh * 2 + slot_ // 2, slot_ % 2, c_, y_), jnp.logical_not(mine),
                )
    run_later(1)
    for k, (kx, ky) in enumerate(group):
        push(db.at[x, y], db.at[x, y], s_db.at[k], r_db.at[k], member(kx, ky))
    run_later(2)

    for b in range(16):
        z_, c_, x_, y_ = b // 8, (b // 4) % 2, (b // 2) % 2, b % 2
        arrive(dop.at[z_, c_, x_, y_], r_do.at[b], jnp.logical_and(active, own_block != b))

    @pl.when(active)
    def _():
        pair = turned(dop[...].reshape(1024, 128))
        dot_t[...] = jnp.where(c == 0, pair[0:64], pair[64:128]).astype(LOW)

    for part in range(4):
        cols = pl.ds(part * 256, 256)

        @pl.when(active)
        def _(part=part, cols=cols):
            grad_t = dot_t[:, cols]
            delta = jnp.sum(grad_t.astype(FULL) * ot[part], axis=0, keepdims=True)
            grad_p = dot(vr[...], grad_t)
            score_grad = (pt[:, cols].astype(FULL) * (grad_p - delta)).astype(LOW)
            ds[:, cols] = score_grad
            back = dot(kt[...], score_grad) * score_scale
            cosine, sine = cs[0, :, cols], cs[1, :, cols]
            b1, b2 = back[0:32], back[32:64]
            dqt[0:64, cols] = jnp.concatenate([b1 * cosine + b2 * sine, b2 * cosine - b1 * sine], axis=0).astype(LOW)

        run_later(3 + part)

    @pl.when(active)
    def _():
        for part in range(4):
            cols = pl.ds(part * 256, 256)
            back = dot_nt(qa[0:64, :], ds[cols, :])
            cosine, sine = cs[0, :, cols], cs[1, :, cols]
            b1, b2 = back[0:32], back[32:64]
            dqt[64:128, cols] = jnp.concatenate([b1 * cosine + b2 * sine, b2 * cosine - b1 * sine], axis=0).astype(LOW)
            dqt[128:192, cols] = dot_nt(dot_t[...], pt[cols, :]).astype(LOW)
            dq[cols, :] = turned(dqt[:, cols]).astype(LOW)

    for part in range(4):
        z_, c_ = part % 2, flip(c, 1 - part // 2)

        @pl.when(active)
        def _(z_=z_, c_=c_):
            rows = pl.ds(pl.multiple_of(z_ * 512 + c_ * 256, 256), 256)
            d1[z_, c_] = dot_nt(dq[rows, :], wh[...].reshape(768, 192)).astype(LOW).reshape(2, 2, 64, 768)

        if part < 2:
            push(d1.at[z_, c_], d1_c.at[z_], s_d1.at[0, z_], r_d1.at[0, z_], partner("c"), active)
    run_later(7)

    @pl.when(active)
    def _():
        grad = dot(dqt[...], h1[...])
        grad = grad.T.astype(LOW).reshape(8, 2, 48, 192)
        dw[0], dw[1] = grad[:, 0], grad[:, 1]

    push(dw.at[1 - c], dw_c, s_dw.at[0], r_dw.at[6], partner("c"), active)

    @pl.when(jnp.logical_not(active))
    def _():
        d1_a[...] = jnp.zeros_like(d1_a)

    for z_ in range(2):
        arrive(d1_c.at[z_], r_d1.at[0, z_], active)

        @pl.when(active)
        def _(z_=z_):
            d1_a[z_] = (d1[z_, c].astype(FULL) + d1_c[z_].astype(FULL)).astype(LOW)

    back_orders = (("x", "y", "z"), ("y", "z", "x"), ("z", "x", "y"))

    def remaining(t, step):
        return tuple(d for d in ("z", "x", "y") if d not in back_orders[t][:step])

    landing = (d1_r1, d1_r2, d1_r3)

    def step_view(t, step, flipped):
        dim = back_orders[t][step]
        place = {"z": zb, "x": x, "y": y}[dim]
        place = 1 - place if flipped else place
        index = tuple(place if d == dim else slice(None) for d in remaining(t, step))
        if step == 0:
            return d1_a.at[index + (slice(None), third(t))]
        return (d1_s1, d1_s2)[step - 1].at[(t,) + index]

    def step_push(t, step):
        push(
            step_view(t, step, True), landing[step].at[t], s_d1.at[1 + step, t], r_d1.at[1 + step, t],
            partner(back_orders[t][step]),
        )

    def step_sum(t, step):
        arrive(landing[step].at[t], r_d1.at[1 + step, t])
        return step_view(t, step, False)[...].astype(FULL) + landing[step][t].astype(FULL)

    for t in range(3):
        step_push(t, 0)

    own_pair = zh * 3 + slot3
    arrive(dw_c, r_dw.at[6], active)

    @pl.when(active)
    def _():
        own, other = dw[c], dw_c[...]
        dw_p[:, :, 0:192] = jnp.where(c == 0, own, other)
        dw_p[:, :, 192:384] = jnp.where(c == 0, other, own)
        dw_in[own_pair] = dw_p[z * 2 + x]

    def pair_push(ks):
        for k in ks:
            z_, x_ = far_z(k // 2), flip(x, k % 2)
            push(dw_p.at[z_ * 2 + x_], dw_in.at[own_pair], s_dw.at[k], r_dw.at[own_pair], at(z_, x_, c, y), active)

    pair_push((7, 5, 6, 4))
    for t in range(3):
        d1_s1[t] = step_sum(t, 0).astype(LOW)
        step_push(t, 1)
    pair_push((3, 2, 1))

    run_later(8)
    for t in range(3):
        d1_s2[t] = step_sum(t, 1).astype(LOW)
        step_push(t, 2)
    run_later(9)
    mlp_terms = jnp.zeros((48, 1), FULL)
    for x_, grads in enumerate(ff_sums[4]()):
        lanes = slice(x_ * 288, x_ * 288 + 288)
        for g in range(2):
            ing_ref[:, g, lanes] = grads[:, g * 288 : g * 288 + 288]
        downg_ref[:, lanes] = grads[:, 576:864]
        terms = grads[:, 0:576] * ffp_ref[x_, :, 0:576].astype(FULL)
        mlp_terms = mlp_terms + jnp.sum(terms, axis=1, keepdims=True)
    deliver(1, ing_ref, ing_out)
    deliver(2, downg_ref, downg_out)
    for h_ in range(2):
        for slot_ in range(3):
            mine = jnp.logical_and(zh == h_, slot == slot_)
            arrive(dw_in.at[h_ * 3 + slot_], r_dw.at[h_ * 3 + slot_], jnp.logical_not(mine))
    attn_terms = jnp.zeros((48, 1), FULL)
    for slot_ in range(3):
        both = dw_in[slot_].astype(FULL) + dw_in[3 + slot_].astype(FULL)
        for c_ in range(2):
            for g in range(3):
                lanes, j = c_ * 192 + g * 64, slot_ * 2 + c_
                qkvg_ref[g, :, j * 64 : j * 64 + 64] = both[:, lanes : lanes + 64]
        attn_terms = attn_terms + jnp.sum(both * wq_ref[slot_].astype(FULL), axis=1, keepdims=True)
    deliver(3, qkvg_ref, qkvg_out)
    lane = lax.broadcasted_iota(jnp.int32, (48, 128), 1)
    gy[...] = jnp.where(lane == 0, attn_terms, jnp.where(lane == 1, mlp_terms, 0.0))
    push(gy, gy_in, s_gy.at[0], r_gy.at[0], partner("y"))
    for x_, grads in enumerate(out_sums[4]()):
        outg_ref[:, x_ * 192 : x_ * 192 + 192] = grads
    deliver(4, outg_ref, outg_out)

    unit_one, scale_one = centred_norm(tok_ref[...].astype(FULL))
    for t in range(3):
        res[0, 0, :, third(t)] = step_sum(t, 2)
    tgrad_ref[...] = tgrad_ref[...] + norm_back(unit_one, scale_one, res[0, 0] * gn[0:1, :])
    deliver(5, tgrad_ref, tgrad_out)
    arrive(gy_in, r_gy.at[0])
    sums = (gy[...] + gy_in[...]).T
    count = gain_a.shape[1]
    sums = jnp.where(y == 0, sums[0:2, :count], sums[0:2, count : 2 * count])
    gains_ref[...] = jnp.zeros_like(gains_ref)
    gains_ref[0:2, 0:count] = sums / gain_ref[0:2, 0:count]
    deliver(6, gains_ref, gains_out)
    for copy in delivered:
        copy.wait()
    for when, copy in pending:
        if when is None:
            copy.wait_send()
        else:
            pl.when(when)(copy.wait_send)


def hand_on(*refs):
    sources, results, held, sems = refs[:7], refs[7:15], refs[15:21], refs[21]
    count = results[6].shape[1]
    results[6][...] = sources[6][0:1, :count]
    results[7][...] = sources[6][1:2, :count]
    inward = [pltpu.make_async_copy(a, b, sems.at[0, k]) for k, (a, b) in enumerate(zip(sources[:6], held))]
    outward = [pltpu.make_async_copy(a, b, sems.at[1, k]) for k, (a, b) in enumerate(zip(held, results[:6]))]
    for copy in inward:
        copy.start()
    for first, second in zip(inward, outward):
        first.wait()
        second.start()
    for copy in outward:
        copy.wait()


def on_device_fast(tokens, out_grad, short_lengths, attn_gain, qkv_weight, out_weight, mlp_gain, in_weight, down_weight):
    rows, width = tokens.shape
    depth = qkv_weight.shape[0]
    heads_here = qkv_weight.shape[2] // HEAD_DIM
    count = attn_gain.shape[0]
    ff = in_weight.shape[2] // 2 * 3
    feats = out_weight.shape[0]

    def vm(shape, kind=LOW):
        return pltpu.VMEM(shape, kind)

    def sem(*shape):
        return pltpu.SemaphoreType.DMA(shape)

    finals = [
        ((rows, width), LOW), ((rows, width), FULL), ((8, 128), FULL), ((3, depth, 384), FULL),
        ((depth, feats), FULL), ((depth, 2, 576), FULL), ((depth, 576), FULL),
    ]
    scratch = [vm(*shape) for shape in finals] + [
        vm((rows, width)), vm((rows, width)), vm((3, depth, 384)), vm((depth, feats)), vm((depth, 2, 576)), vm((depth, 576)),
        vm((8, 128), FULL), vm((heads_here // 2, depth, 384)), vm((2, depth, ff)),
        vm((2, 2, 2, 2, 64, 768)), vm((2, 2, 2, 2, 2, 8, 128), FULL), vm((8, 768), FULL), vm((2, 2, 64, 768)),
        vm((2, 8, 48, 384)), vm((8, 2, 48, 192)), vm((192, 768)), vm((4, 2, 2, 48, 864)), vm((4, 2, 2, 48, 768)), vm((1024, 768)),
        vm((3, 32, 1024), FULL), vm((128, 1024)), vm((1024, 128)), vm((64, 1024)), vm((64, 1024)), vm((1024, 64)),
        vm((1024, 1024)), vm((4, 64, 256), FULL), vm((4, 64, 256)), vm((2, 3, 2, 64, 256)), vm((2, 2, 64, 768), FULL),
        vm((2, 2, 2, 64, 768)), vm((2, 2, 2, 64, 384)), vm((2, 2, 64, 384)), vm((2, 2, 64, 384)), vm((3, 64, 768)), vm((2, 2, 64, 768)),
        vm((2, 3, 64, 128)), vm((2, 2, 2, 2, 64, 128)), vm((64, 1024)), vm((1024, 1024)), vm((192, 1024)),
        vm((1024, 192)), vm((2, 2, 2, 2, 64, 768)), vm((2, 2, 2, 64, 768)), vm((2, 2, 2, 64, 768)),
        vm((3, 2, 2, 64, 256)), vm((3, 2, 2, 64, 256)), vm((3, 2, 64, 256)), vm((3, 2, 64, 256)), vm((3, 64, 256)),
        vm((2, 8, 48, 192)), vm((8, 48, 192)), vm((8, 48, 384)), vm((6, 48, 384)),
        vm((4, 2, 2, 48, 864)), vm((4, 2, 48, 864)), vm((4, 2, 48, 864)), vm((2, 2, 48, 864)), vm((2, 48, 864)),
        vm((2, 48, 864), FULL), vm((48, 864)), vm((48, 864)),
        vm((4, 2, 2, 48, 192)), vm((4, 2, 48, 192)), vm((4, 2, 48, 192)), vm((2, 2, 48, 192)), vm((2, 48, 192)),
        vm((2, 48, 192), FULL), vm((48, 192)), vm((48, 192)),
        vm((48, 128), FULL), vm((48, 128), FULL),
        sem(4, 3), sem(4, 3), sem(11), sem(11), sem(8), sem(8), sem(6), sem(6), sem(12), sem(12), sem(7), sem(7),
        sem(4, 4), sem(3, 2, 2), sem(2, 2, 2), sem(2, 2, 2), sem(3), sem(3), sem(12), sem(16), sem(4, 4), sem(4, 4),
        sem(8), sem(7), sem(4, 4), sem(4, 4), sem(4, 4), sem(4, 4), sem(1), sem(1), sem(7), sem(6),
    ]
    vmem = pl.BlockSpec(memory_space=pltpu.VMEM)
    anywhere = pl.BlockSpec(memory_space=pl.ANY)
    shapes = [jax.ShapeDtypeStruct(*shape) for shape in finals]
    mixed, tokens_grad, gains, qkv_grad, out_grads, in_grad, down_grad = pl.pallas_call(
        whole_layer,
        out_shape=shapes,
        in_specs=[pl.BlockSpec(memory_space=pltpu.SMEM)] + [vmem] * 2 + [anywhere] * 6,
        out_specs=[anywhere] * 7,
        scratch_shapes=scratch,
        compiler_params=pltpu.CompilerParams(collective_id=0, has_side_effects=True, vmem_limit_bytes=60 << 20),
    )(
        short_lengths, attn_gain[None], mlp_gain[None], tokens, out_grad,
        qkv_weight.transpose(1, 0, 2), out_weight.T, in_weight, down_weight.T,
    )
    grads = (mixed, tokens_grad, qkv_grad, out_grads, in_grad, down_grad)
    count = attn_gain.shape[0]
    mixed, tokens_grad, qkv_grad, out_grads, in_grad, down_grad, attn_gain_grad, mlp_gain_grad = pl.pallas_call(
        hand_on,
        out_shape=[jax.ShapeDtypeStruct(a.shape, a.dtype) for a in grads] + [jax.ShapeDtypeStruct((1, count), FULL)] * 2,
        in_specs=[anywhere] * 6 + [vmem],
        out_specs=[anywhere] * 6 + [vmem] * 2,
        scratch_shapes=[vm(a.shape, a.dtype) for a in grads] + [sem(2, 6)],
    )(*grads, gains)
    return (
        mixed, tokens_grad, attn_gain_grad[0], qkv_grad.transpose(1, 0, 2), out_grads.T, mlp_gain_grad[0],
        in_grad, down_grad.T,
    )


def solution(mesh):
    placed = (
        P(("seq", "head"), None),
        P(("seq", "head"), None),
        P(),
        P(("seq", "head")),
        P("seq", None, "head"),
        P("head", "seq"),
        P(("seq", "head")),
        P("seq", None, "head"),
        P("head", "seq"),
    )
    fits = mesh.shape["seq"] == 16 and mesh.shape["head"] == 2
    return jax.shard_map(
        on_device_fast if fits else on_device,
        mesh=mesh,
        in_specs=placed,
        out_specs=(
            P(("seq", "head"), None),
            P(("seq", "head"), None),
            P(("seq", "head")),
            P("seq", None, "head"),
            P("head", "seq"),
            P(("seq", "head")),
            P("seq", None, "head"),
            P("head", "seq"),
        ),
        check_vma=False,
    )
```

```python
import math

import jax
import jax.numpy as jnp
from jax import lax
from jax.experimental import pallas as pl
from jax.experimental.pallas import tpu as pltpu
from jax.sharding import PartitionSpec as P

HEAD_DIM = 64


norm_eps = 1e-05
rope_base = 160000.0
score_scale = 0.125
masked_low = -1e30


def layer_norm(inputs, gain_vector):
    row_mean = jnp.mean(inputs, axis=-1, keepdims=True)
    centred = inputs - row_mean
    spread = jnp.mean(centred * centred, axis=-1, keepdims=True)
    return centred * lax.rsqrt(spread + norm_eps) * gain_vector


def doc_layout(short_lengths, row_ids, total_rows):
    long_end = total_rows - jnp.sum(short_lengths)
    before = jnp.cumsum(short_lengths) - short_lengths
    bounds = long_end + before
    passed = row_ids[:, None] >= bounds[None, :]
    doc_ids = jnp.sum(passed.astype(jnp.int32), axis=1)
    starts = jnp.max(jnp.where(passed, bounds[None, :], jnp.zeros_like(bounds)[None, :]), axis=1)
    return (doc_ids, row_ids - starts)


def rope_tables(positions):
    steps_half = jnp.arange(HEAD_DIM // 2, dtype=jnp.float32)
    inverse = jnp.exp(steps_half * (-2.0 * math.log(rope_base) / HEAD_DIM))
    angles = positions.astype(jnp.float32)[:, None] * inverse[None, :]
    cosines = jnp.cos(angles)
    sines = jnp.sin(angles)
    return (jnp.concatenate([cosines, cosines], axis=1), jnp.concatenate([sines, sines], axis=1))


def rotate(heads_in, cosines, sines):
    half_dim = heads_in.shape[-1] // 2
    turned = jnp.concatenate([-heads_in[..., half_dim:], heads_in[..., :half_dim]], axis=-1)
    return heads_in * cosines[:, None, :] + turned * sines[:, None, :]


def block_length(row_count, shard_rows):
    shards = row_count // shard_rows
    return shard_rows * math.gcd(shards, max(1, 1024 // shard_rows))


def over_blocks(carry_state, row_count, shard_rows, block_fn):
    block_size = block_length(row_count, shard_rows)

    def block_step(inner_state, block_index):
        return (block_fn(inner_state, block_index * block_size, block_size), None)

    carry_state, _ = lax.scan(
        block_step, carry_state, jnp.arange(row_count // block_size, dtype=jnp.int32)
    )
    return carry_state


def scores_of(queries, key_part):
    return (
        jnp.einsum("qhd,khd->hqk", queries, key_part, preferred_element_type=jnp.float32)
        * score_scale
    )


def block_grads(queries, grad_rows, log_sums, row_dots, key_part, value_part, same_doc):
    scores = scores_of(queries, key_part)
    softmax_part = jnp.where(same_doc, jnp.exp(scores - log_sums[:, :, None]), 0.0)
    grad_probs = jnp.einsum(
        "qhd,khd->hqk", grad_rows, value_part, preferred_element_type=jnp.float32
    )
    dscore = (softmax_part * (grad_probs - row_dots[:, :, None])).astype(jnp.bfloat16)
    return (softmax_part, dscore)


def on_device(
    tokens,
    out_grad,
    short_lengths,
    attn_gain,
    qkv_weight,
    out_weight,
    mlp_gain,
    in_weight,
    down_weight,
):
    half_rows = tokens.shape[0]
    head_count = lax.axis_size("head")
    seq_count = lax.axis_size("seq")
    block_rows = half_rows * head_count
    total_rows = block_rows * seq_count
    local_ids = lax.axis_index("seq") * block_rows + jnp.arange(block_rows, dtype=jnp.int32)
    local_docs, local_pos = doc_layout(short_lengths, local_ids, total_rows)
    cosines, sines = rope_tables(local_pos)
    qkv_full, out_full = (
        lax.all_gather(qkv_weight, "seq", axis=0, tiled=True),
        lax.all_gather(out_weight, "seq", axis=1, tiled=True),
    )
    gain_first, gain_second, in_parts, down_parts = (
        lax.all_gather(attn_gain, ("seq", "head"), axis=0, tiled=True),
        lax.all_gather(mlp_gain, ("seq", "head"), axis=0, tiled=True),
        lax.all_gather(in_weight[None], ("seq", "head"), axis=0, tiled=True),
        lax.all_gather(down_weight[None], ("seq", "head"), axis=0, tiled=True),
    )
    in_parts = in_parts.reshape(seq_count, head_count, in_weight.shape[0], 2, in_weight.shape[2])
    down_parts = down_parts.reshape(
        seq_count, head_count, down_weight.shape[0], down_weight.shape[1]
    )
    heads_here = qkv_full.shape[2] // HEAD_DIM
    inputs = tokens.astype(jnp.float32)
    gain_one = gain_first.astype(jnp.float32)
    normed = layer_norm(inputs, gain_one).astype(jnp.bfloat16)
    normed_block = lax.all_gather(normed, "head", axis=0, tiled=True)
    projected = jnp.einsum(
        "rd,dgc->rgc", normed_block, qkv_full, preferred_element_type=jnp.float32
    )
    queries = rotate(
        projected[:, 0].reshape(block_rows, heads_here, HEAD_DIM), cosines, sines
    ).astype(jnp.bfloat16)
    key_rows = rotate(
        projected[:, 1].reshape(block_rows, heads_here, HEAD_DIM), cosines, sines
    ).astype(jnp.bfloat16)
    value_flat = projected[:, 2].astype(jnp.bfloat16)
    value_rows = value_flat.reshape(block_rows, heads_here, HEAD_DIM)
    key_flat = key_rows.reshape(block_rows, -1)
    query_flat = queries.reshape(block_rows, -1)

    def forward_fold(carry_state, portion):
        piece_keys, piece_values = portion

        def forward_block(inner_state, block_begin, block_size):
            running_max, running_sum, weighted = inner_state
            key_part = lax.dynamic_slice_in_dim(piece_keys, block_begin, block_size, 0).reshape(
                block_size, heads_here, HEAD_DIM
            )
            value_part = lax.dynamic_slice_in_dim(piece_values, block_begin, block_size, 0).reshape(
                block_size, heads_here, HEAD_DIM
            )
            other_docs, _ = doc_layout(
                short_lengths, block_begin + jnp.arange(block_size, dtype=jnp.int32), total_rows
            )
            same_doc = (local_docs[:, None] == other_docs[None, :])[None]
            scores = scores_of(queries, key_part)
            new_max = jnp.maximum(
                running_max, jnp.max(jnp.where(same_doc, scores, masked_low), axis=2)
            )
            factor = jnp.exp(running_max - new_max)
            softmax_part = jnp.where(same_doc, jnp.exp(scores - new_max[:, :, None]), 0.0)
            running_sum = running_sum * factor + jnp.sum(softmax_part, axis=2)
            weighted = weighted * factor.T[:, :, None] + jnp.einsum(
                "hqk,khd->qhd",
                softmax_part.astype(jnp.bfloat16),
                value_part,
                preferred_element_type=jnp.float32,
            )
            return (new_max, running_sum, weighted)

        return over_blocks(carry_state, piece_keys.shape[0], block_rows, forward_block)

    zeros_three = jnp.zeros((block_rows, heads_here, HEAD_DIM), jnp.float32)
    start_state = (
        jnp.full((heads_here, block_rows), masked_low, jnp.float32),
        jnp.zeros((heads_here, block_rows), jnp.float32),
        zeros_three,
    )
    running_max, running_sum, weighted = forward_fold(
        start_state,
        (
            lax.all_gather(key_flat, "seq", axis=0, tiled=True),
            lax.all_gather(value_flat, "seq", axis=0, tiled=True),
        ),
    )
    attended = weighted / running_sum.T[:, :, None]
    log_sums = running_max + jnp.log(running_sum)
    attended_low = attended.reshape(block_rows, -1).astype(jnp.bfloat16)
    branch = jnp.dot(attended_low, out_full, preferred_element_type=jnp.float32)
    branch_rows = lax.psum_scatter(
        branch.astype(jnp.bfloat16), "head", scatter_dimension=0, tiled=True
    ).astype(jnp.float32)
    resid = inputs + branch_rows
    gain_two = gain_second.astype(jnp.float32)
    normed_two = layer_norm(resid, gain_two).astype(jnp.bfloat16)
    normed_split = normed_two.reshape(half_rows, seq_count, -1)
    gate_up = jnp.einsum(
        "rse,shegf->rghf", normed_split, in_parts, preferred_element_type=jnp.float32
    ).reshape(half_rows, 2, -1)

    def activate(gate_part, up_part):
        return jax.nn.gelu(gate_part, approximate=False) * up_part

    hidden, activate_pull = jax.vjp(activate, gate_up[:, 0], gate_up[:, 1])
    hidden_low = hidden.astype(jnp.bfloat16)
    hidden_split = hidden_low.reshape(half_rows, head_count, -1)
    mlp_out = jnp.einsum(
        "rhf,shfe->rse", hidden_split, down_parts, preferred_element_type=jnp.float32
    ).reshape(half_rows, -1)
    mixed = (resid + mlp_out).astype(jnp.bfloat16)
    grad_out = out_grad.astype(jnp.float32)
    grad_split = out_grad.reshape(half_rows, seq_count, -1)
    grad_hidden = jnp.einsum(
        "rse,shfe->rhf", grad_split, down_parts, preferred_element_type=jnp.float32
    ).reshape(half_rows, -1)
    grad_gate, grad_up = activate_pull(grad_hidden)
    grad_gate_up = (
        jnp.stack([grad_gate, grad_up], axis=1)
        .astype(jnp.bfloat16)
        .reshape(half_rows, 2, head_count, -1)
    )
    down_grad = jnp.einsum(
        "rhf,rse->shfe", hidden_split, grad_split, preferred_element_type=jnp.float32
    ).reshape(seq_count * head_count, down_weight.shape[0], down_weight.shape[1])
    in_grad = jnp.einsum(
        "rse,rghf->shegf", normed_split, grad_gate_up, preferred_element_type=jnp.float32
    ).reshape(seq_count * head_count, in_weight.shape[0], 2, in_weight.shape[2])
    grad_normed_two = jnp.einsum(
        "rghf,shegf->rse", grad_gate_up, in_parts, preferred_element_type=jnp.float32
    ).reshape(half_rows, -1)
    _, norm_two_pull = jax.vjp(layer_norm, resid, gain_two)
    grad_resid_norm, gain_two_grad = norm_two_pull(grad_normed_two)
    grad_resid = grad_out + grad_resid_norm
    grad_branch = lax.all_gather(grad_resid.astype(jnp.bfloat16), "head", axis=0, tiled=True)
    out_grad_weight = jnp.einsum(
        "rc,rd->cd", attended_low, grad_branch, preferred_element_type=jnp.float32
    )
    grad_attended = jnp.einsum(
        "rd,cd->rc", grad_branch, out_full, preferred_element_type=jnp.float32
    ).astype(jnp.bfloat16)
    grad_three = grad_attended.reshape(block_rows, heads_here, HEAD_DIM)
    row_dots = jnp.sum(grad_three.astype(jnp.float32) * attended, axis=2).T
    all_sums, all_dots = (
        lax.all_gather(log_sums.T, "seq", axis=0, tiled=True),
        lax.all_gather(row_dots.T, "seq", axis=0, tiled=True),
    )

    def query_terms(query_grad, key_part, value_part, other_docs):
        same_doc = (local_docs[:, None] == other_docs[None, :])[None]
        _, dscore = block_grads(
            queries, grad_three, log_sums, row_dots, key_part, value_part, same_doc
        )
        return (
            query_grad
            + jnp.einsum("hqk,khd->qhd", dscore, key_part, preferred_element_type=jnp.float32)
            * score_scale
        )

    def key_terms(key_grad, value_grad, query_part, grad_part, sums_part, dots_part, other_docs):
        same_doc = (other_docs[:, None] == local_docs[None, :])[None]
        softmax_part, dscore = block_grads(
            query_part, grad_part, sums_part, dots_part, key_rows, value_rows, same_doc
        )
        value_grad = value_grad + jnp.einsum(
            "hqk,qhd->khd",
            softmax_part.astype(jnp.bfloat16),
            grad_part,
            preferred_element_type=jnp.float32,
        )
        key_grad = (
            key_grad
            + jnp.einsum("hqk,qhd->khd", dscore, query_part, preferred_element_type=jnp.float32)
            * score_scale
        )
        return (key_grad, value_grad)

    def piece_rows(source, block_begin, block_size):
        return lax.dynamic_slice_in_dim(source, block_begin, block_size, 0).reshape(
            block_size, heads_here, HEAD_DIM
        )

    def piece_stats(block_begin, block_size):
        sums_part = lax.dynamic_slice_in_dim(all_sums, block_begin, block_size, 0).T
        dots_part = lax.dynamic_slice_in_dim(all_dots, block_begin, block_size, 0).T
        other_docs, _ = doc_layout(
            short_lengths, block_begin + jnp.arange(block_size, dtype=jnp.int32), total_rows
        )
        return (sums_part, dots_part, other_docs)

    def fold_keys(carry_state, portion):
        piece_keys, piece_values = portion

        def key_block(inner_state, block_begin, block_size):
            _, _, other_docs = piece_stats(block_begin, block_size)
            return query_terms(
                inner_state,
                piece_rows(piece_keys, block_begin, block_size),
                piece_rows(piece_values, block_begin, block_size),
                other_docs,
            )

        return over_blocks(carry_state, piece_keys.shape[0], block_rows, key_block)

    query_grad = fold_keys(
        zeros_three,
        (
            lax.all_gather(key_flat, "seq", axis=0, tiled=True),
            lax.all_gather(value_flat, "seq", axis=0, tiled=True),
        ),
    )

    def fold_queries(carry_state, portion):
        piece_queries, piece_grads = portion

        def query_block(inner_state, block_begin, block_size):
            sums_part, dots_part, other_docs = piece_stats(block_begin, block_size)
            return key_terms(
                inner_state[0],
                inner_state[1],
                piece_rows(piece_queries, block_begin, block_size),
                piece_rows(piece_grads, block_begin, block_size),
                sums_part,
                dots_part,
                other_docs,
            )

        return over_blocks(carry_state, piece_queries.shape[0], block_rows, query_block)

    key_grad, value_grad = fold_queries(
        (zeros_three, zeros_three),
        (
            lax.all_gather(query_flat, "seq", axis=0, tiled=True),
            lax.all_gather(grad_attended, "seq", axis=0, tiled=True),
        ),
    )

    def rotate_local(heads_in):
        return rotate(heads_in, cosines, sines)

    _, rotate_pull = jax.vjp(rotate_local, zeros_three)
    query_back = rotate_pull(query_grad)[0]
    key_back = rotate_pull(key_grad)[0]
    grad_qkv = jnp.stack(
        [
            query_back.reshape(block_rows, -1),
            key_back.reshape(block_rows, -1),
            value_grad.reshape(block_rows, -1),
        ],
        axis=1,
    ).astype(jnp.bfloat16)
    qkv_grad = jnp.einsum("rd,rgc->dgc", normed_block, grad_qkv, preferred_element_type=jnp.float32)
    grad_normed_one = jnp.einsum(
        "rgc,dgc->rd", grad_qkv, qkv_full, preferred_element_type=jnp.float32
    )
    grad_normed_rows = lax.psum_scatter(
        grad_normed_one.astype(jnp.bfloat16), "head", scatter_dimension=0, tiled=True
    ).astype(jnp.float32)
    _, norm_one_pull = jax.vjp(layer_norm, inputs, gain_one)
    grad_inputs_norm, gain_one_grad = norm_one_pull(grad_normed_rows)
    tokens_grad = grad_resid + grad_inputs_norm
    qkv_weight_grad, out_weight_grad = (
        lax.psum_scatter(qkv_grad, "seq", scatter_dimension=0, tiled=True),
        lax.psum_scatter(out_grad_weight, "seq", scatter_dimension=1, tiled=True),
    )
    attn_gain_grad, mlp_gain_grad, in_weight_grad, down_weight_grad = (
        lax.psum_scatter(gain_one_grad, ("seq", "head"), scatter_dimension=0, tiled=True),
        lax.psum_scatter(gain_two_grad, ("seq", "head"), scatter_dimension=0, tiled=True),
        lax.psum_scatter(in_grad, ("seq", "head"), scatter_dimension=0, tiled=True),
        lax.psum_scatter(down_grad, ("seq", "head"), scatter_dimension=0, tiled=True),
    )
    return (
        mixed,
        tokens_grad,
        attn_gain_grad,
        qkv_weight_grad,
        out_weight_grad,
        mlp_gain_grad,
        in_weight_grad.reshape(in_weight.shape),
        down_weight_grad.reshape(down_weight.shape),
    )


LOW = jnp.bfloat16
FULL = jnp.float32


def dot(a, b):
    return jnp.dot(a, b, preferred_element_type=FULL)


def dot_nt(a, b):
    return lax.dot_general(a, b, (((1,), (1,)), ((), ())), preferred_element_type=FULL)


def turned(a):
    return a.astype(FULL).T


def centred_norm(rows):
    centred = rows - jnp.mean(rows, axis=-1, keepdims=True)
    scale = lax.rsqrt(jnp.mean(centred * centred, axis=-1, keepdims=True) + norm_eps)
    return centred * scale, scale


def norm_back(unit, scale, weighted):
    mean_w = jnp.mean(weighted, axis=-1, keepdims=True)
    mean_wn = jnp.mean(weighted * unit, axis=-1, keepdims=True)
    return (weighted - mean_w - unit * mean_wn) * scale


def whole_layer(*refs):
    (
        short_ref, gain_a, gain_m, tok_in, gout_in, qkv_in, out_in, in_in, down_in,
        mixed_out, tgrad_out, gains_out, qkvg_out, outg_out, ing_out, downg_out,
        mixed_ref, tgrad_ref, gains_ref, qkvg_ref, outg_ref, ing_ref, downg_ref,
        tok_ref, gout_ref, qkv_ref, wot_ref, in_ref, down_ref, gain_ref, wq_ref, ffp_ref, xh, gt, gn, gb, wh_p, wh, wht, ffw, wo, h1, cs, qa, ka, kt, vt, vr, pt, ot, ol, og, res,
        ms, ms_c, ms_a, ms_y, ms_d, db, dos, dop, dot_t, ds, dqt, dq, d1, d1_c, d1_a, d1_r1, d1_s1, d1_r2, d1_s2, d1_r3,
        dw, dw_c, dw_p, dw_in, gf, gf_k, gf_s, gf_z, gf_y, gf_f, gf_b, gf_c, go, go_k, go_s, go_z, gy, gy_in,
        s_tok, r_tok, s_gain, r_gain, s_wq, r_wq, s_g, r_g, s_ff, r_ff, s_wo, r_wo,
        s_o, r_o, s_ms, r_ms, s_db, r_db, s_do, r_do, s_d1, r_d1, s_dw, r_dw, s_gf, r_gf, s_go, r_go, s_gy, r_gy, s_out, s_in,
    ) = refs
    seq, head = lax.axis_index("seq"), lax.axis_index("head")
    z, x, c, y = seq // 4, (seq // 2) % 2, seq % 2, head
    zh, zb = z // 2, z % 2
    slot = zb * 2 + x
    active = slot < 3
    slot3 = jnp.minimum(slot, 2)
    pending, delivered = [], []

    def flip(value, bit):
        return value if bit == 0 else 1 - value

    def at(z_, x_, c_, y_):
        return (z_ * 4 + x_ * 2 + c_, y_)

    def far_z(k):
        return flip(zh, k // 2) * 2 + flip(zb, k % 2)

    def partner(dim):
        return {
            "x": at(z, 1 - x, c, y),
            "y": at(z, x, c, 1 - y),
            "z": at(far_z(1), x, c, y),
            "c": at(z, x, 1 - c, y),
            "h": at(far_z(2), x, c, y),
        }[dim]

    def push(src, dst, send, recv, device, when=None):
        copy = pltpu.make_async_remote_copy(
            src_ref=src, dst_ref=dst, send_sem=send, recv_sem=recv,
            device_id=device, device_id_type=pl.DeviceIdType.MESH,
        )
        if when is None:
            copy.start()
        else:
            pl.when(when)(copy.start)
        pending.append((when, copy))

    def deliver(k, src, dst):
        copy = pltpu.make_async_copy(src, dst, s_out.at[k])
        copy.start()
        delivered.append(copy)

    def arrive(dst, recv, when=None):
        copy = pltpu.make_async_remote_copy(
            src_ref=dst, dst_ref=dst, send_sem=recv, recv_sem=recv,
            device_id=partner("c"), device_id_type=pl.DeviceIdType.MESH,
        )
        if when is None:
            copy.wait_recv()
        else:
            pl.when(when)(copy.wait_recv)

    loads = (
        (tok_in, tok_ref), (qkv_in, qkv_ref), (in_in, in_ref), (down_in, down_ref), (out_in, wot_ref), (gout_in, gout_ref),
    )
    loads = [pltpu.make_async_copy(a, b, s_in.at[k]) for k, (a, b) in enumerate(loads)]
    barrier = pltpu.get_barrier_semaphore()
    peers = []
    for k in range(1, 32):
        kz, kx, kc, ky = k // 8, (k // 4) % 2, (k // 2) % 2, k % 2
        if kz < 2 or ky == 0:
            peers.append(at(far_z(kz), flip(x, kx), flip(c, kc), flip(y, ky)))
    for peer in peers:
        pl.semaphore_signal(barrier, inc=1, device_id=peer, device_id_type=pl.DeviceIdType.MESH)

    for load in loads:
        load.start()
    gain_ref[...] = jnp.zeros_like(gain_ref)
    gain_ref[0:1, 0 : gain_a.shape[1]] = gain_a[...].astype(FULL)
    gain_ref[1:2, 0 : gain_m.shape[1]] = gain_m[...].astype(FULL)
    for load in loads:
        load.wait()
    for g in range(3):
        for j in range(6):
            lanes = j % 2 * 192 + g * 64
            wq_ref[j // 2, :, lanes : lanes + 64] = qkv_ref[g, :, j * 64 : j * 64 + 64]
    for c_ in range(2):
        lanes = slice(c_ * 288, c_ * 288 + 288)
        for g in range(2):
            ffp_ref[c_, :, g * 288 : g * 288 + 288] = in_ref[:, g, lanes]
        ffp_ref[c_, :, 576:864] = down_ref[:, lanes]
    pl.semaphore_wait(barrier, len(peers))

    xh[zb, c, x, y] = tok_ref[...]
    orders = (("z", "x", "y"), ("z", "y", "x"), ("z", "x", "y"))

    def third(t):
        return pl.ds(t * 256, 256)

    def blocks(ref, opened, lanes, flipped=None, core=None):
        there = {"z": zb, "x": x, "y": y, "c": c if core is None else core}
        if flipped is not None:
            there[flipped] = 1 - there[flipped]
        index = tuple(slice(None) if d in opened else there[d] for d in ("z", "c", "x", "y"))
        return ref.at[index + (slice(None), lanes)]

    for t in range(3):
        view = blocks(xh, (), third(t))
        push(view, view, s_tok.at[0, t], r_tok.at[0, t], partner(orders[t][0]))

    gt[zh, zb, x, c, y] = gain_ref[...]

    def gain_place(k):
        return gt.at[flip(zh, k // 2), flip(zb, k % 2), x, c, y]

    for k in range(1, 4):
        push(gain_place(0), gain_place(0), s_gain.at[k], r_gain.at[k], at(far_z(k), x, c, y))

    def plane(k):
        return flip(x, k // 4), flip(c, k // 2 % 2), flip(y, k % 2)

    def gain_share():
        for k in range(1, 4):
            arrive(gain_place(k), r_gain.at[k])
        for k in range(1, 8):
            x_, c_, y_ = plane(k)
            view = gt.at[:, :, x, c, y]
            push(view, view, s_gain.at[3 + k], r_gain.at[3 + k], at(z, x_, c_, y_))

    def gain_all():
        for k in range(1, 8):
            x_, c_, y_ = plane(k)
            arrive(gt.at[:, :, x_, c_, y_], r_gain.at[3 + k])

    wo_lanes = pl.ds(pl.multiple_of(y * 384, 128), 384)
    wo_others = pl.ds(pl.multiple_of((1 - y) * 384, 128), 384)

    def ff_share(src, z_, x_, k, dim):
        push(src, ffw.at[z_, x_, c], s_ff.at[k], r_ff.at[k], partner(dim))

    def ff_arrive(kz, kx, k):
        arrive(ffw.at[far_z(kz), flip(x, kx), c], r_ff.at[k])

    def ff_cross():
        ff_arrive(0, 1, 0)
        ff_share(ffw.at[z, 1 - x, c], z, 1 - x, 2, "h")
        ff_share(ffw.at[z, 1 - x, c], z, 1 - x, 4, "z")

    def ff_relay():
        for kx in range(2):
            ff_arrive(2, kx, 1 + kx)
            z_, x_ = far_z(2), flip(x, kx)
            ff_share(ffw.at[z_, x_, c], z_, x_, 5 + kx, "z")

    def ff_core(kz):
        z_ = far_z(kz)
        push(ffw.at[z_, :, c], ffw.at[z_, :, c], s_ff.at[8 + kz], r_ff.at[8 + kz], partner("c"))

    def ff_near():
        for kx in range(2):
            ff_arrive(1, kx, 3 + kx)
        ff_core(1)

    def ff_last():
        for kx in range(2):
            ff_arrive(3, kx, 5 + kx)
        ff_core(3)

    def wo_forward_x():
        for k in range(1, 4):
            arrive(wo.at[far_z(k), x, c, :, wo_lanes], r_wo.at[k])
        view = wo.at[:, x, c, :, wo_lanes]
        push(view, view, s_wo.at[4], r_wo.at[4], partner("x"))

    def wo_forward_y():
        arrive(wo.at[:, 1 - x, c, :, wo_lanes], r_wo.at[4])
        view = wo.at[:, :, c, :, wo_lanes]
        push(view, view, s_wo.at[5], r_wo.at[5], partner("y"))

    def wo_forward_core():
        arrive(wo.at[:, :, c, :, wo_others], r_wo.at[5])
        push(wo.at[:, :, c], wo.at[:, :, c], s_wo.at[6], r_wo.at[6], partner("c"))

    ffw[z, x, c] = ffp_ref[x]
    wo[z, x, c, :, wo_lanes] = wot_ref[...]
    def wo_push():
        for k in (2, 3, 1):
            push(wot_ref, wo.at[z, x, c, :, wo_lanes], s_wo.at[k], r_wo.at[k], at(far_z(k), x, c, y))

    own_pair_at = z * 2 + x
    wh_p[c, own_pair_at] = wq_ref[slot3]

    def head_push():
        for k in (7, 5, 6, 4, 3, 2, 1):
            z_, x_ = far_z(k // 2), flip(x, k % 2)
            slot_ = z_ % 2 * 2 + x_
            piece = wq_ref.at[jnp.minimum(slot_, 2)]
            push(piece, wh_p.at[c, own_pair_at], s_wq.at[k], r_wq.at[k], at(z_, x_, c, y), slot_ < 3)

    gb[x, y] = gout_ref[...]
    group = ((0, 1), (1, 0), (1, 1))

    def member(kx, ky):
        return at(z, flip(x, kx), c, flip(y, ky))

    def grad_push():
        for k, (kx, ky) in enumerate(group):
            push(gb.at[x, y], gb.at[x, y], s_g.at[k], r_g.at[k], member(kx, ky))

    def token_step(step):
        for t in range(3):
            arrive(blocks(xh, orders[t][: step - 1], third(t), orders[t][step - 1]), r_tok.at[step - 1, t])
            view = blocks(xh, orders[t][:step], third(t))
            push(view, view, s_tok.at[step, t], r_tok.at[step, t], partner(orders[t][step]))

    events = {
        "fx": lambda: ff_share(ffp_ref.at[1 - x], z, x, 0, "x"),
        "f2": lambda: ff_share(ffp_ref.at[x], z, x, 1, "h"),
        "f1": lambda: ff_share(ffp_ref.at[x], z, x, 3, "z"),
        "fc": ff_cross,
        "fr": ff_relay,
        "c0": lambda: ff_core(0),
        "c1": ff_near,
        "c2": lambda: ff_core(2),
        "c3": ff_last,
        "w": head_push,
        "g": grad_push,
        "oz": wo_push,
        "ox": wo_forward_x,
        "oy": wo_forward_y,
        "oc": wo_forward_core,
    }

    def run(point):
        for name in plan[point]:
            events[name]()

    plan = (
        ("w",),
        ("oz", "fx", "f2", "f1"),
        ("ox", "fc", "g"),
        ("oy", "fr", "c0", "c1"),
        ("c2",),
        (),
        (),
        (),
        ("oc", "c3"),
    )
    run(0)
    token_step(1)
    gain_share()
    run(1)
    token_step(2)
    run(2)
    run(3)

    half_rows = 1024
    lane = lax.broadcasted_iota(jnp.int32, (32, half_rows), 1)
    row = lane % 64 + (lane // 64 % 2) * 64 + (lane // 256 % 2) * 128 + (lane // 128 % 2) * 256 + (lane // 512) * 512
    row = row + zh * half_rows
    feature = lax.broadcasted_iota(jnp.int32, (32, half_rows), 0)
    bound = jnp.int32(2 * half_rows)
    for b in range(short_ref.shape[0]):
        bound = bound - short_ref[b]
    doc = jnp.zeros_like(row)
    start = jnp.zeros_like(row)
    for b in range(short_ref.shape[0]):
        passed = row >= bound
        doc = doc + jnp.where(passed, 1, 0)
        start = jnp.where(passed, bound, start)
        bound = bound + short_ref[b]
    inverse = jnp.exp(feature.astype(FULL) * (-2.0 * math.log(rope_base) / HEAD_DIM))
    angles = (row - start).astype(FULL) * inverse
    cs[0] = jnp.cos(angles)
    cs[1] = jnp.sin(angles)
    same = jnp.where(feature == doc, 1.0, 0.0)
    cs[2] = same
    qa[64:96, :] = ((same - 1.0) * 1e30).astype(LOW)
    qa[96:128, :] = jnp.zeros((32, half_rows), LOW)

    gain_all()
    tiles = gt[...].reshape(256, 128).astype(LOW)
    width = 24
    pick = lax.broadcasted_iota(jnp.int32, (128, 768), 1) % width == lax.broadcasted_iota(jnp.int32, (128, 768), 0)
    spread = dot(tiles, jnp.where(pick, 1.0, 0.0).astype(LOW))
    source = lax.broadcasted_iota(jnp.int32, (256, 768), 0)
    wanted = (lax.broadcasted_iota(jnp.int32, (256, 768), 1) // width) * 8
    gn[0:1, :] = jnp.sum(jnp.where(source == wanted, spread, 0.0), axis=0, keepdims=True)
    gn[1:2, :] = jnp.sum(jnp.where(source == wanted + 1, spread, 0.0), axis=0, keepdims=True)

    for t in range(3):
        arrive(blocks(xh, orders[t][:2], third(t), orders[t][2]), r_tok.at[2, t])

    def rows_of(z_, c_):
        return pl.ds(pl.multiple_of(z_ * 512 + c_ * 256, 256), 256)

    for k in range(1, 8):
        arrive(wh_p.at[c, far_z(k // 2) * 2 + flip(x, k % 2)], r_wq.at[k], active)
    push(wh_p.at[c], wh_p.at[c], s_wq.at[0], r_wq.at[0], partner("c"), active)

    for z_ in range(2):
        rows = rows_of(z_, c)

        @pl.when(active)
        def _(z_=z_, rows=rows):
            unit, _ = centred_norm(xh[z_, c].reshape(256, 768).astype(FULL))
            h1[rows, :] = (unit * gn[0:1, :]).astype(LOW)

        push(h1.at[rows, :], h1.at[rows, :], s_tok.at[3, z_], r_tok.at[3, z_], partner("c"), active)
    arrive(wh_p.at[1 - c], r_wq.at[0], active)

    @pl.when(active)
    def _():
        for c_ in range(2):
            wh[:, c_] = jnp.where(c == 0, wh_p[c_, :, :, 0:192], wh_p[c_, :, :, 192:384])
        wht[...] = turned(wh[...].reshape(768, 192)).astype(LOW)

    for part in range(4):
        z_, c_ = part % 2, flip(c, part // 2)
        cols = rows_of(z_, c_)
        if part >= 2:
            arrive(h1.at[cols, :], r_tok.at[3, z_], active)

        @pl.when(active)
        def _(cols=cols):
            proj = dot_nt(wht[...], h1[cols, :])
            cosine, sine = cs[0, :, cols], cs[1, :, cols]
            q1, q2, k1, k2 = proj[0:32], proj[32:64], proj[64:96], proj[96:128]
            qr = jnp.concatenate([q1 * cosine - q2 * sine, q2 * cosine + q1 * sine], axis=0)
            kr = jnp.concatenate([k1 * cosine - k2 * sine, k2 * cosine + k1 * sine], axis=0)
            qa[0:64, cols] = (qr * score_scale).astype(LOW)
            kt[:, cols] = kr.astype(LOW)
            vt[:, cols] = proj[128:192].astype(LOW)
            pad = jnp.zeros((32, 256), FULL)
            ka[cols, :] = jnp.concatenate([kr, cs[2, :, cols], pad], axis=0).T.astype(LOW)
            vr[cols, :] = proj[128:192].T.astype(LOW)

    run(4)

    for part in range(4):
        cols = pl.ds(part * 256, 256)

        @pl.when(active)
        def _(part=part, cols=cols):
            scores = dot(ka[...], qa[:, cols])
            expo = jnp.exp(scores - jnp.max(scores, axis=0, keepdims=True))
            prob = (expo * (1.0 / jnp.sum(expo, axis=0, keepdims=True))).astype(LOW)
            pt[:, cols] = prob
            result = dot(vt[...], prob)
            ot[part] = result
            ol[part] = result.astype(LOW)

        own_group = jnp.logical_and(zb == part // 2, c == part % 2)
        for k in range(4):
            x_, y_ = k // 2, k % 2
            mine = jnp.logical_and(own_group, jnp.logical_and(x == x_, y == y_))

            @pl.when(jnp.logical_and(active, mine))
            def _(part=part):
                og[y, slot3, c] = ol[part]

            push(
                ol.at[part], og.at[y, slot3, c], s_o.at[part, k], r_o.at[slot3, c, y],
                at(zh * 2 + part // 2, x_, part % 2, y_), jnp.logical_and(active, jnp.logical_not(mine)),
            )
        run(5 + part)

    for slot_ in range(3):
        for c_ in range(2):
            for y_ in range(2):
                mine = jnp.logical_and(slot == slot_, jnp.logical_and(c == c_, y == y_))
                arrive(og.at[y_, slot_, c_], r_o.at[slot_, c_, y_], jnp.logical_not(mine))
    arrive(wo.at[:, :, 1 - c], r_wo.at[6])

    gain_two = gn[1:2, :]
    branch = dot(wo[...].reshape(768, 768), og[...].reshape(768, 256)).T
    resid = xh[zb, c].reshape(256, 768).astype(FULL) + branch
    res[...] = resid.reshape(2, 2, 64, 768)
    unit_two, _ = centred_norm(resid)
    h2 = (unit_two * gain_two).astype(LOW)

    for kz in range(4):
        arrive(ffw.at[far_z(kz), :, 1 - c], r_ff.at[8 + kz])
    for k, (kx, ky) in enumerate(group):
        arrive(gb.at[flip(x, kx), flip(y, ky)], r_g.at[k])
    w_in = ffw[:, :, :, :, 0:576].reshape(768, 576)
    w_down = ffw[:, :, :, :, 576:864].reshape(768, 288)
    gate_up = dot(h2, w_in)
    gate, up = gate_up[:, :288], gate_up[:, 288:]
    grad_out = gb[...].reshape(256, 768)
    grad_hidden = dot(grad_out, w_down)
    chance = 0.5 * (1.0 + lax.erf(gate * (1.0 / math.sqrt(2.0))))
    density = jnp.exp(gate * gate * -0.5) * (1.0 / math.sqrt(2.0 * math.pi))
    curve = gate * chance
    hidden = (curve * up).astype(LOW)
    grad_gate = grad_hidden * up * (chance + gate * density)
    grad_gate_up = jnp.concatenate([grad_gate, grad_hidden * curve], axis=1).astype(LOW)

    columns = (slice(0, 384), slice(384, 768))

    def halve(kind, part):
        ms[kind] = part.astype(LOW).reshape(2, 2, 64, 768)
        push(ms.at[kind, 1 - x, :, :, columns[0]], ms_c.at[kind, 0], s_ms.at[kind, 0, 0], r_ms.at[kind, 0, 0], partner("x"))
        push(ms.at[kind, :, 1 - y, :, columns[1]], ms_c.at[kind, 1], s_ms.at[kind, 1, 0], r_ms.at[kind, 1, 0], partner("y"))

    def quarter(kind):
        for t in range(2):
            arrive(ms_c.at[kind, t], r_ms.at[kind, t, 0])
            mine = ms[kind, x, 1 - y, :, columns[0]] if t == 0 else ms[kind, 1 - x, y, :, columns[1]]
            other = ms_c[kind, t, 1 - y] if t == 0 else ms_c[kind, t, 1 - x]
            ms_a[kind, t] = (mine.astype(FULL) + other.astype(FULL)).astype(LOW)
            push(ms_a.at[kind, t], ms_y.at[kind, t], s_ms.at[kind, t, 1], r_ms.at[kind, t, 1], partner("yx"[t]))

    def quarter_sum(kind):
        sums = []
        for t in range(2):
            arrive(ms_y.at[kind, t], r_ms.at[kind, t, 1])
            other = ms_c[kind, t, y] if t == 0 else ms_c[kind, t, x]
            mine = ms[kind, x, y, :, columns[t]].astype(FULL) + other.astype(FULL)
            sums.append(mine + ms_y[kind, t].astype(FULL))
        return jnp.concatenate(sums, axis=1)

    ms[0] = dot_nt(grad_gate_up, w_in).astype(LOW).reshape(2, 2, 64, 768)
    for k, (kx, ky) in enumerate(group):
        push(ms.at[0, flip(x, kx), flip(y, ky)], ms_d.at[k], s_g.at[3 + k], r_g.at[3 + k], member(kx, ky))
    h2_t = turned(h2).astype(LOW)
    gf[:, :, :, :, 0:576] = dot(h2_t, grad_gate_up).astype(LOW).reshape(4, 2, 2, 48, 576)
    g_t = turned(grad_out).astype(LOW)
    gf[:, :, :, :, 576:864] = dot(g_t, hidden).astype(LOW).reshape(4, 2, 2, 48, 288)

    def sums_of(whole, crossed, low, near, far, wide, last, coming, send, recv):
        def cross():
            for kz in (3, 1, 2, 0):
                z_ = far_z(kz)
                push(whole.at[z_, :, 1 - c], crossed.at[z_], send.at[0, kz], recv.at[0, kz], partner("c"))

        def pair(kz):
            z_ = far_z(kz)
            arrive(crossed.at[z_], recv.at[0, kz])
            return whole[z_, :, c].astype(FULL) + crossed[z_].astype(FULL)

        def to_near(kz):
            z_ = far_z(kz)
            low[z_] = pair(kz).astype(LOW)
            push(low.at[z_], near.at[kz // 2], send.at[1, kz // 2], recv.at[1, kz // 2], partner("z"))

        def to_far():
            value = pair(2)
            arrive(near.at[1], recv.at[1, 1])
            low[far_z(2)] = (value + near[1].astype(FULL)).astype(LOW)
            push(low.at[far_z(2)], far, send.at[2, 0], recv.at[2, 0], partner("h"))

        def finish():
            value = pair(0)
            arrive(near.at[0], recv.at[1, 0])
            arrive(far, recv.at[2, 0])
            wide[...] = value + near[0].astype(FULL) + far[...].astype(FULL)
            last[...] = wide[1 - x].astype(LOW)
            push(last, coming, send.at[3, 0], recv.at[3, 0], partner("x"))

        def result():
            arrive(coming, recv.at[3, 0])
            own, other = wide[x], coming[...].astype(FULL)
            return jnp.where(x == 0, own, other), jnp.where(x == 0, other, own)

        return cross, to_near, to_far, finish, result

    ff_sums = sums_of(gf, gf_k, gf_s, gf_z, gf_y, gf_f, gf_b, gf_c, s_gf, r_gf)

    def out_share():
        for k, (kx, ky) in enumerate(group):
            arrive(db.at[flip(x, kx), flip(y, ky)], r_db.at[k])
        db_t = turned(db[...].reshape(256, 768)).astype(LOW)
        o_part = og[...].reshape(2, 6, 64, 256)
        o_pick = jnp.where(y == 0, o_part[0], o_part[1])
        o_pick = jnp.where(x == 0, o_pick[0:3], o_pick[3:6]).reshape(192, 256)
        go[...] = dot_nt(db_t, o_pick).astype(LOW).reshape(4, 2, 2, 48, 192)
        push(go.at[:, :, 1 - c], go_k, s_go.at[0], r_go.at[0], partner("c"))

    def out_send():
        arrive(go_k, r_go.at[0])
        go_s[...] = (go[:, :, c].astype(FULL) + go_k[...].astype(FULL)).astype(LOW)
        for k in (7, 5, 6, 4, 3, 2, 1):
            z_, x_ = far_z(k // 2), flip(x, k % 2)
            push(go_s.at[z_, x_], go_z.at[k - 1], s_go.at[k], r_go.at[k], at(z_, x_, c, y))

    def out_result():
        sums = [go_s[z, x].astype(FULL), jnp.zeros((48, 192), FULL)]
        for k in range(1, 8):
            arrive(go_z.at[k - 1], r_go.at[k])
            sums[k % 2] = sums[k % 2] + go_z[k - 1].astype(FULL)
        return jnp.where(x == 0, sums[0], sums[1]), jnp.where(x == 0, sums[1], sums[0])

    def mixed_done():
        mixed_ref[...] = (res[x, y] + quarter_sum(1)).astype(LOW)
        deliver(0, mixed_ref, mixed_out)

    later = {
        "md": mixed_done,
        "mx": lambda: quarter(1),
        "n3": lambda: ff_sums[1](3),
        "n1": lambda: ff_sums[1](1),
        "f": ff_sums[2],
        "e": ff_sums[3],
        "O": out_share,
        "S": out_send,
    }
    then = (
        ("n3",),
        ("n1", "mx"),
        (),
        (),
        ("f", "md"),
        (),
        (),
        ("O",),
        ("e", "S"),
        (),
        (),
    )

    def run_later(point):
        for name in then[point]:
            later[name]()

    ff_sums[0]()
    halve(1, dot_nt(hidden, w_down))
    run_later(0)
    own_res = res[x, y]
    unit_two, scale_two = centred_norm(own_res)
    grad_h2 = ms[0, x, y].astype(FULL)
    for k in range(3):
        arrive(ms_d.at[k], r_g.at[3 + k])
        grad_h2 = grad_h2 + ms_d[k].astype(FULL)
    grad_resid = gout_ref[...].astype(FULL) + norm_back(unit_two, scale_two, grad_h2 * gain_two)
    tgrad_ref[...] = grad_resid
    grad_branch = grad_resid.astype(LOW)
    db[x, y] = grad_branch
    grad_o = dot(grad_branch, wo[...].reshape(768, 768)).astype(LOW)
    own_block = zb * 8 + c * 4 + x * 2 + y
    for slot_ in range(3):
        for y_ in range(2):
            lanes = y_ * 384 + slot_ * 128
            dos[y_, slot_] = grad_o[:, lanes : lanes + 128]
            for c_ in range(2):
                mine = jnp.logical_and(jnp.logical_and(slot == slot_, y == y_), c == c_)

                @pl.when(mine)
                def _(slot_=slot_, y_=y_):
                    dop[zb, c, x, y] = dos[y_, slot_]

                push(
                    dos.at[y_, slot_], dop.at[zb, c, x, y], s_do.at[slot_ * 4 + y_ * 2 + c_], r_do.at[own_block],
                    at(zh * 2 + slot_ // 2, slot_ % 2, c_, y_), jnp.logical_not(mine),
                )
    run_later(1)
    for k, (kx, ky) in enumerate(group):
        push(db.at[x, y], db.at[x, y], s_db.at[k], r_db.at[k], member(kx, ky))
    run_later(2)

    for b in range(16):
        z_, c_, x_, y_ = b // 8, (b // 4) % 2, (b // 2) % 2, b % 2
        arrive(dop.at[z_, c_, x_, y_], r_do.at[b], jnp.logical_and(active, own_block != b))

    @pl.when(active)
    def _():
        pair = turned(dop[...].reshape(1024, 128))
        dot_t[...] = jnp.where(c == 0, pair[0:64], pair[64:128]).astype(LOW)

    for part in range(4):
        cols = pl.ds(part * 256, 256)

        @pl.when(active)
        def _(part=part, cols=cols):
            grad_t = dot_t[:, cols]
            delta = jnp.sum(grad_t.astype(FULL) * ot[part], axis=0, keepdims=True)
            grad_p = dot(vr[...], grad_t)
            score_grad = (pt[:, cols].astype(FULL) * (grad_p - delta)).astype(LOW)
            ds[:, cols] = score_grad
            back = dot(kt[...], score_grad) * score_scale
            cosine, sine = cs[0, :, cols], cs[1, :, cols]
            b1, b2 = back[0:32], back[32:64]
            dqt[0:64, cols] = jnp.concatenate([b1 * cosine + b2 * sine, b2 * cosine - b1 * sine], axis=0).astype(LOW)

        run_later(3 + part)

    @pl.when(active)
    def _():
        for part in range(4):
            cols = pl.ds(part * 256, 256)
            back = dot_nt(qa[0:64, :], ds[cols, :])
            cosine, sine = cs[0, :, cols], cs[1, :, cols]
            b1, b2 = back[0:32], back[32:64]
            dqt[64:128, cols] = jnp.concatenate([b1 * cosine + b2 * sine, b2 * cosine - b1 * sine], axis=0).astype(LOW)
            dqt[128:192, cols] = dot_nt(dot_t[...], pt[cols, :]).astype(LOW)
            dq[cols, :] = turned(dqt[:, cols]).astype(LOW)

    for part in range(4):
        z_, c_ = part % 2, flip(c, 1 - part // 2)

        @pl.when(active)
        def _(z_=z_, c_=c_):
            rows = pl.ds(pl.multiple_of(z_ * 512 + c_ * 256, 256), 256)
            d1[z_, c_] = dot_nt(dq[rows, :], wh[...].reshape(768, 192)).astype(LOW).reshape(2, 2, 64, 768)

        if part < 2:
            push(d1.at[z_, c_], d1_c.at[z_], s_d1.at[0, z_], r_d1.at[0, z_], partner("c"), active)
    run_later(7)

    @pl.when(active)
    def _():
        grad = dot(dqt[...], h1[...])
        grad = grad.T.astype(LOW).reshape(8, 2, 48, 192)
        dw[0], dw[1] = grad[:, 0], grad[:, 1]

    push(dw.at[1 - c], dw_c, s_dw.at[0], r_dw.at[6], partner("c"), active)

    @pl.when(jnp.logical_not(active))
    def _():
        d1_a[...] = jnp.zeros_like(d1_a)

    for z_ in range(2):
        arrive(d1_c.at[z_], r_d1.at[0, z_], active)

        @pl.when(active)
        def _(z_=z_):
            d1_a[z_] = (d1[z_, c].astype(FULL) + d1_c[z_].astype(FULL)).astype(LOW)

    back_orders = (("x", "y", "z"), ("y", "z", "x"), ("z", "x", "y"))

    spots = {"z": zb, "x": x, "y": y}

    def halves(t, first, second):
        a, b, _ = back_orders[t]
        place = {a: flip(spots[a], first), b: flip(spots[b], second)}
        return d1_a.at[tuple(place.get(d, slice(None)) for d in ("z", "x", "y")) + (slice(None), third(t))]

    for h in (0, 1):
        for t in range(3):
            push(
                halves(t, 1, 1 - h), d1_r1.at[t, h], s_d1.at[1, t * 2 + h], r_d1.at[1, t * 2 + h],
                partner(back_orders[t][0]),
            )

    def first_sum(t, h):
        arrive(d1_r1.at[t, h], r_d1.at[1, t * 2 + h])
        d1_s1[t, h] = (halves(t, 0, 1 - h)[...].astype(FULL) + d1_r1[t, h].astype(FULL)).astype(LOW)

    own_pair = zh * 3 + slot3
    arrive(dw_c, r_dw.at[6], active)

    @pl.when(active)
    def _():
        own, other = dw[c], dw_c[...]
        dw_p[:, :, 0:192] = jnp.where(c == 0, own, other)
        dw_p[:, :, 192:384] = jnp.where(c == 0, other, own)
        dw_in[own_pair] = dw_p[z * 2 + x]

    def pair_push(ks):
        for k in ks:
            z_, x_ = far_z(k // 2), flip(x, k % 2)
            push(dw_p.at[z_ * 2 + x_], dw_in.at[own_pair], s_dw.at[k], r_dw.at[own_pair], at(z_, x_, c, y), active)

    run_later(10)
    pair_push((7, 5, 6, 4))
    for t in range(3):
        first_sum(t, 0)
        last = spots[back_orders[t][2]]
        for h in (0, 1):
            push(
                d1_s1.at[t, 0, flip(last, 1 - h)], d1_r2.at[t, h], s_d1.at[2, t * 2 + h], r_d1.at[2, t * 2 + h],
                partner(back_orders[t][1]),
            )
    pair_push((3, 2, 1))
    for t in range(3):
        first_sum(t, 1)
    run_later(8)
    for t in range(3):
        last = spots[back_orders[t][2]]
        arrive(d1_r2.at[t, 0], r_d1.at[2, t * 2])
        d1_s2[t] = (d1_s1[t, 1, 1 - last].astype(FULL) + d1_r2[t, 0].astype(FULL)).astype(LOW)
        push(d1_s2.at[t], d1_r3.at[t], s_d1.at[3, t], r_d1.at[3, t], partner(back_orders[t][2]))
    run_later(9)
    mlp_terms = jnp.zeros((48, 1), FULL)
    for x_, grads in enumerate(ff_sums[4]()):
        lanes = slice(x_ * 288, x_ * 288 + 288)
        for g in range(2):
            ing_ref[:, g, lanes] = grads[:, g * 288 : g * 288 + 288]
        downg_ref[:, lanes] = grads[:, 576:864]
        terms = grads[:, 0:576] * ffp_ref[x_, :, 0:576].astype(FULL)
        mlp_terms = mlp_terms + jnp.sum(terms, axis=1, keepdims=True)
    deliver(1, ing_ref, ing_out)
    deliver(2, downg_ref, downg_out)
    for h_ in range(2):
        for slot_ in range(3):
            mine = jnp.logical_and(zh == h_, slot == slot_)
            arrive(dw_in.at[h_ * 3 + slot_], r_dw.at[h_ * 3 + slot_], jnp.logical_not(mine))
    attn_terms = jnp.zeros((48, 1), FULL)
    for slot_ in range(3):
        both = dw_in[slot_].astype(FULL) + dw_in[3 + slot_].astype(FULL)
        for c_ in range(2):
            for g in range(3):
                lanes, j = c_ * 192 + g * 64, slot_ * 2 + c_
                qkvg_ref[g, :, j * 64 : j * 64 + 64] = both[:, lanes : lanes + 64]
        attn_terms = attn_terms + jnp.sum(both * wq_ref[slot_].astype(FULL), axis=1, keepdims=True)
    deliver(3, qkvg_ref, qkvg_out)
    lane = lax.broadcasted_iota(jnp.int32, (48, 128), 1)
    gy[...] = jnp.where(lane == 0, attn_terms, jnp.where(lane == 1, mlp_terms, 0.0))
    push(gy, gy_in, s_gy.at[0], r_gy.at[0], partner("y"))
    for x_, grads in enumerate(out_result()):
        outg_ref[:, x_ * 192 : x_ * 192 + 192] = grads
    deliver(4, outg_ref, outg_out)

    unit_one, scale_one = centred_norm(tok_ref[...].astype(FULL))
    for t in range(3):
        arrive(d1_r2.at[t, 1], r_d1.at[2, t * 2 + 1])
        arrive(d1_r3.at[t], r_d1.at[3, t])
        total = d1_s1[t, 1, spots[back_orders[t][2]]].astype(FULL) + d1_r2[t, 1].astype(FULL)
        res[0, 0, :, third(t)] = total + d1_r3[t].astype(FULL)
    tgrad_ref[...] = tgrad_ref[...] + norm_back(unit_one, scale_one, res[0, 0] * gn[0:1, :])
    deliver(5, tgrad_ref, tgrad_out)
    arrive(gy_in, r_gy.at[0])
    sums = (gy[...] + gy_in[...]).T
    count = gain_a.shape[1]
    sums = jnp.where(y == 0, sums[0:2, :count], sums[0:2, count : 2 * count])
    gains_ref[...] = jnp.zeros_like(gains_ref)
    gains_ref[0:2, 0:count] = sums / gain_ref[0:2, 0:count]
    deliver(6, gains_ref, gains_out)
    for copy in delivered:
        copy.wait()
    for when, copy in pending:
        if when is None:
            copy.wait_send()
        else:
            pl.when(when)(copy.wait_send)


def hand_on(*refs):
    sources, results, held, sems = refs[:7], refs[7:15], refs[15:21], refs[21]
    count = results[6].shape[1]
    results[6][...] = sources[6][0:1, :count]
    results[7][...] = sources[6][1:2, :count]
    inward = [pltpu.make_async_copy(a, b, sems.at[0, k]) for k, (a, b) in enumerate(zip(sources[:6], held))]
    outward = [pltpu.make_async_copy(a, b, sems.at[1, k]) for k, (a, b) in enumerate(zip(held, results[:6]))]
    for copy in inward:
        copy.start()
    for first, second in zip(inward, outward):
        first.wait()
        second.start()
    for copy in outward:
        copy.wait()


def on_device_fast(tokens, out_grad, short_lengths, attn_gain, qkv_weight, out_weight, mlp_gain, in_weight, down_weight):
    rows, width = tokens.shape
    depth = qkv_weight.shape[0]
    heads_here = qkv_weight.shape[2] // HEAD_DIM
    count = attn_gain.shape[0]
    ff = in_weight.shape[2] // 2 * 3
    feats = out_weight.shape[0]

    def vm(shape, kind=LOW):
        return pltpu.VMEM(shape, kind)

    def sem(*shape):
        return pltpu.SemaphoreType.DMA(shape)

    finals = [
        ((rows, width), LOW), ((rows, width), FULL), ((8, 128), FULL), ((3, depth, 384), FULL),
        ((depth, feats), FULL), ((depth, 2, 576), FULL), ((depth, 576), FULL),
    ]
    scratch = [vm(*shape) for shape in finals] + [
        vm((rows, width)), vm((rows, width)), vm((3, depth, 384)), vm((depth, feats)), vm((depth, 2, 576)), vm((depth, 576)),
        vm((8, 128), FULL), vm((heads_here // 2, depth, 384)), vm((2, depth, ff)),
        vm((2, 2, 2, 2, 64, 768)), vm((2, 2, 2, 2, 2, 8, 128), FULL), vm((8, 768), FULL), vm((2, 2, 64, 768)),
        vm((2, 8, 48, 384)), vm((8, 2, 48, 192)), vm((192, 768)), vm((4, 2, 2, 48, 864)), vm((4, 2, 2, 48, 768)), vm((1024, 768)),
        vm((3, 32, 1024), FULL), vm((128, 1024)), vm((1024, 128)), vm((64, 1024)), vm((64, 1024)), vm((1024, 64)),
        vm((1024, 1024)), vm((4, 64, 256), FULL), vm((4, 64, 256)), vm((2, 3, 2, 64, 256)), vm((2, 2, 64, 768), FULL),
        vm((2, 2, 2, 64, 768)), vm((2, 2, 2, 64, 384)), vm((2, 2, 64, 384)), vm((2, 2, 64, 384)), vm((3, 64, 768)), vm((2, 2, 64, 768)),
        vm((2, 3, 64, 128)), vm((2, 2, 2, 2, 64, 128)), vm((64, 1024)), vm((1024, 1024)), vm((192, 1024)),
        vm((1024, 192)), vm((2, 2, 2, 2, 64, 768)), vm((2, 2, 2, 64, 768)), vm((2, 2, 2, 64, 768)),
        vm((3, 2, 2, 64, 256)), vm((3, 2, 2, 64, 256)), vm((3, 2, 64, 256)), vm((3, 64, 256)), vm((3, 64, 256)),
        vm((2, 8, 48, 192)), vm((8, 48, 192)), vm((8, 48, 384)), vm((6, 48, 384)),
        vm((4, 2, 2, 48, 864)), vm((4, 2, 48, 864)), vm((4, 2, 48, 864)), vm((2, 2, 48, 864)), vm((2, 48, 864)),
        vm((2, 48, 864), FULL), vm((48, 864)), vm((48, 864)),
        vm((4, 2, 2, 48, 192)), vm((4, 2, 48, 192)), vm((4, 2, 48, 192)), vm((7, 48, 192)),
        vm((48, 128), FULL), vm((48, 128), FULL),
        sem(4, 3), sem(4, 3), sem(11), sem(11), sem(8), sem(8), sem(6), sem(6), sem(12), sem(12), sem(7), sem(7),
        sem(4, 4), sem(3, 2, 2), sem(2, 2, 2), sem(2, 2, 2), sem(3), sem(3), sem(12), sem(16), sem(4, 6), sem(4, 6),
        sem(8), sem(7), sem(4, 4), sem(4, 4), sem(8), sem(8), sem(1), sem(1), sem(7), sem(6),
    ]
    vmem = pl.BlockSpec(memory_space=pltpu.VMEM)
    anywhere = pl.BlockSpec(memory_space=pl.ANY)
    shapes = [jax.ShapeDtypeStruct(*shape) for shape in finals]
    mixed, tokens_grad, gains, qkv_grad, out_grads, in_grad, down_grad = pl.pallas_call(
        whole_layer,
        out_shape=shapes,
        in_specs=[pl.BlockSpec(memory_space=pltpu.SMEM)] + [vmem] * 2 + [anywhere] * 6,
        out_specs=[anywhere] * 7,
        scratch_shapes=scratch,
        compiler_params=pltpu.CompilerParams(collective_id=0, has_side_effects=True, vmem_limit_bytes=60 << 20),
    )(
        short_lengths, attn_gain[None], mlp_gain[None], tokens, out_grad,
        qkv_weight.transpose(1, 0, 2), out_weight.T, in_weight, down_weight.T,
    )
    grads = (mixed, tokens_grad, qkv_grad, out_grads, in_grad, down_grad)
    count = attn_gain.shape[0]
    mixed, tokens_grad, qkv_grad, out_grads, in_grad, down_grad, attn_gain_grad, mlp_gain_grad = pl.pallas_call(
        hand_on,
        out_shape=[jax.ShapeDtypeStruct(a.shape, a.dtype) for a in grads] + [jax.ShapeDtypeStruct((1, count), FULL)] * 2,
        in_specs=[anywhere] * 6 + [vmem],
        out_specs=[anywhere] * 6 + [vmem] * 2,
        scratch_shapes=[vm(a.shape, a.dtype) for a in grads] + [sem(2, 6)],
    )(*grads, gains)
    return (
        mixed, tokens_grad, attn_gain_grad[0], qkv_grad.transpose(1, 0, 2), out_grads.T, mlp_gain_grad[0],
        in_grad, down_grad.T,
    )


def solution(mesh):
    placed = (
        P(("seq", "head"), None),
        P(("seq", "head"), None),
        P(),
        P(("seq", "head")),
        P("seq", None, "head"),
        P("head", "seq"),
        P(("seq", "head")),
        P("seq", None, "head"),
        P("head", "seq"),
    )
    fits = mesh.shape["seq"] == 16 and mesh.shape["head"] == 2
    return jax.shard_map(
        on_device_fast if fits else on_device,
        mesh=mesh,
        in_specs=placed,
        out_specs=(
            P(("seq", "head"), None),
            P(("seq", "head"), None),
            P(("seq", "head")),
            P("seq", None, "head"),
            P("head", "seq"),
            P(("seq", "head")),
            P("seq", None, "head"),
            P("head", "seq"),
        ),
        check_vma=False,
    )
```

```python
import math

import jax
import jax.numpy as jnp
from jax import lax
from jax.experimental import pallas as pl
from jax.experimental.pallas import tpu as pltpu
from jax.sharding import PartitionSpec as P

HEAD_DIM = 64


norm_eps = 1e-05
rope_base = 160000.0
score_scale = 0.125
masked_low = -1e30


def layer_norm(inputs, gain_vector):
    row_mean = jnp.mean(inputs, axis=-1, keepdims=True)
    centred = inputs - row_mean
    spread = jnp.mean(centred * centred, axis=-1, keepdims=True)
    return centred * lax.rsqrt(spread + norm_eps) * gain_vector


def doc_layout(short_lengths, row_ids, total_rows):
    long_end = total_rows - jnp.sum(short_lengths)
    before = jnp.cumsum(short_lengths) - short_lengths
    bounds = long_end + before
    passed = row_ids[:, None] >= bounds[None, :]
    doc_ids = jnp.sum(passed.astype(jnp.int32), axis=1)
    starts = jnp.max(jnp.where(passed, bounds[None, :], jnp.zeros_like(bounds)[None, :]), axis=1)
    return (doc_ids, row_ids - starts)


def rope_tables(positions):
    steps_half = jnp.arange(HEAD_DIM // 2, dtype=jnp.float32)
    inverse = jnp.exp(steps_half * (-2.0 * math.log(rope_base) / HEAD_DIM))
    angles = positions.astype(jnp.float32)[:, None] * inverse[None, :]
    cosines = jnp.cos(angles)
    sines = jnp.sin(angles)
    return (jnp.concatenate([cosines, cosines], axis=1), jnp.concatenate([sines, sines], axis=1))


def rotate(heads_in, cosines, sines):
    half_dim = heads_in.shape[-1] // 2
    turned = jnp.concatenate([-heads_in[..., half_dim:], heads_in[..., :half_dim]], axis=-1)
    return heads_in * cosines[:, None, :] + turned * sines[:, None, :]


def block_length(row_count, shard_rows):
    shards = row_count // shard_rows
    return shard_rows * math.gcd(shards, max(1, 1024 // shard_rows))


def over_blocks(carry_state, row_count, shard_rows, block_fn):
    block_size = block_length(row_count, shard_rows)

    def block_step(inner_state, block_index):
        return (block_fn(inner_state, block_index * block_size, block_size), None)

    carry_state, _ = lax.scan(
        block_step, carry_state, jnp.arange(row_count // block_size, dtype=jnp.int32)
    )
    return carry_state


def scores_of(queries, key_part):
    return (
        jnp.einsum("qhd,khd->hqk", queries, key_part, preferred_element_type=jnp.float32)
        * score_scale
    )


def block_grads(queries, grad_rows, log_sums, row_dots, key_part, value_part, same_doc):
    scores = scores_of(queries, key_part)
    softmax_part = jnp.where(same_doc, jnp.exp(scores - log_sums[:, :, None]), 0.0)
    grad_probs = jnp.einsum(
        "qhd,khd->hqk", grad_rows, value_part, preferred_element_type=jnp.float32
    )
    dscore = (softmax_part * (grad_probs - row_dots[:, :, None])).astype(jnp.bfloat16)
    return (softmax_part, dscore)


def on_device(
    tokens,
    out_grad,
    short_lengths,
    attn_gain,
    qkv_weight,
    out_weight,
    mlp_gain,
    in_weight,
    down_weight,
):
    half_rows = tokens.shape[0]
    head_count = lax.axis_size("head")
    seq_count = lax.axis_size("seq")
    block_rows = half_rows * head_count
    total_rows = block_rows * seq_count
    local_ids = lax.axis_index("seq") * block_rows + jnp.arange(block_rows, dtype=jnp.int32)
    local_docs, local_pos = doc_layout(short_lengths, local_ids, total_rows)
    cosines, sines = rope_tables(local_pos)
    qkv_full, out_full = (
        lax.all_gather(qkv_weight, "seq", axis=0, tiled=True),
        lax.all_gather(out_weight, "seq", axis=1, tiled=True),
    )
    gain_first, gain_second, in_parts, down_parts = (
        lax.all_gather(attn_gain, ("seq", "head"), axis=0, tiled=True),
        lax.all_gather(mlp_gain, ("seq", "head"), axis=0, tiled=True),
        lax.all_gather(in_weight[None], ("seq", "head"), axis=0, tiled=True),
        lax.all_gather(down_weight[None], ("seq", "head"), axis=0, tiled=True),
    )
    in_parts = in_parts.reshape(seq_count, head_count, in_weight.shape[0], 2, in_weight.shape[2])
    down_parts = down_parts.reshape(
        seq_count, head_count, down_weight.shape[0], down_weight.shape[1]
    )
    heads_here = qkv_full.shape[2] // HEAD_DIM
    inputs = tokens.astype(jnp.float32)
    gain_one = gain_first.astype(jnp.float32)
    normed = layer_norm(inputs, gain_one).astype(jnp.bfloat16)
    normed_block = lax.all_gather(normed, "head", axis=0, tiled=True)
    projected = jnp.einsum(
        "rd,dgc->rgc", normed_block, qkv_full, preferred_element_type=jnp.float32
    )
    queries = rotate(
        projected[:, 0].reshape(block_rows, heads_here, HEAD_DIM), cosines, sines
    ).astype(jnp.bfloat16)
    key_rows = rotate(
        projected[:, 1].reshape(block_rows, heads_here, HEAD_DIM), cosines, sines
    ).astype(jnp.bfloat16)
    value_flat = projected[:, 2].astype(jnp.bfloat16)
    value_rows = value_flat.reshape(block_rows, heads_here, HEAD_DIM)
    key_flat = key_rows.reshape(block_rows, -1)
    query_flat = queries.reshape(block_rows, -1)

    def forward_fold(carry_state, portion):
        piece_keys, piece_values = portion

        def forward_block(inner_state, block_begin, block_size):
            running_max, running_sum, weighted = inner_state
            key_part = lax.dynamic_slice_in_dim(piece_keys, block_begin, block_size, 0).reshape(
                block_size, heads_here, HEAD_DIM
            )
            value_part = lax.dynamic_slice_in_dim(piece_values, block_begin, block_size, 0).reshape(
                block_size, heads_here, HEAD_DIM
            )
            other_docs, _ = doc_layout(
                short_lengths, block_begin + jnp.arange(block_size, dtype=jnp.int32), total_rows
            )
            same_doc = (local_docs[:, None] == other_docs[None, :])[None]
            scores = scores_of(queries, key_part)
            new_max = jnp.maximum(
                running_max, jnp.max(jnp.where(same_doc, scores, masked_low), axis=2)
            )
            factor = jnp.exp(running_max - new_max)
            softmax_part = jnp.where(same_doc, jnp.exp(scores - new_max[:, :, None]), 0.0)
            running_sum = running_sum * factor + jnp.sum(softmax_part, axis=2)
            weighted = weighted * factor.T[:, :, None] + jnp.einsum(
                "hqk,khd->qhd",
                softmax_part.astype(jnp.bfloat16),
                value_part,
                preferred_element_type=jnp.float32,
            )
            return (new_max, running_sum, weighted)

        return over_blocks(carry_state, piece_keys.shape[0], block_rows, forward_block)

    zeros_three = jnp.zeros((block_rows, heads_here, HEAD_DIM), jnp.float32)
    start_state = (
        jnp.full((heads_here, block_rows), masked_low, jnp.float32),
        jnp.zeros((heads_here, block_rows), jnp.float32),
        zeros_three,
    )
    running_max, running_sum, weighted = forward_fold(
        start_state,
        (
            lax.all_gather(key_flat, "seq", axis=0, tiled=True),
            lax.all_gather(value_flat, "seq", axis=0, tiled=True),
        ),
    )
    attended = weighted / running_sum.T[:, :, None]
    log_sums = running_max + jnp.log(running_sum)
    attended_low = attended.reshape(block_rows, -1).astype(jnp.bfloat16)
    branch = jnp.dot(attended_low, out_full, preferred_element_type=jnp.float32)
    branch_rows = lax.psum_scatter(
        branch.astype(jnp.bfloat16), "head", scatter_dimension=0, tiled=True
    ).astype(jnp.float32)
    resid = inputs + branch_rows
    gain_two = gain_second.astype(jnp.float32)
    normed_two = layer_norm(resid, gain_two).astype(jnp.bfloat16)
    normed_split = normed_two.reshape(half_rows, seq_count, -1)
    gate_up = jnp.einsum(
        "rse,shegf->rghf", normed_split, in_parts, preferred_element_type=jnp.float32
    ).reshape(half_rows, 2, -1)

    def activate(gate_part, up_part):
        return jax.nn.gelu(gate_part, approximate=False) * up_part

    hidden, activate_pull = jax.vjp(activate, gate_up[:, 0], gate_up[:, 1])
    hidden_low = hidden.astype(jnp.bfloat16)
    hidden_split = hidden_low.reshape(half_rows, head_count, -1)
    mlp_out = jnp.einsum(
        "rhf,shfe->rse", hidden_split, down_parts, preferred_element_type=jnp.float32
    ).reshape(half_rows, -1)
    mixed = (resid + mlp_out).astype(jnp.bfloat16)
    grad_out = out_grad.astype(jnp.float32)
    grad_split = out_grad.reshape(half_rows, seq_count, -1)
    grad_hidden = jnp.einsum(
        "rse,shfe->rhf", grad_split, down_parts, preferred_element_type=jnp.float32
    ).reshape(half_rows, -1)
    grad_gate, grad_up = activate_pull(grad_hidden)
    grad_gate_up = (
        jnp.stack([grad_gate, grad_up], axis=1)
        .astype(jnp.bfloat16)
        .reshape(half_rows, 2, head_count, -1)
    )
    down_grad = jnp.einsum(
        "rhf,rse->shfe", hidden_split, grad_split, preferred_element_type=jnp.float32
    ).reshape(seq_count * head_count, down_weight.shape[0], down_weight.shape[1])
    in_grad = jnp.einsum(
        "rse,rghf->shegf", normed_split, grad_gate_up, preferred_element_type=jnp.float32
    ).reshape(seq_count * head_count, in_weight.shape[0], 2, in_weight.shape[2])
    grad_normed_two = jnp.einsum(
        "rghf,shegf->rse", grad_gate_up, in_parts, preferred_element_type=jnp.float32
    ).reshape(half_rows, -1)
    _, norm_two_pull = jax.vjp(layer_norm, resid, gain_two)
    grad_resid_norm, gain_two_grad = norm_two_pull(grad_normed_two)
    grad_resid = grad_out + grad_resid_norm
    grad_branch = lax.all_gather(grad_resid.astype(jnp.bfloat16), "head", axis=0, tiled=True)
    out_grad_weight = jnp.einsum(
        "rc,rd->cd", attended_low, grad_branch, preferred_element_type=jnp.float32
    )
    grad_attended = jnp.einsum(
        "rd,cd->rc", grad_branch, out_full, preferred_element_type=jnp.float32
    ).astype(jnp.bfloat16)
    grad_three = grad_attended.reshape(block_rows, heads_here, HEAD_DIM)
    row_dots = jnp.sum(grad_three.astype(jnp.float32) * attended, axis=2).T
    all_sums, all_dots = (
        lax.all_gather(log_sums.T, "seq", axis=0, tiled=True),
        lax.all_gather(row_dots.T, "seq", axis=0, tiled=True),
    )

    def query_terms(query_grad, key_part, value_part, other_docs):
        same_doc = (local_docs[:, None] == other_docs[None, :])[None]
        _, dscore = block_grads(
            queries, grad_three, log_sums, row_dots, key_part, value_part, same_doc
        )
        return (
            query_grad
            + jnp.einsum("hqk,khd->qhd", dscore, key_part, preferred_element_type=jnp.float32)
            * score_scale
        )

    def key_terms(key_grad, value_grad, query_part, grad_part, sums_part, dots_part, other_docs):
        same_doc = (other_docs[:, None] == local_docs[None, :])[None]
        softmax_part, dscore = block_grads(
            query_part, grad_part, sums_part, dots_part, key_rows, value_rows, same_doc
        )
        value_grad = value_grad + jnp.einsum(
            "hqk,qhd->khd",
            softmax_part.astype(jnp.bfloat16),
            grad_part,
            preferred_element_type=jnp.float32,
        )
        key_grad = (
            key_grad
            + jnp.einsum("hqk,qhd->khd", dscore, query_part, preferred_element_type=jnp.float32)
            * score_scale
        )
        return (key_grad, value_grad)

    def piece_rows(source, block_begin, block_size):
        return lax.dynamic_slice_in_dim(source, block_begin, block_size, 0).reshape(
            block_size, heads_here, HEAD_DIM
        )

    def piece_stats(block_begin, block_size):
        sums_part = lax.dynamic_slice_in_dim(all_sums, block_begin, block_size, 0).T
        dots_part = lax.dynamic_slice_in_dim(all_dots, block_begin, block_size, 0).T
        other_docs, _ = doc_layout(
            short_lengths, block_begin + jnp.arange(block_size, dtype=jnp.int32), total_rows
        )
        return (sums_part, dots_part, other_docs)

    def fold_keys(carry_state, portion):
        piece_keys, piece_values = portion

        def key_block(inner_state, block_begin, block_size):
            _, _, other_docs = piece_stats(block_begin, block_size)
            return query_terms(
                inner_state,
                piece_rows(piece_keys, block_begin, block_size),
                piece_rows(piece_values, block_begin, block_size),
                other_docs,
            )

        return over_blocks(carry_state, piece_keys.shape[0], block_rows, key_block)

    query_grad = fold_keys(
        zeros_three,
        (
            lax.all_gather(key_flat, "seq", axis=0, tiled=True),
            lax.all_gather(value_flat, "seq", axis=0, tiled=True),
        ),
    )

    def fold_queries(carry_state, portion):
        piece_queries, piece_grads = portion

        def query_block(inner_state, block_begin, block_size):
            sums_part, dots_part, other_docs = piece_stats(block_begin, block_size)
            return key_terms(
                inner_state[0],
                inner_state[1],
                piece_rows(piece_queries, block_begin, block_size),
                piece_rows(piece_grads, block_begin, block_size),
                sums_part,
                dots_part,
                other_docs,
            )

        return over_blocks(carry_state, piece_queries.shape[0], block_rows, query_block)

    key_grad, value_grad = fold_queries(
        (zeros_three, zeros_three),
        (
            lax.all_gather(query_flat, "seq", axis=0, tiled=True),
            lax.all_gather(grad_attended, "seq", axis=0, tiled=True),
        ),
    )

    def rotate_local(heads_in):
        return rotate(heads_in, cosines, sines)

    _, rotate_pull = jax.vjp(rotate_local, zeros_three)
    query_back = rotate_pull(query_grad)[0]
    key_back = rotate_pull(key_grad)[0]
    grad_qkv = jnp.stack(
        [
            query_back.reshape(block_rows, -1),
            key_back.reshape(block_rows, -1),
            value_grad.reshape(block_rows, -1),
        ],
        axis=1,
    ).astype(jnp.bfloat16)
    qkv_grad = jnp.einsum("rd,rgc->dgc", normed_block, grad_qkv, preferred_element_type=jnp.float32)
    grad_normed_one = jnp.einsum(
        "rgc,dgc->rd", grad_qkv, qkv_full, preferred_element_type=jnp.float32
    )
    grad_normed_rows = lax.psum_scatter(
        grad_normed_one.astype(jnp.bfloat16), "head", scatter_dimension=0, tiled=True
    ).astype(jnp.float32)
    _, norm_one_pull = jax.vjp(layer_norm, inputs, gain_one)
    grad_inputs_norm, gain_one_grad = norm_one_pull(grad_normed_rows)
    tokens_grad = grad_resid + grad_inputs_norm
    qkv_weight_grad, out_weight_grad = (
        lax.psum_scatter(qkv_grad, "seq", scatter_dimension=0, tiled=True),
        lax.psum_scatter(out_grad_weight, "seq", scatter_dimension=1, tiled=True),
    )
    attn_gain_grad, mlp_gain_grad, in_weight_grad, down_weight_grad = (
        lax.psum_scatter(gain_one_grad, ("seq", "head"), scatter_dimension=0, tiled=True),
        lax.psum_scatter(gain_two_grad, ("seq", "head"), scatter_dimension=0, tiled=True),
        lax.psum_scatter(in_grad, ("seq", "head"), scatter_dimension=0, tiled=True),
        lax.psum_scatter(down_grad, ("seq", "head"), scatter_dimension=0, tiled=True),
    )
    return (
        mixed,
        tokens_grad,
        attn_gain_grad,
        qkv_weight_grad,
        out_weight_grad,
        mlp_gain_grad,
        in_weight_grad.reshape(in_weight.shape),
        down_weight_grad.reshape(down_weight.shape),
    )


LOW = jnp.bfloat16
FULL = jnp.float32


def dot(a, b):
    return jnp.dot(a, b, preferred_element_type=FULL)


def dot_nt(a, b):
    return lax.dot_general(a, b, (((1,), (1,)), ((), ())), preferred_element_type=FULL)


def turned(a):
    return a.astype(FULL).T


def centred_norm(rows):
    centred = rows - jnp.mean(rows, axis=-1, keepdims=True)
    scale = lax.rsqrt(jnp.mean(centred * centred, axis=-1, keepdims=True) + norm_eps)
    return centred * scale, scale


def norm_back(unit, scale, weighted):
    mean_w = jnp.mean(weighted, axis=-1, keepdims=True)
    mean_wn = jnp.mean(weighted * unit, axis=-1, keepdims=True)
    return (weighted - mean_w - unit * mean_wn) * scale


def whole_layer(*refs):
    (
        short_ref, gain_a, gain_m, tok_in, gout_in, qkv_in, out_in, in_in, down_in,
        mixed_out, tgrad_out, gains_out, qkvg_out, outg_out, ing_out, downg_out,
        mixed_ref, tgrad_ref, gains_ref, qkvg_ref, outg_ref, ing_ref, downg_ref,
        tok_ref, gout_ref, qkv_ref, wot_ref, in_ref, down_ref, gain_ref, wq_ref, ffp_ref, xh, gt, gn, gb, wh_p, wh, wht, ffw, wo, h1, cs, qa, ka, kt, vt, vr, pt, ot, ol, og, res,
        ms, ms_c, ms_a, ms_y, ms_d, db, dos, dop, dot_t, ds, dqt, dq, d1, d1_c, d1_a, d1_r1, d1_s1, d1_r2, d1_s2, d1_r3,
        dw, dw_c, dw_p, dw_in, gf, gf_k, gf_s, gf_z, gf_y, gf_f, gf_b, gf_c, go, go_k, go_s, go_z, gy, gy_in,
        s_tok, r_tok, s_gain, r_gain, s_wq, r_wq, s_g, r_g, s_ff, r_ff, s_wo, r_wo,
        s_o, r_o, s_ms, r_ms, s_db, r_db, s_do, r_do, s_d1, r_d1, s_dw, r_dw, s_gf, r_gf, s_go, r_go, s_gy, r_gy, s_out, s_in,
    ) = refs
    seq, head = lax.axis_index("seq"), lax.axis_index("head")
    z, x, c, y = seq // 4, (seq // 2) % 2, seq % 2, head
    zh, zb = z // 2, z % 2
    slot = zb * 2 + x
    active = slot < 3
    slot3 = jnp.minimum(slot, 2)
    pending, delivered = [], []

    def flip(value, bit):
        return value if bit == 0 else 1 - value

    def at(z_, x_, c_, y_):
        return (z_ * 4 + x_ * 2 + c_, y_)

    def far_z(k):
        return flip(zh, k // 2) * 2 + flip(zb, k % 2)

    def partner(dim):
        return {
            "x": at(z, 1 - x, c, y),
            "y": at(z, x, c, 1 - y),
            "z": at(far_z(1), x, c, y),
            "c": at(z, x, 1 - c, y),
            "h": at(far_z(2), x, c, y),
        }[dim]

    def push(src, dst, send, recv, device, when=None):
        copy = pltpu.make_async_remote_copy(
            src_ref=src, dst_ref=dst, send_sem=send, recv_sem=recv,
            device_id=device, device_id_type=pl.DeviceIdType.MESH,
        )
        if when is None:
            copy.start()
        else:
            pl.when(when)(copy.start)
        pending.append((when, copy))

    def deliver(k, src, dst):
        copy = pltpu.make_async_copy(src, dst, s_out.at[k])
        copy.start()
        delivered.append(copy)

    def arrive(dst, recv, when=None):
        copy = pltpu.make_async_remote_copy(
            src_ref=dst, dst_ref=dst, send_sem=recv, recv_sem=recv,
            device_id=partner("c"), device_id_type=pl.DeviceIdType.MESH,
        )
        if when is None:
            copy.wait_recv()
        else:
            pl.when(when)(copy.wait_recv)

    loads = (
        (tok_in, tok_ref), (qkv_in, qkv_ref), (in_in, in_ref), (down_in, down_ref), (out_in, wot_ref), (gout_in, gout_ref),
    )
    loads = [pltpu.make_async_copy(a, b, s_in.at[k]) for k, (a, b) in enumerate(loads)]
    barrier = pltpu.get_barrier_semaphore()
    peers = []
    for k in range(1, 32):
        kz, kx, kc, ky = k // 8, (k // 4) % 2, (k // 2) % 2, k % 2
        if kz < 2 or ky == 0:
            peers.append(at(far_z(kz), flip(x, kx), flip(c, kc), flip(y, ky)))
    for peer in peers:
        pl.semaphore_signal(barrier, inc=1, device_id=peer, device_id_type=pl.DeviceIdType.MESH)

    for load in loads:
        load.start()
    gain_ref[...] = jnp.zeros_like(gain_ref)
    gain_ref[0:1, 0 : gain_a.shape[1]] = gain_a[...].astype(FULL)
    gain_ref[1:2, 0 : gain_m.shape[1]] = gain_m[...].astype(FULL)
    for load in loads:
        load.wait()
    for g in range(3):
        for j in range(6):
            lanes = j % 2 * 192 + g * 64
            wq_ref[j // 2, :, lanes : lanes + 64] = qkv_ref[g, :, j * 64 : j * 64 + 64]
    for c_ in range(2):
        lanes = slice(c_ * 288, c_ * 288 + 288)
        for g in range(2):
            ffp_ref[c_, :, g * 288 : g * 288 + 288] = in_ref[:, g, lanes]
        ffp_ref[c_, :, 576:864] = down_ref[:, lanes]
    pl.semaphore_wait(barrier, len(peers))

    xh[zb, c, x, y] = tok_ref[...]
    orders = (("z", "x", "y"), ("z", "y", "x"), ("z", "x", "y"))

    def third(t):
        return pl.ds(t * 256, 256)

    def blocks(ref, opened, lanes, flipped=None, core=None):
        there = {"z": zb, "x": x, "y": y, "c": c if core is None else core}
        if flipped is not None:
            there[flipped] = 1 - there[flipped]
        index = tuple(slice(None) if d in opened else there[d] for d in ("z", "c", "x", "y"))
        return ref.at[index + (slice(None), lanes)]

    for t in range(3):
        view = blocks(xh, (), third(t))
        push(view, view, s_tok.at[0, t], r_tok.at[0, t], partner(orders[t][0]))

    gt[zh, zb, x, c, y] = gain_ref[...]

    def gain_place(k):
        return gt.at[flip(zh, k // 2), flip(zb, k % 2), x, c, y]

    for k in range(1, 4):
        push(gain_place(0), gain_place(0), s_gain.at[k], r_gain.at[k], at(far_z(k), x, c, y))

    def plane(k):
        return flip(x, k // 4), flip(c, k // 2 % 2), flip(y, k % 2)

    def gain_share():
        for k in range(1, 4):
            arrive(gain_place(k), r_gain.at[k])
        for k in range(1, 8):
            x_, c_, y_ = plane(k)
            view = gt.at[:, :, x, c, y]
            push(view, view, s_gain.at[3 + k], r_gain.at[3 + k], at(z, x_, c_, y_))

    def gain_all():
        for k in range(1, 8):
            x_, c_, y_ = plane(k)
            arrive(gt.at[:, :, x_, c_, y_], r_gain.at[3 + k])

    wo_lanes = pl.ds(pl.multiple_of(y * 384, 128), 384)
    wo_others = pl.ds(pl.multiple_of((1 - y) * 384, 128), 384)

    def ff_share(src, z_, x_, k, dim):
        push(src, ffw.at[z_, x_, c], s_ff.at[k], r_ff.at[k], partner(dim))

    def ff_arrive(kz, kx, k):
        arrive(ffw.at[far_z(kz), flip(x, kx), c], r_ff.at[k])

    def ff_cross():
        ff_arrive(0, 1, 0)
        ff_share(ffw.at[z, 1 - x, c], z, 1 - x, 2, "h")
        ff_share(ffw.at[z, 1 - x, c], z, 1 - x, 4, "z")

    def ff_relay():
        for kx in range(2):
            ff_arrive(2, kx, 1 + kx)
            z_, x_ = far_z(2), flip(x, kx)
            ff_share(ffw.at[z_, x_, c], z_, x_, 5 + kx, "z")

    def ff_core(kz):
        z_ = far_z(kz)
        push(ffw.at[z_, :, c], ffw.at[z_, :, c], s_ff.at[8 + kz], r_ff.at[8 + kz], partner("c"))

    def ff_near():
        for kx in range(2):
            ff_arrive(1, kx, 3 + kx)
        ff_core(1)

    def ff_last():
        for kx in range(2):
            ff_arrive(3, kx, 5 + kx)
        ff_core(3)

    def wo_forward_x():
        for k in range(1, 4):
            arrive(wo.at[far_z(k), x, c, :, wo_lanes], r_wo.at[k])
        view = wo.at[:, x, c, :, wo_lanes]
        push(view, view, s_wo.at[4], r_wo.at[4], partner("x"))

    def wo_forward_y():
        arrive(wo.at[:, 1 - x, c, :, wo_lanes], r_wo.at[4])
        view = wo.at[:, :, c, :, wo_lanes]
        push(view, view, s_wo.at[5], r_wo.at[5], partner("y"))

    def wo_forward_core():
        arrive(wo.at[:, :, c, :, wo_others], r_wo.at[5])
        push(wo.at[:, :, c], wo.at[:, :, c], s_wo.at[6], r_wo.at[6], partner("c"))

    ffw[z, x, c] = ffp_ref[x]
    wo[z, x, c, :, wo_lanes] = wot_ref[...]
    def wo_push():
        for k in (2, 3, 1):
            push(wot_ref, wo.at[z, x, c, :, wo_lanes], s_wo.at[k], r_wo.at[k], at(far_z(k), x, c, y))

    own_pair_at = z * 2 + x
    wh_p[c, own_pair_at] = wq_ref[slot3]

    def head_push():
        for k in (7, 5, 6, 4, 3, 2, 1):
            z_, x_ = far_z(k // 2), flip(x, k % 2)
            slot_ = z_ % 2 * 2 + x_
            piece = wq_ref.at[jnp.minimum(slot_, 2)]
            push(piece, wh_p.at[c, own_pair_at], s_wq.at[k], r_wq.at[k], at(z_, x_, c, y), slot_ < 3)

    gb[x, y] = gout_ref[...]
    group = ((0, 1), (1, 0), (1, 1))

    def member(kx, ky):
        return at(z, flip(x, kx), c, flip(y, ky))

    def grad_push():
        for k, (kx, ky) in enumerate(group):
            push(gb.at[x, y], gb.at[x, y], s_g.at[k], r_g.at[k], member(kx, ky))

    def token_step(step):
        for t in range(3):
            arrive(blocks(xh, orders[t][: step - 1], third(t), orders[t][step - 1]), r_tok.at[step - 1, t])
            view = blocks(xh, orders[t][:step], third(t))
            push(view, view, s_tok.at[step, t], r_tok.at[step, t], partner(orders[t][step]))

    events = {
        "fx": lambda: ff_share(ffp_ref.at[1 - x], z, x, 0, "x"),
        "f2": lambda: ff_share(ffp_ref.at[x], z, x, 1, "h"),
        "f1": lambda: ff_share(ffp_ref.at[x], z, x, 3, "z"),
        "fc": ff_cross,
        "fr": ff_relay,
        "c0": lambda: ff_core(0),
        "c1": ff_near,
        "c2": lambda: ff_core(2),
        "c3": ff_last,
        "w": head_push,
        "g": grad_push,
        "oz": wo_push,
        "ox": wo_forward_x,
        "oy": wo_forward_y,
        "oc": wo_forward_core,
    }

    def run(point):
        for name in plan[point]:
            events[name]()

    plan = (
        ("w",),
        ("oz", "fx", "f2", "f1"),
        ("ox", "fc", "g"),
        ("oy", "fr", "c0", "c1"),
        ("c2",),
        (),
        (),
        (),
        ("oc", "c3"),
    )
    run(0)
    token_step(1)
    gain_share()
    run(1)
    token_step(2)
    run(2)
    run(3)

    half_rows = 1024
    lane = lax.broadcasted_iota(jnp.int32, (32, half_rows), 1)
    row = lane % 64 + (lane // 64 % 2) * 64 + (lane // 256 % 2) * 128 + (lane // 128 % 2) * 256 + (lane // 512) * 512
    row = row + zh * half_rows
    feature = lax.broadcasted_iota(jnp.int32, (32, half_rows), 0)
    bound = jnp.int32(2 * half_rows)
    for b in range(short_ref.shape[0]):
        bound = bound - short_ref[b]
    doc = jnp.zeros_like(row)
    start = jnp.zeros_like(row)
    for b in range(short_ref.shape[0]):
        passed = row >= bound
        doc = doc + jnp.where(passed, 1, 0)
        start = jnp.where(passed, bound, start)
        bound = bound + short_ref[b]
    inverse = jnp.exp(feature.astype(FULL) * (-2.0 * math.log(rope_base) / HEAD_DIM))
    angles = (row - start).astype(FULL) * inverse
    cs[0] = jnp.cos(angles)
    cs[1] = jnp.sin(angles)
    same = jnp.where(feature == doc, 1.0, 0.0)
    cs[2] = same
    qa[64:96, :] = ((same - 1.0) * 1e30).astype(LOW)
    qa[96:128, :] = jnp.zeros((32, half_rows), LOW)

    gain_all()
    tiles = gt[...].reshape(256, 128).astype(LOW)
    width = 24
    pick = lax.broadcasted_iota(jnp.int32, (128, 768), 1) % width == lax.broadcasted_iota(jnp.int32, (128, 768), 0)
    spread = dot(tiles, jnp.where(pick, 1.0, 0.0).astype(LOW))
    source = lax.broadcasted_iota(jnp.int32, (256, 768), 0)
    wanted = (lax.broadcasted_iota(jnp.int32, (256, 768), 1) // width) * 8
    gn[0:1, :] = jnp.sum(jnp.where(source == wanted, spread, 0.0), axis=0, keepdims=True)
    gn[1:2, :] = jnp.sum(jnp.where(source == wanted + 1, spread, 0.0), axis=0, keepdims=True)

    for t in range(3):
        arrive(blocks(xh, orders[t][:2], third(t), orders[t][2]), r_tok.at[2, t])

    def rows_of(z_, c_):
        return pl.ds(pl.multiple_of(z_ * 512 + c_ * 256, 256), 256)

    for k in range(1, 8):
        arrive(wh_p.at[c, far_z(k // 2) * 2 + flip(x, k % 2)], r_wq.at[k], active)
    push(wh_p.at[c], wh_p.at[c], s_wq.at[0], r_wq.at[0], partner("c"), active)

    for z_ in range(2):
        rows = rows_of(z_, c)

        @pl.when(active)
        def _(z_=z_, rows=rows):
            unit, _ = centred_norm(xh[z_, c].reshape(256, 768).astype(FULL))
            h1[rows, :] = (unit * gn[0:1, :]).astype(LOW)

        push(h1.at[rows, :], h1.at[rows, :], s_tok.at[3, z_], r_tok.at[3, z_], partner("c"), active)
    arrive(wh_p.at[1 - c], r_wq.at[0], active)

    @pl.when(active)
    def _():
        for c_ in range(2):
            wh[:, c_] = jnp.where(c == 0, wh_p[c_, :, :, 0:192], wh_p[c_, :, :, 192:384])
        wht[...] = turned(wh[...].reshape(768, 192)).astype(LOW)

    for part in range(4):
        z_, c_ = part % 2, flip(c, part // 2)
        cols = rows_of(z_, c_)
        if part >= 2:
            arrive(h1.at[cols, :], r_tok.at[3, z_], active)

        @pl.when(active)
        def _(cols=cols):
            proj = dot_nt(wht[...], h1[cols, :])
            cosine, sine = cs[0, :, cols], cs[1, :, cols]
            q1, q2, k1, k2 = proj[0:32], proj[32:64], proj[64:96], proj[96:128]
            qr = jnp.concatenate([q1 * cosine - q2 * sine, q2 * cosine + q1 * sine], axis=0)
            kr = jnp.concatenate([k1 * cosine - k2 * sine, k2 * cosine + k1 * sine], axis=0)
            qa[0:64, cols] = (qr * score_scale).astype(LOW)
            kt[:, cols] = kr.astype(LOW)
            vt[:, cols] = proj[128:192].astype(LOW)
            pad = jnp.zeros((32, 256), FULL)
            ka[cols, :] = jnp.concatenate([kr, cs[2, :, cols], pad], axis=0).T.astype(LOW)
            vr[cols, :] = proj[128:192].T.astype(LOW)

    run(4)

    for part in range(4):
        cols = pl.ds(part * 256, 256)

        @pl.when(active)
        def _(part=part, cols=cols):
            scores = dot(ka[...], qa[:, cols])
            expo = jnp.exp(scores - jnp.max(scores, axis=0, keepdims=True))
            prob = (expo * (1.0 / jnp.sum(expo, axis=0, keepdims=True))).astype(LOW)
            pt[:, cols] = prob
            result = dot(vt[...], prob)
            ot[part] = result
            ol[part] = result.astype(LOW)

        own_group = jnp.logical_and(zb == part // 2, c == part % 2)
        for k in range(4):
            x_, y_ = k // 2, k % 2
            mine = jnp.logical_and(own_group, jnp.logical_and(x == x_, y == y_))

            @pl.when(jnp.logical_and(active, mine))
            def _(part=part):
                og[y, slot3, c] = ol[part]

            push(
                ol.at[part], og.at[y, slot3, c], s_o.at[part, k], r_o.at[slot3, c, y],
                at(zh * 2 + part // 2, x_, part % 2, y_), jnp.logical_and(active, jnp.logical_not(mine)),
            )
        run(5 + part)

    for slot_ in range(3):
        for c_ in range(2):
            for y_ in range(2):
                mine = jnp.logical_and(slot == slot_, jnp.logical_and(c == c_, y == y_))
                arrive(og.at[y_, slot_, c_], r_o.at[slot_, c_, y_], jnp.logical_not(mine))
    arrive(wo.at[:, :, 1 - c], r_wo.at[6])

    gain_two = gn[1:2, :]
    branch = dot(wo[...].reshape(768, 768), og[...].reshape(768, 256)).T
    resid = xh[zb, c].reshape(256, 768).astype(FULL) + branch
    res[...] = resid.reshape(2, 2, 64, 768)
    unit_two, _ = centred_norm(resid)
    h2 = (unit_two * gain_two).astype(LOW)

    for kz in range(4):
        arrive(ffw.at[far_z(kz), :, 1 - c], r_ff.at[8 + kz])
    for k, (kx, ky) in enumerate(group):
        arrive(gb.at[flip(x, kx), flip(y, ky)], r_g.at[k])
    w_in = ffw[:, :, :, :, 0:576].reshape(768, 576)
    w_down = ffw[:, :, :, :, 576:864].reshape(768, 288)
    gate_up = dot(h2, w_in)
    gate, up = gate_up[:, :288], gate_up[:, 288:]
    grad_out = gb[...].reshape(256, 768)
    grad_hidden = dot(grad_out, w_down)
    chance = 0.5 * (1.0 + lax.erf(gate * (1.0 / math.sqrt(2.0))))
    density = jnp.exp(gate * gate * -0.5) * (1.0 / math.sqrt(2.0 * math.pi))
    curve = gate * chance
    hidden = (curve * up).astype(LOW)
    grad_gate = grad_hidden * up * (chance + gate * density)
    grad_gate_up = jnp.concatenate([grad_gate, grad_hidden * curve], axis=1).astype(LOW)

    columns = (slice(0, 384), slice(384, 768))

    def halve(kind, part):
        ms[kind] = part.astype(LOW).reshape(2, 2, 64, 768)
        push(ms.at[kind, 1 - x, :, :, columns[0]], ms_c.at[kind, 0], s_ms.at[kind, 0, 0], r_ms.at[kind, 0, 0], partner("x"))
        push(ms.at[kind, :, 1 - y, :, columns[1]], ms_c.at[kind, 1], s_ms.at[kind, 1, 0], r_ms.at[kind, 1, 0], partner("y"))

    def quarter(kind):
        for t in range(2):
            arrive(ms_c.at[kind, t], r_ms.at[kind, t, 0])
            mine = ms[kind, x, 1 - y, :, columns[0]] if t == 0 else ms[kind, 1 - x, y, :, columns[1]]
            other = ms_c[kind, t, 1 - y] if t == 0 else ms_c[kind, t, 1 - x]
            ms_a[kind, t] = (mine.astype(FULL) + other.astype(FULL)).astype(LOW)
            push(ms_a.at[kind, t], ms_y.at[kind, t], s_ms.at[kind, t, 1], r_ms.at[kind, t, 1], partner("yx"[t]))

    def quarter_sum(kind):
        sums = []
        for t in range(2):
            arrive(ms_y.at[kind, t], r_ms.at[kind, t, 1])
            other = ms_c[kind, t, y] if t == 0 else ms_c[kind, t, x]
            mine = ms[kind, x, y, :, columns[t]].astype(FULL) + other.astype(FULL)
            sums.append(mine + ms_y[kind, t].astype(FULL))
        return jnp.concatenate(sums, axis=1)

    ms[0] = dot_nt(grad_gate_up, w_in).astype(LOW).reshape(2, 2, 64, 768)
    for k, (kx, ky) in enumerate(group):
        push(ms.at[0, flip(x, kx), flip(y, ky)], ms_d.at[k], s_g.at[3 + k], r_g.at[3 + k], member(kx, ky))
    h2_t = turned(h2).astype(LOW)
    gf[:, :, :, :, 0:576] = dot(h2_t, grad_gate_up).astype(LOW).reshape(4, 2, 2, 48, 576)
    g_t = turned(grad_out).astype(LOW)
    gf[:, :, :, :, 576:864] = dot(g_t, hidden).astype(LOW).reshape(4, 2, 2, 48, 288)

    def sums_of(whole, crossed, low, near, far, wide, last, coming, send, recv):
        def cross():
            for kz in (3, 1, 2, 0):
                z_ = far_z(kz)
                push(whole.at[z_, :, 1 - c], crossed.at[z_], send.at[0, kz], recv.at[0, kz], partner("c"))

        def pair(kz):
            z_ = far_z(kz)
            arrive(crossed.at[z_], recv.at[0, kz])
            return whole[z_, :, c].astype(FULL) + crossed[z_].astype(FULL)

        def to_near(kz):
            z_ = far_z(kz)
            low[z_] = pair(kz).astype(LOW)
            push(low.at[z_], near.at[kz // 2], send.at[1, kz // 2], recv.at[1, kz // 2], partner("z"))

        def to_far():
            value = pair(2)
            arrive(near.at[1], recv.at[1, 1])
            low[far_z(2)] = (value + near[1].astype(FULL)).astype(LOW)
            push(low.at[far_z(2)], far, send.at[2, 0], recv.at[2, 0], partner("h"))

        def finish():
            value = pair(0)
            arrive(near.at[0], recv.at[1, 0])
            arrive(far, recv.at[2, 0])
            wide[...] = value + near[0].astype(FULL) + far[...].astype(FULL)
            last[...] = wide[1 - x].astype(LOW)
            push(last, coming, send.at[3, 0], recv.at[3, 0], partner("x"))

        def result():
            arrive(coming, recv.at[3, 0])
            own, other = wide[x], coming[...].astype(FULL)
            return jnp.where(x == 0, own, other), jnp.where(x == 0, other, own)

        return cross, to_near, to_far, finish, result

    ff_sums = sums_of(gf, gf_k, gf_s, gf_z, gf_y, gf_f, gf_b, gf_c, s_gf, r_gf)

    def out_share():
        for k, (kx, ky) in enumerate(group):
            arrive(db.at[flip(x, kx), flip(y, ky)], r_db.at[k])
        db_t = turned(db[...].reshape(256, 768)).astype(LOW)
        o_part = og[...].reshape(2, 6, 64, 256)
        o_pick = jnp.where(y == 0, o_part[0], o_part[1])
        o_pick = jnp.where(x == 0, o_pick[0:3], o_pick[3:6]).reshape(192, 256)
        go[...] = dot_nt(db_t, o_pick).astype(LOW).reshape(4, 2, 2, 48, 192)
        push(go.at[:, :, 1 - c], go_k, s_go.at[0], r_go.at[0], partner("c"))

    def out_send():
        arrive(go_k, r_go.at[0])
        go_s[...] = (go[:, :, c].astype(FULL) + go_k[...].astype(FULL)).astype(LOW)
        for k in (7, 5, 6, 4, 3, 2, 1):
            z_, x_ = far_z(k // 2), flip(x, k % 2)
            push(go_s.at[z_, x_], go_z.at[k - 1], s_go.at[k], r_go.at[k], at(z_, x_, c, y))

    def out_result():
        sums = [go_s[z, x].astype(FULL), jnp.zeros((48, 192), FULL)]
        for k in range(1, 8):
            arrive(go_z.at[k - 1], r_go.at[k])
            sums[k % 2] = sums[k % 2] + go_z[k - 1].astype(FULL)
        return jnp.where(x == 0, sums[0], sums[1]), jnp.where(x == 0, sums[1], sums[0])

    def mixed_done():
        mixed_ref[...] = (res[x, y] + quarter_sum(1)).astype(LOW)
        deliver(0, mixed_ref, mixed_out)

    later = {
        "md": mixed_done,
        "mx": lambda: quarter(1),
        "n3": lambda: ff_sums[1](3),
        "n1": lambda: ff_sums[1](1),
        "f": ff_sums[2],
        "e": ff_sums[3],
        "O": out_share,
        "S": out_send,
    }
    then = (
        ("n3",),
        ("n1", "mx"),
        (),
        (),
        ("f", "md"),
        (),
        (),
        ("O",),
        ("e", "S"),
        (),
        (),
    )

    def run_later(point):
        for name in then[point]:
            later[name]()

    ff_sums[0]()
    halve(1, dot_nt(hidden, w_down))
    run_later(0)
    own_res = res[x, y]
    unit_two, scale_two = centred_norm(own_res)
    grad_h2 = ms[0, x, y].astype(FULL)
    for k in range(3):
        arrive(ms_d.at[k], r_g.at[3 + k])
        grad_h2 = grad_h2 + ms_d[k].astype(FULL)
    grad_resid = gout_ref[...].astype(FULL) + norm_back(unit_two, scale_two, grad_h2 * gain_two)
    tgrad_ref[...] = grad_resid
    grad_branch = grad_resid.astype(LOW)
    db[x, y] = grad_branch
    grad_o = dot(grad_branch, wo[...].reshape(768, 768)).astype(LOW)
    own_block = zb * 8 + c * 4 + x * 2 + y
    for slot_ in range(3):
        for y_ in range(2):
            lanes = y_ * 384 + slot_ * 128
            dos[y_, slot_] = grad_o[:, lanes : lanes + 128]
    for turn in (1, 2, 0):
        slot_ = (slot3 + turn) % 3
        for k in (3, 2, 1, 0):
            y_, c_ = flip(y, k // 2), flip(c, k % 2)
            mine = jnp.logical_and(slot == slot_, k == 0)

            @pl.when(mine)
            def _(slot_=slot_, y_=y_):
                dop[zb, c, x, y] = dos[y_, slot_]

            push(
                dos.at[y_, slot_], dop.at[zb, c, x, y], s_do.at[turn * 4 + k], r_do.at[own_block],
                at(zh * 2 + slot_ // 2, slot_ % 2, c_, y_), jnp.logical_not(mine),
            )
    run_later(1)
    for k, (kx, ky) in enumerate(group):
        push(db.at[x, y], db.at[x, y], s_db.at[k], r_db.at[k], member(kx, ky))
    run_later(2)

    for b in range(16):
        z_, c_, x_, y_ = b // 8, (b // 4) % 2, (b // 2) % 2, b % 2
        arrive(dop.at[z_, c_, x_, y_], r_do.at[b], jnp.logical_and(active, own_block != b))

    @pl.when(active)
    def _():
        pair = turned(dop[...].reshape(1024, 128))
        dot_t[...] = jnp.where(c == 0, pair[0:64], pair[64:128]).astype(LOW)

    for part in range(4):
        cols = pl.ds(part * 256, 256)

        @pl.when(active)
        def _(part=part, cols=cols):
            grad_t = dot_t[:, cols]
            delta = jnp.sum(grad_t.astype(FULL) * ot[part], axis=0, keepdims=True)
            grad_p = dot(vr[...], grad_t)
            score_grad = (pt[:, cols].astype(FULL) * (grad_p - delta)).astype(LOW)
            ds[:, cols] = score_grad
            back = dot(kt[...], score_grad) * score_scale
            cosine, sine = cs[0, :, cols], cs[1, :, cols]
            b1, b2 = back[0:32], back[32:64]
            dqt[0:64, cols] = jnp.concatenate([b1 * cosine + b2 * sine, b2 * cosine - b1 * sine], axis=0).astype(LOW)

        run_later(3 + part)

    @pl.when(active)
    def _():
        for part in range(4):
            cols = pl.ds(part * 256, 256)
            back = dot_nt(qa[0:64, :], ds[cols, :])
            cosine, sine = cs[0, :, cols], cs[1, :, cols]
            b1, b2 = back[0:32], back[32:64]
            dqt[64:128, cols] = jnp.concatenate([b1 * cosine + b2 * sine, b2 * cosine - b1 * sine], axis=0).astype(LOW)
            dqt[128:192, cols] = dot_nt(dot_t[...], pt[cols, :]).astype(LOW)
            dq[cols, :] = turned(dqt[:, cols]).astype(LOW)

    for part in range(4):
        z_, c_ = part % 2, flip(c, 1 - part // 2)

        @pl.when(active)
        def _(z_=z_, c_=c_):
            rows = pl.ds(pl.multiple_of(z_ * 512 + c_ * 256, 256), 256)
            d1[z_, c_] = dot_nt(dq[rows, :], wh[...].reshape(768, 192)).astype(LOW).reshape(2, 2, 64, 768)

        if part < 2:
            push(d1.at[z_, c_], d1_c.at[z_], s_d1.at[0, z_], r_d1.at[0, z_], partner("c"), active)
    run_later(7)

    @pl.when(active)
    def _():
        grad = dot(dqt[...], h1[...])
        grad = grad.T.astype(LOW).reshape(8, 2, 48, 192)
        dw[0], dw[1] = grad[:, 0], grad[:, 1]

    push(dw.at[1 - c], dw_c, s_dw.at[0], r_dw.at[6], partner("c"), active)

    @pl.when(jnp.logical_not(active))
    def _():
        d1_a[...] = jnp.zeros_like(d1_a)

    for z_ in range(2):
        arrive(d1_c.at[z_], r_d1.at[0, z_], active)

        @pl.when(active)
        def _(z_=z_):
            d1_a[z_] = (d1[z_, c].astype(FULL) + d1_c[z_].astype(FULL)).astype(LOW)

    back_orders = (("x", "y", "z"), ("y", "z", "x"), ("z", "x", "y"))

    spots = {"z": zb, "x": x, "y": y}

    def halves(t, first, second):
        a, b, _ = back_orders[t]
        place = {a: flip(spots[a], first), b: flip(spots[b], second)}
        return d1_a.at[tuple(place.get(d, slice(None)) for d in ("z", "x", "y")) + (slice(None), third(t))]

    for h in (0, 1):
        for t in range(3):
            push(
                halves(t, 1, 1 - h), d1_r1.at[t, h], s_d1.at[1, t * 2 + h], r_d1.at[1, t * 2 + h],
                partner(back_orders[t][0]),
            )

    def first_sum(t, h):
        arrive(d1_r1.at[t, h], r_d1.at[1, t * 2 + h])
        d1_s1[t, h] = (halves(t, 0, 1 - h)[...].astype(FULL) + d1_r1[t, h].astype(FULL)).astype(LOW)

    own_pair = zh * 3 + slot3
    arrive(dw_c, r_dw.at[6], active)

    @pl.when(active)
    def _():
        own, other = dw[c], dw_c[...]
        dw_p[:, :, 0:192] = jnp.where(c == 0, own, other)
        dw_p[:, :, 192:384] = jnp.where(c == 0, other, own)
        dw_in[own_pair] = dw_p[z * 2 + x]

    def pair_push(ks):
        for k in ks:
            z_, x_ = far_z(k // 2), flip(x, k % 2)
            push(dw_p.at[z_ * 2 + x_], dw_in.at[own_pair], s_dw.at[k], r_dw.at[own_pair], at(z_, x_, c, y), active)

    run_later(10)
    pair_push((7, 5, 6, 4))
    for t in range(3):
        first_sum(t, 0)
        last = spots[back_orders[t][2]]
        for h in (0, 1):
            push(
                d1_s1.at[t, 0, flip(last, 1 - h)], d1_r2.at[t, h], s_d1.at[2, t * 2 + h], r_d1.at[2, t * 2 + h],
                partner(back_orders[t][1]),
            )
    pair_push((3, 2, 1))
    for t in range(3):
        first_sum(t, 1)
    run_later(8)
    for t in range(3):
        last = spots[back_orders[t][2]]
        arrive(d1_r2.at[t, 0], r_d1.at[2, t * 2])
        d1_s2[t] = (d1_s1[t, 1, 1 - last].astype(FULL) + d1_r2[t, 0].astype(FULL)).astype(LOW)
        push(d1_s2.at[t], d1_r3.at[t], s_d1.at[3, t], r_d1.at[3, t], partner(back_orders[t][2]))
    run_later(9)
    def share_terms(which, terms):
        gy[which] = jnp.broadcast_to(terms, (48, 128))
        push(gy.at[which], gy_in.at[which], s_gy.at[which], r_gy.at[which], partner("y"))

    mlp_terms = jnp.zeros((48, 1), FULL)
    for x_, grads in enumerate(ff_sums[4]()):
        lanes = slice(x_ * 288, x_ * 288 + 288)
        for g in range(2):
            ing_ref[:, g, lanes] = grads[:, g * 288 : g * 288 + 288]
        downg_ref[:, lanes] = grads[:, 576:864]
        terms = grads[:, 0:576] * ffp_ref[x_, :, 0:576].astype(FULL)
        mlp_terms = mlp_terms + jnp.sum(terms, axis=1, keepdims=True)
    deliver(1, ing_ref, ing_out)
    deliver(2, downg_ref, downg_out)
    share_terms(1, mlp_terms)
    for h_ in range(2):
        for slot_ in range(3):
            mine = jnp.logical_and(zh == h_, slot == slot_)
            arrive(dw_in.at[h_ * 3 + slot_], r_dw.at[h_ * 3 + slot_], jnp.logical_not(mine))
    attn_terms = jnp.zeros((48, 1), FULL)
    for slot_ in range(3):
        both = dw_in[slot_].astype(FULL) + dw_in[3 + slot_].astype(FULL)
        for c_ in range(2):
            for g in range(3):
                lanes, j = c_ * 192 + g * 64, slot_ * 2 + c_
                qkvg_ref[g, :, j * 64 : j * 64 + 64] = both[:, lanes : lanes + 64]
        attn_terms = attn_terms + jnp.sum(both * wq_ref[slot_].astype(FULL), axis=1, keepdims=True)
    deliver(3, qkvg_ref, qkvg_out)
    share_terms(0, attn_terms)
    for x_, grads in enumerate(out_result()):
        outg_ref[:, x_ * 192 : x_ * 192 + 192] = grads
    deliver(4, outg_ref, outg_out)

    unit_one, scale_one = centred_norm(tok_ref[...].astype(FULL))
    for t in range(3):
        arrive(d1_r2.at[t, 1], r_d1.at[2, t * 2 + 1])
        arrive(d1_r3.at[t], r_d1.at[3, t])
        total = d1_s1[t, 1, spots[back_orders[t][2]]].astype(FULL) + d1_r2[t, 1].astype(FULL)
        res[0, 0, :, third(t)] = total + d1_r3[t].astype(FULL)
    tgrad_ref[...] = tgrad_ref[...] + norm_back(unit_one, scale_one, res[0, 0] * gn[0:1, :])
    deliver(5, tgrad_ref, tgrad_out)
    for which in range(2):
        arrive(gy_in.at[which], r_gy.at[which])
    lane = lax.broadcasted_iota(jnp.int32, (48, 128), 1)
    sums = gy[...] + gy_in[...]
    sums = jnp.where(lane == 0, sums[0], sums[1]).T
    count = gain_a.shape[1]
    sums = jnp.where(y == 0, sums[0:2, :count], sums[0:2, count : 2 * count])
    gains_ref[...] = jnp.zeros_like(gains_ref)
    gains_ref[0:2, 0:count] = sums / gain_ref[0:2, 0:count]
    deliver(6, gains_ref, gains_out)
    for copy in delivered:
        copy.wait()
    for when, copy in pending:
        if when is None:
            copy.wait_send()
        else:
            pl.when(when)(copy.wait_send)


def hand_on(*refs):
    sources, results, held, sems = refs[:7], refs[7:15], refs[15:21], refs[21]
    count = results[6].shape[1]
    results[6][...] = sources[6][0:1, :count]
    results[7][...] = sources[6][1:2, :count]
    inward = [pltpu.make_async_copy(a, b, sems.at[0, k]) for k, (a, b) in enumerate(zip(sources[:6], held))]
    outward = [pltpu.make_async_copy(a, b, sems.at[1, k]) for k, (a, b) in enumerate(zip(held, results[:6]))]
    for copy in inward:
        copy.start()
    for first, second in zip(inward, outward):
        first.wait()
        second.start()
    for copy in outward:
        copy.wait()


def on_device_fast(tokens, out_grad, short_lengths, attn_gain, qkv_weight, out_weight, mlp_gain, in_weight, down_weight):
    rows, width = tokens.shape
    depth = qkv_weight.shape[0]
    heads_here = qkv_weight.shape[2] // HEAD_DIM
    count = attn_gain.shape[0]
    ff = in_weight.shape[2] // 2 * 3
    feats = out_weight.shape[0]

    def vm(shape, kind=LOW):
        return pltpu.VMEM(shape, kind)

    def sem(*shape):
        return pltpu.SemaphoreType.DMA(shape)

    finals = [
        ((rows, width), LOW), ((rows, width), FULL), ((8, 128), FULL), ((3, depth, 384), FULL),
        ((depth, feats), FULL), ((depth, 2, 576), FULL), ((depth, 576), FULL),
    ]
    scratch = [vm(*shape) for shape in finals] + [
        vm((rows, width)), vm((rows, width)), vm((3, depth, 384)), vm((depth, feats)), vm((depth, 2, 576)), vm((depth, 576)),
        vm((8, 128), FULL), vm((heads_here // 2, depth, 384)), vm((2, depth, ff)),
        vm((2, 2, 2, 2, 64, 768)), vm((2, 2, 2, 2, 2, 8, 128), FULL), vm((8, 768), FULL), vm((2, 2, 64, 768)),
        vm((2, 8, 48, 384)), vm((8, 2, 48, 192)), vm((192, 768)), vm((4, 2, 2, 48, 864)), vm((4, 2, 2, 48, 768)), vm((1024, 768)),
        vm((3, 32, 1024), FULL), vm((128, 1024)), vm((1024, 128)), vm((64, 1024)), vm((64, 1024)), vm((1024, 64)),
        vm((1024, 1024)), vm((4, 64, 256), FULL), vm((4, 64, 256)), vm((2, 3, 2, 64, 256)), vm((2, 2, 64, 768), FULL),
        vm((2, 2, 2, 64, 768)), vm((2, 2, 2, 64, 384)), vm((2, 2, 64, 384)), vm((2, 2, 64, 384)), vm((3, 64, 768)), vm((2, 2, 64, 768)),
        vm((2, 3, 64, 128)), vm((2, 2, 2, 2, 64, 128)), vm((64, 1024)), vm((1024, 1024)), vm((192, 1024)),
        vm((1024, 192)), vm((2, 2, 2, 2, 64, 768)), vm((2, 2, 2, 64, 768)), vm((2, 2, 2, 64, 768)),
        vm((3, 2, 2, 64, 256)), vm((3, 2, 2, 64, 256)), vm((3, 2, 64, 256)), vm((3, 64, 256)), vm((3, 64, 256)),
        vm((2, 8, 48, 192)), vm((8, 48, 192)), vm((8, 48, 384)), vm((6, 48, 384)),
        vm((4, 2, 2, 48, 864)), vm((4, 2, 48, 864)), vm((4, 2, 48, 864)), vm((2, 2, 48, 864)), vm((2, 48, 864)),
        vm((2, 48, 864), FULL), vm((48, 864)), vm((48, 864)),
        vm((4, 2, 2, 48, 192)), vm((4, 2, 48, 192)), vm((4, 2, 48, 192)), vm((7, 48, 192)),
        vm((2, 48, 128), FULL), vm((2, 48, 128), FULL),
        sem(4, 3), sem(4, 3), sem(11), sem(11), sem(8), sem(8), sem(6), sem(6), sem(12), sem(12), sem(7), sem(7),
        sem(4, 4), sem(3, 2, 2), sem(2, 2, 2), sem(2, 2, 2), sem(3), sem(3), sem(12), sem(16), sem(4, 6), sem(4, 6),
        sem(8), sem(7), sem(4, 4), sem(4, 4), sem(8), sem(8), sem(2), sem(2), sem(7), sem(6),
    ]
    vmem = pl.BlockSpec(memory_space=pltpu.VMEM)
    anywhere = pl.BlockSpec(memory_space=pl.ANY)
    shapes = [jax.ShapeDtypeStruct(*shape) for shape in finals]
    mixed, tokens_grad, gains, qkv_grad, out_grads, in_grad, down_grad = pl.pallas_call(
        whole_layer,
        out_shape=shapes,
        in_specs=[pl.BlockSpec(memory_space=pltpu.SMEM)] + [vmem] * 2 + [anywhere] * 6,
        out_specs=[anywhere] * 7,
        scratch_shapes=scratch,
        compiler_params=pltpu.CompilerParams(collective_id=0, has_side_effects=True, vmem_limit_bytes=60 << 20),
    )(
        short_lengths, attn_gain[None], mlp_gain[None], tokens, out_grad,
        qkv_weight.transpose(1, 0, 2), out_weight.T, in_weight, down_weight.T,
    )
    grads = (mixed, tokens_grad, qkv_grad, out_grads, in_grad, down_grad)
    count = attn_gain.shape[0]
    mixed, tokens_grad, qkv_grad, out_grads, in_grad, down_grad, attn_gain_grad, mlp_gain_grad = pl.pallas_call(
        hand_on,
        out_shape=[jax.ShapeDtypeStruct(a.shape, a.dtype) for a in grads] + [jax.ShapeDtypeStruct((1, count), FULL)] * 2,
        in_specs=[anywhere] * 6 + [vmem],
        out_specs=[anywhere] * 6 + [vmem] * 2,
        scratch_shapes=[vm(a.shape, a.dtype) for a in grads] + [sem(2, 6)],
    )(*grads, gains)
    return (
        mixed, tokens_grad, attn_gain_grad[0], qkv_grad.transpose(1, 0, 2), out_grads.T, mlp_gain_grad[0],
        in_grad, down_grad.T,
    )


def solution(mesh):
    placed = (
        P(("seq", "head"), None),
        P(("seq", "head"), None),
        P(),
        P(("seq", "head")),
        P("seq", None, "head"),
        P("head", "seq"),
        P(("seq", "head")),
        P("seq", None, "head"),
        P("head", "seq"),
    )
    fits = mesh.shape["seq"] == 16 and mesh.shape["head"] == 2
    return jax.shard_map(
        on_device_fast if fits else on_device,
        mesh=mesh,
        in_specs=placed,
        out_specs=(
            P(("seq", "head"), None),
            P(("seq", "head"), None),
            P(("seq", "head")),
            P("seq", None, "head"),
            P("head", "seq"),
            P(("seq", "head")),
            P("seq", None, "head"),
            P("head", "seq"),
        ),
        check_vma=False,
    )
```

```python
import math

import jax
import jax.numpy as jnp
from jax import lax
from jax.experimental import pallas as pl
from jax.experimental.pallas import tpu as pltpu
from jax.sharding import PartitionSpec as P

HEAD_DIM = 64


norm_eps = 1e-05
rope_base = 160000.0
score_scale = 0.125
masked_low = -1e30


def layer_norm(inputs, gain_vector):
    row_mean = jnp.mean(inputs, axis=-1, keepdims=True)
    centred = inputs - row_mean
    spread = jnp.mean(centred * centred, axis=-1, keepdims=True)
    return centred * lax.rsqrt(spread + norm_eps) * gain_vector


def doc_layout(short_lengths, row_ids, total_rows):
    long_end = total_rows - jnp.sum(short_lengths)
    before = jnp.cumsum(short_lengths) - short_lengths
    bounds = long_end + before
    passed = row_ids[:, None] >= bounds[None, :]
    doc_ids = jnp.sum(passed.astype(jnp.int32), axis=1)
    starts = jnp.max(jnp.where(passed, bounds[None, :], jnp.zeros_like(bounds)[None, :]), axis=1)
    return (doc_ids, row_ids - starts)


def rope_tables(positions):
    steps_half = jnp.arange(HEAD_DIM // 2, dtype=jnp.float32)
    inverse = jnp.exp(steps_half * (-2.0 * math.log(rope_base) / HEAD_DIM))
    angles = positions.astype(jnp.float32)[:, None] * inverse[None, :]
    cosines = jnp.cos(angles)
    sines = jnp.sin(angles)
    return (jnp.concatenate([cosines, cosines], axis=1), jnp.concatenate([sines, sines], axis=1))


def rotate(heads_in, cosines, sines):
    half_dim = heads_in.shape[-1] // 2
    turned = jnp.concatenate([-heads_in[..., half_dim:], heads_in[..., :half_dim]], axis=-1)
    return heads_in * cosines[:, None, :] + turned * sines[:, None, :]


def block_length(row_count, shard_rows):
    shards = row_count // shard_rows
    return shard_rows * math.gcd(shards, max(1, 1024 // shard_rows))


def over_blocks(carry_state, row_count, shard_rows, block_fn):
    block_size = block_length(row_count, shard_rows)

    def block_step(inner_state, block_index):
        return (block_fn(inner_state, block_index * block_size, block_size), None)

    carry_state, _ = lax.scan(
        block_step, carry_state, jnp.arange(row_count // block_size, dtype=jnp.int32)
    )
    return carry_state


def scores_of(queries, key_part):
    return (
        jnp.einsum("qhd,khd->hqk", queries, key_part, preferred_element_type=jnp.float32)
        * score_scale
    )


def block_grads(queries, grad_rows, log_sums, row_dots, key_part, value_part, same_doc):
    scores = scores_of(queries, key_part)
    softmax_part = jnp.where(same_doc, jnp.exp(scores - log_sums[:, :, None]), 0.0)
    grad_probs = jnp.einsum(
        "qhd,khd->hqk", grad_rows, value_part, preferred_element_type=jnp.float32
    )
    dscore = (softmax_part * (grad_probs - row_dots[:, :, None])).astype(jnp.bfloat16)
    return (softmax_part, dscore)


def on_device(
    tokens,
    out_grad,
    short_lengths,
    attn_gain,
    qkv_weight,
    out_weight,
    mlp_gain,
    in_weight,
    down_weight,
):
    half_rows = tokens.shape[0]
    head_count = lax.axis_size("head")
    seq_count = lax.axis_size("seq")
    block_rows = half_rows * head_count
    total_rows = block_rows * seq_count
    local_ids = lax.axis_index("seq") * block_rows + jnp.arange(block_rows, dtype=jnp.int32)
    local_docs, local_pos = doc_layout(short_lengths, local_ids, total_rows)
    cosines, sines = rope_tables(local_pos)
    qkv_full, out_full = (
        lax.all_gather(qkv_weight, "seq", axis=0, tiled=True),
        lax.all_gather(out_weight, "seq", axis=1, tiled=True),
    )
    gain_first, gain_second, in_parts, down_parts = (
        lax.all_gather(attn_gain, ("seq", "head"), axis=0, tiled=True),
        lax.all_gather(mlp_gain, ("seq", "head"), axis=0, tiled=True),
        lax.all_gather(in_weight[None], ("seq", "head"), axis=0, tiled=True),
        lax.all_gather(down_weight[None], ("seq", "head"), axis=0, tiled=True),
    )
    in_parts = in_parts.reshape(seq_count, head_count, in_weight.shape[0], 2, in_weight.shape[2])
    down_parts = down_parts.reshape(
        seq_count, head_count, down_weight.shape[0], down_weight.shape[1]
    )
    heads_here = qkv_full.shape[2] // HEAD_DIM
    inputs = tokens.astype(jnp.float32)
    gain_one = gain_first.astype(jnp.float32)
    normed = layer_norm(inputs, gain_one).astype(jnp.bfloat16)
    normed_block = lax.all_gather(normed, "head", axis=0, tiled=True)
    projected = jnp.einsum(
        "rd,dgc->rgc", normed_block, qkv_full, preferred_element_type=jnp.float32
    )
    queries = rotate(
        projected[:, 0].reshape(block_rows, heads_here, HEAD_DIM), cosines, sines
    ).astype(jnp.bfloat16)
    key_rows = rotate(
        projected[:, 1].reshape(block_rows, heads_here, HEAD_DIM), cosines, sines
    ).astype(jnp.bfloat16)
    value_flat = projected[:, 2].astype(jnp.bfloat16)
    value_rows = value_flat.reshape(block_rows, heads_here, HEAD_DIM)
    key_flat = key_rows.reshape(block_rows, -1)
    query_flat = queries.reshape(block_rows, -1)

    def forward_fold(carry_state, portion):
        piece_keys, piece_values = portion

        def forward_block(inner_state, block_begin, block_size):
            running_max, running_sum, weighted = inner_state
            key_part = lax.dynamic_slice_in_dim(piece_keys, block_begin, block_size, 0).reshape(
                block_size, heads_here, HEAD_DIM
            )
            value_part = lax.dynamic_slice_in_dim(piece_values, block_begin, block_size, 0).reshape(
                block_size, heads_here, HEAD_DIM
            )
            other_docs, _ = doc_layout(
                short_lengths, block_begin + jnp.arange(block_size, dtype=jnp.int32), total_rows
            )
            same_doc = (local_docs[:, None] == other_docs[None, :])[None]
            scores = scores_of(queries, key_part)
            new_max = jnp.maximum(
                running_max, jnp.max(jnp.where(same_doc, scores, masked_low), axis=2)
            )
            factor = jnp.exp(running_max - new_max)
            softmax_part = jnp.where(same_doc, jnp.exp(scores - new_max[:, :, None]), 0.0)
            running_sum = running_sum * factor + jnp.sum(softmax_part, axis=2)
            weighted = weighted * factor.T[:, :, None] + jnp.einsum(
                "hqk,khd->qhd",
                softmax_part.astype(jnp.bfloat16),
                value_part,
                preferred_element_type=jnp.float32,
            )
            return (new_max, running_sum, weighted)

        return over_blocks(carry_state, piece_keys.shape[0], block_rows, forward_block)

    zeros_three = jnp.zeros((block_rows, heads_here, HEAD_DIM), jnp.float32)
    start_state = (
        jnp.full((heads_here, block_rows), masked_low, jnp.float32),
        jnp.zeros((heads_here, block_rows), jnp.float32),
        zeros_three,
    )
    running_max, running_sum, weighted = forward_fold(
        start_state,
        (
            lax.all_gather(key_flat, "seq", axis=0, tiled=True),
            lax.all_gather(value_flat, "seq", axis=0, tiled=True),
        ),
    )
    attended = weighted / running_sum.T[:, :, None]
    log_sums = running_max + jnp.log(running_sum)
    attended_low = attended.reshape(block_rows, -1).astype(jnp.bfloat16)
    branch = jnp.dot(attended_low, out_full, preferred_element_type=jnp.float32)
    branch_rows = lax.psum_scatter(
        branch.astype(jnp.bfloat16), "head", scatter_dimension=0, tiled=True
    ).astype(jnp.float32)
    resid = inputs + branch_rows
    gain_two = gain_second.astype(jnp.float32)
    normed_two = layer_norm(resid, gain_two).astype(jnp.bfloat16)
    normed_split = normed_two.reshape(half_rows, seq_count, -1)
    gate_up = jnp.einsum(
        "rse,shegf->rghf", normed_split, in_parts, preferred_element_type=jnp.float32
    ).reshape(half_rows, 2, -1)

    def activate(gate_part, up_part):
        return jax.nn.gelu(gate_part, approximate=False) * up_part

    hidden, activate_pull = jax.vjp(activate, gate_up[:, 0], gate_up[:, 1])
    hidden_low = hidden.astype(jnp.bfloat16)
    hidden_split = hidden_low.reshape(half_rows, head_count, -1)
    mlp_out = jnp.einsum(
        "rhf,shfe->rse", hidden_split, down_parts, preferred_element_type=jnp.float32
    ).reshape(half_rows, -1)
    mixed = (resid + mlp_out).astype(jnp.bfloat16)
    grad_out = out_grad.astype(jnp.float32)
    grad_split = out_grad.reshape(half_rows, seq_count, -1)
    grad_hidden = jnp.einsum(
        "rse,shfe->rhf", grad_split, down_parts, preferred_element_type=jnp.float32
    ).reshape(half_rows, -1)
    grad_gate, grad_up = activate_pull(grad_hidden)
    grad_gate_up = (
        jnp.stack([grad_gate, grad_up], axis=1)
        .astype(jnp.bfloat16)
        .reshape(half_rows, 2, head_count, -1)
    )
    down_grad = jnp.einsum(
        "rhf,rse->shfe", hidden_split, grad_split, preferred_element_type=jnp.float32
    ).reshape(seq_count * head_count, down_weight.shape[0], down_weight.shape[1])
    in_grad = jnp.einsum(
        "rse,rghf->shegf", normed_split, grad_gate_up, preferred_element_type=jnp.float32
    ).reshape(seq_count * head_count, in_weight.shape[0], 2, in_weight.shape[2])
    grad_normed_two = jnp.einsum(
        "rghf,shegf->rse", grad_gate_up, in_parts, preferred_element_type=jnp.float32
    ).reshape(half_rows, -1)
    _, norm_two_pull = jax.vjp(layer_norm, resid, gain_two)
    grad_resid_norm, gain_two_grad = norm_two_pull(grad_normed_two)
    grad_resid = grad_out + grad_resid_norm
    grad_branch = lax.all_gather(grad_resid.astype(jnp.bfloat16), "head", axis=0, tiled=True)
    out_grad_weight = jnp.einsum(
        "rc,rd->cd", attended_low, grad_branch, preferred_element_type=jnp.float32
    )
    grad_attended = jnp.einsum(
        "rd,cd->rc", grad_branch, out_full, preferred_element_type=jnp.float32
    ).astype(jnp.bfloat16)
    grad_three = grad_attended.reshape(block_rows, heads_here, HEAD_DIM)
    row_dots = jnp.sum(grad_three.astype(jnp.float32) * attended, axis=2).T
    all_sums, all_dots = (
        lax.all_gather(log_sums.T, "seq", axis=0, tiled=True),
        lax.all_gather(row_dots.T, "seq", axis=0, tiled=True),
    )

    def query_terms(query_grad, key_part, value_part, other_docs):
        same_doc = (local_docs[:, None] == other_docs[None, :])[None]
        _, dscore = block_grads(
            queries, grad_three, log_sums, row_dots, key_part, value_part, same_doc
        )
        return (
            query_grad
            + jnp.einsum("hqk,khd->qhd", dscore, key_part, preferred_element_type=jnp.float32)
            * score_scale
        )

    def key_terms(key_grad, value_grad, query_part, grad_part, sums_part, dots_part, other_docs):
        same_doc = (other_docs[:, None] == local_docs[None, :])[None]
        softmax_part, dscore = block_grads(
            query_part, grad_part, sums_part, dots_part, key_rows, value_rows, same_doc
        )
        value_grad = value_grad + jnp.einsum(
            "hqk,qhd->khd",
            softmax_part.astype(jnp.bfloat16),
            grad_part,
            preferred_element_type=jnp.float32,
        )
        key_grad = (
            key_grad
            + jnp.einsum("hqk,qhd->khd", dscore, query_part, preferred_element_type=jnp.float32)
            * score_scale
        )
        return (key_grad, value_grad)

    def piece_rows(source, block_begin, block_size):
        return lax.dynamic_slice_in_dim(source, block_begin, block_size, 0).reshape(
            block_size, heads_here, HEAD_DIM
        )

    def piece_stats(block_begin, block_size):
        sums_part = lax.dynamic_slice_in_dim(all_sums, block_begin, block_size, 0).T
        dots_part = lax.dynamic_slice_in_dim(all_dots, block_begin, block_size, 0).T
        other_docs, _ = doc_layout(
            short_lengths, block_begin + jnp.arange(block_size, dtype=jnp.int32), total_rows
        )
        return (sums_part, dots_part, other_docs)

    def fold_keys(carry_state, portion):
        piece_keys, piece_values = portion

        def key_block(inner_state, block_begin, block_size):
            _, _, other_docs = piece_stats(block_begin, block_size)
            return query_terms(
                inner_state,
                piece_rows(piece_keys, block_begin, block_size),
                piece_rows(piece_values, block_begin, block_size),
                other_docs,
            )

        return over_blocks(carry_state, piece_keys.shape[0], block_rows, key_block)

    query_grad = fold_keys(
        zeros_three,
        (
            lax.all_gather(key_flat, "seq", axis=0, tiled=True),
            lax.all_gather(value_flat, "seq", axis=0, tiled=True),
        ),
    )

    def fold_queries(carry_state, portion):
        piece_queries, piece_grads = portion

        def query_block(inner_state, block_begin, block_size):
            sums_part, dots_part, other_docs = piece_stats(block_begin, block_size)
            return key_terms(
                inner_state[0],
                inner_state[1],
                piece_rows(piece_queries, block_begin, block_size),
                piece_rows(piece_grads, block_begin, block_size),
                sums_part,
                dots_part,
                other_docs,
            )

        return over_blocks(carry_state, piece_queries.shape[0], block_rows, query_block)

    key_grad, value_grad = fold_queries(
        (zeros_three, zeros_three),
        (
            lax.all_gather(query_flat, "seq", axis=0, tiled=True),
            lax.all_gather(grad_attended, "seq", axis=0, tiled=True),
        ),
    )

    def rotate_local(heads_in):
        return rotate(heads_in, cosines, sines)

    _, rotate_pull = jax.vjp(rotate_local, zeros_three)
    query_back = rotate_pull(query_grad)[0]
    key_back = rotate_pull(key_grad)[0]
    grad_qkv = jnp.stack(
        [
            query_back.reshape(block_rows, -1),
            key_back.reshape(block_rows, -1),
            value_grad.reshape(block_rows, -1),
        ],
        axis=1,
    ).astype(jnp.bfloat16)
    qkv_grad = jnp.einsum("rd,rgc->dgc", normed_block, grad_qkv, preferred_element_type=jnp.float32)
    grad_normed_one = jnp.einsum(
        "rgc,dgc->rd", grad_qkv, qkv_full, preferred_element_type=jnp.float32
    )
    grad_normed_rows = lax.psum_scatter(
        grad_normed_one.astype(jnp.bfloat16), "head", scatter_dimension=0, tiled=True
    ).astype(jnp.float32)
    _, norm_one_pull = jax.vjp(layer_norm, inputs, gain_one)
    grad_inputs_norm, gain_one_grad = norm_one_pull(grad_normed_rows)
    tokens_grad = grad_resid + grad_inputs_norm
    qkv_weight_grad, out_weight_grad = (
        lax.psum_scatter(qkv_grad, "seq", scatter_dimension=0, tiled=True),
        lax.psum_scatter(out_grad_weight, "seq", scatter_dimension=1, tiled=True),
    )
    attn_gain_grad, mlp_gain_grad, in_weight_grad, down_weight_grad = (
        lax.psum_scatter(gain_one_grad, ("seq", "head"), scatter_dimension=0, tiled=True),
        lax.psum_scatter(gain_two_grad, ("seq", "head"), scatter_dimension=0, tiled=True),
        lax.psum_scatter(in_grad, ("seq", "head"), scatter_dimension=0, tiled=True),
        lax.psum_scatter(down_grad, ("seq", "head"), scatter_dimension=0, tiled=True),
    )
    return (
        mixed,
        tokens_grad,
        attn_gain_grad,
        qkv_weight_grad,
        out_weight_grad,
        mlp_gain_grad,
        in_weight_grad.reshape(in_weight.shape),
        down_weight_grad.reshape(down_weight.shape),
    )


LOW = jnp.bfloat16
FULL = jnp.float32


def dot(a, b):
    return jnp.dot(a, b, preferred_element_type=FULL)


def dot_nt(a, b):
    return lax.dot_general(a, b, (((1,), (1,)), ((), ())), preferred_element_type=FULL)


def turned(a):
    return a.astype(FULL).T


def centred_norm(rows):
    centred = rows - jnp.mean(rows, axis=-1, keepdims=True)
    scale = lax.rsqrt(jnp.mean(centred * centred, axis=-1, keepdims=True) + norm_eps)
    return centred * scale, scale


def norm_back(unit, scale, weighted):
    mean_w = jnp.mean(weighted, axis=-1, keepdims=True)
    mean_wn = jnp.mean(weighted * unit, axis=-1, keepdims=True)
    return (weighted - mean_w - unit * mean_wn) * scale


def whole_layer(*refs):
    (
        short_ref, gain_a, gain_m, tok_in, gout_in, qkv_in, out_in, in_in, down_in,
        mixed_out, tgrad_out, gains_out, qkvg_out, outg_out, ing_out, downg_out,
        mixed_ref, tgrad_ref, gains_ref, qkvg_ref, outg_ref, ing_ref, downg_ref,
        tok_ref, gout_ref, qkv_ref, wot_ref, in_ref, down_ref, gain_ref, wq_ref, ffp_ref, xh, gt, gn, gb, wh_p, wh, wht, ffw, wo, h1, cs, qa, ka, kt, vt, vr, pt, ot, ol, og, res,
        ms, ms_c, ms_a, ms_y, ms_d, db, dos, dop, dot_t, ds, dqt, dq, d1, d1_c, d1_a, d1_r1, d1_s1, d1_r2, d1_s2, d1_r3,
        dw, dw_c, dw_p, dw_in, gf, gf_k, gf_s, gf_z, gf_y, gf_f, gf_b, gf_c, go, go_k, go_s, go_z, gy, gy_in,
        s_tok, r_tok, s_gain, r_gain, s_wq, r_wq, s_g, r_g, s_ff, r_ff, s_wo, r_wo,
        s_o, r_o, s_ms, r_ms, s_db, r_db, s_do, r_do, s_d1, r_d1, s_dw, r_dw, s_gf, r_gf, s_go, r_go, s_gy, r_gy, s_out, s_in,
    ) = refs
    seq, head = lax.axis_index("seq"), lax.axis_index("head")
    z, x, c, y = seq // 4, (seq // 2) % 2, seq % 2, head
    zh, zb = z // 2, z % 2
    slot = zb * 2 + x
    active = slot < 3
    slot3 = jnp.minimum(slot, 2)
    pending, delivered = [], []

    def flip(value, bit):
        return value if bit == 0 else 1 - value

    def at(z_, x_, c_, y_):
        return (z_ * 4 + x_ * 2 + c_, y_)

    def far_z(k):
        return flip(zh, k // 2) * 2 + flip(zb, k % 2)

    def partner(dim):
        return {
            "x": at(z, 1 - x, c, y),
            "y": at(z, x, c, 1 - y),
            "z": at(far_z(1), x, c, y),
            "c": at(z, x, 1 - c, y),
            "h": at(far_z(2), x, c, y),
        }[dim]

    def push(src, dst, send, recv, device, when=None):
        copy = pltpu.make_async_remote_copy(
            src_ref=src, dst_ref=dst, send_sem=send, recv_sem=recv,
            device_id=device, device_id_type=pl.DeviceIdType.MESH,
        )
        if when is None:
            copy.start()
        else:
            pl.when(when)(copy.start)
        pending.append((when, copy))

    def deliver(k, src, dst):
        copy = pltpu.make_async_copy(src, dst, s_out.at[k])
        copy.start()
        delivered.append(copy)

    def arrive(dst, recv, when=None):
        copy = pltpu.make_async_remote_copy(
            src_ref=dst, dst_ref=dst, send_sem=recv, recv_sem=recv,
            device_id=partner("c"), device_id_type=pl.DeviceIdType.MESH,
        )
        if when is None:
            copy.wait_recv()
        else:
            pl.when(when)(copy.wait_recv)

    loads = (
        (tok_in, tok_ref), (qkv_in, qkv_ref), (in_in, in_ref), (down_in, down_ref), (out_in, wot_ref), (gout_in, gout_ref),
    )
    loads = [pltpu.make_async_copy(a, b, s_in.at[k]) for k, (a, b) in enumerate(loads)]
    barrier = pltpu.get_barrier_semaphore()
    peers = []
    for k in range(1, 32):
        kz, kx, kc, ky = k // 8, (k // 4) % 2, (k // 2) % 2, k % 2
        if kz < 2 or ky == 0:
            peers.append(at(far_z(kz), flip(x, kx), flip(c, kc), flip(y, ky)))
    for peer in peers:
        pl.semaphore_signal(barrier, inc=1, device_id=peer, device_id_type=pl.DeviceIdType.MESH)

    for load in loads:
        load.start()
    gain_ref[...] = jnp.zeros_like(gain_ref)
    gain_ref[0:1, 0 : gain_a.shape[1]] = gain_a[...].astype(FULL)
    gain_ref[1:2, 0 : gain_m.shape[1]] = gain_m[...].astype(FULL)
    for load in loads:
        load.wait()
    for g in range(3):
        for j in range(6):
            lanes = j % 2 * 192 + g * 64
            wq_ref[j // 2, :, lanes : lanes + 64] = qkv_ref[g, :, j * 64 : j * 64 + 64]
    for c_ in range(2):
        lanes = slice(c_ * 288, c_ * 288 + 288)
        for g in range(2):
            ffp_ref[c_, :, g * 288 : g * 288 + 288] = in_ref[:, g, lanes]
        ffp_ref[c_, :, 576:864] = down_ref[:, lanes]
    pl.semaphore_wait(barrier, len(peers))

    xh[zb, c, x, y] = tok_ref[...]
    orders = (("z", "x", "y"), ("z", "y", "x"), ("z", "x", "y"))

    def third(t):
        return pl.ds(t * 256, 256)

    def blocks(ref, opened, lanes, flipped=None, core=None):
        there = {"z": zb, "x": x, "y": y, "c": c if core is None else core}
        if flipped is not None:
            there[flipped] = 1 - there[flipped]
        index = tuple(slice(None) if d in opened else there[d] for d in ("z", "c", "x", "y"))
        return ref.at[index + (slice(None), lanes)]

    for t in range(3):
        view = blocks(xh, (), third(t))
        push(view, view, s_tok.at[0, t], r_tok.at[0, t], partner(orders[t][0]))

    gt[zh, zb, x, c, y] = gain_ref[...]

    def gain_place(k):
        return gt.at[flip(zh, k // 2), flip(zb, k % 2), x, c, y]

    for k in range(1, 4):
        push(gain_place(0), gain_place(0), s_gain.at[k], r_gain.at[k], at(far_z(k), x, c, y))

    def plane(k):
        return flip(x, k // 4), flip(c, k // 2 % 2), flip(y, k % 2)

    def gain_share():
        for k in range(1, 4):
            arrive(gain_place(k), r_gain.at[k])
        for k in range(1, 8):
            x_, c_, y_ = plane(k)
            view = gt.at[:, :, x, c, y]
            push(view, view, s_gain.at[3 + k], r_gain.at[3 + k], at(z, x_, c_, y_))

    def gain_all():
        for k in range(1, 8):
            x_, c_, y_ = plane(k)
            arrive(gt.at[:, :, x_, c_, y_], r_gain.at[3 + k])

    wo_lanes = pl.ds(pl.multiple_of(y * 384, 128), 384)
    wo_others = pl.ds(pl.multiple_of((1 - y) * 384, 128), 384)

    def ff_share(src, z_, x_, k, dim):
        push(src, ffw.at[z_, x_, c], s_ff.at[k], r_ff.at[k], partner(dim))

    def ff_arrive(kz, kx, k):
        arrive(ffw.at[far_z(kz), flip(x, kx), c], r_ff.at[k])

    def ff_cross():
        ff_arrive(0, 1, 0)
        ff_share(ffw.at[z, 1 - x, c], z, 1 - x, 2, "h")
        ff_share(ffw.at[z, 1 - x, c], z, 1 - x, 4, "z")

    def ff_relay():
        for kx in range(2):
            ff_arrive(2, kx, 1 + kx)
            z_, x_ = far_z(2), flip(x, kx)
            ff_share(ffw.at[z_, x_, c], z_, x_, 5 + kx, "z")

    def ff_core(kz):
        z_ = far_z(kz)
        push(ffw.at[z_, :, c], ffw.at[z_, :, c], s_ff.at[8 + kz], r_ff.at[8 + kz], partner("c"))

    def ff_near():
        for kx in range(2):
            ff_arrive(1, kx, 3 + kx)
        ff_core(1)

    def ff_last():
        for kx in range(2):
            ff_arrive(3, kx, 5 + kx)
        ff_core(3)

    def wo_forward_x():
        for k in range(1, 4):
            arrive(wo.at[far_z(k), x, c, :, wo_lanes], r_wo.at[k])
        view = wo.at[:, x, c, :, wo_lanes]
        push(view, view, s_wo.at[4], r_wo.at[4], partner("x"))

    def wo_forward_y():
        arrive(wo.at[:, 1 - x, c, :, wo_lanes], r_wo.at[4])
        view = wo.at[:, :, c, :, wo_lanes]
        push(view, view, s_wo.at[5], r_wo.at[5], partner("y"))

    def wo_forward_core():
        arrive(wo.at[:, :, c, :, wo_others], r_wo.at[5])
        push(wo.at[:, :, c], wo.at[:, :, c], s_wo.at[6], r_wo.at[6], partner("c"))

    ffw[z, x, c] = ffp_ref[x]
    wo[z, x, c, :, wo_lanes] = wot_ref[...]
    def wo_push():
        for k in (2, 3, 1):
            push(wot_ref, wo.at[z, x, c, :, wo_lanes], s_wo.at[k], r_wo.at[k], at(far_z(k), x, c, y))

    own_pair_at = z * 2 + x
    wh_p[c, own_pair_at] = wq_ref[slot3]

    def head_push():
        for k in (7, 5, 6, 4, 3, 2, 1):
            z_, x_ = far_z(k // 2), flip(x, k % 2)
            slot_ = z_ % 2 * 2 + x_
            piece = wq_ref.at[jnp.minimum(slot_, 2)]
            push(piece, wh_p.at[c, own_pair_at], s_wq.at[k], r_wq.at[k], at(z_, x_, c, y), slot_ < 3)

    gb[x, y] = gout_ref[...]
    group = ((0, 1), (1, 0), (1, 1))

    def member(kx, ky):
        return at(z, flip(x, kx), c, flip(y, ky))

    def grad_push():
        for k, (kx, ky) in enumerate(group):
            push(gb.at[x, y], gb.at[x, y], s_g.at[k], r_g.at[k], member(kx, ky))

    def token_step(step):
        for t in range(3):
            arrive(blocks(xh, orders[t][: step - 1], third(t), orders[t][step - 1]), r_tok.at[step - 1, t])
            view = blocks(xh, orders[t][:step], third(t))
            push(view, view, s_tok.at[step, t], r_tok.at[step, t], partner(orders[t][step]))

    events = {
        "fx": lambda: ff_share(ffp_ref.at[1 - x], z, x, 0, "x"),
        "f2": lambda: ff_share(ffp_ref.at[x], z, x, 1, "h"),
        "f1": lambda: ff_share(ffp_ref.at[x], z, x, 3, "z"),
        "fc": ff_cross,
        "fr": ff_relay,
        "c0": lambda: ff_core(0),
        "c1": ff_near,
        "c2": lambda: ff_core(2),
        "c3": ff_last,
        "w": head_push,
        "g": grad_push,
        "oz": wo_push,
        "ox": wo_forward_x,
        "oy": wo_forward_y,
        "oc": wo_forward_core,
    }

    def run(point):
        for name in plan[point]:
            events[name]()

    plan = (
        ("w",),
        ("oz", "fx", "f2", "f1"),
        ("ox", "fc", "g"),
        ("oy", "fr", "c0", "c1"),
        ("c2",),
        (),
        (),
        (),
        ("oc", "c3"),
    )
    run(0)
    token_step(1)
    gain_share()
    run(1)
    token_step(2)
    run(2)
    run(3)

    half_rows = 1024
    lane = lax.broadcasted_iota(jnp.int32, (32, half_rows), 1)
    row = lane % 64 + (lane // 64 % 2) * 64 + (lane // 256 % 2) * 128 + (lane // 128 % 2) * 256 + (lane // 512) * 512
    row = row + zh * half_rows
    feature = lax.broadcasted_iota(jnp.int32, (32, half_rows), 0)
    bound = jnp.int32(2 * half_rows)
    for b in range(short_ref.shape[0]):
        bound = bound - short_ref[b]
    doc = jnp.zeros_like(row)
    start = jnp.zeros_like(row)
    for b in range(short_ref.shape[0]):
        passed = row >= bound
        doc = doc + jnp.where(passed, 1, 0)
        start = jnp.where(passed, bound, start)
        bound = bound + short_ref[b]
    inverse = jnp.exp(feature.astype(FULL) * (-2.0 * math.log(rope_base) / HEAD_DIM))
    angles = (row - start).astype(FULL) * inverse
    cs[0] = jnp.cos(angles)
    cs[1] = jnp.sin(angles)
    same = jnp.where(feature == doc, 1.0, 0.0)
    cs[2] = same
    qa[64:96, :] = ((same - 1.0) * 1e30).astype(LOW)
    qa[96:128, :] = jnp.zeros((32, half_rows), LOW)

    gain_all()
    tiles = gt[...].reshape(256, 128).astype(LOW)
    width = 24
    pick = lax.broadcasted_iota(jnp.int32, (128, 768), 1) % width == lax.broadcasted_iota(jnp.int32, (128, 768), 0)
    spread = dot(tiles, jnp.where(pick, 1.0, 0.0).astype(LOW))
    source = lax.broadcasted_iota(jnp.int32, (256, 768), 0)
    wanted = (lax.broadcasted_iota(jnp.int32, (256, 768), 1) // width) * 8
    gn[0:1, :] = jnp.sum(jnp.where(source == wanted, spread, 0.0), axis=0, keepdims=True)
    gn[1:2, :] = jnp.sum(jnp.where(source == wanted + 1, spread, 0.0), axis=0, keepdims=True)

    for t in range(3):
        arrive(blocks(xh, orders[t][:2], third(t), orders[t][2]), r_tok.at[2, t])

    def rows_of(z_, c_):
        return pl.ds(pl.multiple_of(z_ * 512 + c_ * 256, 256), 256)

    for k in range(1, 8):
        arrive(wh_p.at[c, far_z(k // 2) * 2 + flip(x, k % 2)], r_wq.at[k], active)
    push(wh_p.at[c], wh_p.at[c], s_wq.at[0], r_wq.at[0], partner("c"), active)

    for z_ in range(2):
        rows = rows_of(z_, c)

        @pl.when(active)
        def _(z_=z_, rows=rows):
            unit, _ = centred_norm(xh[z_, c].reshape(256, 768).astype(FULL))
            h1[rows, :] = (unit * gn[0:1, :]).astype(LOW)

        push(h1.at[rows, :], h1.at[rows, :], s_tok.at[3, z_], r_tok.at[3, z_], partner("c"), active)
    arrive(wh_p.at[1 - c], r_wq.at[0], active)

    @pl.when(active)
    def _():
        for c_ in range(2):
            wh[:, c_] = jnp.where(c == 0, wh_p[c_, :, :, 0:192], wh_p[c_, :, :, 192:384])
        wht[...] = turned(wh[...].reshape(768, 192)).astype(LOW)

    for part in range(4):
        z_, c_ = part % 2, flip(c, part // 2)
        cols = rows_of(z_, c_)
        if part >= 2:
            arrive(h1.at[cols, :], r_tok.at[3, z_], active)

        @pl.when(active)
        def _(cols=cols):
            proj = dot_nt(wht[...], h1[cols, :])
            cosine, sine = cs[0, :, cols], cs[1, :, cols]
            q1, q2, k1, k2 = proj[0:32], proj[32:64], proj[64:96], proj[96:128]
            qr = jnp.concatenate([q1 * cosine - q2 * sine, q2 * cosine + q1 * sine], axis=0)
            kr = jnp.concatenate([k1 * cosine - k2 * sine, k2 * cosine + k1 * sine], axis=0)
            qa[0:64, cols] = (qr * score_scale).astype(LOW)
            kt[:, cols] = kr.astype(LOW)
            vt[:, cols] = proj[128:192].astype(LOW)
            pad = jnp.zeros((32, 256), FULL)
            ka[cols, :] = jnp.concatenate([kr, cs[2, :, cols], pad], axis=0).T.astype(LOW)
            vr[cols, :] = proj[128:192].T.astype(LOW)

    run(4)

    for part in range(4):
        cols = pl.ds(part * 256, 256)

        @pl.when(active)
        def _(part=part, cols=cols):
            scores = dot(ka[...], qa[:, cols])
            expo = jnp.exp(scores - jnp.max(scores, axis=0, keepdims=True))
            prob = (expo * (1.0 / jnp.sum(expo, axis=0, keepdims=True))).astype(LOW)
            pt[:, cols] = prob
            result = dot(vt[...], prob)
            ot[part] = result
            ol[part] = result.astype(LOW)

        own_group = jnp.logical_and(zb == part // 2, c == part % 2)
        for k in range(4):
            x_, y_ = k // 2, k % 2
            mine = jnp.logical_and(own_group, jnp.logical_and(x == x_, y == y_))

            @pl.when(jnp.logical_and(active, mine))
            def _(part=part):
                og[y, slot3, c] = ol[part]

            push(
                ol.at[part], og.at[y, slot3, c], s_o.at[part, k], r_o.at[slot3, c, y],
                at(zh * 2 + part // 2, x_, part % 2, y_), jnp.logical_and(active, jnp.logical_not(mine)),
            )
        run(5 + part)

    for slot_ in range(3):
        for c_ in range(2):
            for y_ in range(2):
                mine = jnp.logical_and(slot == slot_, jnp.logical_and(c == c_, y == y_))
                arrive(og.at[y_, slot_, c_], r_o.at[slot_, c_, y_], jnp.logical_not(mine))
    arrive(wo.at[:, :, 1 - c], r_wo.at[6])

    gain_two = gn[1:2, :]
    branch = dot(wo[...].reshape(768, 768), og[...].reshape(768, 256)).T
    resid = xh[zb, c].reshape(256, 768).astype(FULL) + branch
    res[...] = resid.reshape(2, 2, 64, 768)
    unit_two, _ = centred_norm(resid)
    h2 = (unit_two * gain_two).astype(LOW)

    for kz in range(4):
        arrive(ffw.at[far_z(kz), :, 1 - c], r_ff.at[8 + kz])
    for k, (kx, ky) in enumerate(group):
        arrive(gb.at[flip(x, kx), flip(y, ky)], r_g.at[k])
    w_in = ffw[:, :, :, :, 0:576].reshape(768, 576)
    w_down = ffw[:, :, :, :, 576:864].reshape(768, 288)
    gate_up = dot(h2, w_in)
    gate, up = gate_up[:, :288], gate_up[:, 288:]
    grad_out = gb[...].reshape(256, 768)
    grad_hidden = dot(grad_out, w_down)
    chance = 0.5 * (1.0 + lax.erf(gate * (1.0 / math.sqrt(2.0))))
    density = jnp.exp(gate * gate * -0.5) * (1.0 / math.sqrt(2.0 * math.pi))
    curve = gate * chance
    hidden = (curve * up).astype(LOW)
    grad_gate = grad_hidden * up * (chance + gate * density)
    grad_gate_up = jnp.concatenate([grad_gate, grad_hidden * curve], axis=1).astype(LOW)

    columns = (slice(0, 384), slice(384, 768))

    def halve(kind, part):
        ms[kind] = part.astype(LOW).reshape(2, 2, 64, 768)
        push(ms.at[kind, 1 - x, :, :, columns[0]], ms_c.at[kind, 0], s_ms.at[kind, 0, 0], r_ms.at[kind, 0, 0], partner("x"))
        push(ms.at[kind, :, 1 - y, :, columns[1]], ms_c.at[kind, 1], s_ms.at[kind, 1, 0], r_ms.at[kind, 1, 0], partner("y"))

    def quarter(kind):
        for t in range(2):
            arrive(ms_c.at[kind, t], r_ms.at[kind, t, 0])
            mine = ms[kind, x, 1 - y, :, columns[0]] if t == 0 else ms[kind, 1 - x, y, :, columns[1]]
            other = ms_c[kind, t, 1 - y] if t == 0 else ms_c[kind, t, 1 - x]
            ms_a[kind, t] = (mine.astype(FULL) + other.astype(FULL)).astype(LOW)
            push(ms_a.at[kind, t], ms_y.at[kind, t], s_ms.at[kind, t, 1], r_ms.at[kind, t, 1], partner("yx"[t]))

    def quarter_sum(kind):
        sums = []
        for t in range(2):
            arrive(ms_y.at[kind, t], r_ms.at[kind, t, 1])
            other = ms_c[kind, t, y] if t == 0 else ms_c[kind, t, x]
            mine = ms[kind, x, y, :, columns[t]].astype(FULL) + other.astype(FULL)
            sums.append(mine + ms_y[kind, t].astype(FULL))
        return jnp.concatenate(sums, axis=1)

    ms[0] = dot_nt(grad_gate_up, w_in).astype(LOW).reshape(2, 2, 64, 768)
    for k, (kx, ky) in enumerate(group):
        push(ms.at[0, flip(x, kx), flip(y, ky)], ms_d.at[k], s_g.at[3 + k], r_g.at[3 + k], member(kx, ky))
    halve(1, dot_nt(hidden, w_down))
    h2_t = turned(h2).astype(LOW)
    gf[:, :, :, :, 0:576] = dot(h2_t, grad_gate_up).astype(LOW).reshape(4, 2, 2, 48, 576)
    g_t = turned(grad_out).astype(LOW)
    gf[:, :, :, :, 576:864] = dot(g_t, hidden).astype(LOW).reshape(4, 2, 2, 48, 288)

    def sums_of(whole, crossed, low, near, far, wide, last, coming, send, recv):
        def cross():
            for kz in (3, 1, 2, 0):
                z_ = far_z(kz)
                push(whole.at[z_, :, 1 - c], crossed.at[z_], send.at[0, kz], recv.at[0, kz], partner("c"))

        def pair(kz):
            z_ = far_z(kz)
            arrive(crossed.at[z_], recv.at[0, kz])
            return whole[z_, :, c].astype(FULL) + crossed[z_].astype(FULL)

        def to_near(kz):
            z_ = far_z(kz)
            low[z_] = pair(kz).astype(LOW)
            push(low.at[z_], near.at[kz // 2], send.at[1, kz // 2], recv.at[1, kz // 2], partner("z"))

        def to_far():
            value = pair(2)
            arrive(near.at[1], recv.at[1, 1])
            low[far_z(2)] = (value + near[1].astype(FULL)).astype(LOW)
            push(low.at[far_z(2)], far, send.at[2, 0], recv.at[2, 0], partner("h"))

        def finish():
            value = pair(0)
            arrive(near.at[0], recv.at[1, 0])
            arrive(far, recv.at[2, 0])
            wide[...] = value + near[0].astype(FULL) + far[...].astype(FULL)
            last[...] = wide[1 - x].astype(LOW)
            push(last, coming, send.at[3, 0], recv.at[3, 0], partner("x"))

        def result():
            arrive(coming, recv.at[3, 0])
            own, other = wide[x], coming[...].astype(FULL)
            return jnp.where(x == 0, own, other), jnp.where(x == 0, other, own)

        return cross, to_near, to_far, finish, result

    ff_sums = sums_of(gf, gf_k, gf_s, gf_z, gf_y, gf_f, gf_b, gf_c, s_gf, r_gf)

    def out_share():
        for k, (kx, ky) in enumerate(group):
            arrive(db.at[flip(x, kx), flip(y, ky)], r_db.at[k])
        db_t = turned(db[...].reshape(256, 768)).astype(LOW)
        o_part = og[...].reshape(2, 6, 64, 256)
        o_pick = jnp.where(y == 0, o_part[0], o_part[1])
        o_pick = jnp.where(x == 0, o_pick[0:3], o_pick[3:6]).reshape(192, 256)
        go[...] = dot_nt(db_t, o_pick).astype(LOW).reshape(4, 2, 2, 48, 192)
        push(go.at[:, :, 1 - c], go_k, s_go.at[0], r_go.at[0], partner("c"))

    def out_send():
        arrive(go_k, r_go.at[0])
        go_s[...] = (go[:, :, c].astype(FULL) + go_k[...].astype(FULL)).astype(LOW)
        for k in (7, 5, 6, 4, 3, 2, 1):
            z_, x_ = far_z(k // 2), flip(x, k % 2)
            push(go_s.at[z_, x_], go_z.at[k - 1], s_go.at[k], r_go.at[k], at(z_, x_, c, y))

    def out_result():
        sums = [go_s[z, x].astype(FULL), jnp.zeros((48, 192), FULL)]
        for k in range(1, 8):
            arrive(go_z.at[k - 1], r_go.at[k])
            sums[k % 2] = sums[k % 2] + go_z[k - 1].astype(FULL)
        return jnp.where(x == 0, sums[0], sums[1]), jnp.where(x == 0, sums[1], sums[0])

    def mixed_done():
        mixed_ref[...] = (res[x, y] + quarter_sum(1)).astype(LOW)
        deliver(0, mixed_ref, mixed_out)

    later = {
        "md": mixed_done,
        "mx": lambda: quarter(1),
        "n3": lambda: ff_sums[1](3),
        "n1": lambda: ff_sums[1](1),
        "f": ff_sums[2],
        "e": ff_sums[3],
        "O": out_share,
        "S": out_send,
    }
    then = (
        ("n3",),
        ("n1", "mx"),
        (),
        (),
        ("f", "md"),
        (),
        (),
        ("O",),
        ("e", "S"),
        (),
        (),
    )

    def run_later(point):
        for name in then[point]:
            later[name]()

    ff_sums[0]()
    run_later(0)
    own_res = res[x, y]
    unit_two, scale_two = centred_norm(own_res)
    grad_h2 = ms[0, x, y].astype(FULL)
    for k in range(3):
        arrive(ms_d.at[k], r_g.at[3 + k])
        grad_h2 = grad_h2 + ms_d[k].astype(FULL)
    grad_resid = gout_ref[...].astype(FULL) + norm_back(unit_two, scale_two, grad_h2 * gain_two)
    tgrad_ref[...] = grad_resid
    grad_branch = grad_resid.astype(LOW)
    db[x, y] = grad_branch
    grad_o = dot(grad_branch, wo[...].reshape(768, 768)).astype(LOW)
    own_block = zb * 8 + c * 4 + x * 2 + y
    for slot_ in range(3):
        for y_ in range(2):
            lanes = y_ * 384 + slot_ * 128
            dos[y_, slot_] = grad_o[:, lanes : lanes + 128]
    for turn in (1, 2, 0):
        slot_ = (slot3 + turn) % 3
        for k in (3, 2, 1, 0):
            y_, c_ = flip(y, k // 2), flip(c, k % 2)
            mine = jnp.logical_and(slot == slot_, k == 0)

            @pl.when(mine)
            def _(slot_=slot_, y_=y_):
                dop[zb, c, x, y] = dos[y_, slot_]

            push(
                dos.at[y_, slot_], dop.at[zb, c, x, y], s_do.at[turn * 4 + k], r_do.at[own_block],
                at(zh * 2 + slot_ // 2, slot_ % 2, c_, y_), jnp.logical_not(mine),
            )
    run_later(1)
    for k, (kx, ky) in enumerate(group):
        push(db.at[x, y], db.at[x, y], s_db.at[k], r_db.at[k], member(kx, ky))
    run_later(2)

    for b in range(16):
        z_, c_, x_, y_ = b // 8, (b // 4) % 2, (b // 2) % 2, b % 2
        arrive(dop.at[z_, c_, x_, y_], r_do.at[b], jnp.logical_and(active, own_block != b))

    @pl.when(active)
    def _():
        pair = turned(dop[...].reshape(1024, 128))
        dot_t[...] = jnp.where(c == 0, pair[0:64], pair[64:128]).astype(LOW)

    for part in range(4):
        cols = pl.ds(part * 256, 256)

        @pl.when(active)
        def _(part=part, cols=cols):
            grad_t = dot_t[:, cols]
            delta = jnp.sum(grad_t.astype(FULL) * ot[part], axis=0, keepdims=True)
            grad_p = dot(vr[...], grad_t)
            score_grad = (pt[:, cols].astype(FULL) * (grad_p - delta)).astype(LOW)
            ds[:, cols] = score_grad
            back = dot(kt[...], score_grad) * score_scale
            cosine, sine = cs[0, :, cols], cs[1, :, cols]
            b1, b2 = back[0:32], back[32:64]
            dqt[0:64, cols] = jnp.concatenate([b1 * cosine + b2 * sine, b2 * cosine - b1 * sine], axis=0).astype(LOW)

        run_later(3 + part)

    @pl.when(active)
    def _():
        for part in range(4):
            cols = pl.ds(part * 256, 256)
            back = dot_nt(qa[0:64, :], ds[cols, :])
            cosine, sine = cs[0, :, cols], cs[1, :, cols]
            b1, b2 = back[0:32], back[32:64]
            dqt[64:128, cols] = jnp.concatenate([b1 * cosine + b2 * sine, b2 * cosine - b1 * sine], axis=0).astype(LOW)
            dqt[128:192, cols] = dot_nt(dot_t[...], pt[cols, :]).astype(LOW)
            dq[cols, :] = turned(dqt[:, cols]).astype(LOW)

    for part in range(4):
        z_, c_ = part % 2, flip(c, 1 - part // 2)

        @pl.when(active)
        def _(z_=z_, c_=c_):
            rows = pl.ds(pl.multiple_of(z_ * 512 + c_ * 256, 256), 256)
            d1[z_, c_] = dot_nt(dq[rows, :], wh[...].reshape(768, 192)).astype(LOW).reshape(2, 2, 64, 768)

        if part < 2:
            push(d1.at[z_, c_], d1_c.at[z_], s_d1.at[0, z_], r_d1.at[0, z_], partner("c"), active)
    run_later(7)

    @pl.when(active)
    def _():
        grad = dot(dqt[...], h1[...])
        grad = grad.T.astype(LOW).reshape(8, 2, 48, 192)
        dw[0], dw[1] = grad[:, 0], grad[:, 1]

    push(dw.at[1 - c], dw_c, s_dw.at[0], r_dw.at[6], partner("c"), active)

    @pl.when(jnp.logical_not(active))
    def _():
        d1_a[...] = jnp.zeros_like(d1_a)

    for z_ in range(2):
        arrive(d1_c.at[z_], r_d1.at[0, z_], active)

        @pl.when(active)
        def _(z_=z_):
            d1_a[z_] = (d1[z_, c].astype(FULL) + d1_c[z_].astype(FULL)).astype(LOW)

    back_orders = (("x", "y", "z"), ("y", "z", "x"), ("z", "x", "y"))

    spots = {"z": zb, "x": x, "y": y}

    def halves(t, first, second):
        a, b, _ = back_orders[t]
        place = {a: flip(spots[a], first), b: flip(spots[b], second)}
        return d1_a.at[tuple(place.get(d, slice(None)) for d in ("z", "x", "y")) + (slice(None), third(t))]

    for h in (0, 1):
        for t in range(3):
            push(
                halves(t, 1, 1 - h), d1_r1.at[t, h], s_d1.at[1, t * 2 + h], r_d1.at[1, t * 2 + h],
                partner(back_orders[t][0]),
            )

    def first_sum(t, h):
        arrive(d1_r1.at[t, h], r_d1.at[1, t * 2 + h])
        d1_s1[t, h] = (halves(t, 0, 1 - h)[...].astype(FULL) + d1_r1[t, h].astype(FULL)).astype(LOW)

    own_pair = zh * 3 + slot3
    arrive(dw_c, r_dw.at[6], active)

    @pl.when(active)
    def _():
        own, other = dw[c], dw_c[...]
        dw_p[:, :, 0:192] = jnp.where(c == 0, own, other)
        dw_p[:, :, 192:384] = jnp.where(c == 0, other, own)
        dw_in[own_pair] = dw_p[z * 2 + x]

    def pair_push(ks):
        for k in ks:
            z_, x_ = far_z(k // 2), flip(x, k % 2)
            push(dw_p.at[z_ * 2 + x_], dw_in.at[own_pair], s_dw.at[k], r_dw.at[own_pair], at(z_, x_, c, y), active)

    run_later(10)
    pair_push((7, 5, 6, 4))
    for t in range(3):
        first_sum(t, 0)
        last = spots[back_orders[t][2]]
        for h in (0, 1):
            push(
                d1_s1.at[t, 0, flip(last, 1 - h)], d1_r2.at[t, h], s_d1.at[2, t * 2 + h], r_d1.at[2, t * 2 + h],
                partner(back_orders[t][1]),
            )
    pair_push((3, 2, 1))
    for t in range(3):
        first_sum(t, 1)
    run_later(8)
    for t in range(3):
        last = spots[back_orders[t][2]]
        arrive(d1_r2.at[t, 0], r_d1.at[2, t * 2])
        d1_s2[t] = (d1_s1[t, 1, 1 - last].astype(FULL) + d1_r2[t, 0].astype(FULL)).astype(LOW)
        push(d1_s2.at[t], d1_r3.at[t], s_d1.at[3, t], r_d1.at[3, t], partner(back_orders[t][2]))
    run_later(9)
    def share_terms(which, terms):
        gy[which] = jnp.broadcast_to(terms, (48, 128))
        push(gy.at[which], gy_in.at[which], s_gy.at[which], r_gy.at[which], partner("y"))

    mlp_terms = jnp.zeros((48, 1), FULL)
    for x_, grads in enumerate(ff_sums[4]()):
        lanes = slice(x_ * 288, x_ * 288 + 288)
        for g in range(2):
            ing_ref[:, g, lanes] = grads[:, g * 288 : g * 288 + 288]
        downg_ref[:, lanes] = grads[:, 576:864]
        terms = grads[:, 0:576] * ffp_ref[x_, :, 0:576].astype(FULL)
        mlp_terms = mlp_terms + jnp.sum(terms, axis=1, keepdims=True)
    deliver(1, ing_ref, ing_out)
    deliver(2, downg_ref, downg_out)
    share_terms(1, mlp_terms)
    for h_ in range(2):
        for slot_ in range(3):
            mine = jnp.logical_and(zh == h_, slot == slot_)
            arrive(dw_in.at[h_ * 3 + slot_], r_dw.at[h_ * 3 + slot_], jnp.logical_not(mine))
    attn_terms = jnp.zeros((48, 1), FULL)
    for slot_ in range(3):
        both = dw_in[slot_].astype(FULL) + dw_in[3 + slot_].astype(FULL)
        for c_ in range(2):
            for g in range(3):
                lanes, j = c_ * 192 + g * 64, slot_ * 2 + c_
                qkvg_ref[g, :, j * 64 : j * 64 + 64] = both[:, lanes : lanes + 64]
        attn_terms = attn_terms + jnp.sum(both * wq_ref[slot_].astype(FULL), axis=1, keepdims=True)
    deliver(3, qkvg_ref, qkvg_out)
    share_terms(0, attn_terms)
    for x_, grads in enumerate(out_result()):
        outg_ref[:, x_ * 192 : x_ * 192 + 192] = grads
    deliver(4, outg_ref, outg_out)

    unit_one, scale_one = centred_norm(tok_ref[...].astype(FULL))
    for t in range(3):
        arrive(d1_r2.at[t, 1], r_d1.at[2, t * 2 + 1])
        arrive(d1_r3.at[t], r_d1.at[3, t])
        total = d1_s1[t, 1, spots[back_orders[t][2]]].astype(FULL) + d1_r2[t, 1].astype(FULL)
        res[0, 0, :, third(t)] = total + d1_r3[t].astype(FULL)
    tgrad_ref[...] = tgrad_ref[...] + norm_back(unit_one, scale_one, res[0, 0] * gn[0:1, :])
    deliver(5, tgrad_ref, tgrad_out)
    for which in range(2):
        arrive(gy_in.at[which], r_gy.at[which])
    lane = lax.broadcasted_iota(jnp.int32, (48, 128), 1)
    sums = gy[...] + gy_in[...]
    sums = jnp.where(lane == 0, sums[0], sums[1]).T
    count = gain_a.shape[1]
    sums = jnp.where(y == 0, sums[0:2, :count], sums[0:2, count : 2 * count])
    gains_ref[...] = jnp.zeros_like(gains_ref)
    gains_ref[0:2, 0:count] = sums / gain_ref[0:2, 0:count]
    deliver(6, gains_ref, gains_out)
    for copy in delivered:
        copy.wait()
    for when, copy in pending:
        if when is None:
            copy.wait_send()
        else:
            pl.when(when)(copy.wait_send)


def hand_on(*refs):
    sources, results, held, sems = refs[:7], refs[7:15], refs[15:21], refs[21]
    count = results[6].shape[1]
    results[6][...] = sources[6][0:1, :count]
    results[7][...] = sources[6][1:2, :count]
    inward = [pltpu.make_async_copy(a, b, sems.at[0, k]) for k, (a, b) in enumerate(zip(sources[:6], held))]
    outward = [pltpu.make_async_copy(a, b, sems.at[1, k]) for k, (a, b) in enumerate(zip(held, results[:6]))]
    for copy in inward:
        copy.start()
    for first, second in zip(inward, outward):
        first.wait()
        second.start()
    for copy in outward:
        copy.wait()


def on_device_fast(tokens, out_grad, short_lengths, attn_gain, qkv_weight, out_weight, mlp_gain, in_weight, down_weight):
    rows, width = tokens.shape
    depth = qkv_weight.shape[0]
    heads_here = qkv_weight.shape[2] // HEAD_DIM
    count = attn_gain.shape[0]
    ff = in_weight.shape[2] // 2 * 3
    feats = out_weight.shape[0]

    def vm(shape, kind=LOW):
        return pltpu.VMEM(shape, kind)

    def sem(*shape):
        return pltpu.SemaphoreType.DMA(shape)

    finals = [
        ((rows, width), LOW), ((rows, width), FULL), ((8, 128), FULL), ((3, depth, 384), FULL),
        ((depth, feats), FULL), ((depth, 2, 576), FULL), ((depth, 576), FULL),
    ]
    scratch = [vm(*shape) for shape in finals] + [
        vm((rows, width)), vm((rows, width)), vm((3, depth, 384)), vm((depth, feats)), vm((depth, 2, 576)), vm((depth, 576)),
        vm((8, 128), FULL), vm((heads_here // 2, depth, 384)), vm((2, depth, ff)),
        vm((2, 2, 2, 2, 64, 768)), vm((2, 2, 2, 2, 2, 8, 128), FULL), vm((8, 768), FULL), vm((2, 2, 64, 768)),
        vm((2, 8, 48, 384)), vm((8, 2, 48, 192)), vm((192, 768)), vm((4, 2, 2, 48, 864)), vm((4, 2, 2, 48, 768)), vm((1024, 768)),
        vm((3, 32, 1024), FULL), vm((128, 1024)), vm((1024, 128)), vm((64, 1024)), vm((64, 1024)), vm((1024, 64)),
        vm((1024, 1024)), vm((4, 64, 256), FULL), vm((4, 64, 256)), vm((2, 3, 2, 64, 256)), vm((2, 2, 64, 768), FULL),
        vm((2, 2, 2, 64, 768)), vm((2, 2, 2, 64, 384)), vm((2, 2, 64, 384)), vm((2, 2, 64, 384)), vm((3, 64, 768)), vm((2, 2, 64, 768)),
        vm((2, 3, 64, 128)), vm((2, 2, 2, 2, 64, 128)), vm((64, 1024)), vm((1024, 1024)), vm((192, 1024)),
        vm((1024, 192)), vm((2, 2, 2, 2, 64, 768)), vm((2, 2, 2, 64, 768)), vm((2, 2, 2, 64, 768)),
        vm((3, 2, 2, 64, 256)), vm((3, 2, 2, 64, 256)), vm((3, 2, 64, 256)), vm((3, 64, 256)), vm((3, 64, 256)),
        vm((2, 8, 48, 192)), vm((8, 48, 192)), vm((8, 48, 384)), vm((6, 48, 384)),
        vm((4, 2, 2, 48, 864)), vm((4, 2, 48, 864)), vm((4, 2, 48, 864)), vm((2, 2, 48, 864)), vm((2, 48, 864)),
        vm((2, 48, 864), FULL), vm((48, 864)), vm((48, 864)),
        vm((4, 2, 2, 48, 192)), vm((4, 2, 48, 192)), vm((4, 2, 48, 192)), vm((7, 48, 192)),
        vm((2, 48, 128), FULL), vm((2, 48, 128), FULL),
        sem(4, 3), sem(4, 3), sem(11), sem(11), sem(8), sem(8), sem(6), sem(6), sem(12), sem(12), sem(7), sem(7),
        sem(4, 4), sem(3, 2, 2), sem(2, 2, 2), sem(2, 2, 2), sem(3), sem(3), sem(12), sem(16), sem(4, 6), sem(4, 6),
        sem(8), sem(7), sem(4, 4), sem(4, 4), sem(8), sem(8), sem(2), sem(2), sem(7), sem(6),
    ]
    vmem = pl.BlockSpec(memory_space=pltpu.VMEM)
    anywhere = pl.BlockSpec(memory_space=pl.ANY)
    shapes = [jax.ShapeDtypeStruct(*shape) for shape in finals]
    mixed, tokens_grad, gains, qkv_grad, out_grads, in_grad, down_grad = pl.pallas_call(
        whole_layer,
        out_shape=shapes,
        in_specs=[pl.BlockSpec(memory_space=pltpu.SMEM)] + [vmem] * 2 + [anywhere] * 6,
        out_specs=[anywhere] * 7,
        scratch_shapes=scratch,
        compiler_params=pltpu.CompilerParams(collective_id=0, has_side_effects=True, vmem_limit_bytes=60 << 20),
    )(
        short_lengths, attn_gain[None], mlp_gain[None], tokens, out_grad,
        qkv_weight.transpose(1, 0, 2), out_weight.T, in_weight, down_weight.T,
    )
    grads = (mixed, tokens_grad, qkv_grad, out_grads, in_grad, down_grad)
    count = attn_gain.shape[0]
    mixed, tokens_grad, qkv_grad, out_grads, in_grad, down_grad, attn_gain_grad, mlp_gain_grad = pl.pallas_call(
        hand_on,
        out_shape=[jax.ShapeDtypeStruct(a.shape, a.dtype) for a in grads] + [jax.ShapeDtypeStruct((1, count), FULL)] * 2,
        in_specs=[anywhere] * 6 + [vmem],
        out_specs=[anywhere] * 6 + [vmem] * 2,
        scratch_shapes=[vm(a.shape, a.dtype) for a in grads] + [sem(2, 6)],
    )(*grads, gains)
    return (
        mixed, tokens_grad, attn_gain_grad[0], qkv_grad.transpose(1, 0, 2), out_grads.T, mlp_gain_grad[0],
        in_grad, down_grad.T,
    )


def solution(mesh):
    placed = (
        P(("seq", "head"), None),
        P(("seq", "head"), None),
        P(),
        P(("seq", "head")),
        P("seq", None, "head"),
        P("head", "seq"),
        P(("seq", "head")),
        P("seq", None, "head"),
        P("head", "seq"),
    )
    fits = mesh.shape["seq"] == 16 and mesh.shape["head"] == 2
    return jax.shard_map(
        on_device_fast if fits else on_device,
        mesh=mesh,
        in_specs=placed,
        out_specs=(
            P(("seq", "head"), None),
            P(("seq", "head"), None),
            P(("seq", "head")),
            P("seq", None, "head"),
            P("head", "seq"),
            P(("seq", "head")),
            P("seq", None, "head"),
            P("head", "seq"),
        ),
        check_vma=False,
    )
```
